32 devices in a mesh: gx: 16 (over z, y, x), gy: 2 (over core).
Axes of the slice: x: 2, y: 2, z: 4, core: 2. Of those that a mesh axis runs over, the one named last changes fastest.
Arguments:
- velocity: float32 [512, 64, 128], P('gx', 'gy'), may hold values from -6 to 6
Outputs:
- coefficients: float32 [512, 64, 128], P('gx', 'gy')
The draws below stay inside these ranges and needn't reach their ends.
All inputs are finite; a program needn't handle non-finite values.
Results may differ from the reference program's by a relative error of at most 0.00002.
Values sent between devices are 32-bit elements; how exact they have to be, the bound alone decides.
No kernel may reach another device: no remote copies, remote signals or barrier semaphores. Data moves between devices by JAX's collectives and lax.ppermute only.
A program may use at most 128 MiB of HBM per device.

```python
import jax
import jax.numpy as jnp
from jax import lax

NZ = 128
LEVELS = 4
NX = 512
NY = 64


def shard_levels(rng, extent, shards, least, high):
    level, own = 1.0, jax.random.fold_in(rng, 6)
    for dim, shards_of in shards:
        draws = jnp.exp(jax.random.uniform(jax.random.fold_in(own, dim), (shards_of,), jnp.float32, least / len(shards), high / len(shards)))
        level = level * jnp.repeat(draws, extent[dim] // shards_of).reshape([-1 if axis == dim else 1 for axis in range(len(extent))])
    return level


def normal_values(stream_key, dims, spread, bound, shards=(), dtype=jnp.bfloat16):
    result = jax.random.normal(stream_key, dims, jnp.float32) * spread
    if len(shards) > 0:
        result = shard_levels(stream_key, dims, shards, -0.22, 0.18) * result
    return jnp.clip(result, min=-bound, max=bound).astype(dtype)


def setup_inputs(seed: int = 0) -> dict:
    key_of = jax.random.split(jax.random.key(seed), 2)
    velocity = normal_values(key_of[0], (NX, NY, NZ), 1.0, 6.0, ((0, 16), (1, 2)), jnp.float32)
    return dict(velocity=velocity)


lift_alpha = -1.586134342
lift_beta = -0.05298011854
lift_gamma = 0.8829110762
lift_delta = 0.4435068522
lift_scale = 1.149604398


def lift_core(even, odd, forward, backward):
    odd = odd + lift_alpha * (even + forward(even))
    even = even + lift_beta * (backward(odd) + odd)
    odd = odd + lift_gamma * (even + forward(even))
    even = even + lift_delta * (backward(odd) + odd)
    return even / lift_scale, odd * lift_scale


def periodic_split(array, axis):
    count = array.shape[axis]
    even = lax.slice_in_dim(array, 0, count, 2, axis)
    odd = lax.slice_in_dim(array, 1, count, 2, axis)

    def forward(values):
        return jnp.roll(values, -1, axis)

    def backward(values):
        return jnp.roll(values, 1, axis)

    return lift_core(even, odd, forward, backward)


def split_level(array):
    low, high = periodic_split(array, 0)
    bands = jnp.stack([low, high])
    low, high = periodic_split(bands, 2)
    bands = jnp.stack([low, high])
    low, high = periodic_split(bands, 4)
    return jnp.stack([low, high])


def alternate(bands):
    size_x, size_y, size_z = bands.shape[3], bands.shape[4], bands.shape[5]
    return jnp.transpose(bands, (3, 2, 4, 1, 5, 0)).reshape(2 * size_x, 2 * size_y, 2 * size_z)


def decompose(array, level):
    bands = split_level(array)
    if level < LEVELS:
        coarse = decompose(bands[0, 0, 0], level + 1)
        bands = bands.at[0, 0, 0].set(coarse)
    return alternate(bands)


def reference(velocity):
    return decompose(velocity, 1)
```

```python
import functools

import jax
import jax.numpy as jnp
from jax import lax
from jax.experimental import pallas as pl
from jax.experimental.pallas import tpu as pltpu
from jax.sharding import PartitionSpec as P

LEVELS = 4
STEPS = (-1.586134342, -0.05298011854, 0.8829110762, 0.4435068522)
SCALE = 1.149604398
VMEM_BYTES = 48 * 2**20


def windows(block):
    found = []
    first, last = 0, block - 1
    for _ in range(LEVELS):
        low = first - 4 + (first % 2)
        high = last + 4 - (last % 2)
        found.append((low, high))
        first, last = low // 2, high // 2
    return found


def segments(block, rows, to):
    found, at = [], 0
    for level, (low, high) in enumerate(windows(block)):
        size, height = block >> level, rows >> level
        start, stop = max(low, to * size), min(high + 1, (to + 1) * size)
        if start < stop:
            found.append((level, start, stop, at))
            at += (stop - start) * height
    return found, -(-at // 8) * 8


def places_of(block):
    found = set()
    for level, (low, high) in enumerate(windows(block)):
        size = block >> level
        found |= set(range(low // size, high // size + 1))
    return sorted(found - {0})


def lanes_of(width, spacing, parity):
    lane = lax.broadcasted_iota(jnp.int32, (1, width), 1)
    return lax.rem(lane, 2 * spacing) == (spacing if parity else 0)


def z_lift(value, spacing):
    width = value.shape[-1]
    axis = value.ndim - 1
    for step, weight in enumerate(STEPS):
        factor = jnp.where(lanes_of(width, spacing, step % 2 == 0), weight, 0.0)
        around = pltpu.roll(value, spacing, axis) + pltpu.roll(value, width - spacing, axis)
        value = value + factor * around
    return value


def x_lift(planes):
    def plus(one, other):
        return other if one is None else one if other is None else one + other

    planes = dict(planes)
    for step, weight in enumerate(STEPS):
        parity = 1 if step % 2 == 0 else 0
        for index in range(min(planes) - 1, max(planes) + 2):
            if index % 2 == parity:
                around = plus(planes.get(index - 1), planes.get(index + 1))
                if around is not None:
                    planes[index] = plus(planes.get(index), weight * around)
    return planes


def y_lift_split(even, odd):
    count = even.shape[0]
    a, b, c, d = STEPS
    odd = odd + a * (even + pltpu.roll(even, count - 1, 0))
    even = even + b * (pltpu.roll(odd, 1, 0) + odd)
    odd = odd + c * (even + pltpu.roll(even, count - 1, 0))
    even = even + d * (pltpu.roll(odd, 1, 0) + odd)
    return even, odd


def y_lift_whole(value):
    count = value.shape[0]
    row = lax.broadcasted_iota(jnp.int32, (count, 1), 0)
    for step, weight in enumerate(STEPS):
        factor = jnp.where(lax.rem(row, 2) == (1 if step % 2 == 0 else 0), weight, 0.0)
        value = value + factor * (pltpu.roll(value, 1, 0) + pltpu.roll(value, count - 1, 0))
    return value


def scale_of(width, spacing, x_odd, y_odd):
    at = (SCALE if x_odd else 1 / SCALE) * (SCALE if y_odd else 1 / SCALE)
    odd = lanes_of(width, spacing, True)
    even = lanes_of(width, spacing, False)
    return jnp.where(odd, at * SCALE, jnp.where(even, at / SCALE, 0.0))


def split_kernel(block, rows, width, count, places, *refs):
    blocks = refs[:count]
    own = refs[count]
    messages = dict(zip(places, refs[count + 1 : count + 1 + len(places)]))
    work = refs[count + 1 + len(places) :]
    lifted, coarse = work[:LEVELS], work[LEVELS:]
    spans = windows(block)
    total = count * rows

    def targets(level, plane):
        size = block >> level
        to = plane // size
        if to == 0:
            return None, 0
        for found, start, stop, at in segments(block, rows, to)[0]:
            if found == level and start <= plane < stop:
                return to, at + (plane - start) * (rows >> level)
        raise ValueError(plane)

    def put(level, plane, even, odd, ranges):
        height = rows >> level
        spacing = 1 << level
        if level < LEVELS - 1 and plane % 2 == 0:
            even = jnp.where(lanes_of(width, spacing, True), even, 0.0)
        to, at = targets(level, plane)
        if to is None:
            if level == 0:
                own[plane, pl.ds(0, height // 2, 2), :] = even
                own[plane, pl.ds(1, height // 2, 2), :] = odd
            else:
                x = plane * spacing
                own[x, pl.ds(0, height // 2, 2 * spacing), :] += even
                own[x, pl.ds(spacing, height // 2, 2 * spacing), :] += odd
        else:
            messages[to][pl.ds(at, height // 2, 2), :] = even
            messages[to][pl.ds(at + 1, height // 2, 2), :] = odd

    for to in places:
        parts, length = segments(block, rows, to)
        level, start, stop, at = parts[-1]
        used = at + (stop - start) * (rows >> level)
        if used < length:
            messages[to][length - 8 : length, :] = jnp.zeros((8, width), jnp.float32)

    for level in range(LEVELS):
        low, high = spans[level]
        spacing = 1 << level
        height = total >> level
        into = lifted[level]

        if level == 0:
            for part in range(count):
                def tile(index, carry, part=part):
                    at = pl.multiple_of(index * 8, 8)
                    planes = {
                        x: z_lift(blocks[part][x, pl.ds(at, 8), :], spacing) for x in range(block)
                    }
                    for x, value in x_lift(planes).items():
                        into[x - low, pl.ds(pl.multiple_of(part * rows + at, 8), 8), :] = value
                    return carry

                lax.fori_loop(0, rows // 8, tile, 0)
        else:
            first, last = spans[level - 1][0] // 2, spans[level - 1][1] // 2
            for at in range(0, height, 8):
                planes = {
                    x: z_lift(coarse[level - 1][x - first, at : at + 8, :], spacing)
                    for x in range(first, last + 1)
                }
                for x, value in x_lift(planes).items():
                    into[x - low, at : at + 8, :] = value

        for plane in range(low, high + 1):
            odd_plane = plane % 2 == 1
            at = plane - low
            mine = rows >> level
            even_scale = scale_of(width, spacing, odd_plane, False)
            odd_scale = scale_of(width, spacing, odd_plane, True)
            if (height // 2) % 8 == 0:
                even, odd = y_lift_split(
                    into[at, pl.ds(0, height // 2, 2), :], into[at, pl.ds(1, height // 2, 2), :]
                )
                if level < LEVELS - 1 and not odd_plane:
                    even = even * even_scale
                    coarse[level][(plane - low) // 2] = even
                    even = even[: mine // 2]
                else:
                    even = even[: mine // 2] * even_scale
                put(level, plane, even, odd[: mine // 2] * odd_scale, None)
            else:
                into[at] = y_lift_whole(into[at])
                even = into[at, pl.ds(0, height // 2, 2), :] * even_scale
                odd = into[at, pl.ds(1, mine // 2, 2), :] * odd_scale
                if level < LEVELS - 1 and not odd_plane:
                    coarse[level][(plane - low) // 2] = even
                put(level, plane, even[: mine // 2], odd, None)


def add_kernel(block, rows, width, places, *refs):
    own, received, out = refs[0], refs[1:-1], refs[-1]
    out[...] = own[...]
    for to, message in zip(places, received):
        for level, start, stop, at in segments(block, rows, to)[0]:
            spacing, height = 1 << level, rows >> level
            for plane in range(start, stop):
                x = (plane - to * (block >> level)) * spacing
                here = at + (plane - start) * height
                out[x, pl.ds(0, height, spacing), :] += message[here : here + height, :]


def local(velocity):
    block, rows, width = velocity.shape
    around, count = lax.axis_size("gx"), lax.axis_size("gy")
    places = places_of(block)
    spans = windows(block)
    total = count * rows

    blocks = [velocity] + [
        lax.ppermute(velocity, "gy", [(i, (i - k) % count) for i in range(count)])
        for k in range(1, count)
    ]
    lengths = {to: segments(block, rows, to)[1] for to in places}
    f32 = jnp.float32
    work = [
        pltpu.VMEM((high - low + 1, total >> level, width), f32)
        for level, (low, high) in enumerate(spans)
    ]
    work += [
        pltpu.VMEM(((high // 2) - (low // 2) + 1, total >> (level + 1), width), f32)
        for level, (low, high) in enumerate(spans[:-1])
    ]
    params = pltpu.CompilerParams(vmem_limit_bytes=VMEM_BYTES)
    vmem = pl.BlockSpec(memory_space=pltpu.VMEM)
    own, *messages = pl.pallas_call(
        functools.partial(split_kernel, block, rows, width, count, places),
        out_shape=[jax.ShapeDtypeStruct(velocity.shape, f32)]
        + [jax.ShapeDtypeStruct((lengths[to], width), f32) for to in places],
        in_specs=[vmem] * count,
        out_specs=[vmem] * (1 + len(places)),
        scratch_shapes=work,
        compiler_params=params,
        name="split_blocks",
    )(*blocks)

    sent = dict(zip(places, messages))
    received = {
        to: lax.ppermute(sent[to], "gx", [(i, (i + to) % around) for i in range(around)])
        for to in sorted(places, key=lambda to: (to < 0, abs(to)))
    }
    return pl.pallas_call(
        functools.partial(add_kernel, block, rows, width, places),
        out_shape=jax.ShapeDtypeStruct(velocity.shape, f32),
        in_specs=[vmem] * (1 + len(places)),
        out_specs=vmem,
        compiler_params=params,
        name="add_received",
    )(own, *[received[to] for to in places])


def solution(mesh):
    return jax.shard_map(
        local, mesh=mesh, in_specs=(P("gx", "gy", None),), out_specs=P("gx", "gy", None), check_vma=False
    )
```

```python
import functools

import jax
import jax.numpy as jnp
import ml_dtypes
import numpy as np
from jax import lax
from jax.experimental import pallas as pl
from jax.experimental.pallas import tpu as pltpu
from jax.sharding import PartitionSpec as P

LEVELS = 4
STEPS = (-1.586134342, -0.05298011854, 0.8829110762, 0.4435068522)
SCALE = 1.149604398
VMEM_BYTES = 24 * 2**20
BY_MATRIX = 2


def windows(block):
    found = []
    first, last = 0, block - 1
    for _ in range(LEVELS):
        low = first - 4 + (first % 2)
        high = last + 4 - (last % 2)
        found.append((low, high))
        first, last = low // 2, high // 2
    return found


def segments(block, rows, to):
    found, at = [], 0
    for level, (low, high) in enumerate(windows(block)):
        size, height = block >> level, rows >> level
        start, stop = max(low, to * size), min(high + 1, (to + 1) * size)
        if start < stop:
            found.append((level, start, stop, at))
            at += (stop - start) * height
    return found, -(-at // 8) * 8


def places_of(block):
    found = set()
    for level, (low, high) in enumerate(windows(block)):
        size = block >> level
        found |= set(range(low // size, high // size + 1))
    return sorted(found - {0})


def z_matrix(width, spacing):
    value = np.eye(width)[:, ::spacing]
    even, odd = value[:, 0::2], value[:, 1::2]
    a, b, c, d = STEPS
    odd = odd + a * (even + np.roll(even, -1, 1))
    even = even + b * (np.roll(odd, 1, 1) + odd)
    odd = odd + c * (even + np.roll(even, -1, 1))
    even = even + d * (np.roll(odd, 1, 1) + odd)
    full = np.zeros((width, width))
    full[:, :: 2 * spacing] = even / SCALE
    full[:, spacing :: 2 * spacing] = odd * SCALE
    return full


def z_weights(width, spacing):
    full = z_matrix(width, spacing)
    high = full.astype(ml_dtypes.bfloat16)
    rest = (full - high.astype(np.float64)).astype(ml_dtypes.bfloat16)
    return np.block([[high, rest], [high, np.zeros_like(rest)]])


def z_product(value, weights):
    width = value.shape[-1]
    high = value.astype(jnp.bfloat16)
    rest = (value - high.astype(jnp.float32)).astype(jnp.bfloat16)
    both = jnp.concatenate([high, rest], axis=1)
    product = jnp.dot(both, weights, preferred_element_type=jnp.float32)
    return product[:, :width] + product[:, width:]


def lanes_of(width, spacing, parity):
    lane = lax.broadcasted_iota(jnp.int32, (1, width), 1)
    return lax.rem(lane, 2 * spacing) == (spacing if parity else 0)


def z_lift(value, spacing):
    width = value.shape[-1]
    axis = value.ndim - 1
    for step, weight in enumerate(STEPS):
        factor = jnp.where(lanes_of(width, spacing, step % 2 == 0), weight, 0.0)
        around = pltpu.roll(value, spacing, axis) + pltpu.roll(value, width - spacing, axis)
        value = value + factor * around
    return value


def x_lift(planes):
    def plus(one, other):
        return other if one is None else one if other is None else one + other

    planes = dict(planes)
    for step, weight in enumerate(STEPS):
        parity = 1 if step % 2 == 0 else 0
        for index in range(min(planes) - 1, max(planes) + 2):
            if index % 2 == parity:
                around = plus(planes.get(index - 1), planes.get(index + 1))
                if around is not None:
                    planes[index] = plus(planes.get(index), weight * around)
    return planes


def y_lift_split(even, odd):
    count = even.shape[0]
    a, b, c, d = STEPS
    odd = odd + a * (even + pltpu.roll(even, count - 1, 0))
    even = even + b * (pltpu.roll(odd, 1, 0) + odd)
    odd = odd + c * (even + pltpu.roll(even, count - 1, 0))
    even = even + d * (pltpu.roll(odd, 1, 0) + odd)
    return even, odd


def y_lift_whole(value):
    count = value.shape[0]
    row = lax.broadcasted_iota(jnp.int32, (count, 1), 0)
    for step, weight in enumerate(STEPS):
        factor = jnp.where(lax.rem(row, 2) == (1 if step % 2 == 0 else 0), weight, 0.0)
        value = value + factor * (pltpu.roll(value, 1, 0) + pltpu.roll(value, count - 1, 0))
    return value


def scaled(value, level, x_odd, y_odd):
    at = (SCALE if x_odd else 1 / SCALE) * (SCALE if y_odd else 1 / SCALE)
    if level < BY_MATRIX:
        return value if x_odd != y_odd else value * at
    width, spacing = value.shape[-1], 1 << level
    odd, even = lanes_of(width, spacing, True), lanes_of(width, spacing, False)
    return value * jnp.where(odd, at * SCALE, jnp.where(even, at / SCALE, 0.0))


def lift_block(block, rows, source, weights, spread, into, low, base):
    width = source.shape[-1]
    step = min(block, max(1, 512 // rows))
    for x in range(0, block, step):
        value = source[x : x + step].reshape(step * rows, width)
        spread[x * rows : (x + step) * rows, :] = z_product(value, weights[...])
    for at in range(0, rows, 8):
        planes = {x: spread[x * rows + at : x * rows + at + 8, :] for x in range(block)}
        for x, value in x_lift(planes).items():
            into[x - low, base + at : base + at + 8, :] = value


def own_kernel(block, rows, velocity, weights, into, spread):
    lift_block(block, rows, velocity, weights, spread, into, windows(block)[0][0], 0)


def message_kernel(block, rows, width, count, places, *refs):
    refs = list(refs)

    def take(number):
        taken = refs[:number]
        del refs[:number]
        return taken

    (_,) = take(1)
    others = take(count - 1)
    weights = take(BY_MATRIX)
    (first,) = take(1)
    own = take(LEVELS)
    messages = dict(zip(places, take(len(places))))
    (spread,) = take(1)
    lifted = [first] + take(LEVELS - 1)
    coarse = take(LEVELS - 1)
    spans = windows(block)
    total = count * rows

    def put(level, plane, even, odd):
        half = (rows >> level) // 2
        spacing = 1 << level
        if level < LEVELS - 1 and plane % 2 == 0:
            even = jnp.where(lanes_of(width, spacing, True), even, 0.0)
        size = block >> level
        to = plane // size
        if to == 0:
            own[level][plane, pl.ds(0, half, 2), :] = even
            own[level][plane, pl.ds(1, half, 2), :] = odd
            return
        for found, start, stop, at in segments(block, rows, to)[0]:
            if found == level and start <= plane < stop:
                at += (plane - start) * (rows >> level)
                messages[to][pl.ds(at, half, 2), :] = even
                messages[to][pl.ds(at + 1, half, 2), :] = odd

    for to in places:
        parts, length = segments(block, rows, to)
        level, start, stop, at = parts[-1]
        if at + (stop - start) * (rows >> level) < length:
            messages[to][length - 8 : length, :] = jnp.zeros((8, width), jnp.float32)

    for level in range(LEVELS):
        low, high = spans[level]
        height = total >> level
        half, mine = height // 2, (rows >> level) // 2
        into = lifted[level]

        if level == 0:
            for part, source in enumerate(others):
                lift_block(block, rows, source, weights[0], spread, into, low, (part + 1) * rows)
        else:
            start, stop = spans[level - 1][0] // 2, spans[level - 1][1] // 2 + 1
            source = coarse[level - 1]
            if level < BY_MATRIX:
                size = (stop - start) * height
                for at in range(0, size, 512):
                    end = min(size, at + 512)
                    source[at:end, :] = z_product(source[at:end, :], weights[level][...])
            for at in range(0, height, 8):
                planes = {}
                for x in range(start, stop):
                    row = (x - start) * height + at
                    value = source[row : row + 8, :]
                    planes[x] = value if level < BY_MATRIX else z_lift(value, 1 << level)
                for x, value in x_lift(planes).items():
                    into[x - low, at : at + 8, :] = value

        for plane in range(low, high + 1):
            odd_plane = plane % 2 == 1
            if level == 0 and odd_plane and 0 <= plane < block:
                continue
            at = plane - low
            if half % 8 == 0:
                even, odd = y_lift_split(
                    into[at, pl.ds(0, half, 2), :], into[at, pl.ds(1, half, 2), :]
                )
            else:
                into[at] = y_lift_whole(into[at])
                even, odd = into[at, pl.ds(0, half, 2), :], into[at, pl.ds(1, half, 2), :]
            if level < LEVELS - 1 and not odd_plane:
                even = scaled(even, level, odd_plane, False)
                row = ((plane - low) // 2) * half
                coarse[level][row : row + half, :] = even
                even = even[:mine]
            else:
                even = scaled(even[:mine], level, odd_plane, False)
            put(level, plane, even, scaled(odd[:mine], level, odd_plane, True))


def rest_kernel(block, rows, width, first, kept, *refs):
    coarse, out = refs[:-1], refs[-1]
    low = windows(block)[0][0]
    half, mine = first.shape[1] // 2, rows // 2
    for plane in range(block):
        if plane % 2 == 1:
            even, odd = y_lift_split(
                first[plane - low, pl.ds(0, half, 2), :], first[plane - low, pl.ds(1, half, 2), :]
            )
            out[plane, pl.ds(0, mine, 2), :] = scaled(even[:mine], 0, True, False)
            out[plane, pl.ds(1, mine, 2), :] = scaled(odd[:mine], 0, True, True)
        else:
            out[plane] = kept[plane]
    for level in range(1, LEVELS):
        spacing = 1 << level
        for plane in range(block >> level):
            out[plane * spacing, pl.ds(0, rows >> level, spacing), :] += coarse[level - 1][plane]


def add_kernel(block, rows, places, *refs):
    own, received, out = refs[0], refs[1:-1], refs[-1]
    out[...] = own[...]
    for to, message in zip(places, received):
        for level, start, stop, at in segments(block, rows, to)[0]:
            spacing, height = 1 << level, rows >> level
            for plane in range(start, stop):
                x = (plane - to * (block >> level)) * spacing
                here = at + (plane - start) * height
                out[x, pl.ds(0, height, spacing), :] += message[here : here + height, :]


def call(body, name, outs, ins, scratch=(), aliases=None, flops=0):
    vmem = pl.BlockSpec(memory_space=pltpu.VMEM)
    f32 = jnp.float32
    shapes = [jax.ShapeDtypeStruct(shape, f32) for shape in outs]
    moved = 4 * sum(int(np.prod(shape)) for shape in outs)
    return pl.pallas_call(
        body,
        out_shape=shapes,
        in_specs=[vmem] * len(ins),
        out_specs=[vmem] * len(outs),
        scratch_shapes=[pltpu.VMEM(shape, f32) for shape in scratch],
        input_output_aliases=aliases or {},
        compiler_params=pltpu.CompilerParams(vmem_limit_bytes=VMEM_BYTES),
        cost_estimate=pl.CostEstimate(flops=flops, bytes_accessed=2 * moved, transcendentals=0),
        name=name,
    )(*ins)


def local(velocity):
    block, rows, width = velocity.shape
    around, count = lax.axis_size("gx"), lax.axis_size("gy")
    places = places_of(block)
    spans = windows(block)
    total = count * rows
    weights = [jnp.asarray(z_weights(width, 1 << level)) for level in range(BY_MATRIX)]

    others = [
        lax.ppermute(velocity, "gy", [(i, (i - k) % count) for i in range(count)])
        for k in range(1, count)
    ]
    lifted = [
        (high - low + 1, total >> level, width) for level, (low, high) in enumerate(spans)
    ]
    coarse = [
        ((high // 2 - low // 2 + 1) * (total >> (level + 1)), width)
        for level, (low, high) in enumerate(spans[:-1])
    ]
    spread = (block * rows, width)
    owned = [(block >> level, rows >> level, width) for level in range(LEVELS)]

    (first,) = call(
        functools.partial(own_kernel, block, rows),
        "lift_own",
        [lifted[0]],
        [velocity, weights[0]],
        [spread],
    )
    first, kept, *more = call(
        functools.partial(message_kernel, block, rows, width, count, places),
        "make_messages",
        [lifted[0]] + owned + [(segments(block, rows, to)[1], width) for to in places],
        [first] + others + weights,
        [spread] + lifted[1:] + coarse,
        {0: 0},
    )
    own_coarse, sent = more[: LEVELS - 1], dict(zip(places, more[LEVELS - 1 :]))
    received = {
        to: lax.ppermute(sent[to], "gx", [(i, (i + to) % around) for i in range(around)])
        for to in sorted(places, key=lambda to: (to < 0, abs(to)))
    }
    (result,) = call(
        functools.partial(rest_kernel, block, rows, width),
        "finish_own",
        [owned[0]],
        [first, kept] + own_coarse,
    )
    for side in (1, -1):
        here = [to for to in places if to * side > 0]
        (result,) = call(
            functools.partial(add_kernel, block, rows, here),
            "add_received",
            [owned[0]],
            [result] + [received[to] for to in here],
        )
    return result


def solution(mesh):
    return jax.shard_map(
        local, mesh=mesh, in_specs=(P("gx", "gy", None),), out_specs=P("gx", "gy", None), check_vma=False
    )
```

```python
import functools

import jax
import jax.numpy as jnp
import ml_dtypes
import numpy as np
from jax import lax
from jax.experimental import pallas as pl
from jax.experimental.pallas import tpu as pltpu
from jax.sharding import PartitionSpec as P

LEVELS = 4
STEPS = (-1.586134342, -0.05298011854, 0.8829110762, 0.4435068522)
SCALE = 1.149604398
VMEM_BYTES = 24 * 2**20
FIRST_FLOPS = 10**11
BY_MATRIX = 2


def windows(block):
    found = []
    first, last = 0, block - 1
    for _ in range(LEVELS):
        low = first - 4 + (first % 2)
        high = last + 4 - (last % 2)
        found.append((low, high))
        first, last = low // 2, high // 2
    return found


def segments(block, rows, to):
    found, at = [], 0
    for level, (low, high) in enumerate(windows(block)):
        size, height = block >> level, rows >> level
        start, stop = max(low, to * size), min(high + 1, (to + 1) * size)
        if start < stop:
            found.append((level, start, stop, at))
            at += (stop - start) * height
    return found, -(-at // 8) * 8


def places_of(block):
    found = set()
    for level, (low, high) in enumerate(windows(block)):
        size = block >> level
        found |= set(range(low // size, high // size + 1))
    return sorted(found - {0})


def z_matrix(width, spacing):
    value = np.eye(width)[:, ::spacing]
    even, odd = value[:, 0::2], value[:, 1::2]
    a, b, c, d = STEPS
    odd = odd + a * (even + np.roll(even, -1, 1))
    even = even + b * (np.roll(odd, 1, 1) + odd)
    odd = odd + c * (even + np.roll(even, -1, 1))
    even = even + d * (np.roll(odd, 1, 1) + odd)
    full = np.zeros((width, width))
    full[:, :: 2 * spacing] = even / SCALE
    full[:, spacing :: 2 * spacing] = odd * SCALE
    return full


def z_weights(width, spacing):
    full = z_matrix(width, spacing)
    high = full.astype(ml_dtypes.bfloat16)
    rest = (full - high.astype(np.float64)).astype(ml_dtypes.bfloat16)
    return np.block([[high, rest], [high, np.zeros_like(rest)]])


def z_product(value, weights):
    width = value.shape[-1]
    high = value.astype(jnp.bfloat16)
    rest = (value - high.astype(jnp.float32)).astype(jnp.bfloat16)
    both = jnp.concatenate([high, rest], axis=1)
    product = jnp.dot(both, weights, preferred_element_type=jnp.float32)
    return product[:, :width] + product[:, width:]


def lanes_of(width, spacing, parity):
    lane = lax.broadcasted_iota(jnp.int32, (1, width), 1)
    return lax.rem(lane, 2 * spacing) == (spacing if parity else 0)


def z_lift(value, spacing):
    width = value.shape[-1]
    axis = value.ndim - 1
    for step, weight in enumerate(STEPS):
        factor = jnp.where(lanes_of(width, spacing, step % 2 == 0), weight, 0.0)
        around = pltpu.roll(value, spacing, axis) + pltpu.roll(value, width - spacing, axis)
        value = value + factor * around
    return value


def x_lift(planes):
    def plus(one, other):
        return other if one is None else one if other is None else one + other

    planes = dict(planes)
    for step, weight in enumerate(STEPS):
        parity = 1 if step % 2 == 0 else 0
        for index in range(min(planes) - 1, max(planes) + 2):
            if index % 2 == parity:
                around = plus(planes.get(index - 1), planes.get(index + 1))
                if around is not None:
                    planes[index] = plus(planes.get(index), weight * around)
    return planes


def y_lift_split(even, odd):
    count = even.shape[0]
    a, b, c, d = STEPS
    odd = odd + a * (even + pltpu.roll(even, count - 1, 0))
    even = even + b * (pltpu.roll(odd, 1, 0) + odd)
    odd = odd + c * (even + pltpu.roll(even, count - 1, 0))
    even = even + d * (pltpu.roll(odd, 1, 0) + odd)
    return even, odd


def y_lift_whole(value):
    count = value.shape[0]
    row = lax.broadcasted_iota(jnp.int32, (count, 1), 0)
    for step, weight in enumerate(STEPS):
        factor = jnp.where(lax.rem(row, 2) == (1 if step % 2 == 0 else 0), weight, 0.0)
        value = value + factor * (pltpu.roll(value, 1, 0) + pltpu.roll(value, count - 1, 0))
    return value


def scaled(value, level, x_odd, y_odd):
    at = (SCALE if x_odd else 1 / SCALE) * (SCALE if y_odd else 1 / SCALE)
    if level < BY_MATRIX:
        return value if x_odd != y_odd else value * at
    width, spacing = value.shape[-1], 1 << level
    odd, even = lanes_of(width, spacing, True), lanes_of(width, spacing, False)
    return value * jnp.where(odd, at * SCALE, jnp.where(even, at / SCALE, 0.0))


def lift_block(block, rows, source, weights, spread, into, low, base):
    width = source.shape[-1]
    step = min(block, max(1, 512 // rows))
    for x in range(0, block, step):
        value = source[x : x + step].reshape(step * rows, width)
        spread[x * rows : (x + step) * rows, :] = z_product(value, weights[...])
    for at in range(0, rows, 8):
        planes = {x: spread[x * rows + at : x * rows + at + 8, :] for x in range(block)}
        for x, value in x_lift(planes).items():
            into[x - low, base + at : base + at + 8, :] = value


def own_kernel(block, rows, velocity, weights, into, spread):
    lift_block(block, rows, velocity, weights, spread, into, windows(block)[0][0], 0)


def message_kernel(block, rows, width, count, places, *refs):
    refs = list(refs)

    def take(number):
        taken = refs[:number]
        del refs[:number]
        return taken

    (_,) = take(1)
    others = take(count - 1)
    weights = take(BY_MATRIX)
    (first,) = take(1)
    own = take(LEVELS)
    messages = dict(zip(places, take(len(places))))
    (spread,) = take(1)
    lifted = [first] + take(LEVELS - 1)
    coarse = take(LEVELS - 1)
    spans = windows(block)
    total = count * rows

    def put(level, plane, even, odd):
        half = (rows >> level) // 2
        spacing = 1 << level
        if level < LEVELS - 1 and plane % 2 == 0:
            even = jnp.where(lanes_of(width, spacing, True), even, 0.0)
        size = block >> level
        to = plane // size
        if to == 0:
            own[level][plane, pl.ds(0, half, 2), :] = even
            own[level][plane, pl.ds(1, half, 2), :] = odd
            return
        for found, start, stop, at in segments(block, rows, to)[0]:
            if found == level and start <= plane < stop:
                at += (plane - start) * (rows >> level)
                messages[to][pl.ds(at, half, 2), :] = even
                messages[to][pl.ds(at + 1, half, 2), :] = odd

    for to in places:
        parts, length = segments(block, rows, to)
        level, start, stop, at = parts[-1]
        if at + (stop - start) * (rows >> level) < length:
            messages[to][length - 8 : length, :] = jnp.zeros((8, width), jnp.float32)

    for level in range(LEVELS):
        low, high = spans[level]
        height = total >> level
        half, mine = height // 2, (rows >> level) // 2
        into = lifted[level]

        if level == 0:
            for part, source in enumerate(others):
                lift_block(block, rows, source, weights[0], spread, into, low, (part + 1) * rows)
        else:
            start, stop = spans[level - 1][0] // 2, spans[level - 1][1] // 2 + 1
            source = coarse[level - 1]
            if level < BY_MATRIX:
                size = (stop - start) * height
                for at in range(0, size, 512):
                    end = min(size, at + 512)
                    source[at:end, :] = z_product(source[at:end, :], weights[level][...])
            for at in range(0, height, 8):
                planes = {}
                for x in range(start, stop):
                    row = (x - start) * height + at
                    value = source[row : row + 8, :]
                    planes[x] = value if level < BY_MATRIX else z_lift(value, 1 << level)
                for x, value in x_lift(planes).items():
                    into[x - low, at : at + 8, :] = value

        for plane in range(low, high + 1):
            odd_plane = plane % 2 == 1
            if level == 0 and odd_plane and 0 <= plane < block:
                continue
            at = plane - low
            if half % 8 == 0:
                even, odd = y_lift_split(
                    into[at, pl.ds(0, half, 2), :], into[at, pl.ds(1, half, 2), :]
                )
            else:
                into[at] = y_lift_whole(into[at])
                even, odd = into[at, pl.ds(0, half, 2), :], into[at, pl.ds(1, half, 2), :]
            if level < LEVELS - 1 and not odd_plane:
                even = scaled(even, level, odd_plane, False)
                row = ((plane - low) // 2) * half
                coarse[level][row : row + half, :] = even
                even = even[:mine]
            else:
                even = scaled(even[:mine], level, odd_plane, False)
            put(level, plane, even, scaled(odd[:mine], level, odd_plane, True))


def rest_kernel(block, rows, width, first, kept, *refs):
    coarse, out = refs[:-1], refs[-1]
    low = windows(block)[0][0]
    half, mine = first.shape[1] // 2, rows // 2
    for plane in range(block):
        if plane % 2 == 1:
            even, odd = y_lift_split(
                first[plane - low, pl.ds(0, half, 2), :], first[plane - low, pl.ds(1, half, 2), :]
            )
            out[plane, pl.ds(0, mine, 2), :] = scaled(even[:mine], 0, True, False)
            out[plane, pl.ds(1, mine, 2), :] = scaled(odd[:mine], 0, True, True)
        else:
            out[plane] = kept[plane]
    for level in range(1, LEVELS):
        spacing = 1 << level
        for plane in range(block >> level):
            out[plane * spacing, pl.ds(0, rows >> level, spacing), :] += coarse[level - 1][plane]


def add_kernel(block, rows, places, *refs):
    own, received, out = refs[0], refs[1:-1], refs[-1]
    out[...] = own[...]
    for to, message in zip(places, received):
        for level, start, stop, at in segments(block, rows, to)[0]:
            spacing, height = 1 << level, rows >> level
            for plane in range(start, stop):
                x = (plane - to * (block >> level)) * spacing
                here = at + (plane - start) * height
                out[x, pl.ds(0, height, spacing), :] += message[here : here + height, :]


def call(body, name, outs, ins, scratch=(), aliases=None, flops=0):
    vmem = pl.BlockSpec(memory_space=pltpu.VMEM)
    f32 = jnp.float32
    shapes = [jax.ShapeDtypeStruct(shape, f32) for shape in outs]
    moved = 4 * sum(int(np.prod(shape)) for shape in outs)
    return pl.pallas_call(
        body,
        out_shape=shapes,
        in_specs=[vmem] * len(ins),
        out_specs=[vmem] * len(outs),
        scratch_shapes=[pltpu.VMEM(shape, f32) for shape in scratch],
        input_output_aliases=aliases or {},
        compiler_params=pltpu.CompilerParams(vmem_limit_bytes=VMEM_BYTES),
        cost_estimate=pl.CostEstimate(flops=flops, bytes_accessed=2 * moved, transcendentals=0),
        name=name,
    )(*ins)


def local(velocity):
    block, rows, width = velocity.shape
    around, count = lax.axis_size("gx"), lax.axis_size("gy")
    places = places_of(block)
    spans = windows(block)
    total = count * rows
    weights = [jnp.asarray(z_weights(width, 1 << level)) for level in range(BY_MATRIX)]

    others = [
        lax.ppermute(velocity, "gy", [(i, (i - k) % count) for i in range(count)])
        for k in range(1, count)
    ]
    lifted = [
        (high - low + 1, total >> level, width) for level, (low, high) in enumerate(spans)
    ]
    coarse = [
        ((high // 2 - low // 2 + 1) * (total >> (level + 1)), width)
        for level, (low, high) in enumerate(spans[:-1])
    ]
    spread = (block * rows, width)
    owned = [(block >> level, rows >> level, width) for level in range(LEVELS)]

    (first,) = call(
        functools.partial(own_kernel, block, rows),
        "lift_own",
        [lifted[0]],
        [velocity, weights[0]],
        [spread],
    )
    first, kept, *more = call(
        functools.partial(message_kernel, block, rows, width, count, places),
        "make_messages",
        [lifted[0]] + owned + [(segments(block, rows, to)[1], width) for to in places],
        [first] + others + weights,
        [spread] + lifted[1:] + coarse,
        {0: 0},
    )
    own_coarse, sent = more[: LEVELS - 1], dict(zip(places, more[LEVELS - 1 :]))
    received = {
        to: lax.ppermute(sent[to], "gx", [(i, (i + to) % around) for i in range(around)])
        for to in sorted(places, key=lambda to: (to < 0, abs(to)))
    }
    (result,) = call(
        functools.partial(rest_kernel, block, rows, width),
        "finish_own",
        [owned[0]],
        [first, kept] + own_coarse,
    )
    for side in (1, -1):
        here = [to for to in places if to * side > 0]
        (result,) = call(
            functools.partial(add_kernel, block, rows, here),
            "add_received",
            [owned[0]],
            [result] + [received[to] for to in here],
            flops=FIRST_FLOPS if side > 0 else 0,
        )
    return result


def solution(mesh):
    return jax.shard_map(
        local, mesh=mesh, in_specs=(P("gx", "gy", None),), out_specs=P("gx", "gy", None), check_vma=False
    )
```

```python
import functools

import jax
import jax.numpy as jnp
import numpy as np
from jax import lax
from jax.experimental import pallas as pl
from jax.experimental.pallas import tpu as pltpu
from jax.sharding import PartitionSpec as P

LEVELS = 4
STEPS = (-1.586134342, -0.05298011854, 0.8829110762, 0.4435068522)
SCALE = 1.149604398
VMEM_BYTES = 24 * 2**20
FIRST_FLOPS = 10**11
COPIES = 2
BY_MATRIX = 2


def windows(block):
    found = []
    first, last = 0, block - 1
    for _ in range(LEVELS):
        low = first - 4 + (first % 2)
        high = last + 4 - (last % 2)
        found.append((low, high))
        first, last = low // 2, high // 2
    return found


def message(block, rows, to):
    sent, derived = {}, {}
    spans = windows(block)
    base = ends = 0
    for level, (low, high) in enumerate(spans):
        size, height = block >> level, rows >> level
        first, last = (0, block - 1) if level == 0 else (v // 2 for v in spans[level - 1])
        planes = [p for p in range(low, high + 1) if p // size == to]
        if abs(to) == 1:
            sign = to
            edge = last + 2 - last % 2 if to > 0 else first - 2 + first % 2
            far, near = edge + sign, edge - sign
            if far in planes and edge + 2 * sign in planes:
                derived[level, edge + 2 * sign] = (far, None)
            if far in planes and near in planes:
                derived[level, edge] = (far, near)
        at = base
        for plane in planes:
            if (level, plane) not in derived:
                sent[level, plane] = at
                at += height
        ends = max(ends, at)
        if level == 0:
            base = at
    return sent, derived, -(-ends // 8) * 8


def shift_of(level):
    return (0, 0, 1, 3)[level]


def places_of(block):
    found = set()
    for level, (low, high) in enumerate(windows(block)):
        size = block >> level
        found |= set(range(low // size, high // size + 1))
    return sorted(found - {0})


def z_product(value, weights):
    width = value.shape[-1]
    high = value.astype(jnp.bfloat16)
    rest = (value - high.astype(jnp.float32)).astype(jnp.bfloat16)
    both = jnp.concatenate([high, rest], axis=1)
    product = jnp.dot(both, weights, preferred_element_type=jnp.float32)
    return product[:, :width] + product[:, width:]


def lanes_of(width, spacing, parity):
    lane = lax.broadcasted_iota(jnp.int32, (1, width), 1)
    return lax.rem(lane, 2 * spacing) == (spacing if parity else 0)


def z_lift(value, spacing):
    width = value.shape[-1]
    axis = value.ndim - 1
    for step, weight in enumerate(STEPS):
        factor = jnp.where(lanes_of(width, spacing, step % 2 == 0), weight, 0.0)
        around = pltpu.roll(value, spacing, axis) + pltpu.roll(value, width - spacing, axis)
        value = value + factor * around
    return value


def x_lift(planes):
    def plus(one, other):
        return other if one is None else one if other is None else one + other

    planes = dict(planes)
    for step, weight in enumerate(STEPS):
        parity = 1 if step % 2 == 0 else 0
        for index in range(min(planes) - 1, max(planes) + 2):
            if index % 2 == parity:
                around = plus(planes.get(index - 1), planes.get(index + 1))
                if around is not None:
                    planes[index] = plus(planes.get(index), weight * around)
    return planes


def y_lift_split(even, odd):
    count = even.shape[0]
    a, b, c, d = STEPS
    odd = odd + a * (even + pltpu.roll(even, count - 1, 0))
    even = even + b * (pltpu.roll(odd, 1, 0) + odd)
    odd = odd + c * (even + pltpu.roll(even, count - 1, 0))
    even = even + d * (pltpu.roll(odd, 1, 0) + odd)
    return even, odd


def y_lift_whole(value):
    count = value.shape[0]
    row = lax.broadcasted_iota(jnp.int32, (count, 1), 0)
    for step, weight in enumerate(STEPS):
        factor = jnp.where(lax.rem(row, 2) == (1 if step % 2 == 0 else 0), weight, 0.0)
        value = value + factor * (pltpu.roll(value, 1, 0) + pltpu.roll(value, count - 1, 0))
    return value


def scaled_z(value, spacing, at):
    width = value.shape[-1]
    odd, even = lanes_of(width, spacing, True), lanes_of(width, spacing, False)
    return value * jnp.where(odd, at * SCALE, jnp.where(even, at / SCALE, 0.0))


def scaled(value, level, x_odd, y_odd):
    at = (SCALE if x_odd else 1 / SCALE) * (SCALE if y_odd else 1 / SCALE)
    if level < BY_MATRIX:
        return value if x_odd != y_odd else value * at
    return scaled_z(value, 1 << level, at)


def spread_z(source, weights, spread, rows, start, size):
    width = source.shape[-1]
    value = source[start : start + size].reshape(size * rows, width)
    spread[start * rows : (start + size) * rows, :] = z_product(value, weights[...])


def spread_x(block, rows, spread, into, low, base):
    for at in range(0, rows, 8):
        planes = {x: spread[x * rows + at : x * rows + at + 8, :] for x in range(block)}
        for x, value in x_lift(planes).items():
            into[x - low, base + at : base + at + 8, :] = value


def z_weights(width, spacing):
    row = lax.broadcasted_iota(jnp.int32, (width, width), 0)
    lane = lax.broadcasted_iota(jnp.int32, (width, width), 1)
    full = scaled_z(z_lift(jnp.where(row == lane, 1.0, 0.0), spacing), spacing, 1.0)
    high = full.astype(jnp.bfloat16)
    rest = (full - high.astype(jnp.float32)).astype(jnp.bfloat16)
    return high, rest


def own_kernel(block, rows, velocity, into, *refs):
    weights, spread, held, arrived = refs[:BY_MATRIX], *refs[BY_MATRIX:]
    width = held.shape[-1]
    parts = arrived.shape[0]
    size = block // parts
    copies = [
        pltpu.make_async_copy(
            velocity.at[pl.ds(part * size, size)], held.at[pl.ds(part * size, size)], arrived.at[part]
        )
        for part in range(parts)
    ]
    for copy in copies:
        copy.start()
    for level, weight in enumerate(weights):
        high, rest = z_weights(width, 1 << level)
        weight[:width, :width] = high
        weight[:width, width:] = rest
        weight[width:, :width] = high
        weight[width:, width:] = jnp.zeros_like(rest)
    for part, copy in enumerate(copies):
        copy.wait()
        spread_z(held, weights[0], spread, rows, part * size, size)
    spread_x(block, rows, spread, into, windows(block)[0][0], 0)


def message_kernel(block, rows, width, count, places, *refs):
    refs = list(refs)

    def take(number):
        taken = refs[:number]
        del refs[:number]
        return taken

    (_,) = take(1)
    others = take(count - 1)
    weights = take(BY_MATRIX)
    (first,) = take(1)
    own = take(LEVELS)
    messages = dict(zip(places, take(len(places))))
    (spread,) = take(1)
    lifted = [first] + take(LEVELS - 1)
    coarse = take(LEVELS - 1)
    spans = windows(block)
    total = count * rows

    tables = {to: message(block, rows, to) for to in places}
    written = {to: set() for to in places}

    def post(to, at, half, value):
        here = range(at, at + 2 * half, 2)
        if written[to].isdisjoint(here):
            messages[to][pl.ds(at, half, 2), :] = value
        else:
            messages[to][pl.ds(at, half, 2), :] += value
        written[to].update(here)

    def put(level, plane, even, odd):
        half = (rows >> level) // 2
        spacing = 1 << level
        if level < LEVELS - 1 and plane % 2 == 0:
            even = jnp.where(lanes_of(width, spacing, True), even, 0.0)
        to = plane // (block >> level)
        if to == 0:
            own[level][plane, pl.ds(0, half, 2), :] = even
            own[level][plane, pl.ds(1, half, 2), :] = odd
        elif (level, plane) in tables[to][0]:
            at, shift = tables[to][0][level, plane], shift_of(level)
            post(to, at, half, pltpu.roll(even, shift, 1) if shift else even)
            post(to, at + 1, half, pltpu.roll(odd, shift, 1) if shift else odd)

    for level in range(LEVELS):
        low, high = spans[level]
        height = total >> level
        half, mine = height // 2, (rows >> level) // 2
        into = lifted[level]

        if level == 0:
            for part, source in enumerate(others):
                step = min(block, max(1, 512 // rows))
                for x in range(0, block, step):
                    spread_z(source, weights[0], spread, rows, x, step)
                spread_x(block, rows, spread, into, low, (part + 1) * rows)
        else:
            start, stop = spans[level - 1][0] // 2, spans[level - 1][1] // 2 + 1
            source = coarse[level - 1]
            if level < BY_MATRIX:
                size = (stop - start) * height
                for at in range(0, size, 512):
                    end = min(size, at + 512)
                    source[at:end, :] = z_product(source[at:end, :], weights[level][...])
            for at in range(0, height, 8):
                planes = {}
                for x in range(start, stop):
                    row = (x - start) * height + at
                    value = source[row : row + 8, :]
                    planes[x] = value if level < BY_MATRIX else z_lift(value, 1 << level)
                for x, value in x_lift(planes).items():
                    into[x - low, at : at + 8, :] = value

        for plane in range(low, high + 1):
            odd_plane = plane % 2 == 1
            if level == 0 and odd_plane and 0 <= plane < block:
                continue
            at = plane - low
            if half % 8 == 0:
                even, odd = y_lift_split(
                    into[at, pl.ds(0, half, 2), :], into[at, pl.ds(1, half, 2), :]
                )
            else:
                into[at] = y_lift_whole(into[at])
                even, odd = into[at, pl.ds(0, half, 2), :], into[at, pl.ds(1, half, 2), :]
            if level < LEVELS - 1 and not odd_plane:
                even = scaled(even, level, odd_plane, False)
                row = ((plane - low) // 2) * half
                coarse[level][row : row + half, :] = even
                even = even[:mine]
            else:
                even = scaled(even[:mine], level, odd_plane, False)
            put(level, plane, even, scaled(odd[:mine], level, odd_plane, True))

    for to in places:
        for row in range(tables[to][2]):
            if row not in written[to]:
                messages[to][row : row + 1, :] = jnp.zeros((1, width), jnp.float32)


def rest_kernel(block, rows, width, first, kept, *refs):
    coarse, out = refs[:-1], refs[-1]
    low = windows(block)[0][0]
    half, mine = first.shape[1] // 2, rows // 2
    for plane in range(block):
        if plane % 2 == 1:
            even, odd = y_lift_split(
                first[plane - low, pl.ds(0, half, 2), :], first[plane - low, pl.ds(1, half, 2), :]
            )
            out[plane, pl.ds(0, mine, 2), :] = scaled(even[:mine], 0, True, False)
            out[plane, pl.ds(1, mine, 2), :] = scaled(odd[:mine], 0, True, True)
        else:
            out[plane] = kept[plane]
    for level in range(1, LEVELS):
        spacing = 1 << level
        for plane in range(block >> level):
            out[plane * spacing, pl.ds(0, rows >> level, spacing), :] += coarse[level - 1][plane]


def add_kernel(block, rows, places, *refs):
    own, received, out = refs[0], refs[1 : 1 + len(places)], refs[1 + len(places)]
    clean = refs[2 + len(places) :]
    a, b, c, d = STEPS
    width = out.shape[-1]
    out[...] = own[...]

    for to, arrived in zip(places, received):
        sent, derived, length = message(block, rows, to)
        for level in sorted({level for level, _ in sent}):
            spacing, height = 1 << level, rows >> level
            shape = (height, width)
            if level > 0:
                here = [at for (found, _), at in sent.items() if found == level]
                start, stop = min(here), -(-(max(here) + height) // 8) * 8
                value = arrived[start:stop, :]
                if shift_of(level):
                    value = pltpu.roll(value, width - shift_of(level), 1)
                lane = lax.broadcasted_iota(jnp.int32, (1, width), 1)
                value = jnp.where(lax.rem(lane, spacing) == 0, value, 0.0)
                source = clean[level - 1]
                source[: stop - start, :] = value
            else:
                start, source = 0, arrived

            def read(plane):
                at = sent[level, plane] - start
                return source[at : at + height, :]

            def add(plane, value):
                x = (plane - to * (block >> level)) * spacing
                out[x, pl.ds(0, height, spacing), :] += value

            for found, plane in sent:
                if found == level:
                    add(plane, read(plane))
            for (found, plane), (far, near) in derived.items():
                if found == level:
                    if near is None:
                        value = (d / SCALE**2) * read(far)
                    else:
                        value = ((1 / c + d) / SCALE**2) * read(far) + (d / SCALE**2) * read(near)
                    row = lax.broadcasted_iota(jnp.int32, shape, 0)
                    keep = (lax.rem(row, 2) == 1) | lanes_of(width, spacing, True)
                    add(plane, jnp.where(keep, value, 0.0))


def call(body, name, outs, ins, scratch=(), aliases=None, flops=0, spaces=None):
    vmem = pl.BlockSpec(memory_space=pltpu.VMEM)
    f32 = jnp.float32
    shapes = [out if isinstance(out, jax.ShapeDtypeStruct) else jax.ShapeDtypeStruct(out, f32) for out in outs]
    moved = 4 * sum(int(np.prod(shape.shape)) for shape in shapes)
    return pl.pallas_call(
        body,
        out_shape=shapes,
        in_specs=spaces or [vmem] * len(ins),
        out_specs=[vmem] * len(outs),
        scratch_shapes=[pltpu.VMEM(shape, f32) if isinstance(shape, tuple) else shape for shape in scratch],
        input_output_aliases=aliases or {},
        compiler_params=pltpu.CompilerParams(vmem_limit_bytes=VMEM_BYTES),
        cost_estimate=pl.CostEstimate(flops=flops, bytes_accessed=2 * moved, transcendentals=0),
        name=name,
    )(*ins)


def local(velocity):
    block, rows, width = velocity.shape
    around, count = lax.axis_size("gx"), lax.axis_size("gy")
    places = places_of(block)
    spans = windows(block)
    total = count * rows

    others = [
        lax.ppermute(velocity, "gy", [(i, (i - k) % count) for i in range(count)])
        for k in range(1, count)
    ]
    lifted = [
        (high - low + 1, total >> level, width) for level, (low, high) in enumerate(spans)
    ]
    coarse = [
        ((high // 2 - low // 2 + 1) * (total >> (level + 1)), width)
        for level, (low, high) in enumerate(spans[:-1])
    ]
    spread = (block * rows, width)
    owned = [(block >> level, rows >> level, width) for level in range(LEVELS)]

    square = jax.ShapeDtypeStruct((2 * width, 2 * width), jnp.bfloat16)
    first, *weights = call(
        functools.partial(own_kernel, block, rows),
        "lift_own",
        [lifted[0]] + [square] * BY_MATRIX,
        [velocity],
        [spread, velocity.shape, pltpu.SemaphoreType.DMA((COPIES,))],
        spaces=[pl.BlockSpec(memory_space=pltpu.HBM)],
    )
    first, kept, *more = call(
        functools.partial(message_kernel, block, rows, width, count, places),
        "make_messages",
        [lifted[0]] + owned + [(message(block, rows, to)[2], width) for to in places],
        [first] + others + weights,
        [spread] + lifted[1:] + coarse,
        {0: 0},
    )
    own_coarse, sent = more[: LEVELS - 1], dict(zip(places, more[LEVELS - 1 :]))
    received = {
        to: lax.ppermute(sent[to], "gx", [(i, (i + to) % around) for i in range(around)])
        for to in sorted(places, key=lambda to: (to < 0, abs(to)))
    }
    (result,) = call(
        functools.partial(rest_kernel, block, rows, width),
        "finish_own",
        [owned[0]],
        [first, kept] + own_coarse,
    )
    for side in (1, -1):
        here = [to for to in places if to * side > 0]
        (result,) = call(
            functools.partial(add_kernel, block, rows, here),
            "add_received",
            [owned[0]],
            [result] + [received[to] for to in here],
            [(message(block, rows, side)[2], width)] * (LEVELS - 1),
            flops=FIRST_FLOPS if side > 0 else 0,
        )
    return result


def solution(mesh):
    return jax.shard_map(
        local, mesh=mesh, in_specs=(P("gx", "gy", None),), out_specs=P("gx", "gy", None), check_vma=False
    )
```

```python
import functools

import jax
import jax.numpy as jnp
import numpy as np
from jax import lax
from jax.experimental import pallas as pl
from jax.experimental.pallas import tpu as pltpu
from jax.sharding import PartitionSpec as P

LEVELS = 4
STEPS = (-1.586134342, -0.05298011854, 0.8829110762, 0.4435068522)
SCALE = 1.149604398
VMEM_BYTES = 24 * 2**20
ROUND_FLOPS = (6 * 10**8, 0)
PASS_FLOPS = 2 * 10**8
COPIES = 2
BY_MATRIX = 2


def windows(block):
    found = []
    first, last = 0, block - 1
    for _ in range(LEVELS):
        low = first - 4 + (first % 2)
        high = last + 4 - (last % 2)
        found.append((low, high))
        first, last = low // 2, high // 2
    return found


def message(block, rows, to):
    sent, derived = {}, {}
    spans = windows(block)
    base = ends = 0
    for level, (low, high) in enumerate(spans):
        size, height = block >> level, rows >> level
        first, last = (0, block - 1) if level == 0 else (v // 2 for v in spans[level - 1])
        planes = [p for p in range(low, high + 1) if p // size == to]
        if abs(to) == 1:
            sign = to
            edge = last + 2 - last % 2 if to > 0 else first - 2 + first % 2
            far, near = edge + sign, edge - sign
            if far in planes and edge + 2 * sign in planes:
                derived[level, edge + 2 * sign] = (far, None)
            if far in planes and near in planes:
                derived[level, edge] = (far, near)
        at = base
        for plane in planes:
            if (level, plane) not in derived:
                sent[level, plane] = at
                at += height
        ends = max(ends, at)
        if level == 0:
            base = at
    return sent, derived, -(-ends // 8) * 8


def shift_of(level):
    return (0, 0, 1, 3)[level]


def places_of(block):
    found = set()
    for level, (low, high) in enumerate(windows(block)):
        size = block >> level
        found |= set(range(low // size, high // size + 1))
    return sorted(found - {0})


def z_product(value, weights):
    width = value.shape[-1]
    high = value.astype(jnp.bfloat16)
    rest = (value - high.astype(jnp.float32)).astype(jnp.bfloat16)
    both = jnp.concatenate([high, rest], axis=1)
    product = jnp.dot(both, weights, preferred_element_type=jnp.float32)
    return product[:, :width] + product[:, width:]


def lanes_of(width, spacing, parity):
    lane = lax.broadcasted_iota(jnp.int32, (1, width), 1)
    return lax.rem(lane, 2 * spacing) == (spacing if parity else 0)


def z_lift(value, spacing):
    width = value.shape[-1]
    axis = value.ndim - 1
    for step, weight in enumerate(STEPS):
        factor = jnp.where(lanes_of(width, spacing, step % 2 == 0), weight, 0.0)
        around = pltpu.roll(value, spacing, axis) + pltpu.roll(value, width - spacing, axis)
        value = value + factor * around
    return value


def x_lift(planes):
    def plus(one, other):
        return other if one is None else one if other is None else one + other

    planes = dict(planes)
    for step, weight in enumerate(STEPS):
        parity = 1 if step % 2 == 0 else 0
        for index in range(min(planes) - 1, max(planes) + 2):
            if index % 2 == parity:
                around = plus(planes.get(index - 1), planes.get(index + 1))
                if around is not None:
                    planes[index] = plus(planes.get(index), weight * around)
    return planes


def y_lift_split(even, odd):
    count = even.shape[0]
    a, b, c, d = STEPS
    odd = odd + a * (even + pltpu.roll(even, count - 1, 0))
    even = even + b * (pltpu.roll(odd, 1, 0) + odd)
    odd = odd + c * (even + pltpu.roll(even, count - 1, 0))
    even = even + d * (pltpu.roll(odd, 1, 0) + odd)
    return even, odd


def y_lift_whole(value):
    count = value.shape[0]
    row = lax.broadcasted_iota(jnp.int32, (count, 1), 0)
    for step, weight in enumerate(STEPS):
        factor = jnp.where(lax.rem(row, 2) == (1 if step % 2 == 0 else 0), weight, 0.0)
        value = value + factor * (pltpu.roll(value, 1, 0) + pltpu.roll(value, count - 1, 0))
    return value


def scaled_z(value, spacing, at):
    width = value.shape[-1]
    odd, even = lanes_of(width, spacing, True), lanes_of(width, spacing, False)
    return value * jnp.where(odd, at * SCALE, jnp.where(even, at / SCALE, 0.0))


def scaled(value, level, x_odd, y_odd):
    at = (SCALE if x_odd else 1 / SCALE) * (SCALE if y_odd else 1 / SCALE)
    if level < BY_MATRIX:
        return value if x_odd != y_odd else value * at
    return scaled_z(value, 1 << level, at)


def spread_z(source, weights, spread, rows, start, size):
    width = source.shape[-1]
    value = source[start : start + size].reshape(size * rows, width)
    spread[start * rows : (start + size) * rows, :] = z_product(value, weights[...])


def spread_x(block, rows, spread, into, low, base):
    for at in range(0, rows, 8):
        planes = {x: spread[x * rows + at : x * rows + at + 8, :] for x in range(block)}
        for x, value in x_lift(planes).items():
            into[x - low, base + at : base + at + 8, :] = value


def z_weights(width, spacing):
    row = lax.broadcasted_iota(jnp.int32, (width, width), 0)
    lane = lax.broadcasted_iota(jnp.int32, (width, width), 1)
    full = scaled_z(z_lift(jnp.where(row == lane, 1.0, 0.0), spacing), spacing, 1.0)
    high = full.astype(jnp.bfloat16)
    rest = (full - high.astype(jnp.float32)).astype(jnp.bfloat16)
    return high, rest


def own_kernel(block, rows, velocity, into, *refs):
    weights, spread, held, arrived = refs[:BY_MATRIX], *refs[BY_MATRIX:]
    width = held.shape[-1]
    parts = arrived.shape[0]
    size = block // parts
    copies = [
        pltpu.make_async_copy(
            velocity.at[pl.ds(part * size, size)], held.at[pl.ds(part * size, size)], arrived.at[part]
        )
        for part in range(parts)
    ]
    for copy in copies:
        copy.start()
    for level, weight in enumerate(weights):
        high, rest = z_weights(width, 1 << level)
        weight[:width, :width] = high
        weight[:width, width:] = rest
        weight[width:, :width] = high
        weight[width:, width:] = jnp.zeros_like(rest)
    for part, copy in enumerate(copies):
        copy.wait()
        spread_z(held, weights[0], spread, rows, part * size, size)
    spread_x(block, rows, spread, into, windows(block)[0][0], 0)


def message_kernel(block, rows, width, count, places, *refs):
    refs = list(refs)

    def take(number):
        taken = refs[:number]
        del refs[:number]
        return taken

    (_,) = take(1)
    others = take(count - 1)
    weights = take(BY_MATRIX)
    (first,) = take(1)
    own = take(LEVELS)
    messages = dict(zip(places, take(len(places))))
    (spread,) = take(1)
    lifted = [first] + take(LEVELS - 1)
    coarse = take(LEVELS - 1)
    spans = windows(block)
    total = count * rows

    tables = {to: message(block, rows, to) for to in places}
    written = {to: set() for to in places}

    def post(to, at, half, value):
        here = range(at, at + 2 * half, 2)
        if written[to].isdisjoint(here):
            messages[to][pl.ds(at, half, 2), :] = value
        else:
            messages[to][pl.ds(at, half, 2), :] += value
        written[to].update(here)

    def put(level, plane, even, odd):
        half = (rows >> level) // 2
        spacing = 1 << level
        if level < LEVELS - 1 and plane % 2 == 0:
            even = jnp.where(lanes_of(width, spacing, True), even, 0.0)
        to = plane // (block >> level)
        if to == 0:
            own[level][plane, pl.ds(0, half, 2), :] = even
            own[level][plane, pl.ds(1, half, 2), :] = odd
        elif (level, plane) in tables[to][0]:
            at, shift = tables[to][0][level, plane], shift_of(level)
            post(to, at, half, pltpu.roll(even, shift, 1) if shift else even)
            post(to, at + 1, half, pltpu.roll(odd, shift, 1) if shift else odd)

    for level in range(LEVELS):
        low, high = spans[level]
        height = total >> level
        half, mine = height // 2, (rows >> level) // 2
        into = lifted[level]

        if level == 0:
            for part, source in enumerate(others):
                step = min(block, max(1, 512 // rows))
                for x in range(0, block, step):
                    spread_z(source, weights[0], spread, rows, x, step)
                spread_x(block, rows, spread, into, low, (part + 1) * rows)
        else:
            start, stop = spans[level - 1][0] // 2, spans[level - 1][1] // 2 + 1
            source = coarse[level - 1]
            if level < BY_MATRIX:
                size = (stop - start) * height
                for at in range(0, size, 512):
                    end = min(size, at + 512)
                    source[at:end, :] = z_product(source[at:end, :], weights[level][...])
            for at in range(0, height, 8):
                planes = {}
                for x in range(start, stop):
                    row = (x - start) * height + at
                    value = source[row : row + 8, :]
                    planes[x] = value if level < BY_MATRIX else z_lift(value, 1 << level)
                for x, value in x_lift(planes).items():
                    into[x - low, at : at + 8, :] = value

        for plane in range(low, high + 1):
            odd_plane = plane % 2 == 1
            if level == 0 and odd_plane and 0 <= plane < block:
                continue
            at = plane - low
            if half % 8 == 0:
                even, odd = y_lift_split(
                    into[at, pl.ds(0, half, 2), :], into[at, pl.ds(1, half, 2), :]
                )
            else:
                into[at] = y_lift_whole(into[at])
                even, odd = into[at, pl.ds(0, half, 2), :], into[at, pl.ds(1, half, 2), :]
            if level < LEVELS - 1 and not odd_plane:
                even = scaled(even, level, odd_plane, False)
                row = ((plane - low) // 2) * half
                coarse[level][row : row + half, :] = even
                even = even[:mine]
            else:
                even = scaled(even[:mine], level, odd_plane, False)
            put(level, plane, even, scaled(odd[:mine], level, odd_plane, True))

    for to in places:
        for row in range(tables[to][2]):
            if row not in written[to]:
                messages[to][row : row + 1, :] = jnp.zeros((1, width), jnp.float32)


def rest_kernel(block, rows, width, first, kept, *refs):
    coarse, out = refs[:-1], refs[-1]
    low = windows(block)[0][0]
    half, mine = first.shape[1] // 2, rows // 2
    for plane in range(block):
        if plane % 2 == 1:
            even, odd = y_lift_split(
                first[plane - low, pl.ds(0, half, 2), :], first[plane - low, pl.ds(1, half, 2), :]
            )
            out[plane, pl.ds(0, mine, 2), :] = scaled(even[:mine], 0, True, False)
            out[plane, pl.ds(1, mine, 2), :] = scaled(odd[:mine], 0, True, True)
        else:
            out[plane] = kept[plane]
    for level in range(1, LEVELS):
        spacing = 1 << level
        for plane in range(block >> level):
            out[plane * spacing, pl.ds(0, rows >> level, spacing), :] += coarse[level - 1][plane]


def pass_kernel(*refs):
    half = len(refs) // 2
    for source, target in zip(refs[:half], refs[half:]):
        rows, width = source.shape
        target[:rows, :] = source[...]
        if rows < target.shape[0]:
            target[rows:, :] = jnp.zeros((target.shape[0] - rows, width), jnp.float32)


def add_kernel(block, rows, places, *refs):
    own, received, out = refs[0], refs[1 : 1 + len(places)], refs[1 + len(places)]
    clean = refs[2 + len(places) :]
    a, b, c, d = STEPS
    width = out.shape[-1]
    out[...] = own[...]

    for to, arrived in zip(places, received):
        sent, derived, length = message(block, rows, to)
        for level in sorted({level for level, _ in sent}):
            spacing, height = 1 << level, rows >> level
            shape = (height, width)
            if level > 0:
                here = [at for (found, _), at in sent.items() if found == level]
                start, stop = min(here), -(-(max(here) + height) // 8) * 8
                value = arrived[start:stop, :]
                if shift_of(level):
                    value = pltpu.roll(value, width - shift_of(level), 1)
                lane = lax.broadcasted_iota(jnp.int32, (1, width), 1)
                value = jnp.where(lax.rem(lane, spacing) == 0, value, 0.0)
                source = clean[level - 1]
                source[: stop - start, :] = value
            else:
                start, source = 0, arrived

            def read(plane):
                at = sent[level, plane] - start
                return source[at : at + height, :]

            def add(plane, value):
                x = (plane - to * (block >> level)) * spacing
                out[x, pl.ds(0, height, spacing), :] += value

            for found, plane in sent:
                if found == level:
                    add(plane, read(plane))
            for (found, plane), (far, near) in derived.items():
                if found == level:
                    if near is None:
                        value = (d / SCALE**2) * read(far)
                    else:
                        value = ((1 / c + d) / SCALE**2) * read(far) + (d / SCALE**2) * read(near)
                    row = lax.broadcasted_iota(jnp.int32, shape, 0)
                    keep = (lax.rem(row, 2) == 1) | lanes_of(width, spacing, True)
                    add(plane, jnp.where(keep, value, 0.0))


def call(body, name, outs, ins, scratch=(), aliases=None, flops=0, spaces=None):
    vmem = pl.BlockSpec(memory_space=pltpu.VMEM)
    f32 = jnp.float32
    shapes = [out if isinstance(out, jax.ShapeDtypeStruct) else jax.ShapeDtypeStruct(out, f32) for out in outs]
    moved = 4 * sum(int(np.prod(shape.shape)) for shape in shapes)
    return pl.pallas_call(
        body,
        out_shape=shapes,
        in_specs=spaces or [vmem] * len(ins),
        out_specs=[vmem] * len(outs),
        scratch_shapes=[pltpu.VMEM(shape, f32) if isinstance(shape, tuple) else shape for shape in scratch],
        input_output_aliases=aliases or {},
        compiler_params=pltpu.CompilerParams(vmem_limit_bytes=VMEM_BYTES),
        cost_estimate=pl.CostEstimate(flops=flops, bytes_accessed=2 * moved, transcendentals=0),
        name=name,
    )(*ins)


def local(velocity):
    block, rows, width = velocity.shape
    around, count = lax.axis_size("gx"), lax.axis_size("gy")
    places = places_of(block)
    spans = windows(block)
    total = count * rows

    others = [
        lax.ppermute(velocity, "gy", [(i, (i - k) % count) for i in range(count)])
        for k in range(1, count)
    ]
    lifted = [
        (high - low + 1, total >> level, width) for level, (low, high) in enumerate(spans)
    ]
    coarse = [
        ((high // 2 - low // 2 + 1) * (total >> (level + 1)), width)
        for level, (low, high) in enumerate(spans[:-1])
    ]
    spread = (block * rows, width)
    owned = [(block >> level, rows >> level, width) for level in range(LEVELS)]

    square = jax.ShapeDtypeStruct((2 * width, 2 * width), jnp.bfloat16)
    first, *weights = call(
        functools.partial(own_kernel, block, rows),
        "lift_own",
        [lifted[0]] + [square] * BY_MATRIX,
        [velocity],
        [spread, velocity.shape, pltpu.SemaphoreType.DMA((COPIES,))],
        spaces=[pl.BlockSpec(memory_space=pltpu.HBM)],
    )
    first, kept, *more = call(
        functools.partial(message_kernel, block, rows, width, count, places),
        "make_messages",
        [lifted[0]] + owned + [(message(block, rows, to)[2], width) for to in places],
        [first] + others + weights,
        [spread] + lifted[1:] + coarse,
        {0: 0},
    )
    own_coarse, sent = more[: LEVELS - 1], dict(zip(places, more[LEVELS - 1 :]))
    last = around - 1
    pairs = {to: [(i, (i + to) % around) for i in range(around)] for to in places}
    held = [pair for pair in pairs[2] if pair == (last, 1)]
    left, right, second = call(
        pass_kernel,
        "pass_on",
        [sent[to].shape for to in (-1, 2, -2)],
        [sent[to] for to in (-1, 2, -2)],
    )
    longer = (second.shape[0] + right.shape[0], width)
    right, second = call(pass_kernel, "pass_on", [right.shape, longer], [right, second], flops=PASS_FLOPS)
    moved = {-1: left, 2: right, -2: second}
    rounds = [
        [(1, pairs[1], sent), (2, [pair for pair in pairs[2] if pair not in held], sent)],
        [(-1, pairs[-1], moved), (-2, pairs[-2], moved), (2, held, moved)],
    ]
    received = [[lax.ppermute(source[to], "gx", pair) for to, pair, source in each] for each in rounds]
    (result,) = call(
        functools.partial(rest_kernel, block, rows, width),
        "finish_own",
        [owned[0]],
        [first, kept] + own_coarse,
    )
    for each, arrived, flops in zip(rounds, received, ROUND_FLOPS):
        here = [to for to, _, _ in each]
        (result,) = call(
            functools.partial(add_kernel, block, rows, here),
            "add_received",
            [owned[0]],
            [result] + arrived,
            [(max(message(block, rows, to)[2] for to in here), width)] * (LEVELS - 1),
            flops=flops,
        )
    return result


def solution(mesh):
    return jax.shard_map(
        local, mesh=mesh, in_specs=(P("gx", "gy", None),), out_specs=P("gx", "gy", None), check_vma=False
    )
```

```python
import functools

import jax
import jax.numpy as jnp
import numpy as np
from jax import lax
from jax.experimental import pallas as pl
from jax.experimental.pallas import tpu as pltpu
from jax.sharding import PartitionSpec as P

LEVELS = 4
STEPS = (-1.586134342, -0.05298011854, 0.8829110762, 0.4435068522)
SCALE = 1.149604398
VMEM_BYTES = 24 * 2**20
FIRST_FLOPS = 10**11
COPIES = 2
BY_MATRIX = 2


def windows(block):
    found = []
    first, last = 0, block - 1
    for _ in range(LEVELS):
        low = first - 4 + (first % 2)
        high = last + 4 - (last % 2)
        found.append((low, high))
        first, last = low // 2, high // 2
    return found


def message(block, rows, to):
    sent, derived = {}, {}
    spans = windows(block)
    base = ends = 0
    for level, (low, high) in enumerate(spans):
        size, height = block >> level, rows >> level
        first, last = (0, block - 1) if level == 0 else (v // 2 for v in spans[level - 1])
        planes = [p for p in range(low, high + 1) if p // size == to]
        if abs(to) == 1:
            sign = to
            edge = last + 2 - last % 2 if to > 0 else first - 2 + first % 2
            far, near = edge + sign, edge - sign
            if far in planes and edge + 2 * sign in planes:
                derived[level, edge + 2 * sign] = (far, None)
            if far in planes and near in planes:
                derived[level, edge] = (far, near)
        at = base
        for plane in planes:
            if (level, plane) not in derived:
                sent[level, plane] = at
                at += height
        ends = max(ends, at)
        if level == 0:
            base = at
    return sent, derived, -(-ends // 8) * 8


def shift_of(level):
    return (0, 0, 1, 3)[level]


def places_of(block):
    found = set()
    for level, (low, high) in enumerate(windows(block)):
        size = block >> level
        found |= set(range(low // size, high // size + 1))
    return sorted(found - {0})


def z_product(value, weights):
    width = value.shape[-1]
    high = value.astype(jnp.bfloat16)
    rest = (value - high.astype(jnp.float32)).astype(jnp.bfloat16)
    both = jnp.concatenate([high, rest], axis=1)
    product = jnp.dot(both, weights, preferred_element_type=jnp.float32)
    return product[:, :width] + product[:, width:]


def lanes_of(width, spacing, parity):
    lane = lax.broadcasted_iota(jnp.int32, (1, width), 1)
    return lax.rem(lane, 2 * spacing) == (spacing if parity else 0)


def z_lift(value, spacing):
    width = value.shape[-1]
    axis = value.ndim - 1
    for step, weight in enumerate(STEPS):
        factor = jnp.where(lanes_of(width, spacing, step % 2 == 0), weight, 0.0)
        around = pltpu.roll(value, spacing, axis) + pltpu.roll(value, width - spacing, axis)
        value = value + factor * around
    return value


def x_lift(planes):
    def plus(one, other):
        return other if one is None else one if other is None else one + other

    planes = dict(planes)
    for step, weight in enumerate(STEPS):
        parity = 1 if step % 2 == 0 else 0
        for index in range(min(planes) - 1, max(planes) + 2):
            if index % 2 == parity:
                around = plus(planes.get(index - 1), planes.get(index + 1))
                if around is not None:
                    planes[index] = plus(planes.get(index), weight * around)
    return planes


def y_lift_split(even, odd):
    count = even.shape[0]
    a, b, c, d = STEPS
    odd = odd + a * (even + pltpu.roll(even, count - 1, 0))
    even = even + b * (pltpu.roll(odd, 1, 0) + odd)
    odd = odd + c * (even + pltpu.roll(even, count - 1, 0))
    even = even + d * (pltpu.roll(odd, 1, 0) + odd)
    return even, odd


def y_lift_whole(value):
    count = value.shape[0]
    row = lax.broadcasted_iota(jnp.int32, (count, 1), 0)
    for step, weight in enumerate(STEPS):
        factor = jnp.where(lax.rem(row, 2) == (1 if step % 2 == 0 else 0), weight, 0.0)
        value = value + factor * (pltpu.roll(value, 1, 0) + pltpu.roll(value, count - 1, 0))
    return value


def scaled_z(value, spacing, at):
    width = value.shape[-1]
    odd, even = lanes_of(width, spacing, True), lanes_of(width, spacing, False)
    return value * jnp.where(odd, at * SCALE, jnp.where(even, at / SCALE, 0.0))


def scaled(value, level, x_odd, y_odd):
    at = (SCALE if x_odd else 1 / SCALE) * (SCALE if y_odd else 1 / SCALE)
    if level < BY_MATRIX:
        return value if x_odd != y_odd else value * at
    return scaled_z(value, 1 << level, at)


def spread_z(source, weights, spread, rows, start, size):
    width = source.shape[-1]
    value = source[start : start + size].reshape(size * rows, width)
    spread[start * rows : (start + size) * rows, :] = z_product(value, weights[...])


def spread_x(block, rows, spread, into, low, base):
    for at in range(0, rows, 8):
        planes = {x: spread[x * rows + at : x * rows + at + 8, :] for x in range(block)}
        for x, value in x_lift(planes).items():
            into[x - low, base + at : base + at + 8, :] = value


def z_weights(width, spacing):
    row = lax.broadcasted_iota(jnp.int32, (width, width), 0)
    lane = lax.broadcasted_iota(jnp.int32, (width, width), 1)
    full = scaled_z(z_lift(jnp.where(row == lane, 1.0, 0.0), spacing), spacing, 1.0)
    high = full.astype(jnp.bfloat16)
    rest = (full - high.astype(jnp.float32)).astype(jnp.bfloat16)
    return high, rest


def own_kernel(block, rows, velocity, into, *refs):
    weights, spread, held, arrived = refs[:BY_MATRIX], *refs[BY_MATRIX:]
    width = held.shape[-1]
    parts = arrived.shape[0]
    size = block // parts
    copies = [
        pltpu.make_async_copy(
            velocity.at[pl.ds(part * size, size)], held.at[pl.ds(part * size, size)], arrived.at[part]
        )
        for part in range(parts)
    ]
    for copy in copies:
        copy.start()
    for level, weight in enumerate(weights):
        high, rest = z_weights(width, 1 << level)
        weight[:width, :width] = high
        weight[:width, width:] = rest
        weight[width:, :width] = high
        weight[width:, width:] = jnp.zeros_like(rest)
    for part, copy in enumerate(copies):
        copy.wait()
        spread_z(held, weights[0], spread, rows, part * size, size)
    spread_x(block, rows, spread, into, windows(block)[0][0], 0)


def message_kernel(block, rows, width, count, places, *refs):
    refs = list(refs)

    def take(number):
        taken = refs[:number]
        del refs[:number]
        return taken

    (_,) = take(1)
    others = take(count - 1)
    weights = take(BY_MATRIX)
    (first,) = take(1)
    own = take(LEVELS)
    messages = dict(zip(places, take(len(places))))
    (spread,) = take(1)
    lifted = [first] + take(LEVELS - 1)
    coarse = take(LEVELS - 1)
    spans = windows(block)
    total = count * rows

    tables = {to: message(block, rows, to) for to in places}
    written = {to: set() for to in places}

    def post(to, at, half, value):
        here = range(at, at + 2 * half, 2)
        if written[to].isdisjoint(here):
            messages[to][pl.ds(at, half, 2), :] = value
        else:
            messages[to][pl.ds(at, half, 2), :] += value
        written[to].update(here)

    def put(level, plane, even, odd):
        half = (rows >> level) // 2
        spacing = 1 << level
        if level < LEVELS - 1 and plane % 2 == 0:
            even = jnp.where(lanes_of(width, spacing, True), even, 0.0)
        to = plane // (block >> level)
        if to == 0:
            own[level][plane, pl.ds(0, half, 2), :] = even
            own[level][plane, pl.ds(1, half, 2), :] = odd
        elif (level, plane) in tables[to][0]:
            at, shift = tables[to][0][level, plane], shift_of(level)
            post(to, at, half, pltpu.roll(even, shift, 1) if shift else even)
            post(to, at + 1, half, pltpu.roll(odd, shift, 1) if shift else odd)

    for level in range(LEVELS):
        low, high = spans[level]
        height = total >> level
        half, mine = height // 2, (rows >> level) // 2
        into = lifted[level]

        if level == 0:
            for part, source in enumerate(others):
                step = min(block, max(1, 512 // rows))
                for x in range(0, block, step):
                    spread_z(source, weights[0], spread, rows, x, step)
                spread_x(block, rows, spread, into, low, (part + 1) * rows)
        else:
            start, stop = spans[level - 1][0] // 2, spans[level - 1][1] // 2 + 1
            source = coarse[level - 1]
            if level < BY_MATRIX:
                size = (stop - start) * height
                for at in range(0, size, 512):
                    end = min(size, at + 512)
                    source[at:end, :] = z_product(source[at:end, :], weights[level][...])
            for at in range(0, height, 8):
                planes = {}
                for x in range(start, stop):
                    row = (x - start) * height + at
                    value = source[row : row + 8, :]
                    planes[x] = value if level < BY_MATRIX else z_lift(value, 1 << level)
                for x, value in x_lift(planes).items():
                    into[x - low, at : at + 8, :] = value

        for plane in range(low, high + 1):
            odd_plane = plane % 2 == 1
            if level == 0 and odd_plane and 0 <= plane < block:
                continue
            at = plane - low
            if half % 8 == 0:
                even, odd = y_lift_split(
                    into[at, pl.ds(0, half, 2), :], into[at, pl.ds(1, half, 2), :]
                )
            else:
                into[at] = y_lift_whole(into[at])
                even, odd = into[at, pl.ds(0, half, 2), :], into[at, pl.ds(1, half, 2), :]
            if level < LEVELS - 1 and not odd_plane:
                even = scaled(even, level, odd_plane, False)
                row = ((plane - low) // 2) * half
                coarse[level][row : row + half, :] = even
                even = even[:mine]
            else:
                even = scaled(even[:mine], level, odd_plane, False)
            put(level, plane, even, scaled(odd[:mine], level, odd_plane, True))

    for to in places:
        for row in range(tables[to][2]):
            if row not in written[to]:
                messages[to][row : row + 1, :] = jnp.zeros((1, width), jnp.float32)


def rest_kernel(block, rows, width, first, kept, *refs):
    coarse, out = refs[:-1], refs[-1]
    low = windows(block)[0][0]
    half, mine = first.shape[1] // 2, rows // 2
    for plane in range(block):
        if plane % 2 == 1:
            even, odd = y_lift_split(
                first[plane - low, pl.ds(0, half, 2), :], first[plane - low, pl.ds(1, half, 2), :]
            )
            out[plane, pl.ds(0, mine, 2), :] = scaled(even[:mine], 0, True, False)
            out[plane, pl.ds(1, mine, 2), :] = scaled(odd[:mine], 0, True, True)
        else:
            out[plane] = kept[plane]
    for level in range(1, LEVELS):
        spacing = 1 << level
        for plane in range(block >> level):
            out[plane * spacing, pl.ds(0, rows >> level, spacing), :] += coarse[level - 1][plane]


def add_kernel(block, rows, places, *refs):
    own, received, out = refs[0], refs[1 : 1 + len(places)], refs[1 + len(places)]
    clean = refs[2 + len(places) :]
    a, b, c, d = STEPS
    width = out.shape[-1]
    out[...] = own[...]

    for to, arrived in zip(places, received):
        sent, derived, length = message(block, rows, to)
        for level in sorted({level for level, _ in sent}):
            spacing, height = 1 << level, rows >> level
            shape = (height, width)
            if level > 0:
                here = [at for (found, _), at in sent.items() if found == level]
                start, stop = min(here), -(-(max(here) + height) // 8) * 8
                value = arrived[start:stop, :]
                if shift_of(level):
                    value = pltpu.roll(value, width - shift_of(level), 1)
                lane = lax.broadcasted_iota(jnp.int32, (1, width), 1)
                value = jnp.where(lax.rem(lane, spacing) == 0, value, 0.0)
                source = clean[level - 1]
                source[: stop - start, :] = value
            else:
                start, source = 0, arrived

            def read(plane):
                at = sent[level, plane] - start
                return source[at : at + height, :]

            def add(plane, value):
                x = (plane - to * (block >> level)) * spacing
                out[x, pl.ds(0, height, spacing), :] += value

            for found, plane in sent:
                if found == level:
                    add(plane, read(plane))
            for (found, plane), (far, near) in derived.items():
                if found == level:
                    if near is None:
                        value = (d / SCALE**2) * read(far)
                    else:
                        value = ((1 / c + d) / SCALE**2) * read(far) + (d / SCALE**2) * read(near)
                    row = lax.broadcasted_iota(jnp.int32, shape, 0)
                    keep = (lax.rem(row, 2) == 1) | lanes_of(width, spacing, True)
                    add(plane, jnp.where(keep, value, 0.0))


def call(body, name, outs, ins, scratch=(), aliases=None, flops=0, spaces=None):
    vmem = pl.BlockSpec(memory_space=pltpu.VMEM)
    f32 = jnp.float32
    shapes = [out if isinstance(out, jax.ShapeDtypeStruct) else jax.ShapeDtypeStruct(out, f32) for out in outs]
    moved = 4 * sum(int(np.prod(shape.shape)) for shape in shapes)
    return pl.pallas_call(
        body,
        out_shape=shapes,
        in_specs=spaces or [vmem] * len(ins),
        out_specs=[vmem] * len(outs),
        scratch_shapes=[pltpu.VMEM(shape, f32) if isinstance(shape, tuple) else shape for shape in scratch],
        input_output_aliases=aliases or {},
        compiler_params=pltpu.CompilerParams(vmem_limit_bytes=VMEM_BYTES),
        cost_estimate=pl.CostEstimate(flops=flops, bytes_accessed=2 * moved, transcendentals=0),
        name=name,
    )(*ins)


def local(velocity):
    block, rows, width = velocity.shape
    around, count = lax.axis_size("gx"), lax.axis_size("gy")
    places = places_of(block)
    spans = windows(block)
    total = count * rows

    others = [
        lax.ppermute(velocity, "gy", [(i, (i - k) % count) for i in range(count)])
        for k in range(1, count)
    ]
    lifted = [
        (high - low + 1, total >> level, width) for level, (low, high) in enumerate(spans)
    ]
    coarse = [
        ((high // 2 - low // 2 + 1) * (total >> (level + 1)), width)
        for level, (low, high) in enumerate(spans[:-1])
    ]
    spread = (block * rows, width)
    owned = [(block >> level, rows >> level, width) for level in range(LEVELS)]

    square = jax.ShapeDtypeStruct((2 * width, 2 * width), jnp.bfloat16)
    first, *weights = call(
        functools.partial(own_kernel, block, rows),
        "lift_own",
        [lifted[0]] + [square] * BY_MATRIX,
        [velocity],
        [spread, velocity.shape, pltpu.SemaphoreType.DMA((COPIES,))],
        spaces=[pl.BlockSpec(memory_space=pltpu.HBM)],
    )
    first, kept, *more = call(
        functools.partial(message_kernel, block, rows, width, count, places),
        "make_messages",
        [lifted[0]] + owned + [(message(block, rows, to)[2], width) for to in places],
        [first] + others + weights,
        [spread] + lifted[1:] + coarse,
        {0: 0},
    )
    own_coarse, sent = more[: LEVELS - 1], dict(zip(places, more[LEVELS - 1 :]))
    place = lax.axis_index("gx")
    gathered = lax.all_gather(jnp.concatenate([sent[2], sent[-2]]), "gx")
    split = sent[2].shape[0]
    received = {
        to: lax.ppermute(sent[to], "gx", [(i, (i + to) % around) for i in range(around)])
        for to in (1, -1)
    }
    received[2] = lax.dynamic_index_in_dim(gathered, (place - 2) % around, 0, False)[:split]
    received[-2] = lax.dynamic_index_in_dim(gathered, (place + 2) % around, 0, False)[split:]
    (result,) = call(
        functools.partial(rest_kernel, block, rows, width),
        "finish_own",
        [owned[0]],
        [first, kept] + own_coarse,
    )
    for here, flops in (((1,), FIRST_FLOPS), ((-1, 2, -2), 0)):
        (result,) = call(
            functools.partial(add_kernel, block, rows, here),
            "add_received",
            [owned[0]],
            [result] + [received[to] for to in here],
            [(message(block, rows, -1)[2], width)] * (LEVELS - 1),
            flops=flops,
        )
    return result


def solution(mesh):
    return jax.shard_map(
        local, mesh=mesh, in_specs=(P("gx", "gy", None),), out_specs=P("gx", "gy", None), check_vma=False
    )
```

```python
import functools

import jax
import jax.numpy as jnp
import numpy as np
from jax import lax
from jax.experimental import pallas as pl
from jax.experimental.pallas import tpu as pltpu
from jax.sharding import PartitionSpec as P

LEVELS = 4
STEPS = (-1.586134342, -0.05298011854, 0.8829110762, 0.4435068522)
SCALE = 1.149604398
VMEM_BYTES = 24 * 2**20
FIRST_FLOPS = 10**11


def windows(block):
    found = []
    first, last = 0, block - 1
    for _ in range(LEVELS):
        low = first - 4 + (first % 2)
        high = last + 4 - (last % 2)
        found.append((low, high))
        first, last = low // 2, high // 2
    return found


def message(block, rows, to):
    sent, derived = {}, {}
    spans = windows(block)
    base = ends = 0
    for level, (low, high) in enumerate(spans):
        size, height = block >> level, rows >> level
        first, last = (0, block - 1) if level == 0 else (v // 2 for v in spans[level - 1])
        planes = [p for p in range(low, high + 1) if p // size == to]
        if abs(to) == 1:
            sign = to
            edge = last + 2 - last % 2 if to > 0 else first - 2 + first % 2
            far, near = edge + sign, edge - sign
            if far in planes and edge + 2 * sign in planes:
                derived[level, edge + 2 * sign] = (far, None)
            if far in planes and near in planes:
                derived[level, edge] = (far, near)
        at = base
        for plane in planes:
            if (level, plane) not in derived:
                sent[level, plane] = at
                at += height
        ends = max(ends, at)
        if level == 0:
            base = at
    return sent, derived, -(-ends // 8) * 8


def shift_of(level):
    return (0, 0, 1, 3)[level]


def places_of(block):
    found = set()
    for level, (low, high) in enumerate(windows(block)):
        size = block >> level
        found |= set(range(low // size, high // size + 1))
    return sorted(found - {0})


def z_product(value, weights):
    width = value.shape[-1]
    high = value.astype(jnp.bfloat16)
    rest = (value - high.astype(jnp.float32)).astype(jnp.bfloat16)
    both = jnp.concatenate([high, rest], axis=1)
    product = jnp.dot(both, weights, preferred_element_type=jnp.float32)
    return product[:, :width] + product[:, width:]


def lanes_of(width, spacing, parity):
    lane = lax.broadcasted_iota(jnp.int32, (1, width), 1)
    return lax.rem(lane, 2 * spacing) == (spacing if parity else 0)


def own_lanes(width, level, high_only):
    spacing, shift = 1 << level, shift_of(level)
    lane = lax.broadcasted_iota(jnp.int32, (1, width), 1)
    if high_only:
        return lax.rem(lane, 2 * spacing) == spacing + shift
    return lax.rem(lane, spacing) == shift


def z_lift(value, spacing):
    width = value.shape[-1]
    axis = value.ndim - 1
    for step, weight in enumerate(STEPS):
        factor = jnp.where(lanes_of(width, spacing, step % 2 == 0), weight, 0.0)
        around = pltpu.roll(value, spacing, axis) + pltpu.roll(value, width - spacing, axis)
        value = value + factor * around
    return value


def x_lift(planes):
    def plus(one, other):
        return other if one is None else one if other is None else one + other

    planes = dict(planes)
    for step, weight in enumerate(STEPS):
        parity = 1 if step % 2 == 0 else 0
        for index in range(min(planes) - 1, max(planes) + 2):
            if index % 2 == parity:
                around = plus(planes.get(index - 1), planes.get(index + 1))
                if around is not None:
                    planes[index] = plus(planes.get(index), weight * around)
    return planes


def y_lift_split(even, odd):
    count = even.shape[0]
    a, b, c, d = STEPS
    odd = odd + a * (even + pltpu.roll(even, count - 1, 0))
    even = even + b * (pltpu.roll(odd, 1, 0) + odd)
    odd = odd + c * (even + pltpu.roll(even, count - 1, 0))
    even = even + d * (pltpu.roll(odd, 1, 0) + odd)
    return even, odd


def y_lift_whole(value):
    count = value.shape[0]
    row = lax.broadcasted_iota(jnp.int32, (count, 1), 0)
    for step, weight in enumerate(STEPS):
        factor = jnp.where(lax.rem(row, 2) == (1 if step % 2 == 0 else 0), weight, 0.0)
        value = value + factor * (pltpu.roll(value, 1, 0) + pltpu.roll(value, count - 1, 0))
    return value


def scaled_z(value, spacing):
    width = value.shape[-1]
    odd, even = lanes_of(width, spacing, True), lanes_of(width, spacing, False)
    return value * jnp.where(odd, SCALE, jnp.where(even, 1 / SCALE, 0.0))


def scaled(value, x_odd, y_odd):
    at = (SCALE if x_odd else 1 / SCALE) * (SCALE if y_odd else 1 / SCALE)
    return value if x_odd != y_odd else value * at


def spread_z(source, weights, spread, rows, start, size):
    width = source.shape[-1]
    value = source[start : start + size].reshape(size * rows, width)
    spread[start * rows : (start + size) * rows, :] = z_product(value, weights[...])


def spread_x(block, rows, spread, into, low, base):
    for at in range(0, rows, 8):
        planes = {x: spread[x * rows + at : x * rows + at + 8, :] for x in range(block)}
        for x, value in x_lift(planes).items():
            into[x - low, base + at : base + at + 8, :] = value


def matrix_kernel(*weights):
    width = weights[0].shape[0] // 2
    row = lax.broadcasted_iota(jnp.int32, (width, width), 0)
    lane = lax.broadcasted_iota(jnp.int32, (width, width), 1)
    value = jnp.where(row == lane, 1.0, 0.0)
    full = [scaled_z(z_lift(value, 1), 1), jnp.zeros((width, width), jnp.float32)]
    for level in range(1, LEVELS):
        spacing = 1 << level
        value = scaled_z(z_lift(value, spacing), spacing)
        full[1] += pltpu.roll(value, shift_of(level), 1) if shift_of(level) else value
        value = jnp.where(lanes_of(width, spacing, False), value, 0.0)
    for weight, matrix in zip(weights, full):
        high = matrix.astype(jnp.bfloat16)
        rest = (matrix - high.astype(jnp.float32)).astype(jnp.bfloat16)
        weight[:width, :width] = high
        weight[:width, width:] = rest
        weight[width:, :width] = high
        weight[width:, width:] = jnp.zeros_like(rest)


def own_kernel(block, rows, velocity, weights, into, spread):
    step = max(1, min(block, 512 // rows))
    for x in range(0, block, step):
        spread_z(velocity, weights, spread, rows, x, step)
    spread_x(block, rows, spread, into, windows(block)[0][0], 0)


def message_kernel(block, rows, width, count, places, *refs):
    refs = list(refs)

    def take(number):
        taken = refs[:number]
        del refs[:number]
        return taken

    (_,) = take(1)
    others = take(count - 1)
    weights = take(2)
    (first,) = take(1)
    own = take(LEVELS)
    messages = dict(zip(places, take(len(places))))
    (spread,) = take(1)
    lifted = [first] + take(LEVELS - 1)
    coarse = take(LEVELS - 1)
    spans = windows(block)
    total = count * rows

    tables = {to: message(block, rows, to) for to in places}
    written = {to: set() for to in places}

    def post(to, at, half, value):
        here = range(at, at + 2 * half, 2)
        if written[to].isdisjoint(here):
            messages[to][pl.ds(at, half, 2), :] = value
        else:
            messages[to][pl.ds(at, half, 2), :] += value
        written[to].update(here)

    def put(level, plane, even, odd):
        half = (rows >> level) // 2
        low = level < LEVELS - 1 and plane % 2 == 0
        if level > 0 or low:
            even = jnp.where(own_lanes(width, level, low), even, 0.0)
        if level > 0:
            odd = jnp.where(own_lanes(width, level, False), odd, 0.0)
        to = plane // (block >> level)
        if to == 0:
            own[level][plane, pl.ds(0, half, 2), :] = even
            own[level][plane, pl.ds(1, half, 2), :] = odd
        elif (level, plane) in tables[to][0]:
            at = tables[to][0][level, plane]
            post(to, at, half, even)
            post(to, at + 1, half, odd)

    for level in range(LEVELS):
        low, high = spans[level]
        height = total >> level
        half, mine = height // 2, (rows >> level) // 2
        into = lifted[level]

        if level == 0:
            for part, source in enumerate(others):
                step = min(block, max(1, 512 // rows))
                for x in range(0, block, step):
                    spread_z(source, weights[0], spread, rows, x, step)
                spread_x(block, rows, spread, into, low, (part + 1) * rows)
        else:
            start, stop = spans[level - 1][0] // 2, spans[level - 1][1] // 2 + 1
            source = coarse[level - 1]
            if level == 1:
                size = (stop - start) * height
                for at in range(0, size, 512):
                    end = min(size, at + 512)
                    source[at:end, :] = z_product(source[at:end, :], weights[level][...])
            for at in range(0, height, 8):
                planes = {}
                for x in range(start, stop):
                    row = (x - start) * height + at
                    planes[x] = source[row : row + 8, :]
                for x, value in x_lift(planes).items():
                    into[x - low, at : at + 8, :] = value

        for plane in range(low, high + 1):
            odd_plane = plane % 2 == 1
            if level == 0 and odd_plane and 0 <= plane < block:
                continue
            at = plane - low
            if half % 8 == 0:
                even, odd = y_lift_split(
                    into[at, pl.ds(0, half, 2), :], into[at, pl.ds(1, half, 2), :]
                )
            else:
                into[at] = y_lift_whole(into[at])
                even, odd = into[at, pl.ds(0, half, 2), :], into[at, pl.ds(1, half, 2), :]
            if level < LEVELS - 1 and not odd_plane:
                even = scaled(even, odd_plane, False)
                row = ((plane - low) // 2) * half
                coarse[level][row : row + half, :] = even
                even = even[:mine]
            else:
                even = scaled(even[:mine], odd_plane, False)
            put(level, plane, even, scaled(odd[:mine], odd_plane, True))

    for to in places:
        for row in range(tables[to][2]):
            if row not in written[to]:
                messages[to][row : row + 1, :] = jnp.zeros((1, width), jnp.float32)


def touched(block, rows, places):
    found = set()
    for to in places:
        sent, derived, _ = message(block, rows, to)
        found |= {(plane - to * (block >> level)) << level for level, plane in [*sent, *derived]}
    return runs_of(found)


def runs_of(found):
    runs = []
    for x in sorted(found):
        if runs and runs[-1][1] == x:
            runs[-1] = (runs[-1][0], x + 1)
        else:
            runs.append((x, x + 1))
    return runs


def rest_kernel(block, rows, width, places, first, kept, *refs):
    coarse, (out, whole, done) = refs[:-3], refs[-3:]
    low = windows(block)[0][0]
    half, mine = first.shape[1] // 2, rows // 2
    for plane in range(block):
        if plane % 2 == 1:
            even, odd = y_lift_split(
                first[plane - low, pl.ds(0, half, 2), :], first[plane - low, pl.ds(1, half, 2), :]
            )
            out[plane, pl.ds(0, mine, 2), :] = scaled(even[:mine], True, False)
            out[plane, pl.ds(1, mine, 2), :] = scaled(odd[:mine], True, True)
        else:
            out[plane] = kept[plane]
    for level in range(1, LEVELS):
        spacing, shift = 1 << level, shift_of(level)
        for plane in range(block >> level):
            value = coarse[level - 1][plane]
            if shift:
                value = pltpu.roll(value, width - shift, 1)
            out[plane * spacing, pl.ds(0, rows >> level, spacing), :] += value
    busy = {x for start, stop in touched(block, rows, places) for x in range(start, stop)}
    copies = [
        pltpu.make_async_copy(out.at[pl.ds(start, stop - start)], whole.at[pl.ds(start, stop - start)], done.at[n])
        for n, (start, stop) in enumerate(runs_of(set(range(block)) - busy))
    ]
    for copy in copies:
        copy.start()
    for copy in copies:
        copy.wait()


def add_kernel(block, rows, places, every, *refs):
    own, received, refs = refs[0], refs[1 : 1 + len(places)], refs[1 + len(places) :]
    if every is None:
        out, *clean = refs
    else:
        _, whole, out, done, *clean = refs
    a, b, c, d = STEPS
    width = out.shape[-1]
    if every is None:
        out[...] = own[...]
    else:
        for start, stop in touched(block, rows, every):
            out[start:stop] = own[start:stop]

    for to, arrived in zip(places, received):
        sent, derived, length = message(block, rows, to)
        for level in sorted({level for level, _ in sent}):
            spacing, height = 1 << level, rows >> level
            shape = (height, width)
            if level > 0:
                here = [at for (found, _), at in sent.items() if found == level]
                start, stop = min(here), -(-(max(here) + height) // 8) * 8
                value = arrived[start:stop, :]
                if shift_of(level):
                    value = pltpu.roll(value, width - shift_of(level), 1)
                lane = lax.broadcasted_iota(jnp.int32, (1, width), 1)
                value = jnp.where(lax.rem(lane, spacing) == 0, value, 0.0)
                source = clean[level - 1]
                source[: stop - start, :] = value
            else:
                start, source = 0, arrived

            def read(plane):
                at = sent[level, plane] - start
                return source[at : at + height, :]

            def add(plane, value):
                x = (plane - to * (block >> level)) * spacing
                out[x, pl.ds(0, height, spacing), :] += value

            for found, plane in sent:
                if found == level:
                    add(plane, read(plane))
            for (found, plane), (far, near) in derived.items():
                if found == level:
                    if near is None:
                        value = (d / SCALE**2) * read(far)
                    else:
                        value = ((1 / c + d) / SCALE**2) * read(far) + (d / SCALE**2) * read(near)
                    row = lax.broadcasted_iota(jnp.int32, shape, 0)
                    keep = (lax.rem(row, 2) == 1) | lanes_of(width, spacing, True)
                    add(plane, jnp.where(keep, value, 0.0))

    if every is not None:
        copies = [
            pltpu.make_async_copy(out.at[pl.ds(start, stop - start)], whole.at[pl.ds(start, stop - start)], done.at[n])
            for n, (start, stop) in enumerate(touched(block, rows, every))
        ]
        for copy in copies:
            copy.start()
        for copy in copies:
            copy.wait()


def call(body, name, outs, ins, scratch=(), aliases=None, flops=0, hbm_out=(), hbm_in=()):
    vmem, hbm = pl.BlockSpec(memory_space=pltpu.VMEM), pl.BlockSpec(memory_space=pltpu.HBM)
    f32 = jnp.float32
    shapes = [out if isinstance(out, jax.ShapeDtypeStruct) else jax.ShapeDtypeStruct(out, f32) for out in outs]
    moved = 4 * sum(int(np.prod(shape.shape)) for shape in shapes)
    return pl.pallas_call(
        body,
        out_shape=shapes,
        in_specs=[hbm if n in hbm_in else vmem for n in range(len(ins))],
        out_specs=[hbm if n in hbm_out else vmem for n in range(len(outs))],
        scratch_shapes=[pltpu.VMEM(shape, f32) if isinstance(shape, tuple) else shape for shape in scratch],
        input_output_aliases=aliases or {},
        compiler_params=pltpu.CompilerParams(vmem_limit_bytes=VMEM_BYTES),
        cost_estimate=pl.CostEstimate(flops=flops, bytes_accessed=2 * moved, transcendentals=0),
        name=name,
    )(*ins)


def local(velocity):
    block, rows, width = velocity.shape
    around, count = lax.axis_size("gx"), lax.axis_size("gy")
    places = places_of(block)
    spans = windows(block)
    total = count * rows

    others = [
        lax.ppermute(velocity, "gy", [(i, (i - k) % count) for i in range(count)])
        for k in range(1, count)
    ]
    lifted = [
        (high - low + 1, total >> level, width) for level, (low, high) in enumerate(spans)
    ]
    coarse = [
        ((high // 2 - low // 2 + 1) * (total >> (level + 1)), width)
        for level, (low, high) in enumerate(spans[:-1])
    ]
    spread = (block * rows, width)
    owned = [(block >> level, rows >> level, width) for level in range(LEVELS)]

    square = jax.ShapeDtypeStruct((2 * width, 2 * width), jnp.bfloat16)
    weights = call(matrix_kernel, "make_matrices", [square] * 2, [])
    (first,) = call(
        functools.partial(own_kernel, block, rows),
        "lift_own",
        [lifted[0]],
        [velocity, weights[0]],
        [spread],
    )
    first, kept, *more = call(
        functools.partial(message_kernel, block, rows, width, count, places),
        "make_messages",
        [lifted[0]] + owned + [(message(block, rows, to)[2], width) for to in places],
        [first] + others + list(weights),
        [spread] + lifted[1:] + coarse,
        {0: 0},
    )
    own_coarse, sent = more[: LEVELS - 1], dict(zip(places, more[LEVELS - 1 :]))
    received = {
        to: lax.ppermute(sent[to], "gx", [(i, (i + to) % around) for i in range(around)])
        for to in sorted(places, key=lambda to: (to < 0, abs(to)))
    }
    result, whole = call(
        functools.partial(rest_kernel, block, rows, width, places),
        "finish_own",
        [owned[0]] * 2,
        [first, kept] + own_coarse,
        [pltpu.SemaphoreType.DMA((block,))],
        hbm_out=(1,),
    )
    clean = [(message(block, rows, -1)[2], width)] * (LEVELS - 1)
    right = [to for to in places if to > 0]
    left = [to for to in places if to < 0]
    (result,) = call(
        functools.partial(add_kernel, block, rows, right, None),
        "add_right",
        [owned[0]],
        [result] + [received[to] for to in right],
        clean,
        flops=FIRST_FLOPS,
    )
    (whole,) = call(
        functools.partial(add_kernel, block, rows, left, places),
        "add_left",
        [owned[0]],
        [result] + [received[to] for to in left] + [whole],
        [owned[0], pltpu.SemaphoreType.DMA((block,))] + clean,
        aliases={1 + len(left): 0},
        hbm_out=(0,),
        hbm_in=(1 + len(left),),
    )
    return whole


def solution(mesh):
    return jax.shard_map(
        local, mesh=mesh, in_specs=(P("gx", "gy", None),), out_specs=P("gx", "gy", None), check_vma=False
    )
```

```python
import functools

import jax
import jax.numpy as jnp
import numpy as np
from jax import lax
from jax.experimental import pallas as pl
from jax.experimental.pallas import tpu as pltpu
from jax.sharding import PartitionSpec as P

LEVELS = 4
STEPS = (-1.586134342, -0.05298011854, 0.8829110762, 0.4435068522)
SCALE = 1.149604398
VMEM_BYTES = 24 * 2**20
FIRST_FLOPS = 10**10
COPIES = 4


def windows(block):
    found = []
    first, last = 0, block - 1
    for _ in range(LEVELS):
        low = first - 4 + (first % 2)
        high = last + 4 - (last % 2)
        found.append((low, high))
        first, last = low // 2, high // 2
    return found


def message(block, rows, to):
    sent, derived = {}, {}
    spans = windows(block)
    base = ends = 0
    for level, (low, high) in enumerate(spans):
        size, height = block >> level, rows >> level
        first, last = (0, block - 1) if level == 0 else (v // 2 for v in spans[level - 1])
        planes = [p for p in range(low, high + 1) if p // size == to]
        if abs(to) == 1:
            sign = to
            edge = last + 2 - last % 2 if to > 0 else first - 2 + first % 2
            far, near = edge + sign, edge - sign
            if far in planes and edge + 2 * sign in planes:
                derived[level, edge + 2 * sign] = (far, None)
            if far in planes and near in planes:
                derived[level, edge] = (far, near)
        at = base
        for plane in planes:
            if (level, plane) not in derived:
                sent[level, plane] = at
                at += height
        ends = max(ends, at)
        if level == 0:
            base = at
    return sent, derived, -(-ends // 8) * 8


def shift_of(level):
    return (0, 0, 1, 3)[level]


def places_of(block):
    found = set()
    for level, (low, high) in enumerate(windows(block)):
        size = block >> level
        found |= set(range(low // size, high // size + 1))
    return sorted(found - {0})


def z_product(value, weights):
    width = value.shape[-1]
    high = value.astype(jnp.bfloat16)
    rest = (value - high.astype(jnp.float32)).astype(jnp.bfloat16)
    both = jnp.concatenate([high, rest], axis=1)
    product = jnp.dot(both, weights, preferred_element_type=jnp.float32)
    return product[:, :width] + product[:, width:]


def lanes_of(width, spacing, parity):
    lane = lax.broadcasted_iota(jnp.int32, (1, width), 1)
    return lax.rem(lane, 2 * spacing) == (spacing if parity else 0)


def own_lanes(width, level, high_only):
    spacing, shift = 1 << level, shift_of(level)
    lane = lax.broadcasted_iota(jnp.int32, (1, width), 1)
    if high_only:
        return lax.rem(lane, 2 * spacing) == spacing + shift
    return lax.rem(lane, spacing) == shift


def z_lift(value, spacing):
    width = value.shape[-1]
    axis = value.ndim - 1
    for step, weight in enumerate(STEPS):
        factor = jnp.where(lanes_of(width, spacing, step % 2 == 0), weight, 0.0)
        around = pltpu.roll(value, spacing, axis) + pltpu.roll(value, width - spacing, axis)
        value = value + factor * around
    return value


def x_lift(planes):
    def plus(one, other):
        return other if one is None else one if other is None else one + other

    planes = dict(planes)
    for step, weight in enumerate(STEPS):
        parity = 1 if step % 2 == 0 else 0
        for index in range(min(planes) - 1, max(planes) + 2):
            if index % 2 == parity:
                around = plus(planes.get(index - 1), planes.get(index + 1))
                if around is not None:
                    planes[index] = plus(planes.get(index), weight * around)
    return planes


def y_lift_split(even, odd):
    count = even.shape[0]
    a, b, c, d = STEPS
    odd = odd + a * (even + pltpu.roll(even, count - 1, 0))
    even = even + b * (pltpu.roll(odd, 1, 0) + odd)
    odd = odd + c * (even + pltpu.roll(even, count - 1, 0))
    even = even + d * (pltpu.roll(odd, 1, 0) + odd)
    return even, odd


def y_lift_whole(value):
    count = value.shape[0]
    row = lax.broadcasted_iota(jnp.int32, (count, 1), 0)
    for step, weight in enumerate(STEPS):
        factor = jnp.where(lax.rem(row, 2) == (1 if step % 2 == 0 else 0), weight, 0.0)
        value = value + factor * (pltpu.roll(value, 1, 0) + pltpu.roll(value, count - 1, 0))
    return value


def scaled_z(value, spacing):
    width = value.shape[-1]
    odd, even = lanes_of(width, spacing, True), lanes_of(width, spacing, False)
    return value * jnp.where(odd, SCALE, jnp.where(even, 1 / SCALE, 0.0))


def scaled(value, x_odd, y_odd):
    at = (SCALE if x_odd else 1 / SCALE) * (SCALE if y_odd else 1 / SCALE)
    return value if x_odd != y_odd else value * at


def spread_z(source, weights, spread, rows, start, size):
    width = source.shape[-1]
    value = source[start : start + size].reshape(size * rows, width)
    spread[start * rows : (start + size) * rows, :] = z_product(value, weights[...])


def spread_x(block, rows, spread, into, low, base):
    for at in range(0, rows, 8):
        planes = {x: spread[x * rows + at : x * rows + at + 8, :] for x in range(block)}
        for x, value in x_lift(planes).items():
            into[x - low, base + at : base + at + 8, :] = value


def matrix_kernel(*weights):
    width = weights[0].shape[0] // 2
    row = lax.broadcasted_iota(jnp.int32, (width, width), 0)
    lane = lax.broadcasted_iota(jnp.int32, (width, width), 1)
    value = jnp.where(row == lane, 1.0, 0.0)
    full = [scaled_z(z_lift(value, 1), 1), jnp.zeros((width, width), jnp.float32)]
    for level in range(1, LEVELS):
        spacing = 1 << level
        value = scaled_z(z_lift(value, spacing), spacing)
        full[1] += pltpu.roll(value, shift_of(level), 1) if shift_of(level) else value
        value = jnp.where(lanes_of(width, spacing, False), value, 0.0)
    for weight, matrix in zip(weights, full):
        high = matrix.astype(jnp.bfloat16)
        rest = (matrix - high.astype(jnp.float32)).astype(jnp.bfloat16)
        weight[:width, :width] = high
        weight[:width, width:] = rest
        weight[width:, :width] = high
        weight[width:, width:] = jnp.zeros_like(rest)


def own_kernel(block, rows, velocity, weights, into, spread):
    step = max(1, min(block, 512 // rows))
    for x in range(0, block, step):
        spread_z(velocity, weights, spread, rows, x, step)
    spread_x(block, rows, spread, into, windows(block)[0][0], 0)


def message_kernel(block, rows, width, count, places, *refs):
    refs = list(refs)

    def take(number):
        taken = refs[:number]
        del refs[:number]
        return taken

    shared = count == 2
    halves = 2 if shared else 1
    (_,) = take(1)
    others = take(count - 1)
    weights = take(2)
    (first,) = take(1)
    own = take(LEVELS)
    passed = take(2 if shared else len(places))
    (spread,) = take(1)
    lifted = [first] + take(LEVELS - 1)
    coarse = take(LEVELS - 1)
    messages = dict(zip(places, take(len(places)) if shared else passed))
    spans = windows(block)
    total = count * rows
    tables = {to: message(block, rows, to) for to in places}
    lengths = {to: messages[to].shape[0] // halves for to in places}
    written = {to: set() for to in places}

    def post(to, at, number, value):
        here = range(at, at + 2 * number, 2)
        if written[to].isdisjoint(here):
            messages[to][pl.ds(at, number, 2), :] = value
        else:
            messages[to][pl.ds(at, number, 2), :] += value
        written[to].update(here)

    def put(level, plane, half, even, odd):
        number = (rows >> level) // 2
        low = level < LEVELS - 1 and plane % 2 == 0
        if level > 0 or low:
            even = jnp.where(own_lanes(width, level, low), even, 0.0)
        if level > 0:
            odd = jnp.where(own_lanes(width, level, False), odd, 0.0)
        to = plane // (block >> level)
        if to == 0:
            own[level][plane, pl.ds(0, number, 2), :] = even
            own[level][plane, pl.ds(1, number, 2), :] = odd
        else:
            at = tables[to][0][level, plane] + half * lengths[to]
            post(to, at, number, even)
            post(to, at + 1, number, odd)

    for level in range(LEVELS):
        low, high = spans[level]
        height = total >> level
        half, mine = height // 2, (rows >> level) // 2
        into = lifted[level]

        if level == 0:
            for part, source in enumerate(others):
                step = min(block, max(1, 512 // rows))
                for x in range(0, block, step):
                    spread_z(source, weights[0], spread, rows, x, step)
                spread_x(block, rows, spread, into, low, (part + 1) * rows)
        else:
            start, stop = spans[level - 1][0] // 2, spans[level - 1][1] // 2 + 1
            source = coarse[level - 1]
            if level == 1:
                size = (stop - start) * height
                for at in range(0, size, 512):
                    end = min(size, at + 512)
                    source[at:end, :] = z_product(source[at:end, :], weights[level][...])
            for at in range(0, height, 8):
                planes = {}
                for x in range(start, stop):
                    row = (x - start) * height + at
                    planes[x] = source[row : row + 8, :]
                for x, value in x_lift(planes).items():
                    into[x - low, at : at + 8, :] = value

        for plane in range(low, high + 1):
            odd_plane = plane % 2 == 1
            to = plane // (block >> level)
            if level == 0 and odd_plane and to == 0:
                continue
            goes_on = level < LEVELS - 1 and not odd_plane
            sends = to == 0 or (level, plane) in tables[to][0]
            if not goes_on and not sends:
                continue
            at = plane - low
            split = half % 8 == 0
            if split:
                even, odd = y_lift_split(
                    into[at, pl.ds(0, half, 2), :], into[at, pl.ds(1, half, 2), :]
                )
                even = scaled(even, odd_plane, False)
            else:
                into[at] = y_lift_whole(into[at])
                even = scaled(into[at, pl.ds(0, half, 2), :], odd_plane, False)
            if goes_on:
                row = ((plane - low) // 2) * half
                coarse[level][row : row + half, :] = even
            if not sends:
                continue
            for part in range(halves if to else 1):
                if split:
                    here_even = even[part * mine : (part + 1) * mine]
                    here_odd = odd[part * mine : (part + 1) * mine]
                else:
                    here_even = into[at, pl.ds(2 * part * mine, mine, 2), :]
                    here_even = scaled(here_even, odd_plane, False)
                    here_odd = into[at, pl.ds(2 * part * mine + 1, mine, 2), :]
                put(level, plane, part, here_even, scaled(here_odd, odd_plane, True))

    for to in places:
        for row in range(halves * lengths[to]):
            if row not in written[to]:
                messages[to][row : row + 1, :] = jnp.zeros((1, width), jnp.float32)
    if shared:
        for far, target in enumerate(passed, 1):
            target[...] = jnp.where(lax.axis_index("gy") == 0, messages[-far][...], messages[far][...])


def rest_kernel(block, rows, width, first, _, *refs):
    coarse, out = refs[:-1], refs[-1]
    low = windows(block)[0][0]
    half, mine = first.shape[1] // 2, rows // 2
    for plane in range(1, block, 2):
        even, odd = y_lift_split(
            first[plane - low, pl.ds(0, half, 2), :], first[plane - low, pl.ds(1, half, 2), :]
        )
        out[plane, pl.ds(0, mine, 2), :] = scaled(even[:mine], True, False)
        out[plane, pl.ds(1, mine, 2), :] = scaled(odd[:mine], True, True)
    for level in range(1, LEVELS):
        spacing, shift = 1 << level, shift_of(level)
        for plane in range(block >> level):
            value = coarse[level - 1][plane]
            if shift:
                value = pltpu.roll(value, width - shift, 1)
            out[plane * spacing, pl.ds(0, rows >> level, spacing), :] += value


def add_message(block, rows, to, arrived, base, out, clean):
    sent, derived, _ = message(block, rows, to)
    a, b, c, d = STEPS
    width = out.shape[-1]
    for level in sorted({level for level, _ in sent}):
        spacing, height = 1 << level, rows >> level
        shape = (height, width)
        if level > 0:
            here = [at for (found, _), at in sent.items() if found == level]
            start, stop = min(here), -(-(max(here) + height) // 8) * 8
            value = arrived[base + start : base + stop, :]
            if shift_of(level):
                value = pltpu.roll(value, width - shift_of(level), 1)
            lane = lax.broadcasted_iota(jnp.int32, (1, width), 1)
            value = jnp.where(lax.rem(lane, spacing) == 0, value, 0.0)
            source = clean[level - 1]
            source[: stop - start, :] = value
        else:
            start, source = -base, arrived

        def read(plane):
            at = sent[level, plane] - start
            return source[at : at + height, :]

        def add(plane, value):
            x = (plane - to * (block >> level)) * spacing
            out[x, pl.ds(0, height, spacing), :] += value

        for found, plane in sent:
            if found == level:
                add(plane, read(plane))
        for (found, plane), (far, near) in derived.items():
            if found == level:
                if near is None:
                    value = (d / SCALE**2) * read(far)
                else:
                    value = ((1 / c + d) / SCALE**2) * read(far) + (d / SCALE**2) * read(near)
                row = lax.broadcasted_iota(jnp.int32, shape, 0)
                keep = (lax.rem(row, 2) == 1) | lanes_of(width, spacing, True)
                add(plane, jnp.where(keep, value, 0.0))


def write_out(out, whole, done):
    parts = done.shape[0]
    size = out.shape[0] // parts
    copies = [
        pltpu.make_async_copy(
            out.at[pl.ds(part * size, size)], whole.at[pl.ds(part * size, size)], done.at[part]
        )
        for part in range(parts)
    ]
    for copy in copies:
        copy.start()
    for copy in copies:
        copy.wait()


def add_kernel(block, rows, places, last, _, *refs):
    received, refs = refs[: len(places)], refs[len(places) :]
    if last:
        whole, out, done, *clean = refs
    else:
        out, *clean = refs
    for to, arrived in zip(places, received):
        add_message(block, rows, to, arrived, 0, out, clean)
    if last:
        write_out(out, whole, done)


def keep_kernel(block, rows, _, near, far, out, *clean):
    for core, side in enumerate((-1, 1)):

        @pl.when(lax.axis_index("gy") == core)
        def _():
            add_message(block, rows, side, near, 0, out, clean)
            add_message(block, rows, 2 * side, far, 0, out, clean)


def pack_kernel(near, far, packed):
    one, two = near.shape[0] // 2, far.shape[0] // 2
    packed[:one, :] = near[one:, :]
    packed[one:, :] = far[two:, :]


def swap_kernel(block, rows, one, _, packed, whole, out, done, *clean):
    for core, side in enumerate((1, -1)):

        @pl.when(lax.axis_index("gy") == core)
        def _():
            add_message(block, rows, side, packed, 0, out, clean)
            add_message(block, rows, 2 * side, packed, one, out, clean)

    write_out(out, whole, done)


def call(body, name, outs, ins, scratch=(), aliases=None, flops=0, hbm_out=()):
    vmem, hbm = pl.BlockSpec(memory_space=pltpu.VMEM), pl.BlockSpec(memory_space=pltpu.HBM)
    f32 = jnp.float32
    shapes = [out if isinstance(out, jax.ShapeDtypeStruct) else jax.ShapeDtypeStruct(out, f32) for out in outs]
    moved = 4 * sum(int(np.prod(shape.shape)) for shape in shapes)
    return pl.pallas_call(
        body,
        out_shape=shapes,
        in_specs=[vmem] * len(ins),
        out_specs=[hbm if n in hbm_out else vmem for n in range(len(outs))],
        scratch_shapes=[pltpu.VMEM(shape, f32) if isinstance(shape, tuple) else shape for shape in scratch],
        input_output_aliases=aliases or {},
        compiler_params=pltpu.CompilerParams(vmem_limit_bytes=VMEM_BYTES),
        cost_estimate=pl.CostEstimate(flops=flops, bytes_accessed=2 * moved, transcendentals=0),
        name=name,
    )(*ins)


def local(velocity):
    block, rows, width = velocity.shape
    around, count = lax.axis_size("gx"), lax.axis_size("gy")
    shared = count == 2
    places = places_of(block)
    spans = windows(block)
    total = count * rows

    others = [
        lax.ppermute(velocity, "gy", [(i, (i - k) % count) for i in range(count)])
        for k in range(1, count)
    ]
    lifted = [
        (high - low + 1, total >> level, width) for level, (low, high) in enumerate(spans)
    ]
    coarse = [
        ((high // 2 - low // 2 + 1) * (total >> (level + 1)), width)
        for level, (low, high) in enumerate(spans[:-1])
    ]
    spread = (block * rows, width)
    owned = [(block >> level, rows >> level, width) for level in range(LEVELS)]
    lengths = {to: message(block, rows, to)[2] for to in places}
    one, two = max(lengths[1], lengths[-1]), max(lengths[2], lengths[-2])
    clean = [(one, width)] * (LEVELS - 1)

    square = jax.ShapeDtypeStruct((2 * width, 2 * width), jnp.bfloat16)
    weights = call(matrix_kernel, "make_matrices", [square] * 2, [], flops=FIRST_FLOPS)
    (first,) = call(
        functools.partial(own_kernel, block, rows),
        "lift_own",
        [lifted[0]],
        [velocity, weights[0]],
        [spread],
    )
    if shared:
        each = {to: (2 * (one if abs(to) == 1 else two), width) for to in places}
        outs, scratch = [each[1], each[2]], [each[to] for to in places]
    else:
        outs, scratch = [(lengths[to], width) for to in places], []
    first, kept, *more = call(
        functools.partial(message_kernel, block, rows, width, count, places),
        "make_messages",
        [lifted[0]] + owned + outs,
        [first] + others + list(weights),
        [spread] + lifted[1:] + coarse + scratch,
        {0: 0},
    )
    own_coarse, messages = more[: LEVELS - 1], more[LEVELS - 1 :]

    def rest():
        return call(
            functools.partial(rest_kernel, block, rows, width),
            "finish_own",
            [owned[0]],
            [first, kept] + own_coarse,
            aliases={1: 0},
        )[0]

    written = [pltpu.SemaphoreType.DMA((COPIES,))]
    if shared:
        near, far = (
            lax.ppermute(
                value,
                ("gx", "gy"),
                [
                    (2 * i + core, 2 * ((i + side * step) % around) + core)
                    for i in range(around)
                    for core, side in enumerate((-1, 1))
                ],
            )
            for step, value in enumerate(messages, 1)
        )
        result = rest()
        (packed,) = call(pack_kernel, "pack_other", [(one + two, width)], [near, far])
        packed = lax.ppermute(packed, "gy", [(0, 1), (1, 0)])
        (result,) = call(
            functools.partial(keep_kernel, block, rows),
            "add_kept",
            [owned[0]],
            [result, near, far],
            clean,
            aliases={0: 0},
        )
        whole, _ = call(
            functools.partial(swap_kernel, block, rows, one),
            "add_swapped",
            [owned[0]] * 2,
            [result, packed],
            written + clean,
            aliases={0: 1},
            hbm_out=(0,),
        )
        return whole

    sent = dict(zip(places, messages))
    received = {
        to: lax.ppermute(sent[to], "gx", [(i, (i + to) % around) for i in range(around)])
        for to in sorted(places, key=lambda to: (to < 0, abs(to)))
    }
    right = [to for to in places if to > 0]
    left = [to for to in places if to < 0]
    (result,) = call(
        functools.partial(add_kernel, block, rows, right, False),
        "add_right",
        [owned[0]],
        [rest()] + [received[to] for to in right],
        clean,
        aliases={0: 0},
        flops=FIRST_FLOPS,
    )
    whole, _ = call(
        functools.partial(add_kernel, block, rows, left, True),
        "add_left",
        [owned[0]] * 2,
        [result] + [received[to] for to in left],
        written + clean,
        aliases={0: 1},
        hbm_out=(0,),
    )
    return whole


def solution(mesh):
    return jax.shard_map(
        local, mesh=mesh, in_specs=(P("gx", "gy", None),), out_specs=P("gx", "gy", None), check_vma=False
    )
```

```python
import functools

import jax
import jax.numpy as jnp
import numpy as np
from jax import lax
from jax.experimental import pallas as pl
from jax.experimental.pallas import tpu as pltpu
from jax.sharding import PartitionSpec as P

LEVELS = 4
STEPS = (-1.586134342, -0.05298011854, 0.8829110762, 0.4435068522)
SCALE = 1.149604398
VMEM_BYTES = 24 * 2**20
FIRST_FLOPS = 10**10
COPIES = 2
SHARED = False


def windows(block):
    found = []
    first, last = 0, block - 1
    for _ in range(LEVELS):
        low = first - 4 + (first % 2)
        high = last + 4 - (last % 2)
        found.append((low, high))
        first, last = low // 2, high // 2
    return found


def message(block, rows, to):
    sent, derived = {}, {}
    spans = windows(block)
    base = ends = 0
    for level, (low, high) in enumerate(spans):
        size, height = block >> level, rows >> level
        first, last = (0, block - 1) if level == 0 else (v // 2 for v in spans[level - 1])
        planes = [p for p in range(low, high + 1) if p // size == to]
        if abs(to) == 1:
            sign = to
            edge = last + 2 - last % 2 if to > 0 else first - 2 + first % 2
            far, near = edge + sign, edge - sign
            if far in planes and edge + 2 * sign in planes:
                derived[level, edge + 2 * sign] = (far, None)
            if far in planes and near in planes:
                derived[level, edge] = (far, near)
        at = base
        for plane in planes:
            if (level, plane) not in derived:
                sent[level, plane] = at
                at += height
        ends = max(ends, at)
        if level == 0:
            base = at
    return sent, derived, -(-ends // 8) * 8


def shift_of(level):
    return (0, 0, 1, 3)[level]


def places_of(block):
    found = set()
    for level, (low, high) in enumerate(windows(block)):
        size = block >> level
        found |= set(range(low // size, high // size + 1))
    return sorted(found - {0})


def z_product(value, weights):
    width = value.shape[-1]
    high = value.astype(jnp.bfloat16)
    rest = (value - high.astype(jnp.float32)).astype(jnp.bfloat16)
    both = jnp.concatenate([high, rest], axis=1)
    product = jnp.dot(both, weights, preferred_element_type=jnp.float32)
    return product[:, :width] + product[:, width:]


def lanes_of(width, spacing, parity):
    lane = lax.broadcasted_iota(jnp.int32, (1, width), 1)
    return lax.rem(lane, 2 * spacing) == (spacing if parity else 0)


def own_lanes(width, level, high_only):
    spacing, shift = 1 << level, shift_of(level)
    lane = lax.broadcasted_iota(jnp.int32, (1, width), 1)
    if high_only:
        return lax.rem(lane, 2 * spacing) == spacing + shift
    return lax.rem(lane, spacing) == shift


def z_lift(value, spacing):
    width = value.shape[-1]
    axis = value.ndim - 1
    for step, weight in enumerate(STEPS):
        factor = jnp.where(lanes_of(width, spacing, step % 2 == 0), weight, 0.0)
        around = pltpu.roll(value, spacing, axis) + pltpu.roll(value, width - spacing, axis)
        value = value + factor * around
    return value


def x_lift(planes):
    def plus(one, other):
        return other if one is None else one if other is None else one + other

    planes = dict(planes)
    for step, weight in enumerate(STEPS):
        parity = 1 if step % 2 == 0 else 0
        for index in range(min(planes) - 1, max(planes) + 2):
            if index % 2 == parity:
                around = plus(planes.get(index - 1), planes.get(index + 1))
                if around is not None:
                    planes[index] = plus(planes.get(index), weight * around)
    return planes


def y_lift_split(even, odd):
    count = even.shape[0]
    a, b, c, d = STEPS
    odd = odd + a * (even + pltpu.roll(even, count - 1, 0))
    even = even + b * (pltpu.roll(odd, 1, 0) + odd)
    odd = odd + c * (even + pltpu.roll(even, count - 1, 0))
    even = even + d * (pltpu.roll(odd, 1, 0) + odd)
    return even, odd


def y_lift_whole(value):
    count = value.shape[0]
    row = lax.broadcasted_iota(jnp.int32, (count, 1), 0)
    for step, weight in enumerate(STEPS):
        factor = jnp.where(lax.rem(row, 2) == (1 if step % 2 == 0 else 0), weight, 0.0)
        value = value + factor * (pltpu.roll(value, 1, 0) + pltpu.roll(value, count - 1, 0))
    return value


def scaled_z(value, spacing):
    width = value.shape[-1]
    odd, even = lanes_of(width, spacing, True), lanes_of(width, spacing, False)
    return value * jnp.where(odd, SCALE, jnp.where(even, 1 / SCALE, 0.0))


def scaled(value, x_odd, y_odd):
    at = (SCALE if x_odd else 1 / SCALE) * (SCALE if y_odd else 1 / SCALE)
    return value if x_odd != y_odd else value * at


def spread_z(source, weights, spread, rows, start, size):
    width = source.shape[-1]
    value = source[start : start + size].reshape(size * rows, width)
    spread[start * rows : (start + size) * rows, :] = z_product(value, weights[...])


def spread_x(block, rows, spread, into, low, base):
    for at in range(0, rows, 8):
        planes = {x: spread[x * rows + at : x * rows + at + 8, :] for x in range(block)}
        for x, value in x_lift(planes).items():
            into[x - low, base + at : base + at + 8, :] = value


def matrix_kernel(*weights):
    width = weights[0].shape[0] // 2
    row = lax.broadcasted_iota(jnp.int32, (width, width), 0)
    lane = lax.broadcasted_iota(jnp.int32, (width, width), 1)
    value = jnp.where(row == lane, 1.0, 0.0)
    full = [scaled_z(z_lift(value, 1), 1), jnp.zeros((width, width), jnp.float32)]
    for level in range(1, LEVELS):
        spacing = 1 << level
        value = scaled_z(z_lift(value, spacing), spacing)
        full[1] += pltpu.roll(value, shift_of(level), 1) if shift_of(level) else value
        value = jnp.where(lanes_of(width, spacing, False), value, 0.0)
    for weight, matrix in zip(weights, full):
        high = matrix.astype(jnp.bfloat16)
        rest = (matrix - high.astype(jnp.float32)).astype(jnp.bfloat16)
        weight[:width, :width] = high
        weight[:width, width:] = rest
        weight[width:, :width] = high
        weight[width:, width:] = jnp.zeros_like(rest)


def own_kernel(block, rows, velocity, weights, into, spread):
    step = max(1, min(block, 512 // rows))
    for x in range(0, block, step):
        spread_z(velocity, weights, spread, rows, x, step)
    spread_x(block, rows, spread, into, windows(block)[0][0], 0)


def message_kernel(block, rows, width, count, places, *refs):
    refs = list(refs)

    def take(number):
        taken = refs[:number]
        del refs[:number]
        return taken

    shared = count == 2 and SHARED
    halves = 2 if shared else 1
    (_,) = take(1)
    others = take(count - 1)
    weights = take(2)
    (first,) = take(1)
    own = take(LEVELS)
    passed = take(2 if shared else len(places))
    (spread,) = take(1)
    lifted = [first] + take(LEVELS - 1)
    coarse = take(LEVELS - 1)
    messages = dict(zip(places, take(len(places)) if shared else passed))
    spans = windows(block)
    total = count * rows
    tables = {to: message(block, rows, to) for to in places}
    lengths = {to: messages[to].shape[0] // halves for to in places}
    written = {to: set() for to in places}

    def post(to, at, number, value):
        here = range(at, at + 2 * number, 2)
        if written[to].isdisjoint(here):
            messages[to][pl.ds(at, number, 2), :] = value
        else:
            messages[to][pl.ds(at, number, 2), :] += value
        written[to].update(here)

    def put(level, plane, half, even, odd):
        number = (rows >> level) // 2
        low = level < LEVELS - 1 and plane % 2 == 0
        if level > 0 or low:
            even = jnp.where(own_lanes(width, level, low), even, 0.0)
        if level > 0:
            odd = jnp.where(own_lanes(width, level, False), odd, 0.0)
        to = plane // (block >> level)
        if to == 0:
            own[level][plane, pl.ds(0, number, 2), :] = even
            own[level][plane, pl.ds(1, number, 2), :] = odd
        else:
            at = tables[to][0][level, plane] + half * lengths[to]
            post(to, at, number, even)
            post(to, at + 1, number, odd)

    for level in range(LEVELS):
        low, high = spans[level]
        height = total >> level
        half, mine = height // 2, (rows >> level) // 2
        into = lifted[level]

        if level == 0:
            for part, source in enumerate(others):
                step = min(block, max(1, 512 // rows))
                for x in range(0, block, step):
                    spread_z(source, weights[0], spread, rows, x, step)
                spread_x(block, rows, spread, into, low, (part + 1) * rows)
        else:
            start, stop = spans[level - 1][0] // 2, spans[level - 1][1] // 2 + 1
            source = coarse[level - 1]
            if level == 1:
                size = (stop - start) * height
                for at in range(0, size, 512):
                    end = min(size, at + 512)
                    source[at:end, :] = z_product(source[at:end, :], weights[level][...])
            for at in range(0, height, 8):
                planes = {}
                for x in range(start, stop):
                    row = (x - start) * height + at
                    planes[x] = source[row : row + 8, :]
                for x, value in x_lift(planes).items():
                    into[x - low, at : at + 8, :] = value

        for plane in range(low, high + 1):
            odd_plane = plane % 2 == 1
            to = plane // (block >> level)
            if level == 0 and odd_plane and to == 0:
                continue
            goes_on = level < LEVELS - 1 and not odd_plane
            sends = to == 0 or (level, plane) in tables[to][0]
            if not goes_on and not sends:
                continue
            at = plane - low
            split = half % 8 == 0
            if split:
                even, odd = y_lift_split(
                    into[at, pl.ds(0, half, 2), :], into[at, pl.ds(1, half, 2), :]
                )
                even = scaled(even, odd_plane, False)
            else:
                into[at] = y_lift_whole(into[at])
                even = scaled(into[at, pl.ds(0, half, 2), :], odd_plane, False)
            if goes_on:
                row = ((plane - low) // 2) * half
                coarse[level][row : row + half, :] = even
            if not sends:
                continue
            for part in range(halves if to else 1):
                if split:
                    here_even = even[part * mine : (part + 1) * mine]
                    here_odd = odd[part * mine : (part + 1) * mine]
                else:
                    here_even = into[at, pl.ds(2 * part * mine, mine, 2), :]
                    here_even = scaled(here_even, odd_plane, False)
                    here_odd = into[at, pl.ds(2 * part * mine + 1, mine, 2), :]
                put(level, plane, part, here_even, scaled(here_odd, odd_plane, True))

    for to in places:
        for row in range(halves * lengths[to]):
            if row not in written[to]:
                messages[to][row : row + 1, :] = jnp.zeros((1, width), jnp.float32)
    if shared:
        for far, target in enumerate(passed, 1):
            target[...] = jnp.where(lax.axis_index("gy") == 0, messages[-far][...], messages[far][...])


def rest_kernel(block, rows, width, first, _, *refs):
    coarse, out = refs[:-1], refs[-1]
    low = windows(block)[0][0]
    half, mine = first.shape[1] // 2, rows // 2
    for plane in range(1, block, 2):
        even, odd = y_lift_split(
            first[plane - low, pl.ds(0, half, 2), :], first[plane - low, pl.ds(1, half, 2), :]
        )
        out[plane, pl.ds(0, mine, 2), :] = scaled(even[:mine], True, False)
        out[plane, pl.ds(1, mine, 2), :] = scaled(odd[:mine], True, True)
    for level in range(1, LEVELS):
        spacing, shift = 1 << level, shift_of(level)
        for plane in range(block >> level):
            value = coarse[level - 1][plane]
            if shift:
                value = pltpu.roll(value, width - shift, 1)
            out[plane * spacing, pl.ds(0, rows >> level, spacing), :] += value


def add_message(block, rows, to, arrived, base, out, clean):
    sent, derived, _ = message(block, rows, to)
    a, b, c, d = STEPS
    width = out.shape[-1]
    for level in sorted({level for level, _ in sent}):
        spacing, height = 1 << level, rows >> level
        shape = (height, width)
        if level > 0:
            here = [at for (found, _), at in sent.items() if found == level]
            start, stop = min(here), -(-(max(here) + height) // 8) * 8
            value = arrived[base + start : base + stop, :]
            if shift_of(level):
                value = pltpu.roll(value, width - shift_of(level), 1)
            lane = lax.broadcasted_iota(jnp.int32, (1, width), 1)
            value = jnp.where(lax.rem(lane, spacing) == 0, value, 0.0)
            source = clean[level - 1]
            source[: stop - start, :] = value
        else:
            start, source = -base, arrived

        def read(plane):
            at = sent[level, plane] - start
            return source[at : at + height, :]

        def add(plane, value):
            x = (plane - to * (block >> level)) * spacing
            out[x, pl.ds(0, height, spacing), :] += value

        for found, plane in sent:
            if found == level:
                add(plane, read(plane))
        for (found, plane), (far, near) in derived.items():
            if found == level:
                if near is None:
                    value = (d / SCALE**2) * read(far)
                else:
                    value = ((1 / c + d) / SCALE**2) * read(far) + (d / SCALE**2) * read(near)
                row = lax.broadcasted_iota(jnp.int32, shape, 0)
                keep = (lax.rem(row, 2) == 1) | lanes_of(width, spacing, True)
                add(plane, jnp.where(keep, value, 0.0))


def write_out(out, whole, done):
    parts = done.shape[0]
    size = out.shape[0] // parts
    copies = [
        pltpu.make_async_copy(
            out.at[pl.ds(part * size, size)], whole.at[pl.ds(part * size, size)], done.at[part]
        )
        for part in range(parts)
    ]
    for copy in copies:
        copy.start()
    for copy in copies:
        copy.wait()


def add_kernel(block, rows, places, last, _, *refs):
    received, refs = refs[: len(places)], refs[len(places) :]
    if last:
        whole, out, done, *clean = refs
    else:
        out, *clean = refs
    for to, arrived in zip(places, received):
        add_message(block, rows, to, arrived, 0, out, clean)
    if last:
        write_out(out, whole, done)


def keep_kernel(block, rows, _, near, far, out, *clean):
    for core, side in enumerate((-1, 1)):

        @pl.when(lax.axis_index("gy") == core)
        def _():
            add_message(block, rows, side, near, 0, out, clean)
            add_message(block, rows, 2 * side, far, 0, out, clean)


def pack_kernel(near, far, packed):
    one, two = near.shape[0] // 2, far.shape[0] // 2
    packed[:one, :] = near[one:, :]
    packed[one:, :] = far[two:, :]


def swap_kernel(block, rows, one, _, packed, whole, out, done, *clean):
    for core, side in enumerate((1, -1)):

        @pl.when(lax.axis_index("gy") == core)
        def _():
            add_message(block, rows, side, packed, 0, out, clean)
            add_message(block, rows, 2 * side, packed, one, out, clean)

    write_out(out, whole, done)


def call(body, name, outs, ins, scratch=(), aliases=None, flops=0, hbm_out=()):
    vmem, hbm = pl.BlockSpec(memory_space=pltpu.VMEM), pl.BlockSpec(memory_space=pltpu.HBM)
    f32 = jnp.float32
    shapes = [out if isinstance(out, jax.ShapeDtypeStruct) else jax.ShapeDtypeStruct(out, f32) for out in outs]
    moved = 4 * sum(int(np.prod(shape.shape)) for shape in shapes)
    return pl.pallas_call(
        body,
        out_shape=shapes,
        in_specs=[vmem] * len(ins),
        out_specs=[hbm if n in hbm_out else vmem for n in range(len(outs))],
        scratch_shapes=[pltpu.VMEM(shape, f32) if isinstance(shape, tuple) else shape for shape in scratch],
        input_output_aliases=aliases or {},
        compiler_params=pltpu.CompilerParams(vmem_limit_bytes=VMEM_BYTES),
        cost_estimate=pl.CostEstimate(flops=flops, bytes_accessed=2 * moved, transcendentals=0),
        name=name,
    )(*ins)


def local(velocity):
    block, rows, width = velocity.shape
    around, count = lax.axis_size("gx"), lax.axis_size("gy")
    shared = count == 2 and SHARED
    places = places_of(block)
    spans = windows(block)
    total = count * rows

    others = [
        lax.ppermute(velocity, "gy", [(i, (i - k) % count) for i in range(count)])
        for k in range(1, count)
    ]
    lifted = [
        (high - low + 1, total >> level, width) for level, (low, high) in enumerate(spans)
    ]
    coarse = [
        ((high // 2 - low // 2 + 1) * (total >> (level + 1)), width)
        for level, (low, high) in enumerate(spans[:-1])
    ]
    spread = (block * rows, width)
    owned = [(block >> level, rows >> level, width) for level in range(LEVELS)]
    lengths = {to: message(block, rows, to)[2] for to in places}
    one, two = max(lengths[1], lengths[-1]), max(lengths[2], lengths[-2])
    clean = [(one, width)] * (LEVELS - 1)

    square = jax.ShapeDtypeStruct((2 * width, 2 * width), jnp.bfloat16)
    weights = call(matrix_kernel, "make_matrices", [square] * 2, [], flops=FIRST_FLOPS)
    (first,) = call(
        functools.partial(own_kernel, block, rows),
        "lift_own",
        [lifted[0]],
        [velocity, weights[0]],
        [spread],
    )
    if shared:
        each = {to: (2 * (one if abs(to) == 1 else two), width) for to in places}
        outs, scratch = [each[1], each[2]], [each[to] for to in places]
    else:
        outs, scratch = [(lengths[to], width) for to in places], []
    first, kept, *more = call(
        functools.partial(message_kernel, block, rows, width, count, places),
        "make_messages",
        [lifted[0]] + owned + outs,
        [first] + others + list(weights),
        [spread] + lifted[1:] + coarse + scratch,
        {0: 0},
    )
    own_coarse, messages = more[: LEVELS - 1], more[LEVELS - 1 :]

    def rest():
        return call(
            functools.partial(rest_kernel, block, rows, width),
            "finish_own",
            [owned[0]],
            [first, kept] + own_coarse,
            aliases={1: 0},
        )[0]

    written = [pltpu.SemaphoreType.DMA((COPIES,))]
    if shared:
        near, far = (
            lax.ppermute(
                value,
                ("gx", "gy"),
                [
                    (2 * i + core, 2 * ((i + side * step) % around) + core)
                    for i in range(around)
                    for core, side in enumerate((-1, 1))
                ],
            )
            for step, value in enumerate(messages, 1)
        )
        result = rest()
        (packed,) = call(pack_kernel, "pack_other", [(one + two, width)], [near, far])
        packed = lax.ppermute(packed, "gy", [(0, 1), (1, 0)])
        (result,) = call(
            functools.partial(keep_kernel, block, rows),
            "add_kept",
            [owned[0]],
            [result, near, far],
            clean,
            aliases={0: 0},
        )
        whole, _ = call(
            functools.partial(swap_kernel, block, rows, one),
            "add_swapped",
            [owned[0]] * 2,
            [result, packed],
            written + clean,
            aliases={0: 1},
            hbm_out=(0,),
        )
        return whole

    sent = dict(zip(places, messages))
    received = {
        to: lax.ppermute(sent[to], "gx", [(i, (i + to) % around) for i in range(around)])
        for to in sorted(places, key=lambda to: (to < 0, abs(to)))
    }
    right = [to for to in places if to > 0]
    left = [to for to in places if to < 0]
    (result,) = call(
        functools.partial(add_kernel, block, rows, right, False),
        "add_right",
        [owned[0]],
        [rest()] + [received[to] for to in right],
        clean,
        aliases={0: 0},
        flops=FIRST_FLOPS,
    )
    whole, _ = call(
        functools.partial(add_kernel, block, rows, left, True),
        "add_left",
        [owned[0]] * 2,
        [result] + [received[to] for to in left],
        written + clean,
        aliases={0: 1},
        hbm_out=(0,),
    )
    return whole


def solution(mesh):
    return jax.shard_map(
        local, mesh=mesh, in_specs=(P("gx", "gy", None),), out_specs=P("gx", "gy", None), check_vma=False
    )
```

```python
import functools

import jax
import jax.numpy as jnp
import numpy as np
from jax import lax
from jax.experimental import pallas as pl
from jax.experimental.pallas import tpu as pltpu
from jax.sharding import PartitionSpec as P

LEVELS = 4
STEPS = (-1.586134342, -0.05298011854, 0.8829110762, 0.4435068522)
SCALE = 1.149604398
VMEM_BYTES = 24 * 2**20
FIRST_FLOPS = 10**10
COPIES = 2
SHARED = True
SIDES = (1, -1)


def windows(block):
    found = []
    first, last = 0, block - 1
    for _ in range(LEVELS):
        low = first - 4 + (first % 2)
        high = last + 4 - (last % 2)
        found.append((low, high))
        first, last = low // 2, high // 2
    return found


def message(block, rows, to):
    sent, derived = {}, {}
    spans = windows(block)
    base = ends = 0
    for level, (low, high) in enumerate(spans):
        size, height = block >> level, rows >> level
        first, last = (0, block - 1) if level == 0 else (v // 2 for v in spans[level - 1])
        planes = [p for p in range(low, high + 1) if p // size == to]
        if abs(to) == 1:
            sign = to
            edge = last + 2 - last % 2 if to > 0 else first - 2 + first % 2
            far, near = edge + sign, edge - sign
            if far in planes and edge + 2 * sign in planes:
                derived[level, edge + 2 * sign] = (far, None)
            if far in planes and near in planes:
                derived[level, edge] = (far, near)
        at = base
        for plane in planes:
            if (level, plane) not in derived:
                sent[level, plane] = at
                at += height
        ends = max(ends, at)
        if level == 0:
            base = at
    return sent, derived, -(-ends // 8) * 8


def shift_of(level):
    return (0, 0, 1, 3)[level]


def places_of(block):
    found = set()
    for level, (low, high) in enumerate(windows(block)):
        size = block >> level
        found |= set(range(low // size, high // size + 1))
    return sorted(found - {0})


def z_product(value, weights):
    width = value.shape[-1]
    high = value.astype(jnp.bfloat16)
    rest = (value - high.astype(jnp.float32)).astype(jnp.bfloat16)
    both = jnp.concatenate([high, rest], axis=1)
    product = jnp.dot(both, weights, preferred_element_type=jnp.float32)
    return product[:, :width] + product[:, width:]


def lanes_of(width, spacing, parity):
    lane = lax.broadcasted_iota(jnp.int32, (1, width), 1)
    return lax.rem(lane, 2 * spacing) == (spacing if parity else 0)


def own_lanes(width, level, high_only):
    spacing, shift = 1 << level, shift_of(level)
    lane = lax.broadcasted_iota(jnp.int32, (1, width), 1)
    if high_only:
        return lax.rem(lane, 2 * spacing) == spacing + shift
    return lax.rem(lane, spacing) == shift


def z_lift(value, spacing):
    width = value.shape[-1]
    axis = value.ndim - 1
    for step, weight in enumerate(STEPS):
        factor = jnp.where(lanes_of(width, spacing, step % 2 == 0), weight, 0.0)
        around = pltpu.roll(value, spacing, axis) + pltpu.roll(value, width - spacing, axis)
        value = value + factor * around
    return value


def x_lift(planes):
    def plus(one, other):
        return other if one is None else one if other is None else one + other

    planes = dict(planes)
    for step, weight in enumerate(STEPS):
        parity = 1 if step % 2 == 0 else 0
        for index in range(min(planes) - 1, max(planes) + 2):
            if index % 2 == parity:
                around = plus(planes.get(index - 1), planes.get(index + 1))
                if around is not None:
                    planes[index] = plus(planes.get(index), weight * around)
    return planes


def y_lift_split(even, odd):
    count = even.shape[0]
    a, b, c, d = STEPS
    odd = odd + a * (even + pltpu.roll(even, count - 1, 0))
    even = even + b * (pltpu.roll(odd, 1, 0) + odd)
    odd = odd + c * (even + pltpu.roll(even, count - 1, 0))
    even = even + d * (pltpu.roll(odd, 1, 0) + odd)
    return even, odd


def y_lift_whole(value):
    count = value.shape[0]
    row = lax.broadcasted_iota(jnp.int32, (count, 1), 0)
    for step, weight in enumerate(STEPS):
        factor = jnp.where(lax.rem(row, 2) == (1 if step % 2 == 0 else 0), weight, 0.0)
        value = value + factor * (pltpu.roll(value, 1, 0) + pltpu.roll(value, count - 1, 0))
    return value


def scaled_z(value, spacing):
    width = value.shape[-1]
    odd, even = lanes_of(width, spacing, True), lanes_of(width, spacing, False)
    return value * jnp.where(odd, SCALE, jnp.where(even, 1 / SCALE, 0.0))


def scaled(value, x_odd, y_odd):
    at = (SCALE if x_odd else 1 / SCALE) * (SCALE if y_odd else 1 / SCALE)
    return value if x_odd != y_odd else value * at


def spread_z(source, weights, spread, rows, start, size):
    width = source.shape[-1]
    value = source[start : start + size].reshape(size * rows, width)
    spread[start * rows : (start + size) * rows, :] = z_product(value, weights[...])


def spread_x(block, rows, spread, into, low, base):
    for at in range(0, rows, 8):
        planes = {x: spread[x * rows + at : x * rows + at + 8, :] for x in range(block)}
        for x, value in x_lift(planes).items():
            into[x - low, base + at : base + at + 8, :] = value


def matrix_kernel(*weights):
    width = weights[0].shape[0] // 2
    row = lax.broadcasted_iota(jnp.int32, (width, width), 0)
    lane = lax.broadcasted_iota(jnp.int32, (width, width), 1)
    value = jnp.where(row == lane, 1.0, 0.0)
    full = [scaled_z(z_lift(value, 1), 1), jnp.zeros((width, width), jnp.float32)]
    for level in range(1, LEVELS):
        spacing = 1 << level
        value = scaled_z(z_lift(value, spacing), spacing)
        full[1] += pltpu.roll(value, shift_of(level), 1) if shift_of(level) else value
        value = jnp.where(lanes_of(width, spacing, False), value, 0.0)
    for weight, matrix in zip(weights, full):
        high = matrix.astype(jnp.bfloat16)
        rest = (matrix - high.astype(jnp.float32)).astype(jnp.bfloat16)
        weight[:width, :width] = high
        weight[:width, width:] = rest
        weight[width:, :width] = high
        weight[width:, width:] = jnp.zeros_like(rest)


def own_kernel(block, rows, velocity, weights, into, spread):
    step = max(1, min(block, 512 // rows))
    for x in range(0, block, step):
        spread_z(velocity, weights, spread, rows, x, step)
    spread_x(block, rows, spread, into, windows(block)[0][0], 0)


def message_kernel(block, rows, width, count, places, *refs):
    refs = list(refs)

    def take(number):
        taken = refs[:number]
        del refs[:number]
        return taken

    shared = count == 2 and SHARED
    halves = 2 if shared else 1
    (_,) = take(1)
    others = take(count - 1)
    weights = take(2)
    (first,) = take(1)
    own = take(LEVELS)
    passed = take(2 if shared else len(places))
    (spread,) = take(1)
    lifted = [first] + take(LEVELS - 1)
    coarse = take(LEVELS - 1)
    messages = dict(zip(places, take(len(places)) if shared else passed))
    spans = windows(block)
    total = count * rows
    tables = {to: message(block, rows, to) for to in places}
    lengths = {to: messages[to].shape[0] // halves for to in places}
    written = {to: set() for to in places}

    def post(to, at, number, value):
        here = range(at, at + 2 * number, 2)
        if written[to].isdisjoint(here):
            messages[to][pl.ds(at, number, 2), :] = value
        else:
            messages[to][pl.ds(at, number, 2), :] += value
        written[to].update(here)

    def put(level, plane, half, even, odd):
        number = (rows >> level) // 2
        low = level < LEVELS - 1 and plane % 2 == 0
        if level > 0 or low:
            even = jnp.where(own_lanes(width, level, low), even, 0.0)
        if level > 0:
            odd = jnp.where(own_lanes(width, level, False), odd, 0.0)
        to = plane // (block >> level)
        if to == 0:
            own[level][plane, pl.ds(0, number, 2), :] = even
            own[level][plane, pl.ds(1, number, 2), :] = odd
        else:
            at = tables[to][0][level, plane] + half * lengths[to]
            post(to, at, number, even)
            post(to, at + 1, number, odd)

    for level in range(LEVELS):
        low, high = spans[level]
        height = total >> level
        half, mine = height // 2, (rows >> level) // 2
        into = lifted[level]

        if level == 0:
            for part, source in enumerate(others):
                step = min(block, max(1, 512 // rows))
                for x in range(0, block, step):
                    spread_z(source, weights[0], spread, rows, x, step)
                spread_x(block, rows, spread, into, low, (part + 1) * rows)
        else:
            start, stop = spans[level - 1][0] // 2, spans[level - 1][1] // 2 + 1
            source = coarse[level - 1]
            if level == 1:
                size = (stop - start) * height
                for at in range(0, size, 512):
                    end = min(size, at + 512)
                    source[at:end, :] = z_product(source[at:end, :], weights[level][...])
            for at in range(0, height, 8):
                planes = {}
                for x in range(start, stop):
                    row = (x - start) * height + at
                    planes[x] = source[row : row + 8, :]
                for x, value in x_lift(planes).items():
                    into[x - low, at : at + 8, :] = value

        for plane in range(low, high + 1):
            odd_plane = plane % 2 == 1
            to = plane // (block >> level)
            if level == 0 and odd_plane and to == 0:
                continue
            goes_on = level < LEVELS - 1 and not odd_plane
            sends = to == 0 or (level, plane) in tables[to][0]
            if not goes_on and not sends:
                continue
            at = plane - low
            split = half % 8 == 0
            if split:
                even, odd = y_lift_split(
                    into[at, pl.ds(0, half, 2), :], into[at, pl.ds(1, half, 2), :]
                )
                even = scaled(even, odd_plane, False)
            else:
                into[at] = y_lift_whole(into[at])
                even = scaled(into[at, pl.ds(0, half, 2), :], odd_plane, False)
            if goes_on:
                row = ((plane - low) // 2) * half
                coarse[level][row : row + half, :] = even
            if not sends:
                continue
            for part in range(halves if to else 1):
                if split:
                    here_even = even[part * mine : (part + 1) * mine]
                    here_odd = odd[part * mine : (part + 1) * mine]
                else:
                    here_even = into[at, pl.ds(2 * part * mine, mine, 2), :]
                    here_even = scaled(here_even, odd_plane, False)
                    here_odd = into[at, pl.ds(2 * part * mine + 1, mine, 2), :]
                put(level, plane, part, here_even, scaled(here_odd, odd_plane, True))

    for to in places:
        for row in range(halves * lengths[to]):
            if row not in written[to]:
                messages[to][row : row + 1, :] = jnp.zeros((1, width), jnp.float32)
    if shared:
        for far, target in enumerate(passed, 1):
            target[...] = jnp.where(lax.axis_index("gy") == 0, messages[far][...], messages[-far][...])


def rest_kernel(block, rows, width, first, _, *refs):
    coarse, out = refs[:-1], refs[-1]
    low = windows(block)[0][0]
    half, mine = first.shape[1] // 2, rows // 2
    for plane in range(1, block, 2):
        even, odd = y_lift_split(
            first[plane - low, pl.ds(0, half, 2), :], first[plane - low, pl.ds(1, half, 2), :]
        )
        out[plane, pl.ds(0, mine, 2), :] = scaled(even[:mine], True, False)
        out[plane, pl.ds(1, mine, 2), :] = scaled(odd[:mine], True, True)
    for level in range(1, LEVELS):
        spacing, shift = 1 << level, shift_of(level)
        for plane in range(block >> level):
            value = coarse[level - 1][plane]
            if shift:
                value = pltpu.roll(value, width - shift, 1)
            out[plane * spacing, pl.ds(0, rows >> level, spacing), :] += value


def add_message(block, rows, to, arrived, base, out, clean):
    sent, derived, _ = message(block, rows, to)
    a, b, c, d = STEPS
    width = out.shape[-1]
    for level in sorted({level for level, _ in sent}):
        spacing, height = 1 << level, rows >> level
        shape = (height, width)
        if level > 0:
            here = [at for (found, _), at in sent.items() if found == level]
            start, stop = min(here), -(-(max(here) + height) // 8) * 8
            value = arrived[base + start : base + stop, :]
            if shift_of(level):
                value = pltpu.roll(value, width - shift_of(level), 1)
            lane = lax.broadcasted_iota(jnp.int32, (1, width), 1)
            value = jnp.where(lax.rem(lane, spacing) == 0, value, 0.0)
            source = clean[level - 1]
            source[: stop - start, :] = value
        else:
            start, source = -base, arrived

        def read(plane):
            at = sent[level, plane] - start
            return source[at : at + height, :]

        def add(plane, value):
            x = (plane - to * (block >> level)) * spacing
            out[x, pl.ds(0, height, spacing), :] += value

        for found, plane in sent:
            if found == level:
                add(plane, read(plane))
        for (found, plane), (far, near) in derived.items():
            if found == level:
                if near is None:
                    value = (d / SCALE**2) * read(far)
                else:
                    value = ((1 / c + d) / SCALE**2) * read(far) + (d / SCALE**2) * read(near)
                row = lax.broadcasted_iota(jnp.int32, shape, 0)
                keep = (lax.rem(row, 2) == 1) | lanes_of(width, spacing, True)
                add(plane, jnp.where(keep, value, 0.0))


def write_out(out, whole, done):
    parts = done.shape[0]
    size = out.shape[0] // parts
    copies = [
        pltpu.make_async_copy(
            out.at[pl.ds(part * size, size)], whole.at[pl.ds(part * size, size)], done.at[part]
        )
        for part in range(parts)
    ]
    for copy in copies:
        copy.start()
    for copy in copies:
        copy.wait()


def add_kernel(block, rows, places, last, _, *refs):
    received, refs = refs[: len(places)], refs[len(places) :]
    if last:
        whole, out, done, *clean = refs
    else:
        out, *clean = refs
    for to, arrived in zip(places, received):
        add_message(block, rows, to, arrived, 0, out, clean)
    if last:
        write_out(out, whole, done)


def keep_kernel(block, rows, _, near, far, out, *clean):
    for core, side in enumerate(SIDES):

        @pl.when(lax.axis_index("gy") == core)
        def _():
            add_message(block, rows, side, near, 0, out, clean)
            add_message(block, rows, 2 * side, far, 0, out, clean)


def pack_kernel(near, far, packed):
    one, two = near.shape[0] // 2, far.shape[0] // 2
    packed[:one, :] = near[one:, :]
    packed[one:, :] = far[two:, :]


def swap_kernel(block, rows, one, _, packed, whole, out, done, *clean):
    for core, side in enumerate(SIDES[::-1]):

        @pl.when(lax.axis_index("gy") == core)
        def _():
            add_message(block, rows, side, packed, 0, out, clean)
            add_message(block, rows, 2 * side, packed, one, out, clean)

    write_out(out, whole, done)


def call(body, name, outs, ins, scratch=(), aliases=None, flops=0, hbm_out=()):
    vmem, hbm = pl.BlockSpec(memory_space=pltpu.VMEM), pl.BlockSpec(memory_space=pltpu.HBM)
    f32 = jnp.float32
    shapes = [out if isinstance(out, jax.ShapeDtypeStruct) else jax.ShapeDtypeStruct(out, f32) for out in outs]
    moved = 4 * sum(int(np.prod(shape.shape)) for shape in shapes)
    return pl.pallas_call(
        body,
        out_shape=shapes,
        in_specs=[vmem] * len(ins),
        out_specs=[hbm if n in hbm_out else vmem for n in range(len(outs))],
        scratch_shapes=[pltpu.VMEM(shape, f32) if isinstance(shape, tuple) else shape for shape in scratch],
        input_output_aliases=aliases or {},
        compiler_params=pltpu.CompilerParams(vmem_limit_bytes=VMEM_BYTES),
        cost_estimate=pl.CostEstimate(flops=flops, bytes_accessed=2 * moved, transcendentals=0),
        name=name,
    )(*ins)


def local(velocity):
    block, rows, width = velocity.shape
    around, count = lax.axis_size("gx"), lax.axis_size("gy")
    shared = count == 2 and SHARED
    places = places_of(block)
    spans = windows(block)
    total = count * rows

    others = [
        lax.ppermute(velocity, "gy", [(i, (i - k) % count) for i in range(count)])
        for k in range(1, count)
    ]
    lifted = [
        (high - low + 1, total >> level, width) for level, (low, high) in enumerate(spans)
    ]
    coarse = [
        ((high // 2 - low // 2 + 1) * (total >> (level + 1)), width)
        for level, (low, high) in enumerate(spans[:-1])
    ]
    spread = (block * rows, width)
    owned = [(block >> level, rows >> level, width) for level in range(LEVELS)]
    lengths = {to: message(block, rows, to)[2] for to in places}
    one, two = max(lengths[1], lengths[-1]), max(lengths[2], lengths[-2])
    clean = [(one, width)] * (LEVELS - 1)

    square = jax.ShapeDtypeStruct((2 * width, 2 * width), jnp.bfloat16)
    weights = call(matrix_kernel, "make_matrices", [square] * 2, [], flops=FIRST_FLOPS)
    (first,) = call(
        functools.partial(own_kernel, block, rows),
        "lift_own",
        [lifted[0]],
        [velocity, weights[0]],
        [spread],
    )
    if shared:
        each = {to: (2 * (one if abs(to) == 1 else two), width) for to in places}
        outs, scratch = [each[1], each[2]], [each[to] for to in places]
    else:
        outs, scratch = [(lengths[to], width) for to in places], []
    first, kept, *more = call(
        functools.partial(message_kernel, block, rows, width, count, places),
        "make_messages",
        [lifted[0]] + owned + outs,
        [first] + others + list(weights),
        [spread] + lifted[1:] + coarse + scratch,
        {0: 0},
    )
    own_coarse, messages = more[: LEVELS - 1], more[LEVELS - 1 :]

    def rest():
        return call(
            functools.partial(rest_kernel, block, rows, width),
            "finish_own",
            [owned[0]],
            [first, kept] + own_coarse,
            aliases={1: 0},
        )[0]

    written = [pltpu.SemaphoreType.DMA((COPIES,))]
    if shared:
        near, far = (
            lax.ppermute(
                value,
                ("gx", "gy"),
                [
                    (2 * i + core, 2 * ((i + side * step) % around) + core)
                    for i in range(around)
                    for core, side in enumerate(SIDES)
                ],
            )
            for step, value in enumerate(messages, 1)
        )
        result = rest()
        (packed,) = call(pack_kernel, "pack_other", [(one + two, width)], [near, far])
        packed = lax.ppermute(packed, "gy", [(0, 1), (1, 0)])
        (result,) = call(
            functools.partial(keep_kernel, block, rows),
            "add_kept",
            [owned[0]],
            [result, near, far],
            clean,
            aliases={0: 0},
        )
        whole, _ = call(
            functools.partial(swap_kernel, block, rows, one),
            "add_swapped",
            [owned[0]] * 2,
            [result, packed],
            written + clean,
            aliases={0: 1},
            hbm_out=(0,),
        )
        return whole

    sent = dict(zip(places, messages))
    received = {
        to: lax.ppermute(sent[to], "gx", [(i, (i + to) % around) for i in range(around)])
        for to in sorted(places, key=lambda to: (to < 0, abs(to)))
    }
    right = [to for to in places if to > 0]
    left = [to for to in places if to < 0]
    (result,) = call(
        functools.partial(add_kernel, block, rows, right, False),
        "add_right",
        [owned[0]],
        [rest()] + [received[to] for to in right],
        clean,
        aliases={0: 0},
        flops=FIRST_FLOPS,
    )
    whole, _ = call(
        functools.partial(add_kernel, block, rows, left, True),
        "add_left",
        [owned[0]] * 2,
        [result] + [received[to] for to in left],
        written + clean,
        aliases={0: 1},
        hbm_out=(0,),
    )
    return whole


def solution(mesh):
    return jax.shard_map(
        local, mesh=mesh, in_specs=(P("gx", "gy", None),), out_specs=P("gx", "gy", None), check_vma=False
    )
```

```python
import functools

import jax
import jax.numpy as jnp
import numpy as np
from jax import lax
from jax.experimental import pallas as pl
from jax.experimental.pallas import tpu as pltpu
from jax.sharding import PartitionSpec as P

LEVELS = 4
STEPS = (-1.586134342, -0.05298011854, 0.8829110762, 0.4435068522)
SCALE = 1.149604398
VMEM_BYTES = 24 * 2**20
FIRST_FLOPS = 10**10
SHARED = True
SIDES = (1, -1)


def windows(block):
    found = []
    first, last = 0, block - 1
    for _ in range(LEVELS):
        low = first - 4 + (first % 2)
        high = last + 4 - (last % 2)
        found.append((low, high))
        first, last = low // 2, high // 2
    return found


def message(block, rows, to):
    sent, derived = {}, {}
    spans = windows(block)
    base = ends = 0
    for level, (low, high) in enumerate(spans):
        size, height = block >> level, rows >> level
        first, last = (0, block - 1) if level == 0 else (v // 2 for v in spans[level - 1])
        planes = [p for p in range(low, high + 1) if p // size == to]
        if abs(to) == 1:
            sign = to
            edge = last + 2 - last % 2 if to > 0 else first - 2 + first % 2
            far, near = edge + sign, edge - sign
            if far in planes and edge + 2 * sign in planes:
                derived[level, edge + 2 * sign] = (far, None)
            if far in planes and near in planes:
                derived[level, edge] = (far, near)
        planes = [plane for plane in planes if (level, plane) not in derived]
        at = base
        if level == 1:
            extra = planes[-1] if len(planes) > 3 else None
        elif level > 1 and extra is not None:
            at = base + (rows >> 1)
        for plane in planes:
            if level == 1 and plane == extra:
                sent[level, plane] = base, shift_of(2)
                continue
            sent[level, plane] = at, shift_of(level)
            at += height
        ends = max(ends, at)
        if level == 0:
            base = at
    return sent, derived, -(-ends // 8) * 8


def shift_of(level):
    return (0, 0, 1, 3)[level]


def places_of(block):
    found = set()
    for level, (low, high) in enumerate(windows(block)):
        size = block >> level
        found |= set(range(low // size, high // size + 1))
    return sorted(found - {0})


def z_product(value, weights):
    width = value.shape[-1]
    high = value.astype(jnp.bfloat16)
    rest = (value - high.astype(jnp.float32)).astype(jnp.bfloat16)
    both = jnp.concatenate([high, rest], axis=1)
    product = jnp.dot(both, weights, preferred_element_type=jnp.float32)
    return product[:, :width] + product[:, width:]


def lanes_of(width, spacing, parity):
    lane = lax.broadcasted_iota(jnp.int32, (1, width), 1)
    return lax.rem(lane, 2 * spacing) == (spacing if parity else 0)


def own_lanes(width, level, high_only):
    spacing, shift = 1 << level, shift_of(level)
    lane = lax.broadcasted_iota(jnp.int32, (1, width), 1)
    if high_only:
        return lax.rem(lane, 2 * spacing) == spacing + shift
    return lax.rem(lane, spacing) == shift


def z_lift(value, spacing):
    width = value.shape[-1]
    axis = value.ndim - 1
    for step, weight in enumerate(STEPS):
        factor = jnp.where(lanes_of(width, spacing, step % 2 == 0), weight, 0.0)
        around = pltpu.roll(value, spacing, axis) + pltpu.roll(value, width - spacing, axis)
        value = value + factor * around
    return value


def x_lift(planes):
    def plus(one, other):
        return other if one is None else one if other is None else one + other

    planes = dict(planes)
    for step, weight in enumerate(STEPS):
        parity = 1 if step % 2 == 0 else 0
        for index in range(min(planes) - 1, max(planes) + 2):
            if index % 2 == parity:
                around = plus(planes.get(index - 1), planes.get(index + 1))
                if around is not None:
                    planes[index] = plus(planes.get(index), weight * around)
    return planes


def y_lift_split(even, odd):
    count = even.shape[0]
    a, b, c, d = STEPS
    odd = odd + a * (even + pltpu.roll(even, count - 1, 0))
    even = even + b * (pltpu.roll(odd, 1, 0) + odd)
    odd = odd + c * (even + pltpu.roll(even, count - 1, 0))
    even = even + d * (pltpu.roll(odd, 1, 0) + odd)
    return even, odd


def y_lift_whole(value):
    count = value.shape[0]
    row = lax.broadcasted_iota(jnp.int32, (count, 1), 0)
    for step, weight in enumerate(STEPS):
        factor = jnp.where(lax.rem(row, 2) == (1 if step % 2 == 0 else 0), weight, 0.0)
        value = value + factor * (pltpu.roll(value, 1, 0) + pltpu.roll(value, count - 1, 0))
    return value


def scaled_z(value, spacing):
    width = value.shape[-1]
    odd, even = lanes_of(width, spacing, True), lanes_of(width, spacing, False)
    return value * jnp.where(odd, SCALE, jnp.where(even, 1 / SCALE, 0.0))


def scaled(value, x_odd, y_odd):
    at = (SCALE if x_odd else 1 / SCALE) * (SCALE if y_odd else 1 / SCALE)
    return value if x_odd != y_odd else value * at


def spread_z(source, weights, spread, rows, start, size):
    width = source.shape[-1]
    value = source[start : start + size].reshape(size * rows, width)
    spread[start * rows : (start + size) * rows, :] = z_product(value, weights[...])


def spread_x(block, rows, spread, into, low, base):
    for at in range(0, rows, 8):
        planes = {x: spread[x * rows + at : x * rows + at + 8, :] for x in range(block)}
        for x, value in x_lift(planes).items():
            into[x - low, base + at : base + at + 8, :] = value


def matrix_kernel(*weights):
    width = weights[0].shape[0] // 2
    row = lax.broadcasted_iota(jnp.int32, (width, width), 0)
    lane = lax.broadcasted_iota(jnp.int32, (width, width), 1)
    value = jnp.where(row == lane, 1.0, 0.0)
    full = [scaled_z(z_lift(value, 1), 1), jnp.zeros((width, width), jnp.float32)]
    for level in range(1, LEVELS):
        spacing = 1 << level
        value = scaled_z(z_lift(value, spacing), spacing)
        full[1] += pltpu.roll(value, shift_of(level), 1) if shift_of(level) else value
        value = jnp.where(lanes_of(width, spacing, False), value, 0.0)
    for weight, matrix in zip(weights, full):
        high = matrix.astype(jnp.bfloat16)
        rest = (matrix - high.astype(jnp.float32)).astype(jnp.bfloat16)
        weight[:width, :width] = high
        weight[:width, width:] = rest
        weight[width:, :width] = high
        weight[width:, width:] = jnp.zeros_like(rest)


def own_kernel(block, rows, velocity, weights, into, spread):
    step = max(1, min(block, 512 // rows))
    for x in range(0, block, step):
        spread_z(velocity, weights, spread, rows, x, step)
    spread_x(block, rows, spread, into, windows(block)[0][0], 0)


def message_kernel(block, rows, width, count, places, *refs):
    refs = list(refs)

    def take(number):
        taken = refs[:number]
        del refs[:number]
        return taken

    shared = count == 2 and SHARED
    halves = 2 if shared else 1
    (_,) = take(1)
    others = take(count - 1)
    weights = take(2)
    (first,) = take(1)
    own = take(LEVELS)
    passed = take(2 if shared else len(places))
    (spread,) = take(1)
    lifted = [first] + take(LEVELS - 1)
    coarse = take(LEVELS - 1)
    messages = dict(zip(places, take(len(places)) if shared else passed))
    spans = windows(block)
    total = count * rows
    tables = {to: message(block, rows, to) for to in places}
    lengths = {to: messages[to].shape[0] // halves for to in places}
    written = {to: set() for to in places}

    def post(to, at, number, value):
        here = range(at, at + 2 * number, 2)
        if written[to].isdisjoint(here):
            messages[to][pl.ds(at, number, 2), :] = value
        else:
            messages[to][pl.ds(at, number, 2), :] += value
        written[to].update(here)

    def put(level, plane, half, even, odd):
        number = (rows >> level) // 2
        low = level < LEVELS - 1 and plane % 2 == 0
        if level > 0 or low:
            even = jnp.where(own_lanes(width, level, low), even, 0.0)
        if level > 0:
            odd = jnp.where(own_lanes(width, level, False), odd, 0.0)
        to = plane // (block >> level)
        if to == 0:
            own[level][plane, pl.ds(0, number, 2), :] = even
            own[level][plane, pl.ds(1, number, 2), :] = odd
        else:
            at, shift = tables[to][0][level, plane]
            at += half * lengths[to]
            if shift != shift_of(level):
                even, odd = (pltpu.roll(value, shift - shift_of(level), 1) for value in (even, odd))
            post(to, at, number, even)
            post(to, at + 1, number, odd)

    for level in range(LEVELS):
        low, high = spans[level]
        height = total >> level
        half, mine = height // 2, (rows >> level) // 2
        into = lifted[level]

        if level == 0:
            for part, source in enumerate(others):
                step = min(block, max(1, 512 // rows))
                for x in range(0, block, step):
                    spread_z(source, weights[0], spread, rows, x, step)
                spread_x(block, rows, spread, into, low, (part + 1) * rows)
        else:
            start, stop = spans[level - 1][0] // 2, spans[level - 1][1] // 2 + 1
            source = coarse[level - 1]
            if level == 1:
                size = (stop - start) * height
                for at in range(0, size, 512):
                    end = min(size, at + 512)
                    source[at:end, :] = z_product(source[at:end, :], weights[level][...])
            for at in range(0, height, 8):
                planes = {}
                for x in range(start, stop):
                    row = (x - start) * height + at
                    planes[x] = source[row : row + 8, :]
                for x, value in x_lift(planes).items():
                    into[x - low, at : at + 8, :] = value

        for plane in range(low, high + 1):
            odd_plane = plane % 2 == 1
            to = plane // (block >> level)
            if level == 0 and odd_plane and to == 0:
                continue
            goes_on = level < LEVELS - 1 and not odd_plane
            sends = to == 0 or (level, plane) in tables[to][0]
            if not goes_on and not sends:
                continue
            at = plane - low
            split = half % 8 == 0
            if split:
                even, odd = y_lift_split(
                    into[at, pl.ds(0, half, 2), :], into[at, pl.ds(1, half, 2), :]
                )
                even = scaled(even, odd_plane, False)
            else:
                into[at] = y_lift_whole(into[at])
                even = scaled(into[at, pl.ds(0, half, 2), :], odd_plane, False)
            if goes_on:
                row = ((plane - low) // 2) * half
                coarse[level][row : row + half, :] = even
            if not sends:
                continue
            for part in range(halves if to else 1):
                if split:
                    here_even = even[part * mine : (part + 1) * mine]
                    here_odd = odd[part * mine : (part + 1) * mine]
                else:
                    here_even = into[at, pl.ds(2 * part * mine, mine, 2), :]
                    here_even = scaled(here_even, odd_plane, False)
                    here_odd = into[at, pl.ds(2 * part * mine + 1, mine, 2), :]
                put(level, plane, part, here_even, scaled(here_odd, odd_plane, True))

    for to in places:
        for row in range(halves * lengths[to]):
            if row not in written[to]:
                messages[to][row : row + 1, :] = jnp.zeros((1, width), jnp.float32)
    if shared:
        for far, target in enumerate(passed, 1):
            target[...] = jnp.where(lax.axis_index("gy") == 0, messages[far][...], messages[-far][...])


def rest_kernel(block, rows, width, first, _, *refs):
    coarse, out = refs[:-1], refs[-1]
    low = windows(block)[0][0]
    half, mine = first.shape[1] // 2, rows // 2
    for plane in range(1, block, 2):
        even, odd = y_lift_split(
            first[plane - low, pl.ds(0, half, 2), :], first[plane - low, pl.ds(1, half, 2), :]
        )
        out[plane, pl.ds(0, mine, 2), :] = scaled(even[:mine], True, False)
        out[plane, pl.ds(1, mine, 2), :] = scaled(odd[:mine], True, True)
    for level in range(1, LEVELS):
        spacing, shift = 1 << level, shift_of(level)
        for plane in range(block >> level):
            value = coarse[level - 1][plane]
            if shift:
                value = pltpu.roll(value, width - shift, 1)
            out[plane * spacing, pl.ds(0, rows >> level, spacing), :] += value


def add_message(block, rows, to, arrived, base, out, clean):
    sent, derived, _ = message(block, rows, to)
    a, b, c, d = STEPS
    width = out.shape[-1]
    lane = lax.broadcasted_iota(jnp.int32, (1, width), 1)
    for level in sorted({level for level, _ in sent}):
        spacing, height = 1 << level, rows >> level
        shape = (height, width)
        held = {}
        for shift in sorted({shift for (found, _), (_, shift) in sent.items() if found == level}):
            here = {
                plane: at for (found, plane), (at, by) in sent.items() if (found, by) == (level, shift)
            }
            start, stop = min(here.values()), -(-(max(here.values()) + height) // 8) * 8
            source, offset = arrived, base
            if level > 0:
                value = arrived[base + start : base + stop, :]
                if shift:
                    value = pltpu.roll(value, width - shift, 1)
                source, offset = clean[level if shift == shift_of(level) else 0], -start
                source[: stop - start, :] = jnp.where(lax.rem(lane, spacing) == 0, value, 0.0)
            held |= {plane: (source, at + offset) for plane, at in here.items()}

        def read(plane):
            source, at = held[plane]
            return source[at : at + height, :]

        def add(plane, value):
            x = (plane - to * (block >> level)) * spacing
            out[x, pl.ds(0, height, spacing), :] += value

        for plane in held:
            add(plane, read(plane))
        for (found, plane), (far, near) in derived.items():
            if found == level:
                if near is None:
                    value = (d / SCALE**2) * read(far)
                else:
                    value = ((1 / c + d) / SCALE**2) * read(far) + (d / SCALE**2) * read(near)
                row = lax.broadcasted_iota(jnp.int32, shape, 0)
                keep = (lax.rem(row, 2) == 1) | lanes_of(width, spacing, True)
                add(plane, jnp.where(keep, value, 0.0))


def touched(block, rows, side):
    found = set()
    for to in (side, 2 * side):
        sent, derived, _ = message(block, rows, to)
        found |= {(plane - to * (block >> level)) << level for level, plane in [*sent, *derived]}
    runs = []
    for x in sorted(found):
        if runs and x - runs[-1][1] <= 1:
            runs[-1] = (runs[-1][0], x + 1)
        else:
            runs.append((x, x + 1))
    return runs


def write_out(out, whole, done, runs):
    copies = [
        pltpu.make_async_copy(
            out.at[pl.ds(start, stop - start)], whole.at[pl.ds(start, stop - start)], done.at[n]
        )
        for n, (start, stop) in enumerate(runs)
    ]
    for copy in copies:
        copy.start()
    for copy in copies:
        copy.wait()


def add_kernel(block, rows, places, last, _, *refs):
    received, refs = refs[: len(places)], refs[len(places) :]
    if last:
        whole, out, done, *clean = refs
    else:
        out, *clean = refs
    for to, arrived in zip(places, received):
        add_message(block, rows, to, arrived, 0, out, clean)
    if last:
        write_out(out, whole, done, [(0, block)])


def keep_kernel(block, rows, _, near, far, whole, out, done, *clean):
    for core, side in enumerate(SIDES):

        @pl.when(lax.axis_index("gy") == core)
        def _():
            add_message(block, rows, side, near, 0, out, clean)
            add_message(block, rows, 2 * side, far, 0, out, clean)

    write_out(out, whole, done, [(0, block)])


def pack_kernel(near, far, packed):
    one, two = near.shape[0] // 2, far.shape[0] // 2
    packed[:one, :] = near[one:, :]
    packed[one:, :] = far[two:, :]


def swap_kernel(block, rows, one, own, packed, before, whole, out, done, *clean):
    for core, side in enumerate(SIDES[::-1]):

        @pl.when(lax.axis_index("gy") == core)
        def _():
            add_message(block, rows, side, packed, 0, out, clean)
            add_message(block, rows, 2 * side, packed, one, out, clean)
            write_out(out, whole, done, touched(block, rows, side))


def call(body, name, outs, ins, scratch=(), aliases=None, flops=0, hbm_out=(), hbm_in=()):
    vmem, hbm = pl.BlockSpec(memory_space=pltpu.VMEM), pl.BlockSpec(memory_space=pltpu.HBM)
    f32 = jnp.float32
    shapes = [out if isinstance(out, jax.ShapeDtypeStruct) else jax.ShapeDtypeStruct(out, f32) for out in outs]
    moved = 4 * sum(int(np.prod(shape.shape)) for shape in shapes)
    return pl.pallas_call(
        body,
        out_shape=shapes,
        in_specs=[hbm if n in hbm_in else vmem for n in range(len(ins))],
        out_specs=[hbm if n in hbm_out else vmem for n in range(len(outs))],
        scratch_shapes=[pltpu.VMEM(shape, f32) if isinstance(shape, tuple) else shape for shape in scratch],
        input_output_aliases=aliases or {},
        compiler_params=pltpu.CompilerParams(vmem_limit_bytes=VMEM_BYTES),
        cost_estimate=pl.CostEstimate(flops=flops, bytes_accessed=2 * moved, transcendentals=0),
        name=name,
    )(*ins)


def local(velocity):
    block, rows, width = velocity.shape
    around, count = lax.axis_size("gx"), lax.axis_size("gy")
    shared = count == 2 and SHARED
    places = places_of(block)
    spans = windows(block)
    total = count * rows

    others = [
        lax.ppermute(velocity, "gy", [(i, (i - k) % count) for i in range(count)])
        for k in range(1, count)
    ]
    lifted = [
        (high - low + 1, total >> level, width) for level, (low, high) in enumerate(spans)
    ]
    coarse = [
        ((high // 2 - low // 2 + 1) * (total >> (level + 1)), width)
        for level, (low, high) in enumerate(spans[:-1])
    ]
    spread = (block * rows, width)
    owned = [(block >> level, rows >> level, width) for level in range(LEVELS)]
    lengths = {to: message(block, rows, to)[2] for to in places}
    one, two = max(lengths[1], lengths[-1]), max(lengths[2], lengths[-2])
    clean = [(one, width)] * LEVELS

    square = jax.ShapeDtypeStruct((2 * width, 2 * width), jnp.bfloat16)
    weights = call(matrix_kernel, "make_matrices", [square] * 2, [], flops=FIRST_FLOPS)
    (first,) = call(
        functools.partial(own_kernel, block, rows),
        "lift_own",
        [lifted[0]],
        [velocity, weights[0]],
        [spread],
    )
    if shared:
        each = {to: (2 * (one if abs(to) == 1 else two), width) for to in places}
        outs, scratch = [each[1], each[2]], [each[to] for to in places]
    else:
        outs, scratch = [(lengths[to], width) for to in places], []
    first, kept, *more = call(
        functools.partial(message_kernel, block, rows, width, count, places),
        "make_messages",
        [lifted[0]] + owned + outs,
        [first] + others + list(weights),
        [spread] + lifted[1:] + coarse + scratch,
        {0: 0},
    )
    own_coarse, messages = more[: LEVELS - 1], more[LEVELS - 1 :]

    def rest():
        return call(
            functools.partial(rest_kernel, block, rows, width),
            "finish_own",
            [owned[0]],
            [first, kept] + own_coarse,
            aliases={1: 0},
        )[0]

    written = [pltpu.SemaphoreType.DMA((block,))]
    if shared:
        near, far = (
            lax.ppermute(
                value,
                ("gx", "gy"),
                [
                    (2 * i + core, 2 * ((i + side * step) % around) + core)
                    for i in range(around)
                    for core, side in enumerate(SIDES)
                ],
            )
            for step, value in enumerate(messages, 1)
        )
        result = rest()
        (packed,) = call(pack_kernel, "pack_other", [(one + two, width)], [near, far])
        packed = lax.ppermute(packed, "gy", [(0, 1), (1, 0)])
        whole, result = call(
            functools.partial(keep_kernel, block, rows),
            "add_kept",
            [owned[0]] * 2,
            [result, near, far],
            written + clean,
            aliases={0: 1},
            hbm_out=(0,),
        )
        whole, _ = call(
            functools.partial(swap_kernel, block, rows, one),
            "add_swapped",
            [owned[0]] * 2,
            [result, packed, whole],
            written + clean,
            aliases={0: 1, 2: 0},
            hbm_out=(0,),
            hbm_in=(2,),
        )
        return whole

    sent = dict(zip(places, messages))
    received = {
        to: lax.ppermute(sent[to], "gx", [(i, (i + to) % around) for i in range(around)])
        for to in sorted(places, key=lambda to: (to < 0, abs(to)))
    }
    right = [to for to in places if to > 0]
    left = [to for to in places if to < 0]
    (result,) = call(
        functools.partial(add_kernel, block, rows, right, False),
        "add_right",
        [owned[0]],
        [rest()] + [received[to] for to in right],
        clean,
        aliases={0: 0},
        flops=FIRST_FLOPS,
    )
    whole, _ = call(
        functools.partial(add_kernel, block, rows, left, True),
        "add_left",
        [owned[0]] * 2,
        [result] + [received[to] for to in left],
        written + clean,
        aliases={0: 1},
        hbm_out=(0,),
    )
    return whole


def solution(mesh):
    return jax.shard_map(
        local, mesh=mesh, in_specs=(P("gx", "gy", None),), out_specs=P("gx", "gy", None), check_vma=False
    )
```

```python
import functools

import jax
import jax.numpy as jnp
import numpy as np
from jax import lax
from jax.experimental import pallas as pl
from jax.experimental.pallas import tpu as pltpu
from jax.sharding import PartitionSpec as P

LEVELS = 4
STEPS = (-1.586134342, -0.05298011854, 0.8829110762, 0.4435068522)
SCALE = 1.149604398
VMEM_BYTES = 24 * 2**20
FIRST_FLOPS = 10**10
SHARED = True


def windows(block):
    found = []
    first, last = 0, block - 1
    for _ in range(LEVELS):
        low = first - 4 + (first % 2)
        high = last + 4 - (last % 2)
        found.append((low, high))
        first, last = low // 2, high // 2
    return found


def message(block, rows, to):
    sent, derived = {}, {}
    spans = windows(block)
    base = ends = 0
    for level, (low, high) in enumerate(spans):
        size, height = block >> level, rows >> level
        first, last = (0, block - 1) if level == 0 else (v // 2 for v in spans[level - 1])
        planes = [p for p in range(low, high + 1) if p // size == to]
        if abs(to) == 1:
            sign = to
            edge = last + 2 - last % 2 if to > 0 else first - 2 + first % 2
            far, near = edge + sign, edge - sign
            if far in planes and edge + 2 * sign in planes:
                derived[level, edge + 2 * sign] = (far, None)
            if far in planes and near in planes:
                derived[level, edge] = (far, near)
        planes = [plane for plane in planes if (level, plane) not in derived]
        at = base
        if level == 1:
            extra = planes[-1] if len(planes) > 3 else None
        elif level > 1 and extra is not None:
            at = base + (rows >> 1)
        for plane in planes:
            if level == 1 and plane == extra:
                sent[level, plane] = base, shift_of(2)
                continue
            sent[level, plane] = at, shift_of(level)
            at += height
        ends = max(ends, at)
        if level == 0:
            base = at
    return sent, derived, -(-ends // 8) * 8


def shift_of(level):
    return (0, 0, 1, 3)[level]


def places_of(block):
    found = set()
    for level, (low, high) in enumerate(windows(block)):
        size = block >> level
        found |= set(range(low // size, high // size + 1))
    return sorted(found - {0})


def z_product(value, weights):
    width = value.shape[-1]
    high = value.astype(jnp.bfloat16)
    rest = (value - high.astype(jnp.float32)).astype(jnp.bfloat16)
    both = jnp.concatenate([high, rest], axis=1)
    product = jnp.dot(both, weights, preferred_element_type=jnp.float32)
    return product[:, :width] + product[:, width:]


def lanes_of(width, spacing, parity):
    lane = lax.broadcasted_iota(jnp.int32, (1, width), 1)
    return lax.rem(lane, 2 * spacing) == (spacing if parity else 0)


def own_lanes(width, level, high_only):
    spacing, shift = 1 << level, shift_of(level)
    lane = lax.broadcasted_iota(jnp.int32, (1, width), 1)
    if high_only:
        return lax.rem(lane, 2 * spacing) == spacing + shift
    return lax.rem(lane, spacing) == shift


def z_lift(value, spacing):
    width = value.shape[-1]
    axis = value.ndim - 1
    for step, weight in enumerate(STEPS):
        factor = jnp.where(lanes_of(width, spacing, step % 2 == 0), weight, 0.0)
        around = pltpu.roll(value, spacing, axis) + pltpu.roll(value, width - spacing, axis)
        value = value + factor * around
    return value


def x_lift(planes):
    def plus(one, other):
        return other if one is None else one if other is None else one + other

    planes = dict(planes)
    for step, weight in enumerate(STEPS):
        parity = 1 if step % 2 == 0 else 0
        for index in range(min(planes) - 1, max(planes) + 2):
            if index % 2 == parity:
                around = plus(planes.get(index - 1), planes.get(index + 1))
                if around is not None:
                    planes[index] = plus(planes.get(index), weight * around)
    return planes


def y_lift_split(even, odd):
    count = even.shape[0]
    a, b, c, d = STEPS
    odd = odd + a * (even + pltpu.roll(even, count - 1, 0))
    even = even + b * (pltpu.roll(odd, 1, 0) + odd)
    odd = odd + c * (even + pltpu.roll(even, count - 1, 0))
    even = even + d * (pltpu.roll(odd, 1, 0) + odd)
    return even, odd


def y_lift_whole(value):
    count = value.shape[0]
    row = lax.broadcasted_iota(jnp.int32, (count, 1), 0)
    for step, weight in enumerate(STEPS):
        factor = jnp.where(lax.rem(row, 2) == (1 if step % 2 == 0 else 0), weight, 0.0)
        value = value + factor * (pltpu.roll(value, 1, 0) + pltpu.roll(value, count - 1, 0))
    return value


def scaled_z(value, spacing):
    width = value.shape[-1]
    odd, even = lanes_of(width, spacing, True), lanes_of(width, spacing, False)
    return value * jnp.where(odd, SCALE, jnp.where(even, 1 / SCALE, 0.0))


def scaled(value, x_odd, y_odd):
    at = (SCALE if x_odd else 1 / SCALE) * (SCALE if y_odd else 1 / SCALE)
    return value if x_odd != y_odd else value * at


def spread_z(source, weights, spread, rows, start, size):
    width = source.shape[-1]
    value = source[start : start + size].reshape(size * rows, width)
    spread[start * rows : (start + size) * rows, :] = z_product(value, weights[...])


def spread_x(block, rows, spread, into, low, base):
    for at in range(0, rows, 8):
        planes = {x: spread[x * rows + at : x * rows + at + 8, :] for x in range(block)}
        for x, value in x_lift(planes).items():
            into[x - low, base + at : base + at + 8, :] = value


def matrix_kernel(*weights):
    width = weights[0].shape[0] // 2
    row = lax.broadcasted_iota(jnp.int32, (width, width), 0)
    lane = lax.broadcasted_iota(jnp.int32, (width, width), 1)
    value = jnp.where(row == lane, 1.0, 0.0)
    full = [scaled_z(z_lift(value, 1), 1), jnp.zeros((width, width), jnp.float32)]
    for level in range(1, LEVELS):
        spacing = 1 << level
        value = scaled_z(z_lift(value, spacing), spacing)
        full[1] += pltpu.roll(value, shift_of(level), 1) if shift_of(level) else value
        value = jnp.where(lanes_of(width, spacing, False), value, 0.0)
    for weight, matrix in zip(weights, full):
        high = matrix.astype(jnp.bfloat16)
        rest = (matrix - high.astype(jnp.float32)).astype(jnp.bfloat16)
        weight[:width, :width] = high
        weight[:width, width:] = rest
        weight[width:, :width] = high
        weight[width:, width:] = jnp.zeros_like(rest)


def own_kernel(block, rows, velocity, weights, into, spread):
    step = max(1, min(block, 512 // rows))
    for x in range(0, block, step):
        spread_z(velocity, weights, spread, rows, x, step)
    spread_x(block, rows, spread, into, windows(block)[0][0], 0)


def right_source(step, place, last):
    return place == (last if step == 1 else 0)


def right_target(step, place):
    return (place == 0) & (step == 1)


def sends_right(step):
    core = lax.axis_index("gy") == 1
    return core == right_source(step, lax.axis_index("gx"), lax.axis_size("gx") - 1)


def takes_right(step):
    core = lax.axis_index("gy") == 1
    return core == right_target(step, lax.axis_index("gx"))


def shared_pairs(step, around):
    pairs = []
    for place in range(around):
        to, back = (place + step) % around, (place - step) % around
        source = int(right_source(step, place, around - 1))
        pairs.append((2 * place + source, 2 * to + int(right_target(step, to))))
        pairs.append((2 * place + 1 - source, 2 * back + 1 - int(right_target(step, back))))
    return pairs


def message_kernel(block, rows, width, count, places, *refs):
    refs = list(refs)

    def take(number):
        taken = refs[:number]
        del refs[:number]
        return taken

    shared = count == 2 and SHARED
    halves = 2 if shared else 1
    (_,) = take(1)
    others = take(count - 1)
    weights = take(2)
    (first,) = take(1)
    own = take(LEVELS)
    passed = take(2 if shared else len(places))
    (spread,) = take(1)
    lifted = [first] + take(LEVELS - 1)
    coarse = take(LEVELS - 1)
    messages = dict(zip(places, take(len(places)) if shared else passed))
    spans = windows(block)
    total = count * rows
    tables = {to: message(block, rows, to) for to in places}
    lengths = {to: messages[to].shape[0] // halves for to in places}
    written = {to: set() for to in places}

    def post(to, at, number, value):
        here = range(at, at + 2 * number, 2)
        if written[to].isdisjoint(here):
            messages[to][pl.ds(at, number, 2), :] = value
        else:
            messages[to][pl.ds(at, number, 2), :] += value
        written[to].update(here)

    def put(level, plane, half, even, odd):
        number = (rows >> level) // 2
        low = level < LEVELS - 1 and plane % 2 == 0
        if level > 0 or low:
            even = jnp.where(own_lanes(width, level, low), even, 0.0)
        if level > 0:
            odd = jnp.where(own_lanes(width, level, False), odd, 0.0)
        to = plane // (block >> level)
        if to == 0:
            own[level][plane, pl.ds(0, number, 2), :] = even
            own[level][plane, pl.ds(1, number, 2), :] = odd
        else:
            at, shift = tables[to][0][level, plane]
            at += half * lengths[to]
            if shift != shift_of(level):
                even, odd = (pltpu.roll(value, shift - shift_of(level), 1) for value in (even, odd))
            post(to, at, number, even)
            post(to, at + 1, number, odd)

    for level in range(LEVELS):
        low, high = spans[level]
        height = total >> level
        half, mine = height // 2, (rows >> level) // 2
        into = lifted[level]

        if level == 0:
            for part, source in enumerate(others):
                step = min(block, max(1, 512 // rows))
                for x in range(0, block, step):
                    spread_z(source, weights[0], spread, rows, x, step)
                spread_x(block, rows, spread, into, low, (part + 1) * rows)
        else:
            start, stop = spans[level - 1][0] // 2, spans[level - 1][1] // 2 + 1
            source = coarse[level - 1]
            if level == 1:
                size = (stop - start) * height
                for at in range(0, size, 512):
                    end = min(size, at + 512)
                    source[at:end, :] = z_product(source[at:end, :], weights[level][...])
            for at in range(0, height, 8):
                planes = {}
                for x in range(start, stop):
                    row = (x - start) * height + at
                    planes[x] = source[row : row + 8, :]
                for x, value in x_lift(planes).items():
                    into[x - low, at : at + 8, :] = value

        for plane in range(low, high + 1):
            odd_plane = plane % 2 == 1
            to = plane // (block >> level)
            if level == 0 and odd_plane and to == 0:
                continue
            goes_on = level < LEVELS - 1 and not odd_plane
            sends = to == 0 or (level, plane) in tables[to][0]
            if not goes_on and not sends:
                continue
            at = plane - low
            split = half % 8 == 0
            if split:
                even, odd = y_lift_split(
                    into[at, pl.ds(0, half, 2), :], into[at, pl.ds(1, half, 2), :]
                )
                even = scaled(even, odd_plane, False)
            else:
                into[at] = y_lift_whole(into[at])
                even = scaled(into[at, pl.ds(0, half, 2), :], odd_plane, False)
            if goes_on:
                row = ((plane - low) // 2) * half
                coarse[level][row : row + half, :] = even
            if not sends:
                continue
            for part in range(halves if to else 1):
                if split:
                    here_even = even[part * mine : (part + 1) * mine]
                    here_odd = odd[part * mine : (part + 1) * mine]
                else:
                    here_even = into[at, pl.ds(2 * part * mine, mine, 2), :]
                    here_even = scaled(here_even, odd_plane, False)
                    here_odd = into[at, pl.ds(2 * part * mine + 1, mine, 2), :]
                put(level, plane, part, here_even, scaled(here_odd, odd_plane, True))

    for to in places:
        for row in range(halves * lengths[to]):
            if row not in written[to]:
                messages[to][row : row + 1, :] = jnp.zeros((1, width), jnp.float32)
    if shared:
        for far, target in enumerate(passed, 1):
            size = lengths[far]
            for half in range(2):
                mine, other = (slice(n * size, (n + 1) * size) for n in (half, 1 - half))
                target[mine, :] = jnp.where(
                    lax.axis_index("gy") == 0,
                    jnp.where(sends_right(far), messages[far][mine, :], messages[-far][mine, :]),
                    jnp.where(sends_right(far), messages[far][other, :], messages[-far][other, :]),
                )


def rest_kernel(block, rows, width, first, _, *refs):
    coarse, out = refs[:-1], refs[-1]
    low = windows(block)[0][0]
    half, mine = first.shape[1] // 2, rows // 2
    for plane in range(1, block, 2):
        even, odd = y_lift_split(
            first[plane - low, pl.ds(0, half, 2), :], first[plane - low, pl.ds(1, half, 2), :]
        )
        out[plane, pl.ds(0, mine, 2), :] = scaled(even[:mine], True, False)
        out[plane, pl.ds(1, mine, 2), :] = scaled(odd[:mine], True, True)
    for level in range(1, LEVELS):
        spacing, shift = 1 << level, shift_of(level)
        for plane in range(block >> level):
            value = coarse[level - 1][plane]
            if shift:
                value = pltpu.roll(value, width - shift, 1)
            out[plane * spacing, pl.ds(0, rows >> level, spacing), :] += value


def add_message(block, rows, to, arrived, base, out, clean):
    sent, derived, _ = message(block, rows, to)
    a, b, c, d = STEPS
    width = out.shape[-1]
    lane = lax.broadcasted_iota(jnp.int32, (1, width), 1)
    for level in sorted({level for level, _ in sent}):
        spacing, height = 1 << level, rows >> level
        shape = (height, width)
        held = {}
        for shift in sorted({shift for (found, _), (_, shift) in sent.items() if found == level}):
            here = {
                plane: at for (found, plane), (at, by) in sent.items() if (found, by) == (level, shift)
            }
            start, stop = min(here.values()), -(-(max(here.values()) + height) // 8) * 8
            source, offset = arrived, base
            if level > 0:
                value = arrived[base + start : base + stop, :]
                if shift:
                    value = pltpu.roll(value, width - shift, 1)
                source, offset = clean[level if shift == shift_of(level) else 0], -start
                source[: stop - start, :] = jnp.where(lax.rem(lane, spacing) == 0, value, 0.0)
            held |= {plane: (source, at + offset) for plane, at in here.items()}

        def read(plane):
            source, at = held[plane]
            return source[at : at + height, :]

        def add(plane, value):
            x = (plane - to * (block >> level)) * spacing
            out[x, pl.ds(0, height, spacing), :] += value

        for plane in held:
            add(plane, read(plane))
        for (found, plane), (far, near) in derived.items():
            if found == level:
                if near is None:
                    value = (d / SCALE**2) * read(far)
                else:
                    value = ((1 / c + d) / SCALE**2) * read(far) + (d / SCALE**2) * read(near)
                row = lax.broadcasted_iota(jnp.int32, shape, 0)
                keep = (lax.rem(row, 2) == 1) | lanes_of(width, spacing, True)
                add(plane, jnp.where(keep, value, 0.0))


def write_out(out, whole, done, runs):
    copies = [
        pltpu.make_async_copy(
            out.at[pl.ds(start, stop - start)], whole.at[pl.ds(start, stop - start)], done.at[n]
        )
        for n, (start, stop) in enumerate(runs)
    ]
    for copy in copies:
        copy.start()
    for copy in copies:
        copy.wait()


def add_kernel(block, rows, places, last, _, *refs):
    received, refs = refs[: len(places)], refs[len(places) :]
    if last:
        whole, out, done, *clean = refs
    else:
        out, *clean = refs
    for to, arrived in zip(places, received):
        add_message(block, rows, to, arrived, 0, out, clean)
    if last:
        write_out(out, whole, done, [(0, block)])


def add_either(block, rows, right, step, arrived, base, out, clean):
    for side, here in ((step, right), (-step, jnp.logical_not(right))):

        @pl.when(here)
        def _():
            add_message(block, rows, side, arrived, base, out, clean)


def keep_kernel(block, rows, _, near, far, out, *clean):
    for step, arrived in enumerate((near, far), 1):
        own = half_of(arrived, lax.axis_index("gy"))
        add_either(block, rows, takes_right(step), step, own, 0, out, clean)


def half_of(arrived, core):
    size = arrived.shape[0] // 2
    return arrived.at[pl.ds(pl.multiple_of(core * size, 8), size)]


def pack_kernel(near, far, packed):
    one = near.shape[0] // 2
    other = 1 - lax.axis_index("gy")
    packed[:one, :] = half_of(near, other)[...]
    packed[one:, :] = half_of(far, other)[...]


def swap_kernel(block, rows, one, own, packed, whole, out, done, *clean):
    for step, base in enumerate((0, one), 1):
        right = jnp.logical_not(takes_right(step))
        add_either(block, rows, right, step, packed, base, out, clean)
    write_out(out, whole, done, [(0, block)])


def call(body, name, outs, ins, scratch=(), aliases=None, flops=0, hbm_out=()):
    vmem, hbm = pl.BlockSpec(memory_space=pltpu.VMEM), pl.BlockSpec(memory_space=pltpu.HBM)
    f32 = jnp.float32
    shapes = [out if isinstance(out, jax.ShapeDtypeStruct) else jax.ShapeDtypeStruct(out, f32) for out in outs]
    moved = 4 * sum(int(np.prod(shape.shape)) for shape in shapes)
    return pl.pallas_call(
        body,
        out_shape=shapes,
        in_specs=[vmem] * len(ins),
        out_specs=[hbm if n in hbm_out else vmem for n in range(len(outs))],
        scratch_shapes=[pltpu.VMEM(shape, f32) if isinstance(shape, tuple) else shape for shape in scratch],
        input_output_aliases=aliases or {},
        compiler_params=pltpu.CompilerParams(vmem_limit_bytes=VMEM_BYTES),
        cost_estimate=pl.CostEstimate(flops=flops, bytes_accessed=2 * moved, transcendentals=0),
        name=name,
    )(*ins)


def local(velocity):
    block, rows, width = velocity.shape
    around, count = lax.axis_size("gx"), lax.axis_size("gy")
    shared = count == 2 and SHARED
    places = places_of(block)
    spans = windows(block)
    total = count * rows

    others = [
        lax.ppermute(velocity, "gy", [(i, (i - k) % count) for i in range(count)])
        for k in range(1, count)
    ]
    lifted = [
        (high - low + 1, total >> level, width) for level, (low, high) in enumerate(spans)
    ]
    coarse = [
        ((high // 2 - low // 2 + 1) * (total >> (level + 1)), width)
        for level, (low, high) in enumerate(spans[:-1])
    ]
    spread = (block * rows, width)
    owned = [(block >> level, rows >> level, width) for level in range(LEVELS)]
    lengths = {to: message(block, rows, to)[2] for to in places}
    one, two = max(lengths[1], lengths[-1]), max(lengths[2], lengths[-2])
    clean = [(one, width)] * LEVELS

    square = jax.ShapeDtypeStruct((2 * width, 2 * width), jnp.bfloat16)
    weights = call(matrix_kernel, "make_matrices", [square] * 2, [], flops=FIRST_FLOPS)
    (first,) = call(
        functools.partial(own_kernel, block, rows),
        "lift_own",
        [lifted[0]],
        [velocity, weights[0]],
        [spread],
    )
    if shared:
        each = {to: (2 * (one if abs(to) == 1 else two), width) for to in places}
        outs, scratch = [each[1], each[2]], [each[to] for to in places]
    else:
        outs, scratch = [(lengths[to], width) for to in places], []
    first, kept, *more = call(
        functools.partial(message_kernel, block, rows, width, count, places),
        "make_messages",
        [lifted[0]] + owned + outs,
        [first] + others + list(weights),
        [spread] + lifted[1:] + coarse + scratch,
        {0: 0},
    )
    own_coarse, messages = more[: LEVELS - 1], more[LEVELS - 1 :]

    def rest():
        return call(
            functools.partial(rest_kernel, block, rows, width),
            "finish_own",
            [owned[0]],
            [first, kept] + own_coarse,
            aliases={1: 0},
        )[0]

    written = [pltpu.SemaphoreType.DMA((1,))]
    if shared:
        near, far = (
            lax.ppermute(value, ("gx", "gy"), shared_pairs(step, around))
            for step, value in enumerate(messages, 1)
        )
        result = rest()
        (packed,) = call(pack_kernel, "pack_other", [(one + two, width)], [near, far])
        packed = lax.ppermute(packed, "gy", [(0, 1), (1, 0)])
        (result,) = call(
            functools.partial(keep_kernel, block, rows),
            "add_kept",
            [owned[0]],
            [result, near, far],
            clean,
            aliases={0: 0},
        )
        whole, _ = call(
            functools.partial(swap_kernel, block, rows, one),
            "add_swapped",
            [owned[0]] * 2,
            [result, packed],
            written + clean,
            aliases={0: 1},
            hbm_out=(0,),
        )
        return whole

    sent = dict(zip(places, messages))
    received = {
        to: lax.ppermute(sent[to], "gx", [(i, (i + to) % around) for i in range(around)])
        for to in sorted(places, key=lambda to: (to < 0, abs(to)))
    }
    right = [to for to in places if to > 0]
    left = [to for to in places if to < 0]
    (result,) = call(
        functools.partial(add_kernel, block, rows, right, False),
        "add_right",
        [owned[0]],
        [rest()] + [received[to] for to in right],
        clean,
        aliases={0: 0},
        flops=FIRST_FLOPS,
    )
    whole, _ = call(
        functools.partial(add_kernel, block, rows, left, True),
        "add_left",
        [owned[0]] * 2,
        [result] + [received[to] for to in left],
        written + clean,
        aliases={0: 1},
        hbm_out=(0,),
    )
    return whole


def solution(mesh):
    return jax.shard_map(
        local, mesh=mesh, in_specs=(P("gx", "gy", None),), out_specs=P("gx", "gy", None), check_vma=False
    )
```

```python
import functools

import jax
import jax.numpy as jnp
import numpy as np
from jax import lax
from jax.experimental import pallas as pl
from jax.experimental.pallas import tpu as pltpu
from jax.sharding import PartitionSpec as P

LEVELS = 4
STEPS = (-1.586134342, -0.05298011854, 0.8829110762, 0.4435068522)
SCALE = 1.149604398
VMEM_BYTES = 24 * 2**20
FIRST_FLOPS = 10**10
SHARED = True


def windows(block):
    found = []
    first, last = 0, block - 1
    for _ in range(LEVELS):
        low = first - 4 + (first % 2)
        high = last + 4 - (last % 2)
        found.append((low, high))
        first, last = low // 2, high // 2
    return found


def message(block, rows, to):
    sent, derived = {}, {}
    spans = windows(block)
    base = ends = 0
    for level, (low, high) in enumerate(spans):
        size, height = block >> level, rows >> level
        first, last = (0, block - 1) if level == 0 else (v // 2 for v in spans[level - 1])
        planes = [p for p in range(low, high + 1) if p // size == to]
        if abs(to) == 1:
            sign = to
            edge = last + 2 - last % 2 if to > 0 else first - 2 + first % 2
            far, near = edge + sign, edge - sign
            if far in planes and edge + 2 * sign in planes:
                derived[level, edge + 2 * sign] = (far, None)
            if far in planes and near in planes:
                derived[level, edge] = (far, near)
        planes = [plane for plane in planes if (level, plane) not in derived]
        at = base
        if level == 1:
            extra = planes[-1] if len(planes) > 3 else None
        elif level > 1 and extra is not None:
            at = base + (rows >> 1)
        for plane in planes:
            if level == 1 and plane == extra:
                sent[level, plane] = base, shift_of(2)
                continue
            sent[level, plane] = at, shift_of(level)
            at += height
        ends = max(ends, at)
        if level == 0:
            base = at
    return sent, derived, -(-ends // 8) * 8


def shift_of(level):
    return (0, 0, 1, 3)[level]


def places_of(block):
    found = set()
    for level, (low, high) in enumerate(windows(block)):
        size = block >> level
        found |= set(range(low // size, high // size + 1))
    return sorted(found - {0})


def z_product(value, weights):
    width = value.shape[-1]
    high = value.astype(jnp.bfloat16)
    rest = (value - high.astype(jnp.float32)).astype(jnp.bfloat16)
    both = jnp.concatenate([high, rest], axis=1)
    product = jnp.dot(both, weights, preferred_element_type=jnp.float32)
    return product[:, :width] + product[:, width:]


def lanes_of(width, spacing, parity):
    lane = lax.broadcasted_iota(jnp.int32, (1, width), 1)
    return lax.rem(lane, 2 * spacing) == (spacing if parity else 0)


def own_lanes(width, level, high_only):
    spacing, shift = 1 << level, shift_of(level)
    lane = lax.broadcasted_iota(jnp.int32, (1, width), 1)
    if high_only:
        return lax.rem(lane, 2 * spacing) == spacing + shift
    return lax.rem(lane, spacing) == shift


def z_lift(value, spacing):
    width = value.shape[-1]
    axis = value.ndim - 1
    for step, weight in enumerate(STEPS):
        factor = jnp.where(lanes_of(width, spacing, step % 2 == 0), weight, 0.0)
        around = pltpu.roll(value, spacing, axis) + pltpu.roll(value, width - spacing, axis)
        value = value + factor * around
    return value


def x_lift(planes):
    def plus(one, other):
        return other if one is None else one if other is None else one + other

    planes = dict(planes)
    for step, weight in enumerate(STEPS):
        parity = 1 if step % 2 == 0 else 0
        for index in range(min(planes) - 1, max(planes) + 2):
            if index % 2 == parity:
                around = plus(planes.get(index - 1), planes.get(index + 1))
                if around is not None:
                    planes[index] = plus(planes.get(index), weight * around)
    return planes


def y_lift_split(even, odd):
    count = even.shape[0]
    a, b, c, d = STEPS
    odd = odd + a * (even + pltpu.roll(even, count - 1, 0))
    even = even + b * (pltpu.roll(odd, 1, 0) + odd)
    odd = odd + c * (even + pltpu.roll(even, count - 1, 0))
    even = even + d * (pltpu.roll(odd, 1, 0) + odd)
    return even, odd


def y_lift_whole(value):
    count = value.shape[0]
    row = lax.broadcasted_iota(jnp.int32, (count, 1), 0)
    for step, weight in enumerate(STEPS):
        factor = jnp.where(lax.rem(row, 2) == (1 if step % 2 == 0 else 0), weight, 0.0)
        value = value + factor * (pltpu.roll(value, 1, 0) + pltpu.roll(value, count - 1, 0))
    return value


def scaled_z(value, spacing):
    width = value.shape[-1]
    odd, even = lanes_of(width, spacing, True), lanes_of(width, spacing, False)
    return value * jnp.where(odd, SCALE, jnp.where(even, 1 / SCALE, 0.0))


def scaled(value, x_odd, y_odd):
    at = (SCALE if x_odd else 1 / SCALE) * (SCALE if y_odd else 1 / SCALE)
    return value if x_odd != y_odd else value * at


def spread_z(source, weights, spread, rows, start, size):
    width = source.shape[-1]
    value = source[start : start + size].reshape(size * rows, width)
    spread[start * rows : (start + size) * rows, :] = z_product(value, weights[...])


def spread_x(block, rows, spread, into, low, base):
    for at in range(0, rows, 8):
        planes = {x: spread[x * rows + at : x * rows + at + 8, :] for x in range(block)}
        for x, value in x_lift(planes).items():
            into[x - low, base + at : base + at + 8, :] = value


def matrix_kernel(*weights):
    width = weights[0].shape[0] // 2
    row = lax.broadcasted_iota(jnp.int32, (width, width), 0)
    lane = lax.broadcasted_iota(jnp.int32, (width, width), 1)
    value = jnp.where(row == lane, 1.0, 0.0)
    full = [scaled_z(z_lift(value, 1), 1), jnp.zeros((width, width), jnp.float32)]
    for level in range(1, LEVELS):
        spacing = 1 << level
        value = scaled_z(z_lift(value, spacing), spacing)
        full[1] += pltpu.roll(value, shift_of(level), 1) if shift_of(level) else value
        value = jnp.where(lanes_of(width, spacing, False), value, 0.0)
    for weight, matrix in zip(weights, full):
        high = matrix.astype(jnp.bfloat16)
        rest = (matrix - high.astype(jnp.float32)).astype(jnp.bfloat16)
        weight[:width, :width] = high
        weight[:width, width:] = rest
        weight[width:, :width] = high
        weight[width:, width:] = jnp.zeros_like(rest)


def own_kernel(block, rows, velocity, weights, into, spread):
    step = max(1, min(block, 512 // rows))
    for x in range(0, block, step):
        spread_z(velocity, weights, spread, rows, x, step)
    spread_x(block, rows, spread, into, windows(block)[0][0], 0)


def right_source(step, place, last):
    return place == last if step == 1 else (place == 0) | (place == last - 1)


def right_target(step, place):
    return (place == 0) & (step == 1)


def sends_right(step):
    core = lax.axis_index("gy") == 1
    return core == right_source(step, lax.axis_index("gx"), lax.axis_size("gx") - 1)


def takes_right(step):
    core = lax.axis_index("gy") == 1
    return core == right_target(step, lax.axis_index("gx"))


def shared_pairs(step, around):
    pairs = []
    for place in range(around):
        to, back = (place + step) % around, (place - step) % around
        source = int(right_source(step, place, around - 1))
        pairs.append((2 * place + source, 2 * to + int(right_target(step, to))))
        pairs.append((2 * place + 1 - source, 2 * back + 1 - int(right_target(step, back))))
    return pairs


def message_kernel(block, rows, width, count, places, *refs):
    refs = list(refs)

    def take(number):
        taken = refs[:number]
        del refs[:number]
        return taken

    shared = count == 2 and SHARED
    halves = 2 if shared else 1
    (_,) = take(1)
    others = take(count - 1)
    weights = take(2)
    (first,) = take(1)
    own = [None] + take(LEVELS - 1)
    passed = take(2 if shared else len(places))
    (spread,) = take(1)
    lifted = [first] + take(LEVELS - 1)
    coarse = take(LEVELS - 1)
    messages = dict(zip(places, take(len(places)) if shared else passed))
    spans = windows(block)
    total = count * rows
    tables = {to: message(block, rows, to) for to in places}
    lengths = {to: messages[to].shape[0] // halves for to in places}
    written = {to: set() for to in places}

    def post(to, at, number, value):
        here = range(at, at + 2 * number, 2)
        if written[to].isdisjoint(here):
            messages[to][pl.ds(at, number, 2), :] = value
        else:
            messages[to][pl.ds(at, number, 2), :] += value
        written[to].update(here)

    def put(level, plane, half, even, odd):
        number = (rows >> level) // 2
        low = level < LEVELS - 1 and plane % 2 == 0
        if level > 0 or low:
            even = jnp.where(own_lanes(width, level, low), even, 0.0)
        if level > 0:
            odd = jnp.where(own_lanes(width, level, False), odd, 0.0)
        to = plane // (block >> level)
        if to == 0:
            own[level][plane, pl.ds(0, number, 2), :] = even
            own[level][plane, pl.ds(1, number, 2), :] = odd
        else:
            at, shift = tables[to][0][level, plane]
            at += half * lengths[to]
            if shift != shift_of(level):
                even, odd = (pltpu.roll(value, shift - shift_of(level), 1) for value in (even, odd))
            post(to, at, number, even)
            post(to, at + 1, number, odd)

    for level in range(LEVELS):
        low, high = spans[level]
        height = total >> level
        half, mine = height // 2, (rows >> level) // 2
        into = lifted[level]

        if level == 0:
            for part, source in enumerate(others):
                step = min(block, max(1, 512 // rows))
                for x in range(0, block, step):
                    spread_z(source, weights[0], spread, rows, x, step)
                spread_x(block, rows, spread, into, low, (part + 1) * rows)
        else:
            start, stop = spans[level - 1][0] // 2, spans[level - 1][1] // 2 + 1
            source = coarse[level - 1]
            if level == 1:
                size = (stop - start) * height
                for at in range(0, size, 512):
                    end = min(size, at + 512)
                    source[at:end, :] = z_product(source[at:end, :], weights[level][...])
            for at in range(0, height, 8):
                planes = {}
                for x in range(start, stop):
                    row = (x - start) * height + at
                    planes[x] = source[row : row + 8, :]
                for x, value in x_lift(planes).items():
                    into[x - low, at : at + 8, :] = value

        for plane in range(low, high + 1):
            odd_plane = plane % 2 == 1
            to = plane // (block >> level)
            if level == 0 and odd_plane and to == 0:
                continue
            goes_on = level < LEVELS - 1 and not odd_plane
            sends = level > 0 if to == 0 else (level, plane) in tables[to][0]
            if not goes_on and not sends:
                continue
            at = plane - low
            split = half % 8 == 0
            if split:
                even, odd = y_lift_split(
                    into[at, pl.ds(0, half, 2), :], into[at, pl.ds(1, half, 2), :]
                )
                even = scaled(even, odd_plane, False)
            else:
                into[at] = y_lift_whole(into[at])
                even = scaled(into[at, pl.ds(0, half, 2), :], odd_plane, False)
            if goes_on:
                row = ((plane - low) // 2) * half
                coarse[level][row : row + half, :] = even
            if not sends:
                continue
            for part in range(halves if to else 1):
                if split:
                    here_even = even[part * mine : (part + 1) * mine]
                    here_odd = odd[part * mine : (part + 1) * mine]
                else:
                    here_even = into[at, pl.ds(2 * part * mine, mine, 2), :]
                    here_even = scaled(here_even, odd_plane, False)
                    here_odd = into[at, pl.ds(2 * part * mine + 1, mine, 2), :]
                put(level, plane, part, here_even, scaled(here_odd, odd_plane, True))

    for to in places:
        for row in range(halves * lengths[to]):
            if row not in written[to]:
                messages[to][row : row + 1, :] = jnp.zeros((1, width), jnp.float32)
    if shared:
        for far, target in enumerate(passed, 1):
            size = lengths[far]
            for half in range(2):
                mine, other = (slice(n * size, (n + 1) * size) for n in (half, 1 - half))
                target[mine, :] = jnp.where(
                    lax.axis_index("gy") == 0,
                    jnp.where(sends_right(far), messages[far][mine, :], messages[-far][mine, :]),
                    jnp.where(sends_right(far), messages[far][other, :], messages[-far][other, :]),
                )


def rest_kernel(block, rows, width, first, *refs):
    coarse, out = refs[:-1], refs[-1]
    low = windows(block)[0][0]
    half, mine = first.shape[1] // 2, rows // 2
    for plane in range(block):
        odd_plane = plane % 2 == 1
        even, odd = y_lift_split(
            first[plane - low, pl.ds(0, half, 2), :], first[plane - low, pl.ds(1, half, 2), :]
        )
        even = scaled(even[:mine], odd_plane, False)
        if not odd_plane:
            even = jnp.where(own_lanes(width, 0, True), even, 0.0)
        out[plane, pl.ds(0, mine, 2), :] = even
        out[plane, pl.ds(1, mine, 2), :] = scaled(odd[:mine], odd_plane, True)
    for level in range(1, LEVELS):
        spacing, shift = 1 << level, shift_of(level)
        for plane in range(block >> level):
            value = coarse[level - 1][plane]
            if shift:
                value = pltpu.roll(value, width - shift, 1)
            out[plane * spacing, pl.ds(0, rows >> level, spacing), :] += value


def add_message(block, rows, to, arrived, base, out, clean):
    sent, derived, _ = message(block, rows, to)
    a, b, c, d = STEPS
    width = out.shape[-1]
    lane = lax.broadcasted_iota(jnp.int32, (1, width), 1)
    for level in sorted({level for level, _ in sent}):
        spacing, height = 1 << level, rows >> level
        shape = (height, width)
        held = {}
        for shift in sorted({shift for (found, _), (_, shift) in sent.items() if found == level}):
            here = {
                plane: at for (found, plane), (at, by) in sent.items() if (found, by) == (level, shift)
            }
            start, stop = min(here.values()), -(-(max(here.values()) + height) // 8) * 8
            source, offset = arrived, base
            if level > 0:
                value = arrived[base + start : base + stop, :]
                if shift:
                    value = pltpu.roll(value, width - shift, 1)
                source, offset = clean[level if shift == shift_of(level) else 0], -start
                source[: stop - start, :] = jnp.where(lax.rem(lane, spacing) == 0, value, 0.0)
            held |= {plane: (source, at + offset) for plane, at in here.items()}

        def read(plane):
            source, at = held[plane]
            return source[at : at + height, :]

        def add(plane, value):
            x = (plane - to * (block >> level)) * spacing
            out[x, pl.ds(0, height, spacing), :] += value

        for plane in held:
            add(plane, read(plane))
        for (found, plane), (far, near) in derived.items():
            if found == level:
                if near is None:
                    value = (d / SCALE**2) * read(far)
                else:
                    value = ((1 / c + d) / SCALE**2) * read(far) + (d / SCALE**2) * read(near)
                row = lax.broadcasted_iota(jnp.int32, shape, 0)
                keep = (lax.rem(row, 2) == 1) | lanes_of(width, spacing, True)
                add(plane, jnp.where(keep, value, 0.0))


def write_out(out, whole, done, runs):
    copies = [
        pltpu.make_async_copy(
            out.at[pl.ds(start, stop - start)], whole.at[pl.ds(start, stop - start)], done.at[n]
        )
        for n, (start, stop) in enumerate(runs)
    ]
    for copy in copies:
        copy.start()
    for copy in copies:
        copy.wait()


def add_kernel(block, rows, places, last, _, *refs):
    received, refs = refs[: len(places)], refs[len(places) :]
    if last:
        whole, out, done, *clean = refs
    else:
        out, *clean = refs
    for to, arrived in zip(places, received):
        add_message(block, rows, to, arrived, 0, out, clean)
    if last:
        write_out(out, whole, done, [(0, block)])


def add_either(block, rows, right, step, arrived, base, out, clean):
    for side, here in ((step, right), (-step, jnp.logical_not(right))):

        @pl.when(here)
        def _():
            add_message(block, rows, side, arrived, base, out, clean)


def keep_kernel(block, rows, _, near, far, out, *clean):
    for step, arrived in enumerate((near, far), 1):
        own = half_of(arrived, lax.axis_index("gy"))
        add_either(block, rows, takes_right(step), step, own, 0, out, clean)


def half_of(arrived, core):
    size = arrived.shape[0] // 2
    return arrived.at[pl.ds(pl.multiple_of(core * size, 8), size)]


def pack_kernel(near, far, packed):
    one = near.shape[0] // 2
    other = 1 - lax.axis_index("gy")
    packed[:one, :] = half_of(near, other)[...]
    packed[one:, :] = half_of(far, other)[...]


def swap_kernel(block, rows, one, own, packed, whole, out, done, *clean):
    for step, base in enumerate((0, one), 1):
        right = jnp.logical_not(takes_right(step))
        add_either(block, rows, right, step, packed, base, out, clean)
    write_out(out, whole, done, [(0, block)])


def call(body, name, outs, ins, scratch=(), aliases=None, flops=0, hbm_out=()):
    vmem, hbm = pl.BlockSpec(memory_space=pltpu.VMEM), pl.BlockSpec(memory_space=pltpu.HBM)
    f32 = jnp.float32
    shapes = [out if isinstance(out, jax.ShapeDtypeStruct) else jax.ShapeDtypeStruct(out, f32) for out in outs]
    moved = 4 * sum(int(np.prod(shape.shape)) for shape in shapes)
    return pl.pallas_call(
        body,
        out_shape=shapes,
        in_specs=[vmem] * len(ins),
        out_specs=[hbm if n in hbm_out else vmem for n in range(len(outs))],
        scratch_shapes=[pltpu.VMEM(shape, f32) if isinstance(shape, tuple) else shape for shape in scratch],
        input_output_aliases=aliases or {},
        compiler_params=pltpu.CompilerParams(vmem_limit_bytes=VMEM_BYTES),
        cost_estimate=pl.CostEstimate(flops=flops, bytes_accessed=2 * moved, transcendentals=0),
        name=name,
    )(*ins)


def local(velocity):
    block, rows, width = velocity.shape
    around, count = lax.axis_size("gx"), lax.axis_size("gy")
    shared = count == 2 and SHARED
    places = places_of(block)
    spans = windows(block)
    total = count * rows

    others = [
        lax.ppermute(velocity, "gy", [(i, (i - k) % count) for i in range(count)])
        for k in range(1, count)
    ]
    lifted = [
        (high - low + 1, total >> level, width) for level, (low, high) in enumerate(spans)
    ]
    coarse = [
        ((high // 2 - low // 2 + 1) * (total >> (level + 1)), width)
        for level, (low, high) in enumerate(spans[:-1])
    ]
    spread = (block * rows, width)
    owned = [(block >> level, rows >> level, width) for level in range(LEVELS)]
    lengths = {to: message(block, rows, to)[2] for to in places}
    one, two = max(lengths[1], lengths[-1]), max(lengths[2], lengths[-2])
    clean = [(one, width)] * LEVELS

    square = jax.ShapeDtypeStruct((2 * width, 2 * width), jnp.bfloat16)
    weights = call(matrix_kernel, "make_matrices", [square] * 2, [], flops=FIRST_FLOPS)
    (first,) = call(
        functools.partial(own_kernel, block, rows),
        "lift_own",
        [lifted[0]],
        [velocity, weights[0]],
        [spread],
    )
    if shared:
        each = {to: (2 * (one if abs(to) == 1 else two), width) for to in places}
        outs, scratch = [each[1], each[2]], [each[to] for to in places]
    else:
        outs, scratch = [(lengths[to], width) for to in places], []
    first, *more = call(
        functools.partial(message_kernel, block, rows, width, count, places),
        "make_messages",
        [lifted[0]] + owned[1:] + outs,
        [first] + others + list(weights),
        [spread] + lifted[1:] + coarse + scratch,
        {0: 0},
    )
    own_coarse, messages = more[: LEVELS - 1], more[LEVELS - 1 :]

    def rest():
        return call(
            functools.partial(rest_kernel, block, rows, width),
            "finish_own",
            [owned[0]],
            [first] + own_coarse,
        )[0]

    written = [pltpu.SemaphoreType.DMA((1,))]
    if shared:
        near, far = (
            lax.ppermute(value, ("gx", "gy"), shared_pairs(step, around))
            for step, value in enumerate(messages, 1)
        )
        result = rest()
        (packed,) = call(pack_kernel, "pack_other", [(one + two, width)], [near, far])
        packed = lax.ppermute(packed, "gy", [(0, 1), (1, 0)])
        (result,) = call(
            functools.partial(keep_kernel, block, rows),
            "add_kept",
            [owned[0]],
            [result, near, far],
            clean,
            aliases={0: 0},
        )
        whole, _ = call(
            functools.partial(swap_kernel, block, rows, one),
            "add_swapped",
            [owned[0]] * 2,
            [result, packed],
            written + clean,
            aliases={0: 1},
            hbm_out=(0,),
        )
        return whole

    sent = dict(zip(places, messages))
    received = {
        to: lax.ppermute(sent[to], "gx", [(i, (i + to) % around) for i in range(around)])
        for to in sorted(places, key=lambda to: (to < 0, abs(to)))
    }
    right = [to for to in places if to > 0]
    left = [to for to in places if to < 0]
    (result,) = call(
        functools.partial(add_kernel, block, rows, right, False),
        "add_right",
        [owned[0]],
        [rest()] + [received[to] for to in right],
        clean,
        aliases={0: 0},
        flops=FIRST_FLOPS,
    )
    whole, _ = call(
        functools.partial(add_kernel, block, rows, left, True),
        "add_left",
        [owned[0]] * 2,
        [result] + [received[to] for to in left],
        written + clean,
        aliases={0: 1},
        hbm_out=(0,),
    )
    return whole


def solution(mesh):
    return jax.shard_map(
        local, mesh=mesh, in_specs=(P("gx", "gy", None),), out_specs=P("gx", "gy", None), check_vma=False
    )
```

```python
import functools

import jax
import jax.numpy as jnp
import numpy as np
from jax import lax
from jax.experimental import pallas as pl
from jax.experimental.pallas import tpu as pltpu
from jax.sharding import PartitionSpec as P

LEVELS = 4
STEPS = (-1.586134342, -0.05298011854, 0.8829110762, 0.4435068522)
SCALE = 1.149604398
VMEM_BYTES = 24 * 2**20
FIRST_FLOPS = 10**10
SHARED = True


def windows(block):
    found = []
    first, last = 0, block - 1
    for _ in range(LEVELS):
        low = first - 4 + (first % 2)
        high = last + 4 - (last % 2)
        found.append((low, high))
        first, last = low // 2, high // 2
    return found


def message(block, rows, to):
    sent, derived = {}, {}
    spans = windows(block)
    base = ends = 0
    for level, (low, high) in enumerate(spans):
        size, height = block >> level, rows >> level
        first, last = (0, block - 1) if level == 0 else (v // 2 for v in spans[level - 1])
        planes = [p for p in range(low, high + 1) if p // size == to]
        if abs(to) == 1:
            sign = to
            edge = last + 2 - last % 2 if to > 0 else first - 2 + first % 2
            far, near = edge + sign, edge - sign
            if far in planes and edge + 2 * sign in planes:
                derived[level, edge + 2 * sign] = (far, None)
            if far in planes and near in planes:
                derived[level, edge] = (far, near)
        planes = [plane for plane in planes if (level, plane) not in derived]
        at = base
        if level == 1:
            extra = planes[-1] if len(planes) > 3 else None
        elif level > 1 and extra is not None:
            at = base + (rows >> 1)
        for plane in planes:
            if level == 1 and plane == extra:
                sent[level, plane] = base, shift_of(2)
                continue
            sent[level, plane] = at, shift_of(level)
            at += height
        ends = max(ends, at)
        if level == 0:
            base = at
    return sent, derived, -(-ends // 8) * 8


def shift_of(level):
    return (0, 0, 1, 3)[level]


def places_of(block):
    found = set()
    for level, (low, high) in enumerate(windows(block)):
        size = block >> level
        found |= set(range(low // size, high // size + 1))
    return sorted(found - {0})


def z_product(value, weights):
    width = value.shape[-1]
    high = value.astype(jnp.bfloat16)
    rest = (value - high.astype(jnp.float32)).astype(jnp.bfloat16)
    both = jnp.concatenate([high, rest], axis=1)
    product = jnp.dot(both, weights, preferred_element_type=jnp.float32)
    return product[:, :width] + product[:, width:]


def lanes_of(width, spacing, parity):
    lane = lax.broadcasted_iota(jnp.int32, (1, width), 1)
    return lax.rem(lane, 2 * spacing) == (spacing if parity else 0)


def own_lanes(width, level, high_only):
    spacing, shift = 1 << level, shift_of(level)
    lane = lax.broadcasted_iota(jnp.int32, (1, width), 1)
    if high_only:
        return lax.rem(lane, 2 * spacing) == spacing + shift
    return lax.rem(lane, spacing) == shift


def z_lift(value, spacing):
    width = value.shape[-1]
    axis = value.ndim - 1
    for step, weight in enumerate(STEPS):
        factor = jnp.where(lanes_of(width, spacing, step % 2 == 0), weight, 0.0)
        around = pltpu.roll(value, spacing, axis) + pltpu.roll(value, width - spacing, axis)
        value = value + factor * around
    return value


def x_lift(planes):
    def plus(one, other):
        return other if one is None else one if other is None else one + other

    planes = dict(planes)
    for step, weight in enumerate(STEPS):
        parity = 1 if step % 2 == 0 else 0
        for index in range(min(planes) - 1, max(planes) + 2):
            if index % 2 == parity:
                around = plus(planes.get(index - 1), planes.get(index + 1))
                if around is not None:
                    planes[index] = plus(planes.get(index), weight * around)
    return planes


def y_lift_split(even, odd):
    count = even.shape[0]
    a, b, c, d = STEPS
    odd = odd + a * (even + pltpu.roll(even, count - 1, 0))
    even = even + b * (pltpu.roll(odd, 1, 0) + odd)
    odd = odd + c * (even + pltpu.roll(even, count - 1, 0))
    even = even + d * (pltpu.roll(odd, 1, 0) + odd)
    return even, odd


def y_lift_whole(value):
    count = value.shape[0]
    row = lax.broadcasted_iota(jnp.int32, (count, 1), 0)
    for step, weight in enumerate(STEPS):
        factor = jnp.where(lax.rem(row, 2) == (1 if step % 2 == 0 else 0), weight, 0.0)
        value = value + factor * (pltpu.roll(value, 1, 0) + pltpu.roll(value, count - 1, 0))
    return value


def scaled_z(value, spacing):
    width = value.shape[-1]
    odd, even = lanes_of(width, spacing, True), lanes_of(width, spacing, False)
    return value * jnp.where(odd, SCALE, jnp.where(even, 1 / SCALE, 0.0))


def scaled(value, x_odd, y_odd):
    at = (SCALE if x_odd else 1 / SCALE) * (SCALE if y_odd else 1 / SCALE)
    return value if x_odd != y_odd else value * at


def spread_z(source, weights, spread, rows, start, size):
    width = source.shape[-1]
    value = source[start : start + size].reshape(size * rows, width)
    spread[start * rows : (start + size) * rows, :] = z_product(value, weights[...])


def spread_x(block, rows, spread, into, low, base):
    for at in range(0, rows, 8):
        planes = {x: spread[x * rows + at : x * rows + at + 8, :] for x in range(block)}
        for x, value in x_lift(planes).items():
            into[x - low, base + at : base + at + 8, :] = value


def matrix_kernel(*weights):
    width = weights[0].shape[0] // 2
    row = lax.broadcasted_iota(jnp.int32, (width, width), 0)
    lane = lax.broadcasted_iota(jnp.int32, (width, width), 1)
    value = jnp.where(row == lane, 1.0, 0.0)
    full = [scaled_z(z_lift(value, 1), 1), jnp.zeros((width, width), jnp.float32)]
    for level in range(1, LEVELS):
        spacing = 1 << level
        value = scaled_z(z_lift(value, spacing), spacing)
        full[1] += pltpu.roll(value, shift_of(level), 1) if shift_of(level) else value
        value = jnp.where(lanes_of(width, spacing, False), value, 0.0)
    for weight, matrix in zip(weights, full):
        high = matrix.astype(jnp.bfloat16)
        rest = (matrix - high.astype(jnp.float32)).astype(jnp.bfloat16)
        weight[:width, :width] = high
        weight[:width, width:] = rest
        weight[width:, :width] = high
        weight[width:, width:] = jnp.zeros_like(rest)


def own_kernel(block, rows, velocity, weights, into, spread):
    step = max(1, min(block, 512 // rows))
    for x in range(0, block, step):
        spread_z(velocity, weights, spread, rows, x, step)
    spread_x(block, rows, spread, into, windows(block)[0][0], 0)


def right_source(step, place, last):
    return place == last if step == 1 else (place == 0) | (place == last - 1)


def right_target(step, place):
    return (place == 0) & (step == 1)


def sends_right(step):
    core = lax.axis_index("gy") == 1
    return core == right_source(step, lax.axis_index("gx"), lax.axis_size("gx") - 1)


def takes_right(step):
    core = lax.axis_index("gy") == 1
    return core == right_target(step, lax.axis_index("gx"))


def shared_pairs(step, around):
    pairs = []
    for place in range(around):
        to, back = (place + step) % around, (place - step) % around
        source = int(right_source(step, place, around - 1))
        pairs.append((2 * place + source, 2 * to + int(right_target(step, to))))
        pairs.append((2 * place + 1 - source, 2 * back + 1 - int(right_target(step, back))))
    return pairs


def message_kernel(block, rows, width, count, places, *refs):
    refs = list(refs)

    def take(number):
        taken = refs[:number]
        del refs[:number]
        return taken

    shared = count == 2 and SHARED
    halves = 2 if shared else 1
    (_,) = take(1)
    others = take(count - 1)
    weights = take(2)
    lifted = take(LEVELS)
    passed = take(2 if shared else len(places))
    (spread,) = take(1)
    coarse = take(LEVELS - 1)
    both = take(2) if shared else []
    messages = dict(zip(places, passed))
    spans = windows(block)
    total = count * rows
    tables = {to: message(block, rows, to) for to in places}
    lengths = {to: message(block, rows, to)[2] for to in places}
    if shared:
        for step, buffer in enumerate(both, 1):
            size = buffer.shape[0] // 4
            for side, to in enumerate((step, -step)):
                lengths[to] = size
                messages[to] = buffer.at[pl.ds(2 * side * size, 2 * size)]
    written = {to: set() for to in places}

    def post(to, at, number, value):
        here = range(at, at + 2 * number, 2)
        if written[to].isdisjoint(here):
            messages[to][pl.ds(at, number, 2), :] = value
        else:
            messages[to][pl.ds(at, number, 2), :] += value
        written[to].update(here)

    def put(level, plane, half, even, odd):
        number = (rows >> level) // 2
        low = level < LEVELS - 1 and plane % 2 == 0
        if level > 0 or low:
            even = jnp.where(own_lanes(width, level, low), even, 0.0)
        if level > 0:
            odd = jnp.where(own_lanes(width, level, False), odd, 0.0)
        to = plane // (block >> level)
        at, shift = tables[to][0][level, plane]
        at += half * lengths[to]
        if shift != shift_of(level):
            even, odd = (pltpu.roll(value, shift - shift_of(level), 1) for value in (even, odd))
        post(to, at, number, even)
        post(to, at + 1, number, odd)

    for level in range(LEVELS):
        low, high = spans[level]
        height = total >> level
        half, mine = height // 2, (rows >> level) // 2
        into = lifted[level]

        if level == 0:
            for part, source in enumerate(others):
                step = min(block, max(1, 512 // rows))
                for x in range(0, block, step):
                    spread_z(source, weights[0], spread, rows, x, step)
                spread_x(block, rows, spread, into, low, (part + 1) * rows)
        else:
            start, stop = spans[level - 1][0] // 2, spans[level - 1][1] // 2 + 1
            source = coarse[level - 1]
            if level == 1:
                size = (stop - start) * height
                for at in range(0, size, 512):
                    end = min(size, at + 512)
                    source[at:end, :] = z_product(source[at:end, :], weights[level][...])
            for at in range(0, height, 8):
                planes = {}
                for x in range(start, stop):
                    row = (x - start) * height + at
                    planes[x] = source[row : row + 8, :]
                for x, value in x_lift(planes).items():
                    into[x - low, at : at + 8, :] = value

        for plane in range(low, high + 1):
            odd_plane = plane % 2 == 1
            to = plane // (block >> level)
            goes_on = level < LEVELS - 1 and not odd_plane
            sends = to != 0 and (level, plane) in tables[to][0]
            if not goes_on and not sends:
                continue
            at = plane - low
            split = half % 8 == 0
            if split:
                even, odd = y_lift_split(
                    into[at, pl.ds(0, half, 2), :], into[at, pl.ds(1, half, 2), :]
                )
                even = scaled(even, odd_plane, False)
            else:
                into[at] = y_lift_whole(into[at])
                even = scaled(into[at, pl.ds(0, half, 2), :], odd_plane, False)
            if goes_on:
                row = ((plane - low) // 2) * half
                coarse[level][row : row + half, :] = even
            if not sends:
                continue
            for part in range(halves):
                if split:
                    here_even = even[part * mine : (part + 1) * mine]
                    here_odd = odd[part * mine : (part + 1) * mine]
                else:
                    here_even = into[at, pl.ds(2 * part * mine, mine, 2), :]
                    here_even = scaled(here_even, odd_plane, False)
                    here_odd = into[at, pl.ds(2 * part * mine + 1, mine, 2), :]
                put(level, plane, part, here_even, scaled(here_odd, odd_plane, True))

    for to in places:
        for row in range(halves * lengths[to]):
            if row not in written[to]:
                messages[to][row : row + 1, :] = jnp.zeros((1, width), jnp.float32)
    if shared:
        core = lax.axis_index("gy")
        for step, (target, buffer) in enumerate(zip(passed, both), 1):
            size = lengths[step]
            side = jnp.where(sends_right(step), 0, 2 * size)
            for half in range(2):
                here = side + (core if half == 0 else 1 - core) * size
                target[half * size : (half + 1) * size, :] = buffer[pl.ds(pl.multiple_of(here, 8), size), :]


def rest_kernel(block, rows, width, *refs):
    lifted, out, spare = refs[:LEVELS], refs[LEVELS], refs[LEVELS + 1]
    for level, (low, _) in enumerate(windows(block)):
        into, spacing, shift = lifted[level], 1 << level, shift_of(level)
        half, mine = into.shape[1] // 2, (rows >> level) // 2
        for plane in range(block >> level):
            odd_plane = plane % 2 == 1
            at = plane - low
            if half % 8 == 0:
                even, odd = y_lift_split(
                    into[at, pl.ds(0, half, 2), :], into[at, pl.ds(1, half, 2), :]
                )
                even, odd = even[:mine], odd[:mine]
            else:
                spare[plane] = y_lift_whole(into[at])
                even, odd = spare[plane, pl.ds(0, mine, 2), :], spare[plane, pl.ds(1, mine, 2), :]
            even, odd = scaled(even, odd_plane, False), scaled(odd, odd_plane, True)
            further = level < LEVELS - 1 and not odd_plane
            if level > 0 or further:
                even = jnp.where(own_lanes(width, level, further), even, 0.0)
            x = plane * spacing
            if level == 0:
                out[x, pl.ds(0, mine, 2), :] = even
                out[x, pl.ds(1, mine, 2), :] = odd
                continue
            odd = jnp.where(own_lanes(width, level, False), odd, 0.0)
            if shift:
                even, odd = (pltpu.roll(value, width - shift, 1) for value in (even, odd))
            out[x, pl.ds(0, mine, 2 * spacing), :] += even
            out[x, pl.ds(spacing, mine, 2 * spacing), :] += odd


def add_message(block, rows, to, arrived, base, out, clean):
    sent, derived, _ = message(block, rows, to)
    a, b, c, d = STEPS
    width = out.shape[-1]
    lane = lax.broadcasted_iota(jnp.int32, (1, width), 1)
    for level in sorted({level for level, _ in sent}):
        spacing, height = 1 << level, rows >> level
        shape = (height, width)
        held = {}
        for shift in sorted({shift for (found, _), (_, shift) in sent.items() if found == level}):
            here = {
                plane: at for (found, plane), (at, by) in sent.items() if (found, by) == (level, shift)
            }
            start, stop = min(here.values()), -(-(max(here.values()) + height) // 8) * 8
            source, offset = arrived, base
            if level > 0:
                value = arrived[base + start : base + stop, :]
                if shift:
                    value = pltpu.roll(value, width - shift, 1)
                source, offset = clean[level if shift == shift_of(level) else 0], -start
                source[: stop - start, :] = jnp.where(lax.rem(lane, spacing) == 0, value, 0.0)
            held |= {plane: (source, at + offset) for plane, at in here.items()}

        def read(plane):
            source, at = held[plane]
            return source[at : at + height, :]

        def add(plane, value):
            x = (plane - to * (block >> level)) * spacing
            out[x, pl.ds(0, height, spacing), :] += value

        for plane in held:
            add(plane, read(plane))
        for (found, plane), (far, near) in derived.items():
            if found == level:
                if near is None:
                    value = (d / SCALE**2) * read(far)
                else:
                    value = ((1 / c + d) / SCALE**2) * read(far) + (d / SCALE**2) * read(near)
                row = lax.broadcasted_iota(jnp.int32, shape, 0)
                keep = (lax.rem(row, 2) == 1) | lanes_of(width, spacing, True)
                add(plane, jnp.where(keep, value, 0.0))


def write_out(out, whole, done, runs):
    copies = [
        pltpu.make_async_copy(
            out.at[pl.ds(start, stop - start)], whole.at[pl.ds(start, stop - start)], done.at[n]
        )
        for n, (start, stop) in enumerate(runs)
    ]
    for copy in copies:
        copy.start()
    for copy in copies:
        copy.wait()


def add_kernel(block, rows, places, last, _, *refs):
    received, refs = refs[: len(places)], refs[len(places) :]
    if last:
        whole, out, done, *clean = refs
    else:
        out, *clean = refs
    for to, arrived in zip(places, received):
        add_message(block, rows, to, arrived, 0, out, clean)
    if last:
        write_out(out, whole, done, [(0, block)])


def add_far(block, rows, right, arrived, base, out, clean):
    width, level = out.shape[-1], LEVELS - 1
    spacing, height, shift = 1 << level, rows >> level, shift_of(level)
    length = max(message(block, rows, to)[2] for to in (2, -2))
    lane = lax.broadcasted_iota(jnp.int32, (1, width), 1)
    value = pltpu.roll(arrived[base : base + length, :], width - shift, 1)
    value = jnp.where(lax.rem(lane, spacing) == 0, value, 0.0)
    for to, here in ((2, right), (-2, jnp.logical_not(right))):
        source = clean[0 if to > 0 else level]
        source[:length, :] = jnp.where(here, value, 0.0)
        for (found, plane), (at, _) in message(block, rows, to)[0].items():
            x = (plane - to * (block >> level)) * spacing
            out[x, pl.ds(0, height, spacing), :] += source[at : at + height, :]


def add_either(block, rows, right, step, arrived, base, out, clean):
    for side, here in ((step, right), (-step, jnp.logical_not(right))):

        @pl.when(here)
        def _():
            add_message(block, rows, side, arrived, base, out, clean)


def keep_kernel(block, rows, _, near, far, out, *clean):
    core = lax.axis_index("gy")
    add_either(block, rows, takes_right(1), 1, half_of(near, core), 0, out, clean)
    add_far(block, rows, takes_right(2), half_of(far, core), 0, out, clean)


def half_of(arrived, core):
    size = arrived.shape[0] // 2
    return arrived.at[pl.ds(pl.multiple_of(core * size, 8), size)]


def pack_kernel(near, far, packed):
    one = near.shape[0] // 2
    other = 1 - lax.axis_index("gy")
    packed[:one, :] = half_of(near, other)[...]
    packed[one:, :] = half_of(far, other)[...]


def swap_kernel(block, rows, one, own, packed, whole, out, done, *clean):
    add_either(block, rows, jnp.logical_not(takes_right(1)), 1, packed, 0, out, clean)
    add_far(block, rows, jnp.logical_not(takes_right(2)), packed, one, out, clean)
    write_out(out, whole, done, [(0, block)])


def call(body, name, outs, ins, scratch=(), aliases=None, flops=0, hbm_out=()):
    vmem, hbm = pl.BlockSpec(memory_space=pltpu.VMEM), pl.BlockSpec(memory_space=pltpu.HBM)
    f32 = jnp.float32
    shapes = [out if isinstance(out, jax.ShapeDtypeStruct) else jax.ShapeDtypeStruct(out, f32) for out in outs]
    moved = 4 * sum(int(np.prod(shape.shape)) for shape in shapes)
    return pl.pallas_call(
        body,
        out_shape=shapes,
        in_specs=[vmem] * len(ins),
        out_specs=[hbm if n in hbm_out else vmem for n in range(len(outs))],
        scratch_shapes=[pltpu.VMEM(shape, f32) if isinstance(shape, tuple) else shape for shape in scratch],
        input_output_aliases=aliases or {},
        compiler_params=pltpu.CompilerParams(vmem_limit_bytes=VMEM_BYTES),
        cost_estimate=pl.CostEstimate(flops=flops, bytes_accessed=2 * moved, transcendentals=0),
        name=name,
    )(*ins)


def local(velocity):
    block, rows, width = velocity.shape
    around, count = lax.axis_size("gx"), lax.axis_size("gy")
    shared = count == 2 and SHARED
    places = places_of(block)
    spans = windows(block)
    total = count * rows

    others = [
        lax.ppermute(velocity, "gy", [(i, (i - k) % count) for i in range(count)])
        for k in range(1, count)
    ]
    lifted = [
        (high - low + 1, total >> level, width) for level, (low, high) in enumerate(spans)
    ]
    coarse = [
        ((high // 2 - low // 2 + 1) * (total >> (level + 1)), width)
        for level, (low, high) in enumerate(spans[:-1])
    ]
    spread = (block * rows, width)
    owned = [(block >> level, rows >> level, width) for level in range(LEVELS)]
    lengths = {to: message(block, rows, to)[2] for to in places}
    one, two = max(lengths[1], lengths[-1]), max(lengths[2], lengths[-2])
    clean = [(one, width)] * LEVELS

    square = jax.ShapeDtypeStruct((2 * width, 2 * width), jnp.bfloat16)
    weights = call(matrix_kernel, "make_matrices", [square] * 2, [], flops=FIRST_FLOPS)
    (first,) = call(
        functools.partial(own_kernel, block, rows),
        "lift_own",
        [lifted[0]],
        [velocity, weights[0]],
        [spread],
    )
    if shared:
        outs, scratch = ([(many * size, width) for size in (one, two)] for many in (2, 4))
    else:
        outs, scratch = [(lengths[to], width) for to in places], []
    values = call(
        functools.partial(message_kernel, block, rows, width, count, places),
        "make_messages",
        lifted + outs,
        [first] + others + list(weights),
        [spread] + coarse + scratch,
        {0: 0},
    )
    before, messages = values[:LEVELS], values[LEVELS:]

    def rest():
        return call(
            functools.partial(rest_kernel, block, rows, width),
            "finish_own",
            [owned[0]],
            before,
            [(block >> LEVELS - 1, total >> LEVELS - 1, width)],
        )[0]

    written = [pltpu.SemaphoreType.DMA((1,))]
    if shared:
        near, far = (
            lax.ppermute(value, ("gx", "gy"), shared_pairs(step, around))
            for step, value in enumerate(messages, 1)
        )
        result = rest()
        (packed,) = call(pack_kernel, "pack_other", [(one + two, width)], [near, far])
        packed = lax.ppermute(packed, "gy", [(0, 1), (1, 0)])
        (result,) = call(
            functools.partial(keep_kernel, block, rows),
            "add_kept",
            [owned[0]],
            [result, near, far],
            clean,
            aliases={0: 0},
        )
        whole, _ = call(
            functools.partial(swap_kernel, block, rows, one),
            "add_swapped",
            [owned[0]] * 2,
            [result, packed],
            written + clean,
            aliases={0: 1},
            hbm_out=(0,),
        )
        return whole

    sent = dict(zip(places, messages))
    received = {
        to: lax.ppermute(sent[to], "gx", [(i, (i + to) % around) for i in range(around)])
        for to in sorted(places, key=lambda to: (to < 0, abs(to)))
    }
    right = [to for to in places if to > 0]
    left = [to for to in places if to < 0]
    (result,) = call(
        functools.partial(add_kernel, block, rows, right, False),
        "add_right",
        [owned[0]],
        [rest()] + [received[to] for to in right],
        clean,
        aliases={0: 0},
        flops=FIRST_FLOPS,
    )
    whole, _ = call(
        functools.partial(add_kernel, block, rows, left, True),
        "add_left",
        [owned[0]] * 2,
        [result] + [received[to] for to in left],
        written + clean,
        aliases={0: 1},
        hbm_out=(0,),
    )
    return whole


def solution(mesh):
    return jax.shard_map(
        local, mesh=mesh, in_specs=(P("gx", "gy", None),), out_specs=P("gx", "gy", None), check_vma=False
    )
```

```python
import functools

import jax
import jax.numpy as jnp
import numpy as np
from jax import lax
from jax.experimental import pallas as pl
from jax.experimental.pallas import tpu as pltpu
from jax.sharding import PartitionSpec as P

LEVELS = 4
STEPS = (-1.586134342, -0.05298011854, 0.8829110762, 0.4435068522)
SCALE = 1.149604398
VMEM_BYTES = 24 * 2**20
FIRST_FLOPS = 10**10
SHARED = True


def windows(block):
    found = []
    first, last = 0, block - 1
    for _ in range(LEVELS):
        low = first - 4 + (first % 2)
        high = last + 4 - (last % 2)
        found.append((low, high))
        first, last = low // 2, high // 2
    return found


def message(block, rows, to):
    sent, derived = {}, {}
    spans = windows(block)
    base = ends = 0
    for level, (low, high) in enumerate(spans):
        size, height = block >> level, rows >> level
        first, last = (0, block - 1) if level == 0 else (v // 2 for v in spans[level - 1])
        planes = [p for p in range(low, high + 1) if p // size == to]
        if abs(to) == 1:
            sign = to
            edge = last + 2 - last % 2 if to > 0 else first - 2 + first % 2
            far, near = edge + sign, edge - sign
            if far in planes and edge + 2 * sign in planes:
                derived[level, edge + 2 * sign] = (far, None)
            if far in planes and near in planes:
                derived[level, edge] = (far, near)
        planes = [plane for plane in planes if (level, plane) not in derived]
        at = base
        if level == 1:
            extra = planes[-1] if len(planes) > 3 else None
        elif level > 1 and extra is not None:
            at = base + (rows >> 1)
        for plane in planes:
            if level == 1 and plane == extra:
                sent[level, plane] = base, shift_of(2)
                continue
            sent[level, plane] = at, shift_of(level)
            at += height
        ends = max(ends, at)
        if level == 0:
            base = at
    return sent, derived, -(-ends // 8) * 8


def shift_of(level):
    return (0, 0, 1, 3)[level]


def places_of(block):
    found = set()
    for level, (low, high) in enumerate(windows(block)):
        size = block >> level
        found |= set(range(low // size, high // size + 1))
    return sorted(found - {0})


def z_product(value, weights):
    width = value.shape[-1]
    high = value.astype(jnp.bfloat16)
    rest = (value - high.astype(jnp.float32)).astype(jnp.bfloat16)
    both = jnp.concatenate([high, rest], axis=1)
    product = jnp.dot(both, weights, preferred_element_type=jnp.float32)
    return product[:, :width] + product[:, width:]


def lanes_of(width, spacing, parity):
    lane = lax.broadcasted_iota(jnp.int32, (1, width), 1)
    return lax.rem(lane, 2 * spacing) == (spacing if parity else 0)


def own_lanes(width, level, high_only):
    spacing, shift = 1 << level, shift_of(level)
    lane = lax.broadcasted_iota(jnp.int32, (1, width), 1)
    if high_only:
        return lax.rem(lane, 2 * spacing) == spacing + shift
    return lax.rem(lane, spacing) == shift


def z_lift(value, spacing):
    width = value.shape[-1]
    axis = value.ndim - 1
    for step, weight in enumerate(STEPS):
        factor = jnp.where(lanes_of(width, spacing, step % 2 == 0), weight, 0.0)
        around = pltpu.roll(value, spacing, axis) + pltpu.roll(value, width - spacing, axis)
        value = value + factor * around
    return value


def x_lift(planes):
    def plus(one, other):
        return other if one is None else one if other is None else one + other

    planes = dict(planes)
    for step, weight in enumerate(STEPS):
        parity = 1 if step % 2 == 0 else 0
        for index in range(min(planes) - 1, max(planes) + 2):
            if index % 2 == parity:
                around = plus(planes.get(index - 1), planes.get(index + 1))
                if around is not None:
                    planes[index] = plus(planes.get(index), weight * around)
    return planes


def y_lift_split(even, odd):
    count = even.shape[0]
    a, b, c, d = STEPS
    odd = odd + a * (even + pltpu.roll(even, count - 1, 0))
    even = even + b * (pltpu.roll(odd, 1, 0) + odd)
    odd = odd + c * (even + pltpu.roll(even, count - 1, 0))
    even = even + d * (pltpu.roll(odd, 1, 0) + odd)
    return even, odd


def y_lift_whole(value):
    count = value.shape[0]
    row = lax.broadcasted_iota(jnp.int32, (count, 1), 0)
    for step, weight in enumerate(STEPS):
        factor = jnp.where(lax.rem(row, 2) == (1 if step % 2 == 0 else 0), weight, 0.0)
        value = value + factor * (pltpu.roll(value, 1, 0) + pltpu.roll(value, count - 1, 0))
    return value


def scaled_z(value, spacing):
    width = value.shape[-1]
    odd, even = lanes_of(width, spacing, True), lanes_of(width, spacing, False)
    return value * jnp.where(odd, SCALE, jnp.where(even, 1 / SCALE, 0.0))


def scaled(value, x_odd, y_odd):
    at = (SCALE if x_odd else 1 / SCALE) * (SCALE if y_odd else 1 / SCALE)
    return value if x_odd != y_odd else value * at


def spread_z(source, weights, spread, rows, start, size):
    width = source.shape[-1]
    value = source[start : start + size].reshape(size * rows, width)
    spread[start * rows : (start + size) * rows, :] = z_product(value, weights[...])


def spread_x(block, rows, spread, into, low, base):
    for at in range(0, rows, 8):
        planes = {x: spread[x * rows + at : x * rows + at + 8, :] for x in range(block)}
        for x, value in x_lift(planes).items():
            into[x - low, base + at : base + at + 8, :] = value


def matrix_kernel(*weights):
    width = weights[0].shape[0] // 2
    row = lax.broadcasted_iota(jnp.int32, (width, width), 0)
    lane = lax.broadcasted_iota(jnp.int32, (width, width), 1)
    value = jnp.where(row == lane, 1.0, 0.0)
    full = [scaled_z(z_lift(value, 1), 1), jnp.zeros((width, width), jnp.float32)]
    for level in range(1, LEVELS):
        spacing = 1 << level
        value = scaled_z(z_lift(value, spacing), spacing)
        full[1] += pltpu.roll(value, shift_of(level), 1) if shift_of(level) else value
        value = jnp.where(lanes_of(width, spacing, False), value, 0.0)
    for weight, matrix in zip(weights, full):
        high = matrix.astype(jnp.bfloat16)
        rest = (matrix - high.astype(jnp.float32)).astype(jnp.bfloat16)
        weight[:width, :width] = high
        weight[:width, width:] = rest
        weight[width:, :width] = high
        weight[width:, width:] = jnp.zeros_like(rest)


def own_kernel(block, rows, velocity, weights, into, spread):
    step = max(1, min(block, 512 // rows))
    for x in range(0, block, step):
        spread_z(velocity, weights, spread, rows, x, step)
    spread_x(block, rows, spread, into, windows(block)[0][0], 0)


def right_source(step, place, last):
    return place == last if step == 1 else (place == 0) | (place == last - 1)


def right_target(step, place):
    return (place == 0) & (step == 1)


def sends_right(step):
    core = lax.axis_index("gy") == 1
    return core == right_source(step, lax.axis_index("gx"), lax.axis_size("gx") - 1)


def takes_right(step):
    core = lax.axis_index("gy") == 1
    return core == right_target(step, lax.axis_index("gx"))


def shared_pairs(step, around):
    pairs = []
    for place in range(around):
        to, back = (place + step) % around, (place - step) % around
        source = int(right_source(step, place, around - 1))
        pairs.append((2 * place + source, 2 * to + int(right_target(step, to))))
        pairs.append((2 * place + 1 - source, 2 * back + 1 - int(right_target(step, back))))
    return pairs


def message_kernel(block, rows, width, count, places, *refs):
    refs = list(refs)

    def take(number):
        taken = refs[:number]
        del refs[:number]
        return taken

    shared = count == 2 and SHARED
    halves = 2 if shared else 1
    (_,) = take(1)
    others = take(count - 1)
    weights = take(2)
    lifted = take(LEVELS)
    passed = take(2 if shared else len(places))
    (spread,) = take(1)
    coarse = take(LEVELS - 1)
    both = take(2) if shared else []
    messages = dict(zip(places, passed))
    spans = windows(block)
    total = count * rows
    tables = {to: message(block, rows, to) for to in places}
    lengths = {to: message(block, rows, to)[2] for to in places}
    if shared:
        for step, buffer in enumerate(both, 1):
            size = buffer.shape[0] // 4
            for side, to in enumerate((step, -step)):
                lengths[to] = size
                messages[to] = buffer.at[pl.ds(2 * side * size, 2 * size)]
    written = {to: set() for to in places}

    def post(to, at, number, value):
        here = range(at, at + 2 * number, 2)
        if written[to].isdisjoint(here):
            messages[to][pl.ds(at, number, 2), :] = value
        else:
            messages[to][pl.ds(at, number, 2), :] += value
        written[to].update(here)

    def put(level, plane, half, even, odd):
        number = (rows >> level) // 2
        low = level < LEVELS - 1 and plane % 2 == 0
        if level > 0 or low:
            even = jnp.where(own_lanes(width, level, low), even, 0.0)
        if level > 0:
            odd = jnp.where(own_lanes(width, level, False), odd, 0.0)
        to = plane // (block >> level)
        at, shift = tables[to][0][level, plane]
        at += half * lengths[to]
        if shift != shift_of(level):
            even, odd = (pltpu.roll(value, shift - shift_of(level), 1) for value in (even, odd))
        post(to, at, number, even)
        post(to, at + 1, number, odd)

    for level in range(LEVELS):
        low, high = spans[level]
        height = total >> level
        half, mine = height // 2, (rows >> level) // 2
        into = lifted[level]

        if level == 0:
            for part, source in enumerate(others):
                step = min(block, max(1, 512 // rows))
                for x in range(0, block, step):
                    spread_z(source, weights[0], spread, rows, x, step)
                spread_x(block, rows, spread, into, low, (part + 1) * rows)
        else:
            start, stop = spans[level - 1][0] // 2, spans[level - 1][1] // 2 + 1
            source = coarse[level - 1]
            if level == 1:
                size = (stop - start) * height
                for at in range(0, size, 512):
                    end = min(size, at + 512)
                    source[at:end, :] = z_product(source[at:end, :], weights[level][...])
            for at in range(0, height, 8):
                planes = {}
                for x in range(start, stop):
                    row = (x - start) * height + at
                    planes[x] = source[row : row + 8, :]
                for x, value in x_lift(planes).items():
                    into[x - low, at : at + 8, :] = value

        for plane in range(low, high + 1):
            odd_plane = plane % 2 == 1
            to = plane // (block >> level)
            goes_on = level < LEVELS - 1 and not odd_plane
            sends = to != 0 and (level, plane) in tables[to][0]
            if not goes_on and not sends:
                continue
            at = plane - low
            split = half % 8 == 0
            if split:
                even, odd = y_lift_split(
                    into[at, pl.ds(0, half, 2), :], into[at, pl.ds(1, half, 2), :]
                )
                even = scaled(even, odd_plane, False)
            else:
                into[at] = y_lift_whole(into[at])
                even = scaled(into[at, pl.ds(0, half, 2), :], odd_plane, False)
            if goes_on:
                row = ((plane - low) // 2) * half
                coarse[level][row : row + half, :] = even
            if not sends:
                continue
            for part in range(halves):
                if split:
                    here_even = even[part * mine : (part + 1) * mine]
                    here_odd = odd[part * mine : (part + 1) * mine]
                else:
                    here_even = into[at, pl.ds(2 * part * mine, mine, 2), :]
                    here_even = scaled(here_even, odd_plane, False)
                    here_odd = into[at, pl.ds(2 * part * mine + 1, mine, 2), :]
                put(level, plane, part, here_even, scaled(here_odd, odd_plane, True))

    for to in places:
        for row in range(halves * lengths[to]):
            if row not in written[to]:
                messages[to][row : row + 1, :] = jnp.zeros((1, width), jnp.float32)
    if shared:
        core = lax.axis_index("gy")
        for step, (target, buffer) in enumerate(zip(passed, both), 1):
            size = lengths[step]
            side = jnp.where(sends_right(step), 0, 2 * size)
            for half in range(2):
                here = side + (core if half == 0 else 1 - core) * size
                target[half * size : (half + 1) * size, :] = buffer[pl.ds(pl.multiple_of(here, 8), size), :]


def rest_kernel(block, rows, width, *refs):
    lifted, out, spare = refs[:LEVELS], refs[LEVELS], refs[LEVELS + 1]
    for level, (low, _) in enumerate(windows(block)):
        into, spacing, shift = lifted[level], 1 << level, shift_of(level)
        half, mine = into.shape[1] // 2, (rows >> level) // 2
        for plane in range(block >> level):
            odd_plane = plane % 2 == 1
            at = plane - low
            if half % 8 == 0:
                even, odd = y_lift_split(
                    into[at, pl.ds(0, half, 2), :], into[at, pl.ds(1, half, 2), :]
                )
                even, odd = even[:mine], odd[:mine]
            else:
                spare[plane] = y_lift_whole(into[at])
                even, odd = spare[plane, pl.ds(0, mine, 2), :], spare[plane, pl.ds(1, mine, 2), :]
            even, odd = scaled(even, odd_plane, False), scaled(odd, odd_plane, True)
            further = level < LEVELS - 1 and not odd_plane
            if level > 0 or further:
                even = jnp.where(own_lanes(width, level, further), even, 0.0)
            x = plane * spacing
            if level == 0:
                out[x, pl.ds(0, mine, 2), :] = even
                out[x, pl.ds(1, mine, 2), :] = odd
                continue
            odd = jnp.where(own_lanes(width, level, False), odd, 0.0)
            if shift:
                even, odd = (pltpu.roll(value, width - shift, 1) for value in (even, odd))
            out[x, pl.ds(0, mine, 2 * spacing), :] += even
            out[x, pl.ds(spacing, mine, 2 * spacing), :] += odd


def additions(block, rows, to, arrived, base, out, clean):
    sent, derived, _ = message(block, rows, to)
    a, b, c, d = STEPS
    width = out.shape[-1]
    lane = lax.broadcasted_iota(jnp.int32, (1, width), 1)
    found_here = []
    for level in sorted({level for level, _ in sent}):
        spacing, height = 1 << level, rows >> level
        shape = (height, width)
        held = {}
        for shift in sorted({shift for (found, _), (_, shift) in sent.items() if found == level}):
            here = {
                plane: at for (found, plane), (at, by) in sent.items() if (found, by) == (level, shift)
            }
            start, stop = min(here.values()), -(-(max(here.values()) + height) // 8) * 8
            source, offset = arrived, base
            if level > 0:
                value = arrived[base + start : base + stop, :]
                if shift:
                    value = pltpu.roll(value, width - shift, 1)
                source, offset = clean[level if shift == shift_of(level) else 0], -start
                source[: stop - start, :] = jnp.where(lax.rem(lane, spacing) == 0, value, 0.0)
            held |= {plane: (source, at + offset) for plane, at in here.items()}

        def read(plane, held=held, height=height):
            source, at = held[plane]
            return source[at : at + height, :]

        def derive(far, near, read=read, shape=shape, spacing=spacing):
            if near is None:
                value = (d / SCALE**2) * read(far)
            else:
                value = ((1 / c + d) / SCALE**2) * read(far) + (d / SCALE**2) * read(near)
            row = lax.broadcasted_iota(jnp.int32, shape, 0)
            keep = (lax.rem(row, 2) == 1) | lanes_of(width, spacing, True)
            return jnp.where(keep, value, 0.0)

        values = {plane: functools.partial(read, plane) for plane in held}
        for (found, plane), (far, near) in derived.items():
            if found == level:
                values[plane] = functools.partial(derive, far, near)
        for plane, value in values.items():
            x = (plane - to * (block >> level)) * spacing

            def add(x=x, height=height, spacing=spacing, value=value):
                out[x, pl.ds(0, height, spacing), :] += value()

            found_here.append((x, add))
    return found_here


def add_message(*args):
    for _, add in additions(*args):
        add()


def copy_out(out, whole, done, part, parts):
    size = out.shape[0] // parts
    here = pl.ds(part * size, size)
    copy = pltpu.make_async_copy(out.at[here], whole.at[here], done.at[part])
    copy.start()
    return copy


def add_kernel(block, rows, places, last, _, *refs):
    received, refs = refs[: len(places)], refs[len(places) :]
    if last:
        whole, out, done, *clean = refs
    else:
        out, *clean = refs
    for to, arrived in zip(places, received):
        add_message(block, rows, to, arrived, 0, out, clean)
    if last:
        for copy in [copy_out(out, whole, done, part, 2) for part in range(2)]:
            copy.wait()


def add_far(block, rows, right, arrived, base, out, clean):
    width, level = out.shape[-1], LEVELS - 1
    spacing, height, shift = 1 << level, rows >> level, shift_of(level)
    length = max(message(block, rows, to)[2] for to in (2, -2))
    lane = lax.broadcasted_iota(jnp.int32, (1, width), 1)
    value = pltpu.roll(arrived[base : base + length, :], width - shift, 1)
    value = jnp.where(lax.rem(lane, spacing) == 0, value, 0.0)
    for to, here in ((2, right), (-2, jnp.logical_not(right))):
        source = clean[0 if to > 0 else level]
        source[:length, :] = jnp.where(here, value, 0.0)
        for (found, plane), (at, _) in message(block, rows, to)[0].items():
            x = (plane - to * (block >> level)) * spacing
            out[x, pl.ds(0, height, spacing), :] += source[at : at + height, :]


def add_either(block, rows, right, step, arrived, base, out, clean):
    for side, here in ((step, right), (-step, jnp.logical_not(right))):

        @pl.when(here)
        def _():
            add_message(block, rows, side, arrived, base, out, clean)


def keep_kernel(block, rows, _, near, far, out, *clean):
    core = lax.axis_index("gy")
    add_either(block, rows, takes_right(1), 1, half_of(near, core), 0, out, clean)
    add_far(block, rows, takes_right(2), half_of(far, core), 0, out, clean)


def half_of(arrived, core):
    size = arrived.shape[0] // 2
    return arrived.at[pl.ds(pl.multiple_of(core * size, 8), size)]


def pack_kernel(near, far, packed):
    one = near.shape[0] // 2
    other = 1 - lax.axis_index("gy")
    packed[:one, :] = half_of(near, other)[...]
    packed[one:, :] = half_of(far, other)[...]


def swap_kernel(block, rows, one, own, packed, whole, out, done, *clean):
    add_far(block, rows, jnp.logical_not(takes_right(2)), packed, one, out, clean)
    right = jnp.logical_not(takes_right(1))
    for to, here in ((1, right), (-1, jnp.logical_not(right))):

        @pl.when(here)
        def _():
            tasks = additions(block, rows, to, packed, 0, out, clean)
            copies = []
            for part in ((1, 0) if to > 0 else (0, 1)):
                for x, add in tasks:
                    if 2 * x // block == part:
                        add()
                copies.append(copy_out(out, whole, done, part, 2))
            for copy in copies:
                copy.wait()


def call(body, name, outs, ins, scratch=(), aliases=None, flops=0, hbm_out=()):
    vmem, hbm = pl.BlockSpec(memory_space=pltpu.VMEM), pl.BlockSpec(memory_space=pltpu.HBM)
    f32 = jnp.float32
    shapes = [out if isinstance(out, jax.ShapeDtypeStruct) else jax.ShapeDtypeStruct(out, f32) for out in outs]
    moved = 4 * sum(int(np.prod(shape.shape)) for shape in shapes)
    return pl.pallas_call(
        body,
        out_shape=shapes,
        in_specs=[vmem] * len(ins),
        out_specs=[hbm if n in hbm_out else vmem for n in range(len(outs))],
        scratch_shapes=[pltpu.VMEM(shape, f32) if isinstance(shape, tuple) else shape for shape in scratch],
        input_output_aliases=aliases or {},
        compiler_params=pltpu.CompilerParams(vmem_limit_bytes=VMEM_BYTES),
        cost_estimate=pl.CostEstimate(flops=flops, bytes_accessed=2 * moved, transcendentals=0),
        name=name,
    )(*ins)


def local(velocity):
    block, rows, width = velocity.shape
    around, count = lax.axis_size("gx"), lax.axis_size("gy")
    shared = count == 2 and SHARED
    places = places_of(block)
    spans = windows(block)
    total = count * rows

    others = [
        lax.ppermute(velocity, "gy", [(i, (i - k) % count) for i in range(count)])
        for k in range(1, count)
    ]
    lifted = [
        (high - low + 1, total >> level, width) for level, (low, high) in enumerate(spans)
    ]
    coarse = [
        ((high // 2 - low // 2 + 1) * (total >> (level + 1)), width)
        for level, (low, high) in enumerate(spans[:-1])
    ]
    spread = (block * rows, width)
    owned = [(block >> level, rows >> level, width) for level in range(LEVELS)]
    lengths = {to: message(block, rows, to)[2] for to in places}
    one, two = max(lengths[1], lengths[-1]), max(lengths[2], lengths[-2])
    clean = [(one, width)] * LEVELS

    square = jax.ShapeDtypeStruct((2 * width, 2 * width), jnp.bfloat16)
    weights = call(matrix_kernel, "make_matrices", [square] * 2, [], flops=FIRST_FLOPS)
    (first,) = call(
        functools.partial(own_kernel, block, rows),
        "lift_own",
        [lifted[0]],
        [velocity, weights[0]],
        [spread],
    )
    if shared:
        outs, scratch = ([(many * size, width) for size in (one, two)] for many in (2, 4))
    else:
        outs, scratch = [(lengths[to], width) for to in places], []
    values = call(
        functools.partial(message_kernel, block, rows, width, count, places),
        "make_messages",
        lifted + outs,
        [first] + others + list(weights),
        [spread] + coarse + scratch,
        {0: 0},
    )
    before, messages = values[:LEVELS], values[LEVELS:]

    def rest():
        return call(
            functools.partial(rest_kernel, block, rows, width),
            "finish_own",
            [owned[0]],
            before,
            [(block >> LEVELS - 1, total >> LEVELS - 1, width)],
        )[0]

    written = [pltpu.SemaphoreType.DMA((2,))]
    if shared:
        near, far = (
            lax.ppermute(value, ("gx", "gy"), shared_pairs(step, around))
            for step, value in enumerate(messages, 1)
        )
        result = rest()
        (packed,) = call(pack_kernel, "pack_other", [(one + two, width)], [near, far])
        packed = lax.ppermute(packed, "gy", [(0, 1), (1, 0)])
        (result,) = call(
            functools.partial(keep_kernel, block, rows),
            "add_kept",
            [owned[0]],
            [result, near, far],
            clean,
            aliases={0: 0},
        )
        whole, _ = call(
            functools.partial(swap_kernel, block, rows, one),
            "add_swapped",
            [owned[0]] * 2,
            [result, packed],
            written + clean,
            aliases={0: 1},
            hbm_out=(0,),
        )
        return whole

    sent = dict(zip(places, messages))
    received = {
        to: lax.ppermute(sent[to], "gx", [(i, (i + to) % around) for i in range(around)])
        for to in sorted(places, key=lambda to: (to < 0, abs(to)))
    }
    right = [to for to in places if to > 0]
    left = [to for to in places if to < 0]
    (result,) = call(
        functools.partial(add_kernel, block, rows, right, False),
        "add_right",
        [owned[0]],
        [rest()] + [received[to] for to in right],
        clean,
        aliases={0: 0},
        flops=FIRST_FLOPS,
    )
    whole, _ = call(
        functools.partial(add_kernel, block, rows, left, True),
        "add_left",
        [owned[0]] * 2,
        [result] + [received[to] for to in left],
        written + clean,
        aliases={0: 1},
        hbm_out=(0,),
    )
    return whole


def solution(mesh):
    return jax.shard_map(
        local, mesh=mesh, in_specs=(P("gx", "gy", None),), out_specs=P("gx", "gy", None), check_vma=False
    )
```

```python
import functools

import jax
import jax.numpy as jnp
import numpy as np
from jax import lax
from jax.experimental import pallas as pl
from jax.experimental.pallas import tpu as pltpu
from jax.sharding import PartitionSpec as P

LEVELS = 4
STEPS = (-1.586134342, -0.05298011854, 0.8829110762, 0.4435068522)
SCALE = 1.149604398
VMEM_BYTES = 24 * 2**20
FIRST_FLOPS = 10**10
SHARED = True


def windows(block):
    found = []
    first, last = 0, block - 1
    for _ in range(LEVELS):
        low = first - 4 + (first % 2)
        high = last + 4 - (last % 2)
        found.append((low, high))
        first, last = low // 2, high // 2
    return found


def message(block, rows, to):
    sent, derived = {}, {}
    spans = windows(block)
    base = ends = 0
    for level, (low, high) in enumerate(spans):
        size, height = block >> level, rows >> level
        first, last = (0, block - 1) if level == 0 else (v // 2 for v in spans[level - 1])
        planes = [p for p in range(low, high + 1) if p // size == to]
        if abs(to) == 1:
            sign = to
            edge = last + 2 - last % 2 if to > 0 else first - 2 + first % 2
            far, near = edge + sign, edge - sign
            if far in planes and edge + 2 * sign in planes:
                derived[level, edge + 2 * sign] = (far, None)
            if far in planes and near in planes:
                derived[level, edge] = (far, near)
        planes = [plane for plane in planes if (level, plane) not in derived]
        at = base
        if level == 1:
            extra = planes[-1] if len(planes) > 3 else None
        elif level > 1 and extra is not None:
            at = base + (rows >> 1)
        for plane in planes:
            if level == 1 and plane == extra:
                sent[level, plane] = base, shift_of(2)
                continue
            sent[level, plane] = at, shift_of(level)
            at += height
        ends = max(ends, at)
        if level == 0:
            base = at
    return sent, derived, -(-ends // 8) * 8


def shift_of(level):
    return (0, 0, 1, 3)[level]


def places_of(block):
    found = set()
    for level, (low, high) in enumerate(windows(block)):
        size = block >> level
        found |= set(range(low // size, high // size + 1))
    return sorted(found - {0})


def in_parts(value):
    parts = []
    for _ in range(3):
        parts.append(value.astype(jnp.bfloat16))
        value = value - parts[-1].astype(jnp.float32)
    return parts


def z_product(value, weights):
    width = value.shape[-1]
    high, middle, low = in_parts(value)

    def dot(left, right, matrix):
        both = jnp.concatenate([left, right], axis=1)
        return jnp.dot(both, matrix, preferred_element_type=jnp.float32)

    large = dot(high, middle, weights[:, : 2 * width])
    small = dot(low, high, weights[:, 2 * width :])
    return large[:, :width] + (large[:, width:] + small)


def lanes_of(width, spacing, parity):
    lane = lax.broadcasted_iota(jnp.int32, (1, width), 1)
    return lax.rem(lane, 2 * spacing) == (spacing if parity else 0)


def own_lanes(width, level, high_only):
    spacing, shift = 1 << level, shift_of(level)
    lane = lax.broadcasted_iota(jnp.int32, (1, width), 1)
    if high_only:
        return lax.rem(lane, 2 * spacing) == spacing + shift
    return lax.rem(lane, spacing) == shift


def z_lift(value, spacing):
    width = value.shape[-1]
    axis = value.ndim - 1
    for step, weight in enumerate(STEPS):
        factor = jnp.where(lanes_of(width, spacing, step % 2 == 0), weight, 0.0)
        around = pltpu.roll(value, spacing, axis) + pltpu.roll(value, width - spacing, axis)
        value = value + factor * around
    return value


def x_lift(planes):
    def plus(one, other):
        return other if one is None else one if other is None else one + other

    planes = dict(planes)
    for step, weight in enumerate(STEPS):
        parity = 1 if step % 2 == 0 else 0
        for index in range(min(planes) - 1, max(planes) + 2):
            if index % 2 == parity:
                around = plus(planes.get(index - 1), planes.get(index + 1))
                if around is not None:
                    planes[index] = plus(planes.get(index), weight * around)
    return planes


def y_lift_split(even, odd):
    count = even.shape[0]
    a, b, c, d = STEPS
    odd = odd + a * (even + pltpu.roll(even, count - 1, 0))
    even = even + b * (pltpu.roll(odd, 1, 0) + odd)
    odd = odd + c * (even + pltpu.roll(even, count - 1, 0))
    even = even + d * (pltpu.roll(odd, 1, 0) + odd)
    return even, odd


def y_lift_whole(value):
    count = value.shape[0]
    row = lax.broadcasted_iota(jnp.int32, (count, 1), 0)
    for step, weight in enumerate(STEPS):
        factor = jnp.where(lax.rem(row, 2) == (1 if step % 2 == 0 else 0), weight, 0.0)
        value = value + factor * (pltpu.roll(value, 1, 0) + pltpu.roll(value, count - 1, 0))
    return value


def scaled_z(value, spacing):
    width = value.shape[-1]
    odd, even = lanes_of(width, spacing, True), lanes_of(width, spacing, False)
    return value * jnp.where(odd, SCALE, jnp.where(even, 1 / SCALE, 0.0))


def scaled(value, x_odd, y_odd):
    at = (SCALE if x_odd else 1 / SCALE) * (SCALE if y_odd else 1 / SCALE)
    return value if x_odd != y_odd else value * at


def spread_z(source, weights, spread, rows, start, size):
    width = source.shape[-1]
    value = source[start : start + size].reshape(size * rows, width)
    spread[start * rows : (start + size) * rows, :] = z_product(value, weights[...])


def spread_x(block, rows, spread, into, low, base):
    for at in range(0, rows, 8):
        planes = {x: spread[x * rows + at : x * rows + at + 8, :] for x in range(block)}
        for x, value in x_lift(planes).items():
            into[x - low, base + at : base + at + 8, :] = value


def matrix_kernel(*weights):
    width = weights[0].shape[0] // 2
    row = lax.broadcasted_iota(jnp.int32, (width, width), 0)
    lane = lax.broadcasted_iota(jnp.int32, (width, width), 1)
    value = jnp.where(row == lane, 1.0, 0.0)
    full = [scaled_z(z_lift(value, 1), 1), jnp.zeros((width, width), jnp.float32)]
    for level in range(1, LEVELS):
        spacing = 1 << level
        value = scaled_z(z_lift(value, spacing), spacing)
        full[1] += pltpu.roll(value, shift_of(level), 1) if shift_of(level) else value
        value = jnp.where(lanes_of(width, spacing, False), value, 0.0)
    for weight, matrix in zip(weights, full):
        high, middle, low = in_parts(matrix)
        for at, column in enumerate(((high, middle), (middle, high), (high, low))):
            for row, part in enumerate(column):
                weight[row * width : (row + 1) * width, at * width : (at + 1) * width] = part


def own_kernel(block, rows, velocity, weights, into, spread):
    step = max(1, min(block, 512 // rows))
    for x in range(0, block, step):
        spread_z(velocity, weights, spread, rows, x, step)
    spread_x(block, rows, spread, into, windows(block)[0][0], 0)


def right_source(step, place, last):
    return place == last if step == 1 else (place == 0) | (place == last - 1)


def right_target(step, place):
    return (place == 0) & (step == 1)


def sends_right(step):
    core = lax.axis_index("gy") == 1
    return core == right_source(step, lax.axis_index("gx"), lax.axis_size("gx") - 1)


def takes_right(step):
    core = lax.axis_index("gy") == 1
    return core == right_target(step, lax.axis_index("gx"))


def shared_pairs(step, around):
    pairs = []
    for place in range(around):
        to, back = (place + step) % around, (place - step) % around
        source = int(right_source(step, place, around - 1))
        pairs.append((2 * place + source, 2 * to + int(right_target(step, to))))
        pairs.append((2 * place + 1 - source, 2 * back + 1 - int(right_target(step, back))))
    return pairs


def message_kernel(block, rows, width, count, places, *refs):
    refs = list(refs)

    def take(number):
        taken = refs[:number]
        del refs[:number]
        return taken

    shared = count == 2 and SHARED
    halves = 2 if shared else 1
    (_,) = take(1)
    others = take(count - 1)
    weights = take(2)
    lifted = take(LEVELS)
    passed = take(2 if shared else len(places))
    (spread,) = take(1)
    coarse = take(LEVELS - 1)
    both = take(2) if shared else []
    messages = dict(zip(places, passed))
    spans = windows(block)
    total = count * rows
    tables = {to: message(block, rows, to) for to in places}
    lengths = {to: message(block, rows, to)[2] for to in places}
    if shared:
        for step, buffer in enumerate(both, 1):
            size = buffer.shape[0] // 4
            for side, to in enumerate((step, -step)):
                lengths[to] = size
                messages[to] = buffer.at[pl.ds(2 * side * size, 2 * size)]
    written = {to: set() for to in places}

    def post(to, at, number, value):
        here = range(at, at + 2 * number, 2)
        if written[to].isdisjoint(here):
            messages[to][pl.ds(at, number, 2), :] = value
        else:
            messages[to][pl.ds(at, number, 2), :] += value
        written[to].update(here)

    def put(level, plane, half, even, odd):
        number = (rows >> level) // 2
        low = level < LEVELS - 1 and plane % 2 == 0
        if level > 0 or low:
            even = jnp.where(own_lanes(width, level, low), even, 0.0)
        if level > 0:
            odd = jnp.where(own_lanes(width, level, False), odd, 0.0)
        to = plane // (block >> level)
        at, shift = tables[to][0][level, plane]
        at += half * lengths[to]
        if shift != shift_of(level):
            even, odd = (pltpu.roll(value, shift - shift_of(level), 1) for value in (even, odd))
        post(to, at, number, even)
        post(to, at + 1, number, odd)

    for level in range(LEVELS):
        low, high = spans[level]
        height = total >> level
        half, mine = height // 2, (rows >> level) // 2
        into = lifted[level]

        if level == 0:
            for part, source in enumerate(others):
                step = min(block, max(1, 512 // rows))
                for x in range(0, block, step):
                    spread_z(source, weights[0], spread, rows, x, step)
                spread_x(block, rows, spread, into, low, (part + 1) * rows)
        else:
            start, stop = spans[level - 1][0] // 2, spans[level - 1][1] // 2 + 1
            source = coarse[level - 1]
            if level == 1:
                size = (stop - start) * height
                for at in range(0, size, 512):
                    end = min(size, at + 512)
                    source[at:end, :] = z_product(source[at:end, :], weights[level][...])
            for at in range(0, height, 8):
                planes = {}
                for x in range(start, stop):
                    row = (x - start) * height + at
                    planes[x] = source[row : row + 8, :]
                for x, value in x_lift(planes).items():
                    into[x - low, at : at + 8, :] = value

        for plane in range(low, high + 1):
            odd_plane = plane % 2 == 1
            to = plane // (block >> level)
            goes_on = level < LEVELS - 1 and not odd_plane
            sends = to != 0 and (level, plane) in tables[to][0]
            if not goes_on and not sends:
                continue
            at = plane - low
            split = half % 8 == 0
            if split:
                even, odd = y_lift_split(
                    into[at, pl.ds(0, half, 2), :], into[at, pl.ds(1, half, 2), :]
                )
                even = scaled(even, odd_plane, False)
            else:
                into[at] = y_lift_whole(into[at])
                even = scaled(into[at, pl.ds(0, half, 2), :], odd_plane, False)
            if goes_on:
                row = ((plane - low) // 2) * half
                coarse[level][row : row + half, :] = even
            if not sends:
                continue
            for part in range(halves):
                if split:
                    here_even = even[part * mine : (part + 1) * mine]
                    here_odd = odd[part * mine : (part + 1) * mine]
                else:
                    here_even = into[at, pl.ds(2 * part * mine, mine, 2), :]
                    here_even = scaled(here_even, odd_plane, False)
                    here_odd = into[at, pl.ds(2 * part * mine + 1, mine, 2), :]
                put(level, plane, part, here_even, scaled(here_odd, odd_plane, True))

    for to in places:
        for row in range(halves * lengths[to]):
            if row not in written[to]:
                messages[to][row : row + 1, :] = jnp.zeros((1, width), jnp.float32)
    if shared:
        core = lax.axis_index("gy")
        for step, (target, buffer) in enumerate(zip(passed, both), 1):
            size = lengths[step]
            side = jnp.where(sends_right(step), 0, 2 * size)
            for half in range(2):
                here = side + (core if half == 0 else 1 - core) * size
                target[half * size : (half + 1) * size, :] = buffer[pl.ds(pl.multiple_of(here, 8), size), :]


def rest_kernel(block, rows, width, *refs):
    lifted, out, spare = refs[:LEVELS], refs[LEVELS], refs[LEVELS + 1]
    for level, (low, _) in enumerate(windows(block)):
        into, spacing, shift = lifted[level], 1 << level, shift_of(level)
        half, mine = into.shape[1] // 2, (rows >> level) // 2
        for plane in range(block >> level):
            odd_plane = plane % 2 == 1
            at = plane - low
            if half % 8 == 0:
                even, odd = y_lift_split(
                    into[at, pl.ds(0, half, 2), :], into[at, pl.ds(1, half, 2), :]
                )
                even, odd = even[:mine], odd[:mine]
            else:
                spare[plane] = y_lift_whole(into[at])
                even, odd = spare[plane, pl.ds(0, mine, 2), :], spare[plane, pl.ds(1, mine, 2), :]
            even, odd = scaled(even, odd_plane, False), scaled(odd, odd_plane, True)
            further = level < LEVELS - 1 and not odd_plane
            if level > 0 or further:
                even = jnp.where(own_lanes(width, level, further), even, 0.0)
            x = plane * spacing
            if level == 0:
                out[x, pl.ds(0, mine, 2), :] = even
                out[x, pl.ds(1, mine, 2), :] = odd
                continue
            odd = jnp.where(own_lanes(width, level, False), odd, 0.0)
            if shift:
                even, odd = (pltpu.roll(value, width - shift, 1) for value in (even, odd))
            out[x, pl.ds(0, mine, 2 * spacing), :] += even
            out[x, pl.ds(spacing, mine, 2 * spacing), :] += odd


def additions(block, rows, to, arrived, base, out, clean):
    sent, derived, _ = message(block, rows, to)
    a, b, c, d = STEPS
    width = out.shape[-1]
    lane = lax.broadcasted_iota(jnp.int32, (1, width), 1)
    found_here = []
    for level in sorted({level for level, _ in sent}):
        spacing, height = 1 << level, rows >> level
        shape = (height, width)
        held = {}
        for shift in sorted({shift for (found, _), (_, shift) in sent.items() if found == level}):
            here = {
                plane: at for (found, plane), (at, by) in sent.items() if (found, by) == (level, shift)
            }
            start, stop = min(here.values()), -(-(max(here.values()) + height) // 8) * 8
            source, offset = arrived, base
            if level > 0:
                value = arrived[base + start : base + stop, :]
                if shift:
                    value = pltpu.roll(value, width - shift, 1)
                source, offset = clean[level if shift == shift_of(level) else 0], -start
                source[: stop - start, :] = jnp.where(lax.rem(lane, spacing) == 0, value, 0.0)
            held |= {plane: (source, at + offset) for plane, at in here.items()}

        def read(plane, held=held, height=height):
            source, at = held[plane]
            return source[at : at + height, :]

        def derive(far, near, read=read, shape=shape, spacing=spacing):
            if near is None:
                value = (d / SCALE**2) * read(far)
            else:
                value = ((1 / c + d) / SCALE**2) * read(far) + (d / SCALE**2) * read(near)
            row = lax.broadcasted_iota(jnp.int32, shape, 0)
            keep = (lax.rem(row, 2) == 1) | lanes_of(width, spacing, True)
            return jnp.where(keep, value, 0.0)

        values = {plane: functools.partial(read, plane) for plane in held}
        for (found, plane), (far, near) in derived.items():
            if found == level:
                values[plane] = functools.partial(derive, far, near)
        for plane, value in values.items():
            x = (plane - to * (block >> level)) * spacing

            def add(x=x, height=height, spacing=spacing, value=value):
                out[x, pl.ds(0, height, spacing), :] += value()

            found_here.append((x, add))
    return found_here


def add_message(*args):
    for _, add in additions(*args):
        add()


def copy_out(out, whole, done, part, parts):
    size = out.shape[0] // parts
    here = pl.ds(part * size, size)
    copy = pltpu.make_async_copy(out.at[here], whole.at[here], done.at[part])
    copy.start()
    return copy


def add_kernel(block, rows, places, last, _, *refs):
    received, refs = refs[: len(places)], refs[len(places) :]
    if last:
        whole, out, done, *clean = refs
    else:
        out, *clean = refs
    for to, arrived in zip(places, received):
        add_message(block, rows, to, arrived, 0, out, clean)
    if last:
        for copy in [copy_out(out, whole, done, part, 2) for part in range(2)]:
            copy.wait()


def add_far(block, rows, right, arrived, base, out, clean):
    width, level = out.shape[-1], LEVELS - 1
    spacing, height, shift = 1 << level, rows >> level, shift_of(level)
    length = max(message(block, rows, to)[2] for to in (2, -2))
    lane = lax.broadcasted_iota(jnp.int32, (1, width), 1)
    value = pltpu.roll(arrived[base : base + length, :], width - shift, 1)
    value = jnp.where(lax.rem(lane, spacing) == 0, value, 0.0)
    for to, here in ((2, right), (-2, jnp.logical_not(right))):
        source = clean[0 if to > 0 else level]
        source[:length, :] = jnp.where(here, value, 0.0)
        for (found, plane), (at, _) in message(block, rows, to)[0].items():
            x = (plane - to * (block >> level)) * spacing
            out[x, pl.ds(0, height, spacing), :] += source[at : at + height, :]


def add_either(block, rows, right, step, arrived, base, out, clean):
    for side, here in ((step, right), (-step, jnp.logical_not(right))):

        @pl.when(here)
        def _():
            add_message(block, rows, side, arrived, base, out, clean)


def keep_kernel(block, rows, _, near, far, out, *clean):
    core = lax.axis_index("gy")
    add_either(block, rows, takes_right(1), 1, half_of(near, core), 0, out, clean)
    add_far(block, rows, takes_right(2), half_of(far, core), 0, out, clean)


def half_of(arrived, core):
    size = arrived.shape[0] // 2
    return arrived.at[pl.ds(pl.multiple_of(core * size, 8), size)]


def pack_kernel(near, far, packed):
    one = near.shape[0] // 2
    other = 1 - lax.axis_index("gy")
    packed[:one, :] = half_of(near, other)[...]
    packed[one:, :] = half_of(far, other)[...]


def swap_kernel(block, rows, one, own, packed, whole, out, done, *clean):
    add_far(block, rows, jnp.logical_not(takes_right(2)), packed, one, out, clean)
    right = jnp.logical_not(takes_right(1))
    for to, here in ((1, right), (-1, jnp.logical_not(right))):

        @pl.when(here)
        def _():
            tasks = additions(block, rows, to, packed, 0, out, clean)
            copies = []
            for part in ((1, 0) if to > 0 else (0, 1)):
                for x, add in tasks:
                    if 2 * x // block == part:
                        add()
                copies.append(copy_out(out, whole, done, part, 2))
            for copy in copies:
                copy.wait()


def call(body, name, outs, ins, scratch=(), aliases=None, flops=0, hbm_out=()):
    vmem, hbm = pl.BlockSpec(memory_space=pltpu.VMEM), pl.BlockSpec(memory_space=pltpu.HBM)
    f32 = jnp.float32
    shapes = [out if isinstance(out, jax.ShapeDtypeStruct) else jax.ShapeDtypeStruct(out, f32) for out in outs]
    moved = 4 * sum(int(np.prod(shape.shape)) for shape in shapes)
    return pl.pallas_call(
        body,
        out_shape=shapes,
        in_specs=[vmem] * len(ins),
        out_specs=[hbm if n in hbm_out else vmem for n in range(len(outs))],
        scratch_shapes=[pltpu.VMEM(shape, f32) if isinstance(shape, tuple) else shape for shape in scratch],
        input_output_aliases=aliases or {},
        compiler_params=pltpu.CompilerParams(vmem_limit_bytes=VMEM_BYTES),
        cost_estimate=pl.CostEstimate(flops=flops, bytes_accessed=2 * moved, transcendentals=0),
        name=name,
    )(*ins)


def local(velocity):
    block, rows, width = velocity.shape
    around, count = lax.axis_size("gx"), lax.axis_size("gy")
    shared = count == 2 and SHARED
    places = places_of(block)
    spans = windows(block)
    total = count * rows

    others = [
        lax.ppermute(velocity, "gy", [(i, (i - k) % count) for i in range(count)])
        for k in range(1, count)
    ]
    lifted = [
        (high - low + 1, total >> level, width) for level, (low, high) in enumerate(spans)
    ]
    coarse = [
        ((high // 2 - low // 2 + 1) * (total >> (level + 1)), width)
        for level, (low, high) in enumerate(spans[:-1])
    ]
    spread = (block * rows, width)
    owned = [(block >> level, rows >> level, width) for level in range(LEVELS)]
    lengths = {to: message(block, rows, to)[2] for to in places}
    one, two = max(lengths[1], lengths[-1]), max(lengths[2], lengths[-2])
    clean = [(one, width)] * LEVELS

    square = jax.ShapeDtypeStruct((2 * width, 3 * width), jnp.bfloat16)
    weights = call(matrix_kernel, "make_matrices", [square] * 2, [], flops=FIRST_FLOPS)
    (first,) = call(
        functools.partial(own_kernel, block, rows),
        "lift_own",
        [lifted[0]],
        [velocity, weights[0]],
        [spread],
    )
    if shared:
        outs, scratch = ([(many * size, width) for size in (one, two)] for many in (2, 4))
    else:
        outs, scratch = [(lengths[to], width) for to in places], []
    values = call(
        functools.partial(message_kernel, block, rows, width, count, places),
        "make_messages",
        lifted + outs,
        [first] + others + list(weights),
        [spread] + coarse + scratch,
        {0: 0},
    )
    before, messages = values[:LEVELS], values[LEVELS:]

    def rest():
        return call(
            functools.partial(rest_kernel, block, rows, width),
            "finish_own",
            [owned[0]],
            before,
            [(block >> LEVELS - 1, total >> LEVELS - 1, width)],
        )[0]

    written = [pltpu.SemaphoreType.DMA((2,))]
    if shared:
        near, far = (
            lax.ppermute(value, ("gx", "gy"), shared_pairs(step, around))
            for step, value in enumerate(messages, 1)
        )
        result = rest()
        (packed,) = call(pack_kernel, "pack_other", [(one + two, width)], [near, far])
        packed = lax.ppermute(packed, "gy", [(0, 1), (1, 0)])
        (result,) = call(
            functools.partial(keep_kernel, block, rows),
            "add_kept",
            [owned[0]],
            [result, near, far],
            clean,
            aliases={0: 0},
        )
        whole, _ = call(
            functools.partial(swap_kernel, block, rows, one),
            "add_swapped",
            [owned[0]] * 2,
            [result, packed],
            written + clean,
            aliases={0: 1},
            hbm_out=(0,),
        )
        return whole

    sent = dict(zip(places, messages))
    received = {
        to: lax.ppermute(sent[to], "gx", [(i, (i + to) % around) for i in range(around)])
        for to in sorted(places, key=lambda to: (to < 0, abs(to)))
    }
    right = [to for to in places if to > 0]
    left = [to for to in places if to < 0]
    (result,) = call(
        functools.partial(add_kernel, block, rows, right, False),
        "add_right",
        [owned[0]],
        [rest()] + [received[to] for to in right],
        clean,
        aliases={0: 0},
        flops=FIRST_FLOPS,
    )
    whole, _ = call(
        functools.partial(add_kernel, block, rows, left, True),
        "add_left",
        [owned[0]] * 2,
        [result] + [received[to] for to in left],
        written + clean,
        aliases={0: 1},
        hbm_out=(0,),
    )
    return whole


def solution(mesh):
    return jax.shard_map(
        local, mesh=mesh, in_specs=(P("gx", "gy", None),), out_specs=P("gx", "gy", None), check_vma=False
    )
```

```python
import functools

import jax
import jax.numpy as jnp
import numpy as np
from jax import lax
from jax.experimental import pallas as pl
from jax.experimental.pallas import tpu as pltpu
from jax.sharding import PartitionSpec as P

LEVELS = 4
STEPS = (-1.586134342, -0.05298011854, 0.8829110762, 0.4435068522)
SCALE = 1.149604398
VMEM_BYTES = 24 * 2**20
FIRST_FLOPS = 10**10
PIECE = 1024
SHARED = True


def windows(block):
    found = []
    first, last = 0, block - 1
    for _ in range(LEVELS):
        low = first - 4 + (first % 2)
        high = last + 4 - (last % 2)
        found.append((low, high))
        first, last = low // 2, high // 2
    return found


def message(block, rows, to):
    sent, derived = {}, {}
    spans = windows(block)
    base = ends = 0
    for level, (low, high) in enumerate(spans):
        size, height = block >> level, rows >> level
        first, last = (0, block - 1) if level == 0 else (v // 2 for v in spans[level - 1])
        planes = [p for p in range(low, high + 1) if p // size == to]
        if abs(to) == 1:
            sign = to
            edge = last + 2 - last % 2 if to > 0 else first - 2 + first % 2
            far, near = edge + sign, edge - sign
            if far in planes and edge + 2 * sign in planes:
                derived[level, edge + 2 * sign] = (far, None)
            if far in planes and near in planes:
                derived[level, edge] = (far, near)
        planes = [plane for plane in planes if (level, plane) not in derived]
        at = base
        if level == 1:
            extra = planes[-1] if len(planes) > 3 else None
        elif level > 1 and extra is not None:
            at = base + (rows >> 1)
        for plane in planes:
            if level == 1 and plane == extra:
                sent[level, plane] = base, shift_of(2)
                continue
            sent[level, plane] = at, shift_of(level)
            at += height
        ends = max(ends, at)
        if level == 0:
            base = at
    return sent, derived, -(-ends // 8) * 8


def shift_of(level):
    return (0, 0, 1, 3)[level]


def places_of(block):
    found = set()
    for level, (low, high) in enumerate(windows(block)):
        size = block >> level
        found |= set(range(low // size, high // size + 1))
    return sorted(found - {0})


def in_parts(value):
    parts = []
    for _ in range(3):
        parts.append(value.astype(jnp.bfloat16))
        value = value - parts[-1].astype(jnp.float32)
    return parts


def z_product(value, weights):
    width = value.shape[-1]
    high, middle, low = in_parts(value)

    def dot(left, right, matrix):
        both = jnp.concatenate([left, right], axis=1)
        return jnp.dot(both, matrix, preferred_element_type=jnp.float32)

    large = dot(high, middle, weights[:, : 2 * width])
    small = dot(low, high, weights[:, 2 * width :])
    return large[:, :width] + (large[:, width:] + small)


def lanes_of(width, spacing, parity):
    lane = lax.broadcasted_iota(jnp.int32, (1, width), 1)
    return lax.rem(lane, 2 * spacing) == (spacing if parity else 0)


def own_lanes(width, level, high_only):
    spacing, shift = 1 << level, shift_of(level)
    lane = lax.broadcasted_iota(jnp.int32, (1, width), 1)
    if high_only:
        return lax.rem(lane, 2 * spacing) == spacing + shift
    return lax.rem(lane, spacing) == shift


def z_lift(value, spacing):
    width = value.shape[-1]
    axis = value.ndim - 1
    for step, weight in enumerate(STEPS):
        factor = jnp.where(lanes_of(width, spacing, step % 2 == 0), weight, 0.0)
        around = pltpu.roll(value, spacing, axis) + pltpu.roll(value, width - spacing, axis)
        value = value + factor * around
    return value


def x_lift(planes):
    def plus(one, other):
        return other if one is None else one if other is None else one + other

    planes = dict(planes)
    for step, weight in enumerate(STEPS):
        parity = 1 if step % 2 == 0 else 0
        for index in range(min(planes) - 1, max(planes) + 2):
            if index % 2 == parity:
                around = plus(planes.get(index - 1), planes.get(index + 1))
                if around is not None:
                    planes[index] = plus(planes.get(index), weight * around)
    return planes


def y_lift_split(even, odd):
    count = even.shape[0]
    a, b, c, d = STEPS
    odd = odd + a * (even + pltpu.roll(even, count - 1, 0))
    even = even + b * (pltpu.roll(odd, 1, 0) + odd)
    odd = odd + c * (even + pltpu.roll(even, count - 1, 0))
    even = even + d * (pltpu.roll(odd, 1, 0) + odd)
    return even, odd


def y_lift_whole(value):
    count = value.shape[0]
    row = lax.broadcasted_iota(jnp.int32, (count, 1), 0)
    for step, weight in enumerate(STEPS):
        factor = jnp.where(lax.rem(row, 2) == (1 if step % 2 == 0 else 0), weight, 0.0)
        value = value + factor * (pltpu.roll(value, 1, 0) + pltpu.roll(value, count - 1, 0))
    return value


def scaled_z(value, spacing):
    width = value.shape[-1]
    odd, even = lanes_of(width, spacing, True), lanes_of(width, spacing, False)
    return value * jnp.where(odd, SCALE, jnp.where(even, 1 / SCALE, 0.0))


def scaled(value, x_odd, y_odd):
    at = (SCALE if x_odd else 1 / SCALE) * (SCALE if y_odd else 1 / SCALE)
    return value if x_odd != y_odd else value * at


def spread_z(source, weights, spread, rows, start, size):
    width = source.shape[-1]
    value = source[start : start + size].reshape(size * rows, width)
    spread[start * rows : (start + size) * rows, :] = z_product(value, weights[...])


def spread_x(block, rows, spread, into, low, base):
    for at in range(0, rows, 8):
        planes = {x: spread[x * rows + at : x * rows + at + 8, :] for x in range(block)}
        for x, value in x_lift(planes).items():
            into[x - low, base + at : base + at + 8, :] = value


def matrix_kernel(*weights):
    width = weights[0].shape[0] // 2
    row = lax.broadcasted_iota(jnp.int32, (width, width), 0)
    lane = lax.broadcasted_iota(jnp.int32, (width, width), 1)
    value = jnp.where(row == lane, 1.0, 0.0)
    full = [scaled_z(z_lift(value, 1), 1), jnp.zeros((width, width), jnp.float32)]
    for level in range(1, LEVELS):
        spacing = 1 << level
        value = scaled_z(z_lift(value, spacing), spacing)
        full[1] += pltpu.roll(value, shift_of(level), 1) if shift_of(level) else value
        value = jnp.where(lanes_of(width, spacing, False), value, 0.0)
    for weight, matrix in zip(weights, full):
        high, middle, low = in_parts(matrix)
        for at, column in enumerate(((high, middle), (middle, high), (high, low))):
            for row, part in enumerate(column):
                weight[row * width : (row + 1) * width, at * width : (at + 1) * width] = part


def own_kernel(block, rows, velocity, weights, into, spread):
    step = max(1, min(block, PIECE // rows))
    for x in range(0, block, step):
        spread_z(velocity, weights, spread, rows, x, step)
    spread_x(block, rows, spread, into, windows(block)[0][0], 0)


def right_source(step, place, last):
    return place == last if step == 1 else (place == 0) | (place == last - 1)


def right_target(step, place):
    return (place == 0) & (step == 1)


def sends_right(step):
    core = lax.axis_index("gy") == 1
    return core == right_source(step, lax.axis_index("gx"), lax.axis_size("gx") - 1)


def takes_right(step):
    core = lax.axis_index("gy") == 1
    return core == right_target(step, lax.axis_index("gx"))


def shared_pairs(step, around):
    pairs = []
    for place in range(around):
        to, back = (place + step) % around, (place - step) % around
        source = int(right_source(step, place, around - 1))
        pairs.append((2 * place + source, 2 * to + int(right_target(step, to))))
        pairs.append((2 * place + 1 - source, 2 * back + 1 - int(right_target(step, back))))
    return pairs


def message_kernel(block, rows, width, count, places, *refs):
    refs = list(refs)

    def take(number):
        taken = refs[:number]
        del refs[:number]
        return taken

    shared = count == 2 and SHARED
    halves = 2 if shared else 1
    (_,) = take(1)
    others = take(count - 1)
    weights = take(2)
    lifted = take(LEVELS)
    passed = take(2 if shared else len(places))
    (spread,) = take(1)
    coarse = take(LEVELS - 1)
    both = take(2) if shared else []
    messages = dict(zip(places, passed))
    spans = windows(block)
    total = count * rows
    tables = {to: message(block, rows, to) for to in places}
    lengths = {to: message(block, rows, to)[2] for to in places}
    if shared:
        for step, buffer in enumerate(both, 1):
            size = buffer.shape[0] // 4
            for side, to in enumerate((step, -step)):
                lengths[to] = size
                messages[to] = buffer.at[pl.ds(2 * side * size, 2 * size)]
    written = {to: set() for to in places}

    def post(to, at, number, value):
        here = range(at, at + 2 * number, 2)
        if written[to].isdisjoint(here):
            messages[to][pl.ds(at, number, 2), :] = value
        else:
            messages[to][pl.ds(at, number, 2), :] += value
        written[to].update(here)

    def put(level, plane, half, even, odd):
        number = (rows >> level) // 2
        low = level < LEVELS - 1 and plane % 2 == 0
        if level > 0 or low:
            even = jnp.where(own_lanes(width, level, low), even, 0.0)
        if level > 0:
            odd = jnp.where(own_lanes(width, level, False), odd, 0.0)
        to = plane // (block >> level)
        at, shift = tables[to][0][level, plane]
        at += half * lengths[to]
        if shift != shift_of(level):
            even, odd = (pltpu.roll(value, shift - shift_of(level), 1) for value in (even, odd))
        post(to, at, number, even)
        post(to, at + 1, number, odd)

    for level in range(LEVELS):
        low, high = spans[level]
        height = total >> level
        half, mine = height // 2, (rows >> level) // 2
        into = lifted[level]

        if level == 0:
            for part, source in enumerate(others):
                step = min(block, max(1, PIECE // rows))
                for x in range(0, block, step):
                    spread_z(source, weights[0], spread, rows, x, step)
                spread_x(block, rows, spread, into, low, (part + 1) * rows)
        else:
            start, stop = spans[level - 1][0] // 2, spans[level - 1][1] // 2 + 1
            source = coarse[level - 1]
            if level == 1:
                size = (stop - start) * height
                for at in range(0, size, PIECE):
                    end = min(size, at + PIECE)
                    source[at:end, :] = z_product(source[at:end, :], weights[level][...])
            for at in range(0, height, 8):
                planes = {}
                for x in range(start, stop):
                    row = (x - start) * height + at
                    planes[x] = source[row : row + 8, :]
                for x, value in x_lift(planes).items():
                    into[x - low, at : at + 8, :] = value

        for plane in range(low, high + 1):
            odd_plane = plane % 2 == 1
            to = plane // (block >> level)
            goes_on = level < LEVELS - 1 and not odd_plane
            sends = to != 0 and (level, plane) in tables[to][0]
            if not goes_on and not sends:
                continue
            at = plane - low
            split = half % 8 == 0
            if split:
                even, odd = y_lift_split(
                    into[at, pl.ds(0, half, 2), :], into[at, pl.ds(1, half, 2), :]
                )
                even = scaled(even, odd_plane, False)
            else:
                into[at] = y_lift_whole(into[at])
                even = scaled(into[at, pl.ds(0, half, 2), :], odd_plane, False)
            if goes_on:
                row = ((plane - low) // 2) * half
                coarse[level][row : row + half, :] = even
            if not sends:
                continue
            for part in range(halves):
                if split:
                    here_even = even[part * mine : (part + 1) * mine]
                    here_odd = odd[part * mine : (part + 1) * mine]
                else:
                    here_even = into[at, pl.ds(2 * part * mine, mine, 2), :]
                    here_even = scaled(here_even, odd_plane, False)
                    here_odd = into[at, pl.ds(2 * part * mine + 1, mine, 2), :]
                put(level, plane, part, here_even, scaled(here_odd, odd_plane, True))

    for to in places:
        for row in range(halves * lengths[to]):
            if row not in written[to]:
                messages[to][row : row + 1, :] = jnp.zeros((1, width), jnp.float32)
    if shared:
        core = lax.axis_index("gy")
        for step, (target, buffer) in enumerate(zip(passed, both), 1):
            size = lengths[step]
            side = jnp.where(sends_right(step), 0, 2 * size)
            for half in range(2):
                here = side + (core if half == 0 else 1 - core) * size
                target[half * size : (half + 1) * size, :] = buffer[pl.ds(pl.multiple_of(here, 8), size), :]


def rest_kernel(block, rows, width, *refs):
    lifted, out, spare = refs[:LEVELS], refs[LEVELS], refs[LEVELS + 1]
    for level, (low, _) in enumerate(windows(block)):
        into, spacing, shift = lifted[level], 1 << level, shift_of(level)
        half, mine = into.shape[1] // 2, (rows >> level) // 2
        for plane in range(block >> level):
            odd_plane = plane % 2 == 1
            at = plane - low
            if half % 8 == 0:
                even, odd = y_lift_split(
                    into[at, pl.ds(0, half, 2), :], into[at, pl.ds(1, half, 2), :]
                )
                even, odd = even[:mine], odd[:mine]
            else:
                spare[plane] = y_lift_whole(into[at])
                even, odd = spare[plane, pl.ds(0, mine, 2), :], spare[plane, pl.ds(1, mine, 2), :]
            even, odd = scaled(even, odd_plane, False), scaled(odd, odd_plane, True)
            further = level < LEVELS - 1 and not odd_plane
            if level > 0 or further:
                even = jnp.where(own_lanes(width, level, further), even, 0.0)
            x = plane * spacing
            if level == 0:
                out[x, pl.ds(0, mine, 2), :] = even
                out[x, pl.ds(1, mine, 2), :] = odd
                continue
            odd = jnp.where(own_lanes(width, level, False), odd, 0.0)
            if shift:
                even, odd = (pltpu.roll(value, width - shift, 1) for value in (even, odd))
            out[x, pl.ds(0, mine, 2 * spacing), :] += even
            out[x, pl.ds(spacing, mine, 2 * spacing), :] += odd


def additions(block, rows, to, arrived, base, out, clean):
    sent, derived, _ = message(block, rows, to)
    a, b, c, d = STEPS
    width = out.shape[-1]
    lane = lax.broadcasted_iota(jnp.int32, (1, width), 1)
    found_here = []
    for level in sorted({level for level, _ in sent}):
        spacing, height = 1 << level, rows >> level
        shape = (height, width)
        held = {}
        for shift in sorted({shift for (found, _), (_, shift) in sent.items() if found == level}):
            here = {
                plane: at for (found, plane), (at, by) in sent.items() if (found, by) == (level, shift)
            }
            start, stop = min(here.values()), -(-(max(here.values()) + height) // 8) * 8
            source, offset = arrived, base
            if level > 0:
                value = arrived[base + start : base + stop, :]
                if shift:
                    value = pltpu.roll(value, width - shift, 1)
                source, offset = clean[level if shift == shift_of(level) else 0], -start
                source[: stop - start, :] = jnp.where(lax.rem(lane, spacing) == 0, value, 0.0)
            held |= {plane: (source, at + offset) for plane, at in here.items()}

        def read(plane, held=held, height=height):
            source, at = held[plane]
            return source[at : at + height, :]

        def derive(far, near, read=read, shape=shape, spacing=spacing):
            if near is None:
                value = (d / SCALE**2) * read(far)
            else:
                value = ((1 / c + d) / SCALE**2) * read(far) + (d / SCALE**2) * read(near)
            row = lax.broadcasted_iota(jnp.int32, shape, 0)
            keep = (lax.rem(row, 2) == 1) | lanes_of(width, spacing, True)
            return jnp.where(keep, value, 0.0)

        values = {plane: functools.partial(read, plane) for plane in held}
        for (found, plane), (far, near) in derived.items():
            if found == level:
                values[plane] = functools.partial(derive, far, near)
        for plane, value in values.items():
            x = (plane - to * (block >> level)) * spacing

            def add(x=x, height=height, spacing=spacing, value=value):
                out[x, pl.ds(0, height, spacing), :] += value()

            found_here.append((x, add))
    return found_here


def add_message(*args):
    for _, add in additions(*args):
        add()


def copy_out(out, whole, done, part, parts):
    size = out.shape[0] // parts
    here = pl.ds(part * size, size)
    copy = pltpu.make_async_copy(out.at[here], whole.at[here], done.at[part])
    copy.start()
    return copy


def add_kernel(block, rows, places, last, _, *refs):
    received, refs = refs[: len(places)], refs[len(places) :]
    if last:
        whole, out, done, *clean = refs
    else:
        out, *clean = refs
    for to, arrived in zip(places, received):
        add_message(block, rows, to, arrived, 0, out, clean)
    if last:
        for copy in [copy_out(out, whole, done, part, 2) for part in range(2)]:
            copy.wait()


def add_far(block, rows, right, arrived, base, out, clean):
    width, level = out.shape[-1], LEVELS - 1
    spacing, height, shift = 1 << level, rows >> level, shift_of(level)
    length = max(message(block, rows, to)[2] for to in (2, -2))
    lane = lax.broadcasted_iota(jnp.int32, (1, width), 1)
    value = pltpu.roll(arrived[base : base + length, :], width - shift, 1)
    value = jnp.where(lax.rem(lane, spacing) == 0, value, 0.0)
    for to, here in ((2, right), (-2, jnp.logical_not(right))):
        source = clean[0 if to > 0 else level]
        source[:length, :] = jnp.where(here, value, 0.0)
        for (found, plane), (at, _) in message(block, rows, to)[0].items():
            x = (plane - to * (block >> level)) * spacing
            out[x, pl.ds(0, height, spacing), :] += source[at : at + height, :]


def add_either(block, rows, right, step, arrived, base, out, clean):
    for side, here in ((step, right), (-step, jnp.logical_not(right))):

        @pl.when(here)
        def _():
            add_message(block, rows, side, arrived, base, out, clean)


def keep_kernel(block, rows, _, near, far, out, *clean):
    core = lax.axis_index("gy")
    add_either(block, rows, takes_right(1), 1, half_of(near, core), 0, out, clean)
    add_far(block, rows, takes_right(2), half_of(far, core), 0, out, clean)


def half_of(arrived, core):
    size = arrived.shape[0] // 2
    return arrived.at[pl.ds(pl.multiple_of(core * size, 8), size)]


def pack_kernel(near, far, packed):
    one = near.shape[0] // 2
    other = 1 - lax.axis_index("gy")
    packed[:one, :] = half_of(near, other)[...]
    packed[one:, :] = half_of(far, other)[...]


def swap_kernel(block, rows, one, own, packed, whole, out, done, *clean):
    add_far(block, rows, jnp.logical_not(takes_right(2)), packed, one, out, clean)
    right = jnp.logical_not(takes_right(1))
    for to, here in ((1, right), (-1, jnp.logical_not(right))):

        @pl.when(here)
        def _():
            tasks = additions(block, rows, to, packed, 0, out, clean)
            copies = []
            for part in ((1, 0) if to > 0 else (0, 1)):
                for x, add in tasks:
                    if 2 * x // block == part:
                        add()
                copies.append(copy_out(out, whole, done, part, 2))
            for copy in copies:
                copy.wait()


def call(body, name, outs, ins, scratch=(), aliases=None, flops=0, hbm_out=()):
    vmem, hbm = pl.BlockSpec(memory_space=pltpu.VMEM), pl.BlockSpec(memory_space=pltpu.HBM)
    f32 = jnp.float32
    shapes = [out if isinstance(out, jax.ShapeDtypeStruct) else jax.ShapeDtypeStruct(out, f32) for out in outs]
    moved = 4 * sum(int(np.prod(shape.shape)) for shape in shapes)
    return pl.pallas_call(
        body,
        out_shape=shapes,
        in_specs=[vmem] * len(ins),
        out_specs=[hbm if n in hbm_out else vmem for n in range(len(outs))],
        scratch_shapes=[pltpu.VMEM(shape, f32) if isinstance(shape, tuple) else shape for shape in scratch],
        input_output_aliases=aliases or {},
        compiler_params=pltpu.CompilerParams(vmem_limit_bytes=VMEM_BYTES),
        cost_estimate=pl.CostEstimate(flops=flops, bytes_accessed=2 * moved, transcendentals=0),
        name=name,
    )(*ins)


def local(velocity):
    block, rows, width = velocity.shape
    around, count = lax.axis_size("gx"), lax.axis_size("gy")
    shared = count == 2 and SHARED
    places = places_of(block)
    spans = windows(block)
    total = count * rows

    others = [
        lax.ppermute(velocity, "gy", [(i, (i - k) % count) for i in range(count)])
        for k in range(1, count)
    ]
    lifted = [
        (high - low + 1, total >> level, width) for level, (low, high) in enumerate(spans)
    ]
    coarse = [
        ((high // 2 - low // 2 + 1) * (total >> (level + 1)), width)
        for level, (low, high) in enumerate(spans[:-1])
    ]
    spread = (block * rows, width)
    owned = [(block >> level, rows >> level, width) for level in range(LEVELS)]
    lengths = {to: message(block, rows, to)[2] for to in places}
    one, two = max(lengths[1], lengths[-1]), max(lengths[2], lengths[-2])
    clean = [(one, width)] * LEVELS

    square = jax.ShapeDtypeStruct((2 * width, 3 * width), jnp.bfloat16)
    weights = call(matrix_kernel, "make_matrices", [square] * 2, [], flops=FIRST_FLOPS)
    (first,) = call(
        functools.partial(own_kernel, block, rows),
        "lift_own",
        [lifted[0]],
        [velocity, weights[0]],
        [spread],
    )
    if shared:
        outs, scratch = ([(many * size, width) for size in (one, two)] for many in (2, 4))
    else:
        outs, scratch = [(lengths[to], width) for to in places], []
    values = call(
        functools.partial(message_kernel, block, rows, width, count, places),
        "make_messages",
        lifted + outs,
        [first] + others + list(weights),
        [spread] + coarse + scratch,
        {0: 0},
    )
    before, messages = values[:LEVELS], values[LEVELS:]

    def rest():
        return call(
            functools.partial(rest_kernel, block, rows, width),
            "finish_own",
            [owned[0]],
            before,
            [(block >> LEVELS - 1, total >> LEVELS - 1, width)],
        )[0]

    written = [pltpu.SemaphoreType.DMA((2,))]
    if shared:
        near, far = (
            lax.ppermute(value, ("gx", "gy"), shared_pairs(step, around))
            for step, value in enumerate(messages, 1)
        )
        result = rest()
        (packed,) = call(pack_kernel, "pack_other", [(one + two, width)], [near, far])
        packed = lax.ppermute(packed, "gy", [(0, 1), (1, 0)])
        (result,) = call(
            functools.partial(keep_kernel, block, rows),
            "add_kept",
            [owned[0]],
            [result, near, far],
            clean,
            aliases={0: 0},
        )
        whole, _ = call(
            functools.partial(swap_kernel, block, rows, one),
            "add_swapped",
            [owned[0]] * 2,
            [result, packed],
            written + clean,
            aliases={0: 1},
            hbm_out=(0,),
        )
        return whole

    sent = dict(zip(places, messages))
    received = {
        to: lax.ppermute(sent[to], "gx", [(i, (i + to) % around) for i in range(around)])
        for to in sorted(places, key=lambda to: (to < 0, abs(to)))
    }
    right = [to for to in places if to > 0]
    left = [to for to in places if to < 0]
    (result,) = call(
        functools.partial(add_kernel, block, rows, right, False),
        "add_right",
        [owned[0]],
        [rest()] + [received[to] for to in right],
        clean,
        aliases={0: 0},
        flops=FIRST_FLOPS,
    )
    whole, _ = call(
        functools.partial(add_kernel, block, rows, left, True),
        "add_left",
        [owned[0]] * 2,
        [result] + [received[to] for to in left],
        written + clean,
        aliases={0: 1},
        hbm_out=(0,),
    )
    return whole


def solution(mesh):
    return jax.shard_map(
        local, mesh=mesh, in_specs=(P("gx", "gy", None),), out_specs=P("gx", "gy", None), check_vma=False
    )
```

```python
import functools

import jax
import jax.numpy as jnp
import numpy as np
from jax import lax
from jax.experimental import pallas as pl
from jax.experimental.pallas import tpu as pltpu
from jax.sharding import PartitionSpec as P

LEVELS = 4
STEPS = (-1.586134342, -0.05298011854, 0.8829110762, 0.4435068522)
SCALE = 1.149604398
VMEM_BYTES = 24 * 2**20
FIRST_FLOPS = 10**10
PIECE = 1024
SHARED = True


def windows(block):
    found = []
    first, last = 0, block - 1
    for _ in range(LEVELS):
        low = first - 4 + (first % 2)
        high = last + 4 - (last % 2)
        found.append((low, high))
        first, last = low // 2, high // 2
    return found


def message(block, rows, to):
    sent, derived = {}, {}
    spans = windows(block)
    base = ends = 0
    for level, (low, high) in enumerate(spans):
        size, height = block >> level, rows >> level
        first, last = (0, block - 1) if level == 0 else (v // 2 for v in spans[level - 1])
        planes = [p for p in range(low, high + 1) if p // size == to]
        if planes:
            sign = 1 if to > 0 else -1
            edge = last + 2 - last % 2 if to > 0 else first - 2 + first % 2
            far, near = edge + sign, edge - sign
            if far in planes and edge + 2 * sign in planes:
                derived[level, edge + 2 * sign] = (far, None)
            if far in planes and near in planes:
                derived[level, edge] = (far, near)
        planes = [plane for plane in planes if (level, plane) not in derived]
        at = base
        if level == 1:
            extra = planes[-1] if len(planes) > 3 else None
        elif level > 1 and extra is not None:
            at = base + (rows >> 1)
        for plane in planes:
            if level == 1 and plane == extra:
                sent[level, plane] = base, shift_of(2)
                continue
            sent[level, plane] = at, shift_of(level)
            at += height
        ends = max(ends, at)
        if level == 0:
            base = at
    return sent, derived, -(-ends // 8) * 8


def shift_of(level):
    return (0, 0, 1, 3)[level]


def places_of(block):
    found = set()
    for level, (low, high) in enumerate(windows(block)):
        size = block >> level
        found |= set(range(low // size, high // size + 1))
    return sorted(found - {0})


def in_parts(value):
    parts = []
    for _ in range(3):
        parts.append(value.astype(jnp.bfloat16))
        value = value - parts[-1].astype(jnp.float32)
    return parts


def z_product(value, weights):
    width = value.shape[-1]
    high, middle, low = in_parts(value)

    def dot(left, right, matrix):
        both = jnp.concatenate([left, right], axis=1)
        return jnp.dot(both, matrix, preferred_element_type=jnp.float32)

    large = dot(high, middle, weights[:, : 2 * width])
    small = dot(low, high, weights[:, 2 * width :])
    return large[:, :width] + (large[:, width:] + small)


def lanes_of(width, spacing, parity):
    lane = lax.broadcasted_iota(jnp.int32, (1, width), 1)
    return lax.rem(lane, 2 * spacing) == (spacing if parity else 0)


def own_lanes(width, level, high_only):
    spacing, shift = 1 << level, shift_of(level)
    lane = lax.broadcasted_iota(jnp.int32, (1, width), 1)
    if high_only:
        return lax.rem(lane, 2 * spacing) == spacing + shift
    return lax.rem(lane, spacing) == shift


def z_lift(value, spacing):
    width = value.shape[-1]
    axis = value.ndim - 1
    for step, weight in enumerate(STEPS):
        factor = jnp.where(lanes_of(width, spacing, step % 2 == 0), weight, 0.0)
        around = pltpu.roll(value, spacing, axis) + pltpu.roll(value, width - spacing, axis)
        value = value + factor * around
    return value


def x_lift(planes):
    def plus(one, other):
        return other if one is None else one if other is None else one + other

    planes = dict(planes)
    for step, weight in enumerate(STEPS):
        parity = 1 if step % 2 == 0 else 0
        for index in range(min(planes) - 1, max(planes) + 2):
            if index % 2 == parity:
                around = plus(planes.get(index - 1), planes.get(index + 1))
                if around is not None:
                    planes[index] = plus(planes.get(index), weight * around)
    return planes


def y_lift_split(even, odd):
    count = even.shape[0]
    a, b, c, d = STEPS
    odd = odd + a * (even + pltpu.roll(even, count - 1, 0))
    even = even + b * (pltpu.roll(odd, 1, 0) + odd)
    odd = odd + c * (even + pltpu.roll(even, count - 1, 0))
    even = even + d * (pltpu.roll(odd, 1, 0) + odd)
    return even, odd


def y_lift_whole(value):
    count = value.shape[0]
    row = lax.broadcasted_iota(jnp.int32, (count, 1), 0)
    for step, weight in enumerate(STEPS):
        factor = jnp.where(lax.rem(row, 2) == (1 if step % 2 == 0 else 0), weight, 0.0)
        value = value + factor * (pltpu.roll(value, 1, 0) + pltpu.roll(value, count - 1, 0))
    return value


def scaled_z(value, spacing):
    width = value.shape[-1]
    odd, even = lanes_of(width, spacing, True), lanes_of(width, spacing, False)
    return value * jnp.where(odd, SCALE, jnp.where(even, 1 / SCALE, 0.0))


def scaled(value, x_odd, y_odd):
    at = (SCALE if x_odd else 1 / SCALE) * (SCALE if y_odd else 1 / SCALE)
    return value if x_odd != y_odd else value * at


def spread_z(source, weights, spread, rows, start, size):
    width = source.shape[-1]
    value = source[start : start + size].reshape(size * rows, width)
    spread[start * rows : (start + size) * rows, :] = z_product(value, weights[...])


def spread_x(block, rows, spread, into, low, base):
    for at in range(0, rows, 8):
        planes = {x: spread[x * rows + at : x * rows + at + 8, :] for x in range(block)}
        for x, value in x_lift(planes).items():
            into[x - low, base + at : base + at + 8, :] = value


def matrix_kernel(*weights):
    width = weights[0].shape[0] // 2
    row = lax.broadcasted_iota(jnp.int32, (width, width), 0)
    lane = lax.broadcasted_iota(jnp.int32, (width, width), 1)
    value = jnp.where(row == lane, 1.0, 0.0)
    full = [scaled_z(z_lift(value, 1), 1), jnp.zeros((width, width), jnp.float32)]
    for level in range(1, LEVELS):
        spacing = 1 << level
        value = scaled_z(z_lift(value, spacing), spacing)
        full[1] += pltpu.roll(value, shift_of(level), 1) if shift_of(level) else value
        value = jnp.where(lanes_of(width, spacing, False), value, 0.0)
    for weight, matrix in zip(weights, full):
        high, middle, low = in_parts(matrix)
        for at, column in enumerate(((high, middle), (middle, high), (high, low))):
            for row, part in enumerate(column):
                weight[row * width : (row + 1) * width, at * width : (at + 1) * width] = part


def own_kernel(block, rows, velocity, weights, into, spread):
    step = max(1, min(block, PIECE // rows))
    for x in range(0, block, step):
        spread_z(velocity, weights, spread, rows, x, step)
    spread_x(block, rows, spread, into, windows(block)[0][0], 0)


def right_source(step, place, last):
    return place == last if step == 1 else (place == 0) | (place == last - 1)


def right_target(step, place):
    return (place == 0) & (step == 1)


def sends_right(step):
    core = lax.axis_index("gy") == 1
    return core == right_source(step, lax.axis_index("gx"), lax.axis_size("gx") - 1)


def takes_right(step):
    core = lax.axis_index("gy") == 1
    return core == right_target(step, lax.axis_index("gx"))


def shared_pairs(step, around):
    pairs = []
    for place in range(around):
        to, back = (place + step) % around, (place - step) % around
        source = int(right_source(step, place, around - 1))
        pairs.append((2 * place + source, 2 * to + int(right_target(step, to))))
        pairs.append((2 * place + 1 - source, 2 * back + 1 - int(right_target(step, back))))
    return pairs


def message_kernel(block, rows, width, count, places, *refs):
    refs = list(refs)

    def take(number):
        taken = refs[:number]
        del refs[:number]
        return taken

    shared = count == 2 and SHARED
    halves = 2 if shared else 1
    (_,) = take(1)
    others = take(count - 1)
    weights = take(2)
    lifted = take(LEVELS)
    passed = take(2 if shared else len(places))
    (spread,) = take(1)
    coarse = take(LEVELS - 1)
    both = take(2) if shared else []
    messages = dict(zip(places, passed))
    spans = windows(block)
    total = count * rows
    tables = {to: message(block, rows, to) for to in places}
    lengths = {to: message(block, rows, to)[2] for to in places}
    if shared:
        for step, buffer in enumerate(both, 1):
            size = buffer.shape[0] // 4
            for side, to in enumerate((step, -step)):
                lengths[to] = size
                messages[to] = buffer.at[pl.ds(2 * side * size, 2 * size)]
    written = {to: set() for to in places}

    def post(to, at, number, value):
        here = range(at, at + 2 * number, 2)
        if written[to].isdisjoint(here):
            messages[to][pl.ds(at, number, 2), :] = value
        else:
            messages[to][pl.ds(at, number, 2), :] += value
        written[to].update(here)

    def put(level, plane, half, even, odd):
        number = (rows >> level) // 2
        low = level < LEVELS - 1 and plane % 2 == 0
        if level > 0 or low:
            even = jnp.where(own_lanes(width, level, low), even, 0.0)
        if level > 0:
            odd = jnp.where(own_lanes(width, level, False), odd, 0.0)
        to = plane // (block >> level)
        at, shift = tables[to][0][level, plane]
        at += half * lengths[to]
        if shift != shift_of(level):
            even, odd = (pltpu.roll(value, shift - shift_of(level), 1) for value in (even, odd))
        post(to, at, number, even)
        post(to, at + 1, number, odd)

    for level in range(LEVELS):
        low, high = spans[level]
        height = total >> level
        half, mine = height // 2, (rows >> level) // 2
        into = lifted[level]

        if level == 0:
            for part, source in enumerate(others):
                step = min(block, max(1, PIECE // rows))
                for x in range(0, block, step):
                    spread_z(source, weights[0], spread, rows, x, step)
                spread_x(block, rows, spread, into, low, (part + 1) * rows)
        else:
            start, stop = spans[level - 1][0] // 2, spans[level - 1][1] // 2 + 1
            source = coarse[level - 1]
            if level == 1:
                size = (stop - start) * height
                for at in range(0, size, PIECE):
                    end = min(size, at + PIECE)
                    source[at:end, :] = z_product(source[at:end, :], weights[level][...])
            for at in range(0, height, 8):
                planes = {}
                for x in range(start, stop):
                    row = (x - start) * height + at
                    planes[x] = source[row : row + 8, :]
                for x, value in x_lift(planes).items():
                    into[x - low, at : at + 8, :] = value

        for plane in range(low, high + 1):
            odd_plane = plane % 2 == 1
            to = plane // (block >> level)
            goes_on = level < LEVELS - 1 and not odd_plane
            sends = to != 0 and (level, plane) in tables[to][0]
            if not goes_on and not sends:
                continue
            at = plane - low
            split = half % 8 == 0
            if split:
                even, odd = y_lift_split(
                    into[at, pl.ds(0, half, 2), :], into[at, pl.ds(1, half, 2), :]
                )
                even = scaled(even, odd_plane, False)
            else:
                into[at] = y_lift_whole(into[at])
                even = scaled(into[at, pl.ds(0, half, 2), :], odd_plane, False)
            if goes_on:
                row = ((plane - low) // 2) * half
                coarse[level][row : row + half, :] = even
            if not sends:
                continue
            for part in range(halves):
                if split:
                    here_even = even[part * mine : (part + 1) * mine]
                    here_odd = odd[part * mine : (part + 1) * mine]
                else:
                    here_even = into[at, pl.ds(2 * part * mine, mine, 2), :]
                    here_even = scaled(here_even, odd_plane, False)
                    here_odd = into[at, pl.ds(2 * part * mine + 1, mine, 2), :]
                put(level, plane, part, here_even, scaled(here_odd, odd_plane, True))

    for to in places:
        for row in range(halves * lengths[to]):
            if row not in written[to]:
                messages[to][row : row + 1, :] = jnp.zeros((1, width), jnp.float32)
    if shared:
        core = lax.axis_index("gy")
        for step, (target, buffer) in enumerate(zip(passed, both), 1):
            size = lengths[step]
            side = jnp.where(sends_right(step), 0, 2 * size)
            for half in range(2):
                here = side + (core if half == 0 else 1 - core) * size
                target[half * size : (half + 1) * size, :] = buffer[pl.ds(pl.multiple_of(here, 8), size), :]


def rest_kernel(block, rows, width, *refs):
    lifted, out, spare = refs[:LEVELS], refs[LEVELS], refs[LEVELS + 1]
    for level, (low, _) in enumerate(windows(block)):
        into, spacing, shift = lifted[level], 1 << level, shift_of(level)
        half, mine = into.shape[1] // 2, (rows >> level) // 2
        for plane in range(block >> level):
            odd_plane = plane % 2 == 1
            at = plane - low
            if half % 8 == 0:
                even, odd = y_lift_split(
                    into[at, pl.ds(0, half, 2), :], into[at, pl.ds(1, half, 2), :]
                )
                even, odd = even[:mine], odd[:mine]
            else:
                spare[plane] = y_lift_whole(into[at])
                even, odd = spare[plane, pl.ds(0, mine, 2), :], spare[plane, pl.ds(1, mine, 2), :]
            even, odd = scaled(even, odd_plane, False), scaled(odd, odd_plane, True)
            further = level < LEVELS - 1 and not odd_plane
            if level > 0 or further:
                even = jnp.where(own_lanes(width, level, further), even, 0.0)
            x = plane * spacing
            if level == 0:
                out[x, pl.ds(0, mine, 2), :] = even
                out[x, pl.ds(1, mine, 2), :] = odd
                continue
            odd = jnp.where(own_lanes(width, level, False), odd, 0.0)
            if shift:
                even, odd = (pltpu.roll(value, width - shift, 1) for value in (even, odd))
            out[x, pl.ds(0, mine, 2 * spacing), :] += even
            out[x, pl.ds(spacing, mine, 2 * spacing), :] += odd


def additions(block, rows, to, arrived, base, out, clean):
    sent, derived, _ = message(block, rows, to)
    a, b, c, d = STEPS
    width = out.shape[-1]
    lane = lax.broadcasted_iota(jnp.int32, (1, width), 1)
    found_here = []
    for level in sorted({level for level, _ in sent}):
        spacing, height = 1 << level, rows >> level
        shape = (height, width)
        held = {}
        for shift in sorted({shift for (found, _), (_, shift) in sent.items() if found == level}):
            here = {
                plane: at for (found, plane), (at, by) in sent.items() if (found, by) == (level, shift)
            }
            start, stop = min(here.values()), -(-(max(here.values()) + height) // 8) * 8
            source, offset = arrived, base
            if level > 0:
                value = arrived[base + start : base + stop, :]
                if shift:
                    value = pltpu.roll(value, width - shift, 1)
                source, offset = clean[level if shift == shift_of(level) else 0], -start
                source[: stop - start, :] = jnp.where(lax.rem(lane, spacing) == 0, value, 0.0)
            held |= {plane: (source, at + offset) for plane, at in here.items()}

        def read(plane, held=held, height=height):
            source, at = held[plane]
            return source[at : at + height, :]

        def derive(far, near, read=read, shape=shape, spacing=spacing, last=level == LEVELS - 1):
            if near is None:
                value = (d / SCALE**2) * read(far)
            else:
                value = ((1 / c + d) / SCALE**2) * read(far) + (d / SCALE**2) * read(near)
            if last:
                return value
            row = lax.broadcasted_iota(jnp.int32, shape, 0)
            keep = (lax.rem(row, 2) == 1) | lanes_of(width, spacing, True)
            return jnp.where(keep, value, 0.0)

        values = {plane: functools.partial(read, plane) for plane in held}
        for (found, plane), (far, near) in derived.items():
            if found == level:
                values[plane] = functools.partial(derive, far, near)
        for plane, value in values.items():
            x = (plane - to * (block >> level)) * spacing

            def add(x=x, height=height, spacing=spacing, value=value):
                out[x, pl.ds(0, height, spacing), :] += value()

            found_here.append((x, add))
    return found_here


def add_message(*args):
    for _, add in additions(*args):
        add()


def copy_out(out, whole, done, part, parts):
    size = out.shape[0] // parts
    here = pl.ds(part * size, size)
    copy = pltpu.make_async_copy(out.at[here], whole.at[here], done.at[part])
    copy.start()
    return copy


def add_kernel(block, rows, places, last, _, *refs):
    received, refs = refs[: len(places)], refs[len(places) :]
    if last:
        whole, out, done, *clean = refs
    else:
        out, *clean = refs
    for to, arrived in zip(places, received):
        add_message(block, rows, to, arrived, 0, out, clean)
    if last:
        for copy in [copy_out(out, whole, done, part, 2) for part in range(2)]:
            copy.wait()


def add_far(block, rows, right, arrived, base, out, clean):
    width, level = out.shape[-1], LEVELS - 1
    spacing, height, shift = 1 << level, rows >> level, shift_of(level)
    length = max(message(block, rows, to)[2] for to in (2, -2))
    lane = lax.broadcasted_iota(jnp.int32, (1, width), 1)
    value = pltpu.roll(arrived[base : base + length, :], width - shift, 1)
    value = jnp.where(lax.rem(lane, spacing) == 0, value, 0.0)
    for to, here in ((2, right), (-2, jnp.logical_not(right))):
        source = clean[0 if to > 0 else level]
        source[:length, :] = jnp.where(here, value, 0.0)
        sent, derived, _ = message(block, rows, to)
        parts = [(plane, at, 1.0) for (_, plane), (at, _) in sent.items()]
        parts += [
            (plane, sent[level, far][0], STEPS[3] / SCALE**2) for (_, plane), (far, _) in derived.items()
        ]
        for plane, at, factor in parts:
            x = (plane - to * (block >> level)) * spacing
            part = source[at : at + height, :]
            out[x, pl.ds(0, height, spacing), :] += part if factor == 1.0 else factor * part


def add_either(block, rows, right, step, arrived, base, out, clean):
    for side, here in ((step, right), (-step, jnp.logical_not(right))):

        @pl.when(here)
        def _():
            add_message(block, rows, side, arrived, base, out, clean)


def keep_kernel(block, rows, _, near, far, out, *clean):
    core = lax.axis_index("gy")
    add_either(block, rows, takes_right(1), 1, half_of(near, core), 0, out, clean)
    add_far(block, rows, takes_right(2), half_of(far, core), 0, out, clean)


def half_of(arrived, core):
    size = arrived.shape[0] // 2
    return arrived.at[pl.ds(pl.multiple_of(core * size, 8), size)]


def pack_kernel(near, far, packed):
    one = near.shape[0] // 2
    other = 1 - lax.axis_index("gy")
    packed[:one, :] = half_of(near, other)[...]
    packed[one:, :] = half_of(far, other)[...]


def swap_kernel(block, rows, one, own, packed, whole, out, done, *clean):
    add_far(block, rows, jnp.logical_not(takes_right(2)), packed, one, out, clean)
    right = jnp.logical_not(takes_right(1))
    for to, here in ((1, right), (-1, jnp.logical_not(right))):

        @pl.when(here)
        def _():
            tasks = additions(block, rows, to, packed, 0, out, clean)
            copies = []
            for part in ((1, 0) if to > 0 else (0, 1)):
                for x, add in tasks:
                    if 2 * x // block == part:
                        add()
                copies.append(copy_out(out, whole, done, part, 2))
            for copy in copies:
                copy.wait()


def call(body, name, outs, ins, scratch=(), aliases=None, flops=0, hbm_out=()):
    vmem, hbm = pl.BlockSpec(memory_space=pltpu.VMEM), pl.BlockSpec(memory_space=pltpu.HBM)
    f32 = jnp.float32
    shapes = [out if isinstance(out, jax.ShapeDtypeStruct) else jax.ShapeDtypeStruct(out, f32) for out in outs]
    moved = 4 * sum(int(np.prod(shape.shape)) for shape in shapes)
    return pl.pallas_call(
        body,
        out_shape=shapes,
        in_specs=[vmem] * len(ins),
        out_specs=[hbm if n in hbm_out else vmem for n in range(len(outs))],
        scratch_shapes=[pltpu.VMEM(shape, f32) if isinstance(shape, tuple) else shape for shape in scratch],
        input_output_aliases=aliases or {},
        compiler_params=pltpu.CompilerParams(vmem_limit_bytes=VMEM_BYTES),
        cost_estimate=pl.CostEstimate(flops=flops, bytes_accessed=2 * moved, transcendentals=0),
        name=name,
    )(*ins)


def local(velocity):
    block, rows, width = velocity.shape
    around, count = lax.axis_size("gx"), lax.axis_size("gy")
    shared = count == 2 and SHARED
    places = places_of(block)
    spans = windows(block)
    total = count * rows

    others = [
        lax.ppermute(velocity, "gy", [(i, (i - k) % count) for i in range(count)])
        for k in range(1, count)
    ]
    lifted = [
        (high - low + 1, total >> level, width) for level, (low, high) in enumerate(spans)
    ]
    coarse = [
        ((high // 2 - low // 2 + 1) * (total >> (level + 1)), width)
        for level, (low, high) in enumerate(spans[:-1])
    ]
    spread = (block * rows, width)
    owned = [(block >> level, rows >> level, width) for level in range(LEVELS)]
    lengths = {to: message(block, rows, to)[2] for to in places}
    one, two = max(lengths[1], lengths[-1]), max(lengths[2], lengths[-2])
    clean = [(one, width)] * LEVELS

    square = jax.ShapeDtypeStruct((2 * width, 3 * width), jnp.bfloat16)
    weights = call(matrix_kernel, "make_matrices", [square] * 2, [], flops=FIRST_FLOPS)
    (first,) = call(
        functools.partial(own_kernel, block, rows),
        "lift_own",
        [lifted[0]],
        [velocity, weights[0]],
        [spread],
    )
    if shared:
        outs, scratch = ([(many * size, width) for size in (one, two)] for many in (2, 4))
    else:
        outs, scratch = [(lengths[to], width) for to in places], []
    values = call(
        functools.partial(message_kernel, block, rows, width, count, places),
        "make_messages",
        lifted + outs,
        [first] + others + list(weights),
        [spread] + coarse + scratch,
        {0: 0},
    )
    before, messages = values[:LEVELS], values[LEVELS:]

    def rest():
        return call(
            functools.partial(rest_kernel, block, rows, width),
            "finish_own",
            [owned[0]],
            before,
            [(block >> LEVELS - 1, total >> LEVELS - 1, width)],
        )[0]

    written = [pltpu.SemaphoreType.DMA((2,))]
    if shared:
        near, far = (
            lax.ppermute(value, ("gx", "gy"), shared_pairs(step, around))
            for step, value in enumerate(messages, 1)
        )
        result = rest()
        (packed,) = call(pack_kernel, "pack_other", [(one + two, width)], [near, far])
        packed = lax.ppermute(packed, "gy", [(0, 1), (1, 0)])
        (result,) = call(
            functools.partial(keep_kernel, block, rows),
            "add_kept",
            [owned[0]],
            [result, near, far],
            clean,
            aliases={0: 0},
        )
        whole, _ = call(
            functools.partial(swap_kernel, block, rows, one),
            "add_swapped",
            [owned[0]] * 2,
            [result, packed],
            written + clean,
            aliases={0: 1},
            hbm_out=(0,),
        )
        return whole

    sent = dict(zip(places, messages))
    received = {
        to: lax.ppermute(sent[to], "gx", [(i, (i + to) % around) for i in range(around)])
        for to in sorted(places, key=lambda to: (to < 0, abs(to)))
    }
    right = [to for to in places if to > 0]
    left = [to for to in places if to < 0]
    (result,) = call(
        functools.partial(add_kernel, block, rows, right, False),
        "add_right",
        [owned[0]],
        [rest()] + [received[to] for to in right],
        clean,
        aliases={0: 0},
        flops=FIRST_FLOPS,
    )
    whole, _ = call(
        functools.partial(add_kernel, block, rows, left, True),
        "add_left",
        [owned[0]] * 2,
        [result] + [received[to] for to in left],
        written + clean,
        aliases={0: 1},
        hbm_out=(0,),
    )
    return whole


def solution(mesh):
    return jax.shard_map(
        local, mesh=mesh, in_specs=(P("gx", "gy", None),), out_specs=P("gx", "gy", None), check_vma=False
    )
```

```python
import functools

import jax
import jax.numpy as jnp
import numpy as np
from jax import lax
from jax.experimental import pallas as pl
from jax.experimental.pallas import tpu as pltpu
from jax.sharding import PartitionSpec as P

LEVELS = 4
STEPS = (-1.586134342, -0.05298011854, 0.8829110762, 0.4435068522)
SCALE = 1.149604398
VMEM_BYTES = 24 * 2**20
FIRST_FLOPS = 10**10
PIECE = 1024
SHARED = True


def windows(block):
    found = []
    first, last = 0, block - 1
    for _ in range(LEVELS):
        low = first - 4 + (first % 2)
        high = last + 4 - (last % 2)
        found.append((low, high))
        first, last = low // 2, high // 2
    return found


def message(block, rows, to):
    sent, derived = {}, {}
    spans = windows(block)
    base = ends = 0
    for level, (low, high) in enumerate(spans):
        size, height = block >> level, rows >> level
        first, last = (0, block - 1) if level == 0 else (v // 2 for v in spans[level - 1])
        planes = [p for p in range(low, high + 1) if p // size == to]
        if planes:
            sign = 1 if to > 0 else -1
            edge = last + 2 - last % 2 if to > 0 else first - 2 + first % 2
            far, near = edge + sign, edge - sign
            if far in planes and edge + 2 * sign in planes:
                derived[level, edge + 2 * sign] = (far, None)
            if far in planes and near in planes:
                derived[level, edge] = (far, near)
        planes = [plane for plane in planes if (level, plane) not in derived]
        at = base
        if level == 1:
            extra = planes[-1] if len(planes) > 3 else None
        elif level > 1 and extra is not None:
            at = base + (rows >> 1)
        for plane in planes:
            if level == 1 and plane == extra:
                sent[level, plane] = base, shift_of(2)
                continue
            sent[level, plane] = at, shift_of(level)
            at += height
        ends = max(ends, at)
        if level == 0:
            base = at
    return sent, derived, -(-ends // 8) * 8


def shift_of(level):
    return (0, 0, 1, 3)[level]


def places_of(block):
    found = set()
    for level, (low, high) in enumerate(windows(block)):
        size = block >> level
        found |= set(range(low // size, high // size + 1))
    return sorted(found - {0})


def in_parts(value):
    parts = []
    for _ in range(3):
        parts.append(value.astype(jnp.bfloat16))
        value = value - parts[-1].astype(jnp.float32)
    return parts


def z_product(value, weights):
    width = value.shape[-1]
    high, middle, low = in_parts(value)

    def dot(left, right, matrix):
        both = jnp.concatenate([left, right], axis=1)
        return jnp.dot(both, matrix, preferred_element_type=jnp.float32)

    large = dot(high, middle, weights[:, : 2 * width])
    small = dot(low, high, weights[:, 2 * width :])
    return large[:, :width] + (large[:, width:] + small)


def lanes_of(width, spacing, parity):
    lane = lax.broadcasted_iota(jnp.int32, (1, width), 1)
    return lax.rem(lane, 2 * spacing) == (spacing if parity else 0)


def own_lanes(width, level, high_only):
    spacing, shift = 1 << level, shift_of(level)
    lane = lax.broadcasted_iota(jnp.int32, (1, width), 1)
    if high_only:
        return lax.rem(lane, 2 * spacing) == spacing + shift
    return lax.rem(lane, spacing) == shift


def z_lift(value, spacing):
    width = value.shape[-1]
    axis = value.ndim - 1
    for step, weight in enumerate(STEPS):
        factor = jnp.where(lanes_of(width, spacing, step % 2 == 0), weight, 0.0)
        around = pltpu.roll(value, spacing, axis) + pltpu.roll(value, width - spacing, axis)
        value = value + factor * around
    return value


def x_lift(planes):
    def plus(one, other):
        return other if one is None else one if other is None else one + other

    planes = dict(planes)
    for step, weight in enumerate(STEPS):
        parity = 1 if step % 2 == 0 else 0
        for index in range(min(planes) - 1, max(planes) + 2):
            if index % 2 == parity:
                around = plus(planes.get(index - 1), planes.get(index + 1))
                if around is not None:
                    planes[index] = plus(planes.get(index), weight * around)
    return planes


def y_lift_split(even, odd):
    count = even.shape[0]
    a, b, c, d = STEPS
    odd = odd + a * (even + pltpu.roll(even, count - 1, 0))
    even = even + b * (pltpu.roll(odd, 1, 0) + odd)
    odd = odd + c * (even + pltpu.roll(even, count - 1, 0))
    even = even + d * (pltpu.roll(odd, 1, 0) + odd)
    return even, odd


def even_and_odd(parts, plane):
    return [
        jnp.concatenate([part[plane, pl.ds(start, part.shape[1] // 2, 2), :] for part in parts])
        for start in (0, 1)
    ]


def y_lift_whole(value):
    count = value.shape[0]
    row = lax.broadcasted_iota(jnp.int32, (count, 1), 0)
    for step, weight in enumerate(STEPS):
        factor = jnp.where(lax.rem(row, 2) == (1 if step % 2 == 0 else 0), weight, 0.0)
        value = value + factor * (pltpu.roll(value, 1, 0) + pltpu.roll(value, count - 1, 0))
    return value


def scaled_z(value, spacing):
    width = value.shape[-1]
    odd, even = lanes_of(width, spacing, True), lanes_of(width, spacing, False)
    return value * jnp.where(odd, SCALE, jnp.where(even, 1 / SCALE, 0.0))


def scaled(value, x_odd, y_odd):
    at = (SCALE if x_odd else 1 / SCALE) * (SCALE if y_odd else 1 / SCALE)
    return value if x_odd != y_odd else value * at


def spread_z(source, weights, spread, rows, start, size):
    width = source.shape[-1]
    value = source[start : start + size].reshape(size * rows, width)
    spread[start * rows : (start + size) * rows, :] = z_product(value, weights[...])


def spread_x(block, rows, spread, into, low, base):
    for at in range(0, rows, 8):
        planes = {x: spread[x * rows + at : x * rows + at + 8, :] for x in range(block)}
        for x, value in x_lift(planes).items():
            into[x - low, base + at : base + at + 8, :] = value


def matrix_kernel(*weights):
    width = weights[0].shape[0] // 2
    row = lax.broadcasted_iota(jnp.int32, (width, width), 0)
    lane = lax.broadcasted_iota(jnp.int32, (width, width), 1)
    value = jnp.where(row == lane, 1.0, 0.0)
    full = [scaled_z(z_lift(value, 1), 1), jnp.zeros((width, width), jnp.float32)]
    for level in range(1, LEVELS):
        spacing = 1 << level
        value = scaled_z(z_lift(value, spacing), spacing)
        full[1] += pltpu.roll(value, shift_of(level), 1) if shift_of(level) else value
        value = jnp.where(lanes_of(width, spacing, False), value, 0.0)
    for weight, matrix in zip(weights, full):
        high, middle, low = in_parts(matrix)
        for at, column in enumerate(((high, middle), (middle, high), (high, low))):
            for row, part in enumerate(column):
                weight[row * width : (row + 1) * width, at * width : (at + 1) * width] = part


def own_kernel(block, rows, velocity, weights, into, spread):
    step = max(1, min(block, PIECE // rows))
    for x in range(0, block, step):
        spread_z(velocity, weights, spread, rows, x, step)
    spread_x(block, rows, spread, into, windows(block)[0][0], 0)


def right_source(step, place, last):
    return place == last if step == 1 else (place == 0) | (place == last - 1)


def right_target(step, place):
    return (place == 0) & (step == 1)


def sends_right(step):
    core = lax.axis_index("gy") == 1
    return core == right_source(step, lax.axis_index("gx"), lax.axis_size("gx") - 1)


def takes_right(step):
    core = lax.axis_index("gy") == 1
    return core == right_target(step, lax.axis_index("gx"))


def shared_pairs(step, around):
    pairs = []
    for place in range(around):
        to, back = (place + step) % around, (place - step) % around
        source = int(right_source(step, place, around - 1))
        pairs.append((2 * place + source, 2 * to + int(right_target(step, to))))
        pairs.append((2 * place + 1 - source, 2 * back + 1 - int(right_target(step, back))))
    return pairs


def message_kernel(block, rows, width, count, places, *refs):
    refs = list(refs)

    def take(number):
        taken = refs[:number]
        del refs[:number]
        return taken

    shared = count == 2 and SHARED
    halves = 2 if shared else 1
    first = take(1)
    others = take(count - 1)
    weights = take(2)
    first += take(count - 1)
    lifted = [None] + take(LEVELS - 1)
    passed = take(2 if shared else len(places))
    (spread,) = take(1)
    coarse = take(LEVELS - 1)
    both = take(2) if shared else []
    messages = dict(zip(places, passed))
    spans = windows(block)
    total = count * rows
    tables = {to: message(block, rows, to) for to in places}
    lengths = {to: message(block, rows, to)[2] for to in places}
    if shared:
        for step, buffer in enumerate(both, 1):
            size = buffer.shape[0] // 4
            for side, to in enumerate((step, -step)):
                lengths[to] = size
                messages[to] = buffer.at[pl.ds(2 * side * size, 2 * size)]
    written = {to: set() for to in places}

    def post(to, at, number, value):
        here = range(at, at + 2 * number, 2)
        if written[to].isdisjoint(here):
            messages[to][pl.ds(at, number, 2), :] = value
        else:
            messages[to][pl.ds(at, number, 2), :] += value
        written[to].update(here)

    def put(level, plane, half, even, odd):
        number = (rows >> level) // 2
        low = level < LEVELS - 1 and plane % 2 == 0
        if level > 0 or low:
            even = jnp.where(own_lanes(width, level, low), even, 0.0)
        if level > 0:
            odd = jnp.where(own_lanes(width, level, False), odd, 0.0)
        to = plane // (block >> level)
        at, shift = tables[to][0][level, plane]
        at += half * lengths[to]
        if shift != shift_of(level):
            even, odd = (pltpu.roll(value, shift - shift_of(level), 1) for value in (even, odd))
        post(to, at, number, even)
        post(to, at + 1, number, odd)

    for level in range(LEVELS):
        low, high = spans[level]
        height = total >> level
        half, mine = height // 2, (rows >> level) // 2
        into = lifted[level]

        if level == 0:
            for part, source in enumerate(others):
                step = min(block, max(1, PIECE // rows))
                for x in range(0, block, step):
                    spread_z(source, weights[0], spread, rows, x, step)
                spread_x(block, rows, spread, first[part + 1], low, 0)
        else:
            start, stop = spans[level - 1][0] // 2, spans[level - 1][1] // 2 + 1
            source = coarse[level - 1]
            if level == 1:
                size = (stop - start) * height
                for at in range(0, size, PIECE):
                    end = min(size, at + PIECE)
                    source[at:end, :] = z_product(source[at:end, :], weights[level][...])
            for at in range(0, height, 8):
                planes = {}
                for x in range(start, stop):
                    row = (x - start) * height + at
                    planes[x] = source[row : row + 8, :]
                for x, value in x_lift(planes).items():
                    into[x - low, at : at + 8, :] = value

        for plane in range(low, high + 1):
            odd_plane = plane % 2 == 1
            to = plane // (block >> level)
            goes_on = level < LEVELS - 1 and not odd_plane
            sends = to != 0 and (level, plane) in tables[to][0]
            if not goes_on and not sends:
                continue
            at = plane - low
            split = half % 8 == 0
            if split:
                even, odd = y_lift_split(*even_and_odd([into] if level else first, at))
                even = scaled(even, odd_plane, False)
            else:
                into[at] = y_lift_whole(into[at])
                even = scaled(into[at, pl.ds(0, half, 2), :], odd_plane, False)
            if goes_on:
                row = ((plane - low) // 2) * half
                coarse[level][row : row + half, :] = even
            if not sends:
                continue
            for part in range(halves):
                if split:
                    here_even = even[part * mine : (part + 1) * mine]
                    here_odd = odd[part * mine : (part + 1) * mine]
                else:
                    here_even = into[at, pl.ds(2 * part * mine, mine, 2), :]
                    here_even = scaled(here_even, odd_plane, False)
                    here_odd = into[at, pl.ds(2 * part * mine + 1, mine, 2), :]
                put(level, plane, part, here_even, scaled(here_odd, odd_plane, True))

    for to in places:
        for row in range(halves * lengths[to]):
            if row not in written[to]:
                messages[to][row : row + 1, :] = jnp.zeros((1, width), jnp.float32)
    if shared:
        core = lax.axis_index("gy")
        for step, (target, buffer) in enumerate(zip(passed, both), 1):
            size = lengths[step]
            side = jnp.where(sends_right(step), 0, 2 * size)
            for half in range(2):
                here = side + (core if half == 0 else 1 - core) * size
                target[half * size : (half + 1) * size, :] = buffer[pl.ds(pl.multiple_of(here, 8), size), :]


def rest_kernel(block, rows, width, *refs):
    first, lifted, (out, spare) = refs[: 1 - LEVELS - 2], refs[1 - LEVELS - 2 : -2], refs[-2:]
    for level, (low, _) in enumerate(windows(block)):
        parts = [lifted[level - 1]] if level else first
        spacing, shift = 1 << level, shift_of(level)
        half, mine = sum(part.shape[1] for part in parts) // 2, (rows >> level) // 2
        for plane in range(block >> level):
            odd_plane = plane % 2 == 1
            at = plane - low
            if half % 8 == 0:
                even, odd = y_lift_split(*even_and_odd(parts, at))
                even, odd = even[:mine], odd[:mine]
            else:
                spare[plane] = y_lift_whole(parts[0][at])
                even, odd = spare[plane, pl.ds(0, mine, 2), :], spare[plane, pl.ds(1, mine, 2), :]
            even, odd = scaled(even, odd_plane, False), scaled(odd, odd_plane, True)
            further = level < LEVELS - 1 and not odd_plane
            if level > 0 or further:
                even = jnp.where(own_lanes(width, level, further), even, 0.0)
            x = plane * spacing
            if level == 0:
                out[x, pl.ds(0, mine, 2), :] = even
                out[x, pl.ds(1, mine, 2), :] = odd
                continue
            odd = jnp.where(own_lanes(width, level, False), odd, 0.0)
            if shift:
                even, odd = (pltpu.roll(value, width - shift, 1) for value in (even, odd))
            out[x, pl.ds(0, mine, 2 * spacing), :] += even
            out[x, pl.ds(spacing, mine, 2 * spacing), :] += odd


def additions(block, rows, to, arrived, base, out, clean):
    sent, derived, _ = message(block, rows, to)
    a, b, c, d = STEPS
    width = out.shape[-1]
    lane = lax.broadcasted_iota(jnp.int32, (1, width), 1)
    found_here = []
    for level in sorted({level for level, _ in sent}):
        spacing, height = 1 << level, rows >> level
        shape = (height, width)
        held = {}
        for shift in sorted({shift for (found, _), (_, shift) in sent.items() if found == level}):
            here = {
                plane: at for (found, plane), (at, by) in sent.items() if (found, by) == (level, shift)
            }
            start, stop = min(here.values()), -(-(max(here.values()) + height) // 8) * 8
            source, offset = arrived, base
            if level > 0:
                value = arrived[base + start : base + stop, :]
                if shift:
                    value = pltpu.roll(value, width - shift, 1)
                source, offset = clean[level if shift == shift_of(level) else 0], -start
                source[: stop - start, :] = jnp.where(lax.rem(lane, spacing) == 0, value, 0.0)
            held |= {plane: (source, at + offset) for plane, at in here.items()}

        def read(plane, held=held, height=height):
            source, at = held[plane]
            return source[at : at + height, :]

        def derive(far, near, read=read, shape=shape, spacing=spacing, last=level == LEVELS - 1):
            if near is None:
                value = (d / SCALE**2) * read(far)
            else:
                value = ((1 / c + d) / SCALE**2) * read(far) + (d / SCALE**2) * read(near)
            if last:
                return value
            row = lax.broadcasted_iota(jnp.int32, shape, 0)
            keep = (lax.rem(row, 2) == 1) | lanes_of(width, spacing, True)
            return jnp.where(keep, value, 0.0)

        values = {plane: functools.partial(read, plane) for plane in held}
        for (found, plane), (far, near) in derived.items():
            if found == level:
                values[plane] = functools.partial(derive, far, near)
        for plane, value in values.items():
            x = (plane - to * (block >> level)) * spacing

            def add(x=x, height=height, spacing=spacing, value=value):
                out[x, pl.ds(0, height, spacing), :] += value()

            found_here.append((x, add))
    return found_here


def add_message(*args):
    for _, add in additions(*args):
        add()


def copy_out(out, whole, done, part, parts):
    size = out.shape[0] // parts
    here = pl.ds(part * size, size)
    copy = pltpu.make_async_copy(out.at[here], whole.at[here], done.at[part])
    copy.start()
    return copy


def add_kernel(block, rows, places, last, own, *refs):
    received, refs = refs[: len(places)], refs[len(places) :]
    if last:
        whole, out, done, *clean = refs
    else:
        out, *clean = refs
    out[...] = own[...]
    for to, arrived in zip(places, received):
        add_message(block, rows, to, arrived, 0, out, clean)
    if last:
        for copy in [copy_out(out, whole, done, part, 2) for part in range(2)]:
            copy.wait()


def add_far(block, rows, right, arrived, base, out, clean):
    width, level = out.shape[-1], LEVELS - 1
    spacing, height, shift = 1 << level, rows >> level, shift_of(level)
    length = max(message(block, rows, to)[2] for to in (2, -2))
    lane = lax.broadcasted_iota(jnp.int32, (1, width), 1)
    value = pltpu.roll(arrived[base : base + length, :], width - shift, 1)
    value = jnp.where(lax.rem(lane, spacing) == 0, value, 0.0)
    for to, here in ((2, right), (-2, jnp.logical_not(right))):
        source = clean[0 if to > 0 else level]
        source[:length, :] = jnp.where(here, value, 0.0)
        sent, derived, _ = message(block, rows, to)
        parts = [(plane, at, 1.0) for (_, plane), (at, _) in sent.items()]
        parts += [
            (plane, sent[level, far][0], STEPS[3] / SCALE**2) for (_, plane), (far, _) in derived.items()
        ]
        for plane, at, factor in parts:
            x = (plane - to * (block >> level)) * spacing
            part = source[at : at + height, :]
            out[x, pl.ds(0, height, spacing), :] += part if factor == 1.0 else factor * part


def add_either(block, rows, right, step, arrived, base, out, clean):
    for side, here in ((step, right), (-step, jnp.logical_not(right))):

        @pl.when(here)
        def _():
            add_message(block, rows, side, arrived, base, out, clean)


def keep_kernel(block, rows, own, near, far, out, *clean):
    out[...] = own[...]
    core = lax.axis_index("gy")
    add_either(block, rows, takes_right(1), 1, half_of(near, core), 0, out, clean)
    add_far(block, rows, takes_right(2), half_of(far, core), 0, out, clean)


def half_of(arrived, core):
    size = arrived.shape[0] // 2
    return arrived.at[pl.ds(pl.multiple_of(core * size, 8), size)]


def pack_kernel(near, far, packed):
    one = near.shape[0] // 2
    other = 1 - lax.axis_index("gy")
    packed[:one, :] = half_of(near, other)[...]
    packed[one:, :] = half_of(far, other)[...]


def swap_kernel(block, rows, one, own, packed, whole, out, done, *clean):
    out[...] = own[...]
    add_far(block, rows, jnp.logical_not(takes_right(2)), packed, one, out, clean)
    right = jnp.logical_not(takes_right(1))
    for to, here in ((1, right), (-1, jnp.logical_not(right))):

        @pl.when(here)
        def _():
            tasks = additions(block, rows, to, packed, 0, out, clean)
            copies = []
            for part in ((1, 0) if to > 0 else (0, 1)):
                for x, add in tasks:
                    if 2 * x // block == part:
                        add()
                copies.append(copy_out(out, whole, done, part, 2))
            for copy in copies:
                copy.wait()


def call(body, name, outs, ins, scratch=(), flops=0, hbm_out=()):
    vmem, hbm = pl.BlockSpec(memory_space=pltpu.VMEM), pl.BlockSpec(memory_space=pltpu.HBM)
    f32 = jnp.float32
    shapes = [out if isinstance(out, jax.ShapeDtypeStruct) else jax.ShapeDtypeStruct(out, f32) for out in outs]
    moved = 4 * sum(int(np.prod(shape.shape)) for shape in shapes)
    return pl.pallas_call(
        body,
        out_shape=shapes,
        in_specs=[vmem] * len(ins),
        out_specs=[hbm if n in hbm_out else vmem for n in range(len(outs))],
        scratch_shapes=[pltpu.VMEM(shape, f32) if isinstance(shape, tuple) else shape for shape in scratch],
        compiler_params=pltpu.CompilerParams(vmem_limit_bytes=VMEM_BYTES),
        cost_estimate=pl.CostEstimate(flops=flops, bytes_accessed=2 * moved, transcendentals=0),
        name=name,
    )(*ins)


def local(velocity):
    block, rows, width = velocity.shape
    around, count = lax.axis_size("gx"), lax.axis_size("gy")
    shared = count == 2 and SHARED
    places = places_of(block)
    spans = windows(block)
    total = count * rows

    others = [
        lax.ppermute(velocity, "gy", [(i, (i - k) % count) for i in range(count)])
        for k in range(1, count)
    ]
    lifted = [
        (high - low + 1, total >> level, width) for level, (low, high) in enumerate(spans)
    ]
    coarse = [
        ((high // 2 - low // 2 + 1) * (total >> (level + 1)), width)
        for level, (low, high) in enumerate(spans[:-1])
    ]
    spread = (block * rows, width)
    part = (lifted[0][0], rows, width)
    owned = [(block >> level, rows >> level, width) for level in range(LEVELS)]
    lengths = {to: message(block, rows, to)[2] for to in places}
    one, two = max(lengths[1], lengths[-1]), max(lengths[2], lengths[-2])
    clean = [(one, width)] * LEVELS

    square = jax.ShapeDtypeStruct((2 * width, 3 * width), jnp.bfloat16)
    weights = call(matrix_kernel, "make_matrices", [square] * 2, [], flops=FIRST_FLOPS)
    (first,) = call(
        functools.partial(own_kernel, block, rows),
        "lift_own",
        [part],
        [velocity, weights[0]],
        [spread],
    )
    if shared:
        outs, scratch = ([(many * size, width) for size in (one, two)] for many in (2, 4))
    else:
        outs, scratch = [(lengths[to], width) for to in places], []
    values = call(
        functools.partial(message_kernel, block, rows, width, count, places),
        "make_messages",
        [part] * (count - 1) + lifted[1:] + outs,
        [first] + others + list(weights),
        [spread] + coarse + scratch,
    )
    before, messages = [first, *values[: count + LEVELS - 2]], values[count + LEVELS - 2 :]

    def rest():
        return call(
            functools.partial(rest_kernel, block, rows, width),
            "finish_own",
            [owned[0]],
            before,
            [(block >> LEVELS - 1, total >> LEVELS - 1, width)],
        )[0]

    written = [pltpu.SemaphoreType.DMA((2,))]
    if shared:
        near, far = (
            lax.ppermute(value, ("gx", "gy"), shared_pairs(step, around))
            for step, value in enumerate(messages, 1)
        )
        result = rest()
        (packed,) = call(pack_kernel, "pack_other", [(one + two, width)], [near, far])
        packed = lax.ppermute(packed, "gy", [(0, 1), (1, 0)])
        (result,) = call(
            functools.partial(keep_kernel, block, rows),
            "add_kept",
            [owned[0]],
            [result, near, far],
            clean,
        )
        (whole,) = call(
            functools.partial(swap_kernel, block, rows, one),
            "add_swapped",
            [owned[0]],
            [result, packed],
            [owned[0]] + written + clean,
            hbm_out=(0,),
        )
        return whole

    sent = dict(zip(places, messages))
    received = {
        to: lax.ppermute(sent[to], "gx", [(i, (i + to) % around) for i in range(around)])
        for to in sorted(places, key=lambda to: (to < 0, abs(to)))
    }
    right = [to for to in places if to > 0]
    left = [to for to in places if to < 0]
    (result,) = call(
        functools.partial(add_kernel, block, rows, right, False),
        "add_right",
        [owned[0]],
        [rest()] + [received[to] for to in right],
        clean,
        flops=FIRST_FLOPS,
    )
    (whole,) = call(
        functools.partial(add_kernel, block, rows, left, True),
        "add_left",
        [owned[0]],
        [result] + [received[to] for to in left],
        [owned[0]] + written + clean,
        hbm_out=(0,),
    )
    return whole


def solution(mesh):
    return jax.shard_map(
        local, mesh=mesh, in_specs=(P("gx", "gy", None),), out_specs=P("gx", "gy", None), check_vma=False
    )
```

```python
import functools

import jax
import jax.numpy as jnp
import numpy as np
from jax import lax
from jax.experimental import pallas as pl
from jax.experimental.pallas import tpu as pltpu
from jax.sharding import PartitionSpec as P

LEVELS = 4
STEPS = (-1.586134342, -0.05298011854, 0.8829110762, 0.4435068522)
SCALE = 1.149604398
VMEM_BYTES = 24 * 2**20
FIRST_FLOPS = 10**10
PIECE = 1024
SHARED = True


def windows(block):
    found = []
    first, last = 0, block - 1
    for _ in range(LEVELS):
        low = first - 4 + (first % 2)
        high = last + 4 - (last % 2)
        found.append((low, high))
        first, last = low // 2, high // 2
    return found


def message(block, rows, to):
    sent, derived = {}, {}
    spans = windows(block)
    base = ends = 0
    for level, (low, high) in enumerate(spans):
        size, height = block >> level, rows >> level
        first, last = (0, block - 1) if level == 0 else (v // 2 for v in spans[level - 1])
        planes = [p for p in range(low, high + 1) if p // size == to]
        if planes:
            sign = 1 if to > 0 else -1
            edge = last + 2 - last % 2 if to > 0 else first - 2 + first % 2
            far, near = edge + sign, edge - sign
            if far in planes and edge + 2 * sign in planes:
                derived[level, edge + 2 * sign] = (far, None)
            if far in planes and near in planes:
                derived[level, edge] = (far, near)
        planes = [plane for plane in planes if (level, plane) not in derived]
        at = base
        if level == 1:
            extra = planes[-1] if len(planes) > 3 else None
        elif level > 1 and extra is not None:
            at = base + (rows >> 1)
        for plane in planes:
            if level == 1 and plane == extra:
                sent[level, plane] = base, shift_of(2)
                continue
            sent[level, plane] = at, shift_of(level)
            at += height
        ends = max(ends, at)
        if level == 0:
            base = at
    return sent, derived, -(-ends // 8) * 8


def shift_of(level):
    return (0, 0, 1, 3)[level]


def places_of(block):
    found = set()
    for level, (low, high) in enumerate(windows(block)):
        size = block >> level
        found |= set(range(low // size, high // size + 1))
    return sorted(found - {0})


def in_parts(value):
    parts = []
    for _ in range(3):
        parts.append(value.astype(jnp.bfloat16))
        value = value - parts[-1].astype(jnp.float32)
    return parts


def z_product(value, weights):
    width = value.shape[-1]
    high, middle, low = in_parts(value)

    def dot(left, right, matrix):
        both = jnp.concatenate([left, right], axis=1)
        return jnp.dot(both, matrix, preferred_element_type=jnp.float32)

    large = dot(high, middle, weights[:, : 2 * width])
    small = dot(low, high, weights[:, 2 * width :])
    return large[:, :width] + (large[:, width:] + small)


def lanes_of(width, spacing, parity):
    lane = lax.broadcasted_iota(jnp.int32, (1, width), 1)
    return lax.rem(lane, 2 * spacing) == (spacing if parity else 0)


def own_lanes(width, level, high_only):
    spacing, shift = 1 << level, shift_of(level)
    lane = lax.broadcasted_iota(jnp.int32, (1, width), 1)
    if high_only:
        return lax.rem(lane, 2 * spacing) == spacing + shift
    return lax.rem(lane, spacing) == shift


def z_lift(value, spacing):
    width = value.shape[-1]
    axis = value.ndim - 1
    for step, weight in enumerate(STEPS):
        factor = jnp.where(lanes_of(width, spacing, step % 2 == 0), weight, 0.0)
        around = pltpu.roll(value, spacing, axis) + pltpu.roll(value, width - spacing, axis)
        value = value + factor * around
    return value


def x_lift(planes):
    def plus(one, other):
        return other if one is None else one if other is None else one + other

    planes = dict(planes)
    for step, weight in enumerate(STEPS):
        parity = 1 if step % 2 == 0 else 0
        for index in range(min(planes) - 1, max(planes) + 2):
            if index % 2 == parity:
                around = plus(planes.get(index - 1), planes.get(index + 1))
                if around is not None:
                    planes[index] = plus(planes.get(index), weight * around)
    return planes


def y_lift_split(even, odd):
    count = even.shape[0]
    a, b, c, d = STEPS
    odd = odd + a * (even + pltpu.roll(even, count - 1, 0))
    even = even + b * (pltpu.roll(odd, 1, 0) + odd)
    odd = odd + c * (even + pltpu.roll(even, count - 1, 0))
    even = even + d * (pltpu.roll(odd, 1, 0) + odd)
    return even, odd


def even_and_odd(parts, plane):
    return [
        jnp.concatenate([part[plane, pl.ds(start, part.shape[1] // 2, 2), :] for part in parts])
        for start in (0, 1)
    ]


def y_lift_whole(value):
    count = value.shape[0]
    row = lax.broadcasted_iota(jnp.int32, (count, 1), 0)
    for step, weight in enumerate(STEPS):
        factor = jnp.where(lax.rem(row, 2) == (1 if step % 2 == 0 else 0), weight, 0.0)
        value = value + factor * (pltpu.roll(value, 1, 0) + pltpu.roll(value, count - 1, 0))
    return value


def scaled_z(value, spacing):
    width = value.shape[-1]
    odd, even = lanes_of(width, spacing, True), lanes_of(width, spacing, False)
    return value * jnp.where(odd, SCALE, jnp.where(even, 1 / SCALE, 0.0))


def scaled(value, x_odd, y_odd):
    at = (SCALE if x_odd else 1 / SCALE) * (SCALE if y_odd else 1 / SCALE)
    return value if x_odd != y_odd else value * at


def spread_z(source, weights, spread, rows, start, size):
    width = source.shape[-1]
    value = source[start : start + size].reshape(size * rows, width)
    spread[start * rows : (start + size) * rows, :] = z_product(value, weights[...])


def spread_x(block, rows, spread, into, low, base):
    for at in range(0, rows, 8):
        planes = {x: spread[x * rows + at : x * rows + at + 8, :] for x in range(block)}
        for x, value in x_lift(planes).items():
            into[x - low, base + at : base + at + 8, :] = value


def matrix_kernel(*weights):
    width = weights[0].shape[0] // 2
    row = lax.broadcasted_iota(jnp.int32, (width, width), 0)
    lane = lax.broadcasted_iota(jnp.int32, (width, width), 1)
    value = jnp.where(row == lane, 1.0, 0.0)
    full = [scaled_z(z_lift(value, 1), 1), jnp.zeros((width, width), jnp.float32)]
    for level in range(1, LEVELS):
        spacing = 1 << level
        value = scaled_z(z_lift(value, spacing), spacing)
        full[1] += pltpu.roll(value, shift_of(level), 1) if shift_of(level) else value
        value = jnp.where(lanes_of(width, spacing, False), value, 0.0)
    for weight, matrix in zip(weights, full):
        high, middle, low = in_parts(matrix)
        for at, column in enumerate(((high, middle), (middle, high), (high, low))):
            for row, part in enumerate(column):
                weight[row * width : (row + 1) * width, at * width : (at + 1) * width] = part


def own_kernel(block, rows, velocity, weights, into, spread):
    step = max(1, min(block, PIECE // rows))
    for x in range(0, block, step):
        spread_z(velocity, weights, spread, rows, x, step)
    spread_x(block, rows, spread, into, windows(block)[0][0], 0)


def right_source(step, place, last):
    return place == (last if step == 1 else last - 1)


def right_target(step, place):
    return (place == 0) & (step == 1)


def sends_right(step):
    core = lax.axis_index("gy") == 1
    return core == right_source(step, lax.axis_index("gx"), lax.axis_size("gx") - 1)


def takes_right(step):
    core = lax.axis_index("gy") == 1
    return core == right_target(step, lax.axis_index("gx"))


def shared_pairs(step, around):
    pairs = []
    for place in range(around):
        to, back = (place + step) % around, (place - step) % around
        source = int(right_source(step, place, around - 1))
        pairs.append((2 * place + source, 2 * to + int(right_target(step, to))))
        pairs.append((2 * place + 1 - source, 2 * back + 1 - int(right_target(step, back))))
    return pairs


def message_kernel(block, rows, width, count, places, *refs):
    refs = list(refs)

    def take(number):
        taken = refs[:number]
        del refs[:number]
        return taken

    shared = count == 2 and SHARED
    halves = 2 if shared else 1
    first = take(1)
    others = take(count - 1)
    weights = take(2)
    first += take(count - 1)
    lifted = [None] + take(LEVELS - 1)
    passed = take(2 if shared else len(places))
    (spread,) = take(1)
    coarse = take(LEVELS - 1)
    both = take(2) if shared else []
    messages = dict(zip(places, passed))
    spans = windows(block)
    total = count * rows
    tables = {to: message(block, rows, to) for to in places}
    lengths = {to: message(block, rows, to)[2] for to in places}
    if shared:
        for step, buffer in enumerate(both, 1):
            size = buffer.shape[0] // 4
            for side, to in enumerate((step, -step)):
                lengths[to] = size
                messages[to] = buffer.at[pl.ds(2 * side * size, 2 * size)]
    written = {to: set() for to in places}

    def post(to, at, number, value):
        here = range(at, at + 2 * number, 2)
        if written[to].isdisjoint(here):
            messages[to][pl.ds(at, number, 2), :] = value
        else:
            messages[to][pl.ds(at, number, 2), :] += value
        written[to].update(here)

    def put(level, plane, half, even, odd):
        number = (rows >> level) // 2
        low = level < LEVELS - 1 and plane % 2 == 0
        if level > 0 or low:
            even = jnp.where(own_lanes(width, level, low), even, 0.0)
        if level > 0:
            odd = jnp.where(own_lanes(width, level, False), odd, 0.0)
        to = plane // (block >> level)
        at, shift = tables[to][0][level, plane]
        at += half * lengths[to]
        if shift != shift_of(level):
            even, odd = (pltpu.roll(value, shift - shift_of(level), 1) for value in (even, odd))
        post(to, at, number, even)
        post(to, at + 1, number, odd)

    for level in range(LEVELS):
        low, high = spans[level]
        height = total >> level
        half, mine = height // 2, (rows >> level) // 2
        into = lifted[level]

        if level == 0:
            for part, source in enumerate(others):
                step = min(block, max(1, PIECE // rows))
                for x in range(0, block, step):
                    spread_z(source, weights[0], spread, rows, x, step)
                spread_x(block, rows, spread, first[part + 1], low, 0)
        else:
            start, stop = spans[level - 1][0] // 2, spans[level - 1][1] // 2 + 1
            source = coarse[level - 1]
            if level == 1:
                size = (stop - start) * height
                for at in range(0, size, PIECE):
                    end = min(size, at + PIECE)
                    source[at:end, :] = z_product(source[at:end, :], weights[level][...])
            for at in range(0, height, 8):
                planes = {}
                for x in range(start, stop):
                    row = (x - start) * height + at
                    planes[x] = source[row : row + 8, :]
                for x, value in x_lift(planes).items():
                    into[x - low, at : at + 8, :] = value

        for plane in range(low, high + 1):
            odd_plane = plane % 2 == 1
            to = plane // (block >> level)
            goes_on = level < LEVELS - 1 and not odd_plane
            sends = to != 0 and (level, plane) in tables[to][0]
            if not goes_on and not sends:
                continue
            at = plane - low
            split = half % 8 == 0
            if split:
                even, odd = y_lift_split(*even_and_odd([into] if level else first, at))
                even = scaled(even, odd_plane, False)
            else:
                into[at] = y_lift_whole(into[at])
                even = scaled(into[at, pl.ds(0, half, 2), :], odd_plane, False)
            if goes_on:
                row = ((plane - low) // 2) * half
                coarse[level][row : row + half, :] = even
            if not sends:
                continue
            for part in range(halves):
                if split:
                    here_even = even[part * mine : (part + 1) * mine]
                    here_odd = odd[part * mine : (part + 1) * mine]
                else:
                    here_even = into[at, pl.ds(2 * part * mine, mine, 2), :]
                    here_even = scaled(here_even, odd_plane, False)
                    here_odd = into[at, pl.ds(2 * part * mine + 1, mine, 2), :]
                put(level, plane, part, here_even, scaled(here_odd, odd_plane, True))

    for to in places:
        for row in range(halves * lengths[to]):
            if row not in written[to]:
                messages[to][row : row + 1, :] = jnp.zeros((1, width), jnp.float32)
    if shared:
        core = lax.axis_index("gy")
        for step, (target, buffer) in enumerate(zip(passed, both), 1):
            size = lengths[step]
            side = jnp.where(sends_right(step), 0, 2 * size)
            for half in range(2):
                here = side + (core if half == 0 else 1 - core) * size
                target[half * size : (half + 1) * size, :] = buffer[pl.ds(pl.multiple_of(here, 8), size), :]


def rest_kernel(block, rows, width, *refs):
    first, lifted, (out, spare) = refs[: 1 - LEVELS - 2], refs[1 - LEVELS - 2 : -2], refs[-2:]
    for level, (low, _) in enumerate(windows(block)):
        parts = [lifted[level - 1]] if level else first
        spacing, shift = 1 << level, shift_of(level)
        half, mine = sum(part.shape[1] for part in parts) // 2, (rows >> level) // 2
        for plane in range(block >> level):
            odd_plane = plane % 2 == 1
            at = plane - low
            if half % 8 == 0:
                even, odd = y_lift_split(*even_and_odd(parts, at))
                even, odd = even[:mine], odd[:mine]
            else:
                spare[plane] = y_lift_whole(parts[0][at])
                even, odd = spare[plane, pl.ds(0, mine, 2), :], spare[plane, pl.ds(1, mine, 2), :]
            even, odd = scaled(even, odd_plane, False), scaled(odd, odd_plane, True)
            further = level < LEVELS - 1 and not odd_plane
            if level > 0 or further:
                even = jnp.where(own_lanes(width, level, further), even, 0.0)
            x = plane * spacing
            if level == 0:
                out[x, pl.ds(0, mine, 2), :] = even
                out[x, pl.ds(1, mine, 2), :] = odd
                continue
            odd = jnp.where(own_lanes(width, level, False), odd, 0.0)
            if shift:
                even, odd = (pltpu.roll(value, width - shift, 1) for value in (even, odd))
            out[x, pl.ds(0, mine, 2 * spacing), :] += even
            out[x, pl.ds(spacing, mine, 2 * spacing), :] += odd


def additions(block, rows, to, arrived, base, out, clean):
    sent, derived, _ = message(block, rows, to)
    a, b, c, d = STEPS
    width = out.shape[-1]
    lane = lax.broadcasted_iota(jnp.int32, (1, width), 1)
    found_here = []
    for level in sorted({level for level, _ in sent}):
        spacing, height = 1 << level, rows >> level
        shape = (height, width)
        held = {}
        for shift in sorted({shift for (found, _), (_, shift) in sent.items() if found == level}):
            here = {
                plane: at for (found, plane), (at, by) in sent.items() if (found, by) == (level, shift)
            }
            start, stop = min(here.values()), -(-(max(here.values()) + height) // 8) * 8
            source, offset = arrived, base
            if level > 0:
                value = arrived[base + start : base + stop, :]
                if shift:
                    value = pltpu.roll(value, width - shift, 1)
                source, offset = clean[level if shift == shift_of(level) else 0], -start
                source[: stop - start, :] = jnp.where(lax.rem(lane, spacing) == 0, value, 0.0)
            held |= {plane: (source, at + offset) for plane, at in here.items()}

        def read(plane, held=held, height=height):
            source, at = held[plane]
            return source[at : at + height, :]

        def derive(far, near, read=read, shape=shape, spacing=spacing, last=level == LEVELS - 1):
            if near is None:
                value = (d / SCALE**2) * read(far)
            else:
                value = ((1 / c + d) / SCALE**2) * read(far) + (d / SCALE**2) * read(near)
            if last:
                return value
            row = lax.broadcasted_iota(jnp.int32, shape, 0)
            keep = (lax.rem(row, 2) == 1) | lanes_of(width, spacing, True)
            return jnp.where(keep, value, 0.0)

        values = {plane: functools.partial(read, plane) for plane in held}
        for (found, plane), (far, near) in derived.items():
            if found == level:
                values[plane] = functools.partial(derive, far, near)
        for plane, value in values.items():
            x = (plane - to * (block >> level)) * spacing

            def add(x=x, height=height, spacing=spacing, value=value):
                out[x, pl.ds(0, height, spacing), :] += value()

            found_here.append((x, add))
    return found_here


def add_message(*args):
    for _, add in additions(*args):
        add()


def copy_out(out, whole, done, part, parts):
    size = out.shape[0] // parts
    here = pl.ds(part * size, size)
    copy = pltpu.make_async_copy(out.at[here], whole.at[here], done.at[part])
    copy.start()
    return copy


def add_kernel(block, rows, places, last, own, *refs):
    received, refs = refs[: len(places)], refs[len(places) :]
    if last:
        whole, out, done, *clean = refs
    else:
        out, *clean = refs
    out[...] = own[...]
    for to, arrived in zip(places, received):
        add_message(block, rows, to, arrived, 0, out, clean)
    if last:
        for copy in [copy_out(out, whole, done, part, 2) for part in range(2)]:
            copy.wait()


def add_far(block, rows, right, arrived, base, out, clean):
    width, level = out.shape[-1], LEVELS - 1
    spacing, height, shift = 1 << level, rows >> level, shift_of(level)
    length = max(message(block, rows, to)[2] for to in (2, -2))
    lane = lax.broadcasted_iota(jnp.int32, (1, width), 1)
    value = pltpu.roll(arrived[base : base + length, :], width - shift, 1)
    value = jnp.where(lax.rem(lane, spacing) == 0, value, 0.0)
    for to, here in ((2, right), (-2, jnp.logical_not(right))):
        source = clean[0 if to > 0 else level]
        source[:length, :] = jnp.where(here, value, 0.0)
        sent, derived, _ = message(block, rows, to)
        parts = [(plane, at, 1.0) for (_, plane), (at, _) in sent.items()]
        parts += [
            (plane, sent[level, far][0], STEPS[3] / SCALE**2) for (_, plane), (far, _) in derived.items()
        ]
        for plane, at, factor in parts:
            x = (plane - to * (block >> level)) * spacing
            part = source[at : at + height, :]
            out[x, pl.ds(0, height, spacing), :] += part if factor == 1.0 else factor * part


def add_either(block, rows, right, step, arrived, base, out, clean):
    for side, here in ((step, right), (-step, jnp.logical_not(right))):

        @pl.when(here)
        def _():
            add_message(block, rows, side, arrived, base, out, clean)


def keep_kernel(block, rows, own, near, far, out, *clean):
    out[...] = own[...]
    core = lax.axis_index("gy")
    add_either(block, rows, takes_right(1), 1, half_of(near, core), 0, out, clean)
    add_far(block, rows, takes_right(2), half_of(far, core), 0, out, clean)


def half_of(arrived, core):
    size = arrived.shape[0] // 2
    return arrived.at[pl.ds(pl.multiple_of(core * size, 8), size)]


def pack_kernel(near, far, packed):
    one = near.shape[0] // 2
    other = 1 - lax.axis_index("gy")
    packed[:one, :] = half_of(near, other)[...]
    packed[one:, :] = half_of(far, other)[...]


def swap_kernel(block, rows, one, own, packed, whole, out, done, *clean):
    out[...] = own[...]
    add_far(block, rows, jnp.logical_not(takes_right(2)), packed, one, out, clean)
    right = jnp.logical_not(takes_right(1))
    for to, here in ((1, right), (-1, jnp.logical_not(right))):

        @pl.when(here)
        def _():
            tasks = additions(block, rows, to, packed, 0, out, clean)
            copies = []
            for part in ((1, 0) if to > 0 else (0, 1)):
                for x, add in tasks:
                    if 2 * x // block == part:
                        add()
                copies.append(copy_out(out, whole, done, part, 2))
            for copy in copies:
                copy.wait()


def call(body, name, outs, ins, scratch=(), flops=0, hbm_out=()):
    vmem, hbm = pl.BlockSpec(memory_space=pltpu.VMEM), pl.BlockSpec(memory_space=pltpu.HBM)
    f32 = jnp.float32
    shapes = [out if isinstance(out, jax.ShapeDtypeStruct) else jax.ShapeDtypeStruct(out, f32) for out in outs]
    moved = 4 * sum(int(np.prod(shape.shape)) for shape in shapes)
    return pl.pallas_call(
        body,
        out_shape=shapes,
        in_specs=[vmem] * len(ins),
        out_specs=[hbm if n in hbm_out else vmem for n in range(len(outs))],
        scratch_shapes=[pltpu.VMEM(shape, f32) if isinstance(shape, tuple) else shape for shape in scratch],
        compiler_params=pltpu.CompilerParams(vmem_limit_bytes=VMEM_BYTES),
        cost_estimate=pl.CostEstimate(flops=flops, bytes_accessed=2 * moved, transcendentals=0),
        name=name,
    )(*ins)


def local(velocity):
    block, rows, width = velocity.shape
    around, count = lax.axis_size("gx"), lax.axis_size("gy")
    shared = count == 2 and SHARED
    places = places_of(block)
    spans = windows(block)
    total = count * rows

    others = [
        lax.ppermute(velocity, "gy", [(i, (i - k) % count) for i in range(count)])
        for k in range(1, count)
    ]
    lifted = [
        (high - low + 1, total >> level, width) for level, (low, high) in enumerate(spans)
    ]
    coarse = [
        ((high // 2 - low // 2 + 1) * (total >> (level + 1)), width)
        for level, (low, high) in enumerate(spans[:-1])
    ]
    spread = (block * rows, width)
    part = (lifted[0][0], rows, width)
    owned = [(block >> level, rows >> level, width) for level in range(LEVELS)]
    lengths = {to: message(block, rows, to)[2] for to in places}
    one, two = max(lengths[1], lengths[-1]), max(lengths[2], lengths[-2])
    clean = [(one, width)] * LEVELS

    square = jax.ShapeDtypeStruct((2 * width, 3 * width), jnp.bfloat16)
    weights = call(matrix_kernel, "make_matrices", [square] * 2, [], flops=FIRST_FLOPS)
    (first,) = call(
        functools.partial(own_kernel, block, rows),
        "lift_own",
        [part],
        [velocity, weights[0]],
        [spread],
    )
    if shared:
        outs, scratch = ([(many * size, width) for size in (one, two)] for many in (2, 4))
    else:
        outs, scratch = [(lengths[to], width) for to in places], []
    values = call(
        functools.partial(message_kernel, block, rows, width, count, places),
        "make_messages",
        [part] * (count - 1) + lifted[1:] + outs,
        [first] + others + list(weights),
        [spread] + coarse + scratch,
    )
    before, messages = [first, *values[: count + LEVELS - 2]], values[count + LEVELS - 2 :]

    def rest():
        return call(
            functools.partial(rest_kernel, block, rows, width),
            "finish_own",
            [owned[0]],
            before,
            [(block >> LEVELS - 1, total >> LEVELS - 1, width)],
        )[0]

    written = [pltpu.SemaphoreType.DMA((2,))]
    if shared:
        near, far = (
            lax.ppermute(value, ("gx", "gy"), shared_pairs(step, around))
            for step, value in enumerate(messages, 1)
        )
        result = rest()
        (packed,) = call(pack_kernel, "pack_other", [(one + two, width)], [near, far])
        packed = lax.ppermute(packed, "gy", [(0, 1), (1, 0)])
        (result,) = call(
            functools.partial(keep_kernel, block, rows),
            "add_kept",
            [owned[0]],
            [result, near, far],
            clean,
        )
        (whole,) = call(
            functools.partial(swap_kernel, block, rows, one),
            "add_swapped",
            [owned[0]],
            [result, packed],
            [owned[0]] + written + clean,
            hbm_out=(0,),
        )
        return whole

    sent = dict(zip(places, messages))
    received = {
        to: lax.ppermute(sent[to], "gx", [(i, (i + to) % around) for i in range(around)])
        for to in sorted(places, key=lambda to: (to < 0, abs(to)))
    }
    right = [to for to in places if to > 0]
    left = [to for to in places if to < 0]
    (result,) = call(
        functools.partial(add_kernel, block, rows, right, False),
        "add_right",
        [owned[0]],
        [rest()] + [received[to] for to in right],
        clean,
        flops=FIRST_FLOPS,
    )
    (whole,) = call(
        functools.partial(add_kernel, block, rows, left, True),
        "add_left",
        [owned[0]],
        [result] + [received[to] for to in left],
        [owned[0]] + written + clean,
        hbm_out=(0,),
    )
    return whole


def solution(mesh):
    return jax.shard_map(
        local, mesh=mesh, in_specs=(P("gx", "gy", None),), out_specs=P("gx", "gy", None), check_vma=False
    )
```

```python
import functools

import jax
import jax.numpy as jnp
import numpy as np
from jax import lax
from jax.experimental import pallas as pl
from jax.experimental.pallas import tpu as pltpu
from jax.sharding import PartitionSpec as P

LEVELS = 4
STEPS = (-1.586134342, -0.05298011854, 0.8829110762, 0.4435068522)
SCALE = 1.149604398
VMEM_BYTES = 24 * 2**20
FIRST_FLOPS = 10**10
PIECE = 1024
SHARED = True


def windows(block):
    found = []
    first, last = 0, block - 1
    for _ in range(LEVELS):
        low = first - 4 + (first % 2)
        high = last + 4 - (last % 2)
        found.append((low, high))
        first, last = low // 2, high // 2
    return found


def message(block, rows, to):
    sent, derived = {}, {}
    spans = windows(block)
    base = ends = 0
    for level, (low, high) in enumerate(spans):
        size, height = block >> level, rows >> level
        first, last = (0, block - 1) if level == 0 else (v // 2 for v in spans[level - 1])
        planes = [p for p in range(low, high + 1) if p // size == to]
        if planes:
            sign = 1 if to > 0 else -1
            edge = last + 2 - last % 2 if to > 0 else first - 2 + first % 2
            far, near = edge + sign, edge - sign
            if far in planes and edge + 2 * sign in planes:
                derived[level, edge + 2 * sign] = (far, None)
            if far in planes and near in planes:
                derived[level, edge] = (far, near)
        planes = [plane for plane in planes if (level, plane) not in derived]
        at = base
        if level == 1:
            extra = planes[-1] if len(planes) > 3 else None
        elif level > 1 and extra is not None:
            at = base + (rows >> 1)
        for plane in planes:
            if level == 1 and plane == extra:
                sent[level, plane] = base, shift_of(2)
                continue
            sent[level, plane] = at, shift_of(level)
            at += height
        ends = max(ends, at)
        if level == 0:
            base = at
    return sent, derived, -(-ends // 8) * 8


def shift_of(level):
    return (0, 0, 1, 3)[level]


def places_of(block):
    found = set()
    for level, (low, high) in enumerate(windows(block)):
        size = block >> level
        found |= set(range(low // size, high // size + 1))
    return sorted(found - {0})


def in_parts(value):
    parts = []
    for _ in range(3):
        parts.append(value.astype(jnp.bfloat16))
        value = value - parts[-1].astype(jnp.float32)
    return parts


def z_product(value, weights):
    width = value.shape[-1]
    high, middle, low = in_parts(value)

    def dot(left, right, matrix):
        both = jnp.concatenate([left, right], axis=1)
        return jnp.dot(both, matrix, preferred_element_type=jnp.float32)

    large = dot(high, middle, weights[:, : 2 * width])
    small = dot(low, high, weights[:, 2 * width :])
    return large[:, :width] + (large[:, width:] + small)


def lanes_of(width, spacing, parity):
    lane = lax.broadcasted_iota(jnp.int32, (1, width), 1)
    return lax.rem(lane, 2 * spacing) == (spacing if parity else 0)


def own_lanes(width, level, high_only):
    spacing, shift = 1 << level, shift_of(level)
    lane = lax.broadcasted_iota(jnp.int32, (1, width), 1)
    if high_only:
        return lax.rem(lane, 2 * spacing) == spacing + shift
    return lax.rem(lane, spacing) == shift


def z_lift(value, spacing):
    width = value.shape[-1]
    axis = value.ndim - 1
    for step, weight in enumerate(STEPS):
        factor = jnp.where(lanes_of(width, spacing, step % 2 == 0), weight, 0.0)
        around = pltpu.roll(value, spacing, axis) + pltpu.roll(value, width - spacing, axis)
        value = value + factor * around
    return value


def x_lift(planes):
    def plus(one, other):
        return other if one is None else one if other is None else one + other

    planes = dict(planes)
    for step, weight in enumerate(STEPS):
        parity = 1 if step % 2 == 0 else 0
        for index in range(min(planes) - 1, max(planes) + 2):
            if index % 2 == parity:
                around = plus(planes.get(index - 1), planes.get(index + 1))
                if around is not None:
                    planes[index] = plus(planes.get(index), weight * around)
    return planes


def y_lift_split(even, odd):
    count = even.shape[0]
    a, b, c, d = STEPS
    odd = odd + a * (even + pltpu.roll(even, count - 1, 0))
    even = even + b * (pltpu.roll(odd, 1, 0) + odd)
    odd = odd + c * (even + pltpu.roll(even, count - 1, 0))
    even = even + d * (pltpu.roll(odd, 1, 0) + odd)
    return even, odd


def even_and_odd(parts, plane):
    return [
        jnp.concatenate([part[plane, pl.ds(start, part.shape[1] // 2, 2), :] for part in parts])
        for start in (0, 1)
    ]


def y_lift_whole(value):
    count = value.shape[0]
    row = lax.broadcasted_iota(jnp.int32, (count, 1), 0)
    for step, weight in enumerate(STEPS):
        factor = jnp.where(lax.rem(row, 2) == (1 if step % 2 == 0 else 0), weight, 0.0)
        value = value + factor * (pltpu.roll(value, 1, 0) + pltpu.roll(value, count - 1, 0))
    return value


def scaled_z(value, spacing):
    width = value.shape[-1]
    odd, even = lanes_of(width, spacing, True), lanes_of(width, spacing, False)
    return value * jnp.where(odd, SCALE, jnp.where(even, 1 / SCALE, 0.0))


def scaled(value, x_odd, y_odd):
    at = (SCALE if x_odd else 1 / SCALE) * (SCALE if y_odd else 1 / SCALE)
    return value if x_odd != y_odd else value * at


def spread_z(source, weights, spread, rows, start, size):
    width = source.shape[-1]
    value = source[start : start + size].reshape(size * rows, width)
    spread[start * rows : (start + size) * rows, :] = z_product(value, weights[...])


def spread_x(block, rows, spread, into, low, base):
    for at in range(0, rows, 8):
        planes = {x: spread[x * rows + at : x * rows + at + 8, :] for x in range(block)}
        for x, value in x_lift(planes).items():
            into[x - low, base + at : base + at + 8, :] = value


def matrix_kernel(*weights):
    width = weights[0].shape[0] // 2
    row = lax.broadcasted_iota(jnp.int32, (width, width), 0)
    lane = lax.broadcasted_iota(jnp.int32, (width, width), 1)
    value = jnp.where(row == lane, 1.0, 0.0)
    full = [scaled_z(z_lift(value, 1), 1), jnp.zeros((width, width), jnp.float32)]
    for level in range(1, LEVELS):
        spacing = 1 << level
        value = scaled_z(z_lift(value, spacing), spacing)
        full[1] += pltpu.roll(value, shift_of(level), 1) if shift_of(level) else value
        value = jnp.where(lanes_of(width, spacing, False), value, 0.0)
    for weight, matrix in zip(weights, full):
        high, middle, low = in_parts(matrix)
        for at, column in enumerate(((high, middle), (middle, high), (high, low))):
            for row, part in enumerate(column):
                weight[row * width : (row + 1) * width, at * width : (at + 1) * width] = part


def own_kernel(block, rows, velocity, weights, into, spread):
    step = max(1, min(block, PIECE // rows))
    for x in range(0, block, step):
        spread_z(velocity, weights, spread, rows, x, step)
    spread_x(block, rows, spread, into, windows(block)[0][0], 0)


def right_source(step, place, last):
    return place == last if step == 1 else (place == 0) | (place == last - 1)


def right_target(step, place):
    return (place == 0) & (step == 1)


def sends_right(step):
    core = lax.axis_index("gy") == 1
    return core == right_source(step, lax.axis_index("gx"), lax.axis_size("gx") - 1)


def takes_right(step):
    core = lax.axis_index("gy") == 1
    return core == right_target(step, lax.axis_index("gx"))


def shared_pairs(step, around):
    pairs = []
    for place in range(around):
        to, back = (place + step) % around, (place - step) % around
        source = int(right_source(step, place, around - 1))
        pairs.append((2 * place + source, 2 * to + int(right_target(step, to))))
        pairs.append((2 * place + 1 - source, 2 * back + 1 - int(right_target(step, back))))
    return pairs


def message_kernel(block, rows, width, count, places, *refs):
    refs = list(refs)

    def take(number):
        taken = refs[:number]
        del refs[:number]
        return taken

    shared = count == 2 and SHARED
    halves = 2 if shared else 1
    first = take(1)
    others = take(count - 1)
    weights = take(2)
    first += take(count - 1)
    lifted = [None] + take(LEVELS - 1)
    passed = take(2 if shared else len(places))
    (spread,) = take(1)
    coarse = take(LEVELS - 1)
    both = take(2) if shared else []
    messages = dict(zip(places, passed))
    spans = windows(block)
    total = count * rows
    tables = {to: message(block, rows, to) for to in places}
    lengths = {to: message(block, rows, to)[2] for to in places}
    if shared:
        for step, buffer in enumerate(both, 1):
            size = buffer.shape[0] // 4
            for side, to in enumerate((step, -step)):
                lengths[to] = size
                messages[to] = buffer.at[pl.ds(2 * side * size, 2 * size)]
    written = {to: set() for to in places}

    def post(to, at, number, value):
        here = range(at, at + 2 * number, 2)
        if written[to].isdisjoint(here):
            messages[to][pl.ds(at, number, 2), :] = value
        else:
            messages[to][pl.ds(at, number, 2), :] += value
        written[to].update(here)

    def put(level, plane, half, even, odd):
        number = (rows >> level) // 2
        low = level < LEVELS - 1 and plane % 2 == 0
        if level > 0 or low:
            even = jnp.where(own_lanes(width, level, low), even, 0.0)
        if level > 0:
            odd = jnp.where(own_lanes(width, level, False), odd, 0.0)
        to = plane // (block >> level)
        at, shift = tables[to][0][level, plane]
        at += half * lengths[to]
        if shift != shift_of(level):
            even, odd = (pltpu.roll(value, shift - shift_of(level), 1) for value in (even, odd))
        post(to, at, number, even)
        post(to, at + 1, number, odd)

    for level in range(LEVELS):
        low, high = spans[level]
        height = total >> level
        half, mine = height // 2, (rows >> level) // 2
        into = lifted[level]

        if level == 0:
            for part, source in enumerate(others):
                step = min(block, max(1, PIECE // rows))
                for x in range(0, block, step):
                    spread_z(source, weights[0], spread, rows, x, step)
                spread_x(block, rows, spread, first[part + 1], low, 0)
        else:
            start, stop = spans[level - 1][0] // 2, spans[level - 1][1] // 2 + 1
            source = coarse[level - 1]
            if level == 1:
                size = (stop - start) * height
                for at in range(0, size, PIECE):
                    end = min(size, at + PIECE)
                    source[at:end, :] = z_product(source[at:end, :], weights[level][...])
            for at in range(0, height, 8):
                planes = {}
                for x in range(start, stop):
                    row = (x - start) * height + at
                    planes[x] = source[row : row + 8, :]
                for x, value in x_lift(planes).items():
                    into[x - low, at : at + 8, :] = value

        for plane in range(low, high + 1):
            odd_plane = plane % 2 == 1
            to = plane // (block >> level)
            goes_on = level < LEVELS - 1 and not odd_plane
            sends = to != 0 and (level, plane) in tables[to][0]
            if not goes_on and not sends:
                continue
            at = plane - low
            split = half % 8 == 0
            if split:
                even, odd = y_lift_split(*even_and_odd([into] if level else first, at))
                even = scaled(even, odd_plane, False)
            else:
                into[at] = y_lift_whole(into[at])
                even = scaled(into[at, pl.ds(0, half, 2), :], odd_plane, False)
            if goes_on:
                row = ((plane - low) // 2) * half
                coarse[level][row : row + half, :] = even
            if not sends:
                continue
            for part in range(halves):
                if split:
                    here_even = even[part * mine : (part + 1) * mine]
                    here_odd = odd[part * mine : (part + 1) * mine]
                else:
                    here_even = into[at, pl.ds(2 * part * mine, mine, 2), :]
                    here_even = scaled(here_even, odd_plane, False)
                    here_odd = into[at, pl.ds(2 * part * mine + 1, mine, 2), :]
                put(level, plane, part, here_even, scaled(here_odd, odd_plane, True))

    for to in places:
        for row in range(halves * lengths[to]):
            if row not in written[to]:
                messages[to][row : row + 1, :] = jnp.zeros((1, width), jnp.float32)
    if shared:
        core = lax.axis_index("gy")
        for step, (target, buffer) in enumerate(zip(passed, both), 1):
            size = lengths[step]
            side = jnp.where(sends_right(step), 0, 2 * size)
            for half in range(2):
                here = side + (core if half == 0 else 1 - core) * size
                target[half * size : (half + 1) * size, :] = buffer[pl.ds(pl.multiple_of(here, 8), size), :]


def rest_kernel(block, rows, width, *refs):
    first, lifted, (out, spare) = refs[: 1 - LEVELS - 2], refs[1 - LEVELS - 2 : -2], refs[-2:]
    for level, (low, _) in enumerate(windows(block)):
        parts = [lifted[level - 1]] if level else first
        spacing, shift = 1 << level, shift_of(level)
        half, mine = sum(part.shape[1] for part in parts) // 2, (rows >> level) // 2
        for plane in range(block >> level):
            odd_plane = plane % 2 == 1
            at = plane - low
            if half % 8 == 0:
                even, odd = y_lift_split(*even_and_odd(parts, at))
                even, odd = even[:mine], odd[:mine]
            else:
                spare[plane] = y_lift_whole(parts[0][at])
                even, odd = spare[plane, pl.ds(0, mine, 2), :], spare[plane, pl.ds(1, mine, 2), :]
            even, odd = scaled(even, odd_plane, False), scaled(odd, odd_plane, True)
            further = level < LEVELS - 1 and not odd_plane
            if level > 0 or further:
                even = jnp.where(own_lanes(width, level, further), even, 0.0)
            x = plane * spacing
            if level == 0:
                out[x, pl.ds(0, mine, 2), :] = even
                out[x, pl.ds(1, mine, 2), :] = odd
                continue
            odd = jnp.where(own_lanes(width, level, False), odd, 0.0)
            if shift:
                even, odd = (pltpu.roll(value, width - shift, 1) for value in (even, odd))
            out[x, pl.ds(0, mine, 2 * spacing), :] += even
            out[x, pl.ds(spacing, mine, 2 * spacing), :] += odd


def additions(block, rows, to, arrived, base, out, clean):
    sent, derived, _ = message(block, rows, to)
    a, b, c, d = STEPS
    width = out.shape[-1]
    lane = lax.broadcasted_iota(jnp.int32, (1, width), 1)
    found_here = []
    for level in sorted({level for level, _ in sent}):
        spacing, height = 1 << level, rows >> level
        shape = (height, width)
        held = {}
        for shift in sorted({shift for (found, _), (_, shift) in sent.items() if found == level}):
            here = {
                plane: at for (found, plane), (at, by) in sent.items() if (found, by) == (level, shift)
            }
            start, stop = min(here.values()), -(-(max(here.values()) + height) // 8) * 8
            source, offset = arrived, base
            if level > 0:
                value = arrived[base + start : base + stop, :]
                if shift:
                    value = pltpu.roll(value, width - shift, 1)
                source, offset = clean[level if shift == shift_of(level) else 0], -start
                source[: stop - start, :] = jnp.where(lax.rem(lane, spacing) == 0, value, 0.0)
            held |= {plane: (source, at + offset) for plane, at in here.items()}

        def read(plane, held=held, height=height):
            source, at = held[plane]
            return source[at : at + height, :]

        def derive(far, near, read=read, shape=shape, spacing=spacing, last=level == LEVELS - 1):
            if near is None:
                value = (d / SCALE**2) * read(far)
            else:
                value = ((1 / c + d) / SCALE**2) * read(far) + (d / SCALE**2) * read(near)
            if last:
                return value
            row = lax.broadcasted_iota(jnp.int32, shape, 0)
            keep = (lax.rem(row, 2) == 1) | lanes_of(width, spacing, True)
            return jnp.where(keep, value, 0.0)

        values = {plane: functools.partial(read, plane) for plane in held}
        for (found, plane), (far, near) in derived.items():
            if found == level:
                values[plane] = functools.partial(derive, far, near)
        for plane, value in values.items():
            x = (plane - to * (block >> level)) * spacing

            def add(x=x, height=height, spacing=spacing, value=value):
                out[x, pl.ds(0, height, spacing), :] += value()

            found_here.append((x, add))
    return found_here


def add_message(*args):
    for _, add in additions(*args):
        add()


def copy_out(out, whole, done, part, parts):
    size = out.shape[0] // parts
    here = pl.ds(part * size, size)
    copy = pltpu.make_async_copy(out.at[here], whole.at[here], done.at[part])
    copy.start(priority=part)
    return copy


def add_kernel(block, rows, places, last, own, *refs):
    received, refs = refs[: len(places)], refs[len(places) :]
    if last:
        whole, out, done, *clean = refs
    else:
        out, *clean = refs
    out[...] = own[...]
    for to, arrived in zip(places, received):
        add_message(block, rows, to, arrived, 0, out, clean)
    if last:
        for copy in [copy_out(out, whole, done, part, 2) for part in range(2)]:
            copy.wait()


def add_far(block, rows, right, arrived, base, out, clean):
    width, level = out.shape[-1], LEVELS - 1
    spacing, height, shift = 1 << level, rows >> level, shift_of(level)
    length = max(message(block, rows, to)[2] for to in (2, -2))
    lane = lax.broadcasted_iota(jnp.int32, (1, width), 1)
    value = pltpu.roll(arrived[base : base + length, :], width - shift, 1)
    value = jnp.where(lax.rem(lane, spacing) == 0, value, 0.0)
    for to, here in ((2, right), (-2, jnp.logical_not(right))):
        source = clean[0 if to > 0 else level]
        source[:length, :] = jnp.where(here, value, 0.0)
        sent, derived, _ = message(block, rows, to)
        parts = [(plane, at, 1.0) for (_, plane), (at, _) in sent.items()]
        parts += [
            (plane, sent[level, far][0], STEPS[3] / SCALE**2) for (_, plane), (far, _) in derived.items()
        ]
        for plane, at, factor in parts:
            x = (plane - to * (block >> level)) * spacing
            part = source[at : at + height, :]
            out[x, pl.ds(0, height, spacing), :] += part if factor == 1.0 else factor * part


def add_either(block, rows, right, step, arrived, base, out, clean):
    for side, here in ((step, right), (-step, jnp.logical_not(right))):

        @pl.when(here)
        def _():
            add_message(block, rows, side, arrived, base, out, clean)


def keep_kernel(block, rows, own, near, far, out, *clean):
    out[...] = own[...]
    core = lax.axis_index("gy")
    add_either(block, rows, takes_right(1), 1, half_of(near, core), 0, out, clean)
    add_far(block, rows, takes_right(2), half_of(far, core), 0, out, clean)


def half_of(arrived, core):
    size = arrived.shape[0] // 2
    return arrived.at[pl.ds(pl.multiple_of(core * size, 8), size)]


def pack_kernel(near, far, packed):
    one = near.shape[0] // 2
    other = 1 - lax.axis_index("gy")
    packed[:one, :] = half_of(near, other)[...]
    packed[one:, :] = half_of(far, other)[...]


def swap_kernel(block, rows, one, own, packed, whole, out, done, *clean):
    out[...] = own[...]
    add_far(block, rows, jnp.logical_not(takes_right(2)), packed, one, out, clean)
    right = jnp.logical_not(takes_right(1))
    for to, here in ((1, right), (-1, jnp.logical_not(right))):

        @pl.when(here)
        def _():
            tasks = additions(block, rows, to, packed, 0, out, clean)
            copies = []
            for part in ((1, 0) if to > 0 else (0, 1)):
                for x, add in tasks:
                    if 2 * x // block == part:
                        add()
                copies.append(copy_out(out, whole, done, part, 2))
            for copy in copies:
                copy.wait()


def call(body, name, outs, ins, scratch=(), flops=0, hbm_out=()):
    vmem, hbm = pl.BlockSpec(memory_space=pltpu.VMEM), pl.BlockSpec(memory_space=pltpu.HBM)
    f32 = jnp.float32
    shapes = [out if isinstance(out, jax.ShapeDtypeStruct) else jax.ShapeDtypeStruct(out, f32) for out in outs]
    moved = 4 * sum(int(np.prod(shape.shape)) for shape in shapes)
    return pl.pallas_call(
        body,
        out_shape=shapes,
        in_specs=[vmem] * len(ins),
        out_specs=[hbm if n in hbm_out else vmem for n in range(len(outs))],
        scratch_shapes=[pltpu.VMEM(shape, f32) if isinstance(shape, tuple) else shape for shape in scratch],
        compiler_params=pltpu.CompilerParams(vmem_limit_bytes=VMEM_BYTES),
        cost_estimate=pl.CostEstimate(flops=flops, bytes_accessed=2 * moved, transcendentals=0),
        name=name,
    )(*ins)


def local(velocity):
    block, rows, width = velocity.shape
    around, count = lax.axis_size("gx"), lax.axis_size("gy")
    shared = count == 2 and SHARED
    places = places_of(block)
    spans = windows(block)
    total = count * rows

    others = [
        lax.ppermute(velocity, "gy", [(i, (i - k) % count) for i in range(count)])
        for k in range(1, count)
    ]
    lifted = [
        (high - low + 1, total >> level, width) for level, (low, high) in enumerate(spans)
    ]
    coarse = [
        ((high // 2 - low // 2 + 1) * (total >> (level + 1)), width)
        for level, (low, high) in enumerate(spans[:-1])
    ]
    spread = (block * rows, width)
    part = (lifted[0][0], rows, width)
    owned = [(block >> level, rows >> level, width) for level in range(LEVELS)]
    lengths = {to: message(block, rows, to)[2] for to in places}
    one, two = max(lengths[1], lengths[-1]), max(lengths[2], lengths[-2])
    clean = [(one, width)] * LEVELS

    square = jax.ShapeDtypeStruct((2 * width, 3 * width), jnp.bfloat16)
    weights = call(matrix_kernel, "make_matrices", [square] * 2, [], flops=FIRST_FLOPS)
    (first,) = call(
        functools.partial(own_kernel, block, rows),
        "lift_own",
        [part],
        [velocity, weights[0]],
        [spread],
    )
    if shared:
        outs, scratch = ([(many * size, width) for size in (one, two)] for many in (2, 4))
    else:
        outs, scratch = [(lengths[to], width) for to in places], []
    values = call(
        functools.partial(message_kernel, block, rows, width, count, places),
        "make_messages",
        [part] * (count - 1) + lifted[1:] + outs,
        [first] + others + list(weights),
        [spread] + coarse + scratch,
    )
    before, messages = [first, *values[: count + LEVELS - 2]], values[count + LEVELS - 2 :]

    def rest():
        return call(
            functools.partial(rest_kernel, block, rows, width),
            "finish_own",
            [owned[0]],
            before,
            [(block >> LEVELS - 1, total >> LEVELS - 1, width)],
        )[0]

    written = [pltpu.SemaphoreType.DMA((2,))]
    if shared:
        near, far = (
            lax.ppermute(value, ("gx", "gy"), shared_pairs(step, around))
            for step, value in enumerate(messages, 1)
        )
        result = rest()
        (packed,) = call(pack_kernel, "pack_other", [(one + two, width)], [near, far])
        packed = lax.ppermute(packed, "gy", [(0, 1), (1, 0)])
        (result,) = call(
            functools.partial(keep_kernel, block, rows),
            "add_kept",
            [owned[0]],
            [result, near, far],
            clean,
        )
        (whole,) = call(
            functools.partial(swap_kernel, block, rows, one),
            "add_swapped",
            [owned[0]],
            [result, packed],
            [owned[0]] + written + clean,
            hbm_out=(0,),
        )
        return whole

    sent = dict(zip(places, messages))
    received = {
        to: lax.ppermute(sent[to], "gx", [(i, (i + to) % around) for i in range(around)])
        for to in sorted(places, key=lambda to: (to < 0, abs(to)))
    }
    right = [to for to in places if to > 0]
    left = [to for to in places if to < 0]
    (result,) = call(
        functools.partial(add_kernel, block, rows, right, False),
        "add_right",
        [owned[0]],
        [rest()] + [received[to] for to in right],
        clean,
        flops=FIRST_FLOPS,
    )
    (whole,) = call(
        functools.partial(add_kernel, block, rows, left, True),
        "add_left",
        [owned[0]],
        [result] + [received[to] for to in left],
        [owned[0]] + written + clean,
        hbm_out=(0,),
    )
    return whole


def solution(mesh):
    return jax.shard_map(
        local, mesh=mesh, in_specs=(P("gx", "gy", None),), out_specs=P("gx", "gy", None), check_vma=False
    )
```

```python
import functools

import jax
import jax.numpy as jnp
import numpy as np
from jax import lax
from jax.experimental import pallas as pl
from jax.experimental.pallas import tpu as pltpu
from jax.sharding import PartitionSpec as P

LEVELS = 4
STEPS = (-1.586134342, -0.05298011854, 0.8829110762, 0.4435068522)
SCALE = 1.149604398
VMEM_BYTES = 24 * 2**20
FIRST_FLOPS = 10**10
PIECE = 256
SHARED = True


def windows(block):
    found = []
    first, last = 0, block - 1
    for _ in range(LEVELS):
        low = first - 4 + (first % 2)
        high = last + 4 - (last % 2)
        found.append((low, high))
        first, last = low // 2, high // 2
    return found


def message(block, rows, to):
    sent, derived = {}, {}
    spans = windows(block)
    base = ends = 0
    for level, (low, high) in enumerate(spans):
        size, height = block >> level, rows >> level
        first, last = (0, block - 1) if level == 0 else (v // 2 for v in spans[level - 1])
        planes = [p for p in range(low, high + 1) if p // size == to]
        if planes:
            sign = 1 if to > 0 else -1
            edge = last + 2 - last % 2 if to > 0 else first - 2 + first % 2
            far, near = edge + sign, edge - sign
            if far in planes and edge + 2 * sign in planes:
                derived[level, edge + 2 * sign] = (far, None)
            if far in planes and near in planes:
                derived[level, edge] = (far, near)
        planes = [plane for plane in planes if (level, plane) not in derived]
        at = base
        if level == 1:
            extra = planes[-1] if len(planes) > 3 else None
        elif level > 1 and extra is not None:
            at = base + (rows >> 1)
        for plane in planes:
            if level == 1 and plane == extra:
                sent[level, plane] = base, shift_of(2)
                continue
            sent[level, plane] = at, shift_of(level)
            at += height
        ends = max(ends, at)
        if level == 0:
            base = at
    return sent, derived, -(-ends // 8) * 8


def shift_of(level):
    return (0, 0, 1, 3)[level]


def places_of(block):
    found = set()
    for level, (low, high) in enumerate(windows(block)):
        size = block >> level
        found |= set(range(low // size, high // size + 1))
    return sorted(found - {0})


def in_parts(value):
    parts = []
    for _ in range(3):
        parts.append(value.astype(jnp.bfloat16))
        value = value - parts[-1].astype(jnp.float32)
    return parts


def z_product(value, weights):
    width = value.shape[-1]
    high, middle, low = in_parts(value)

    def dot(left, right, matrix):
        both = jnp.concatenate([left, right], axis=1)
        return jnp.dot(both, matrix, preferred_element_type=jnp.float32)

    large = dot(high, middle, weights[:, : 2 * width])
    small = dot(low, high, weights[:, 2 * width :])
    return large[:, :width] + (large[:, width:] + small)


def lanes_of(width, spacing, parity):
    lane = lax.broadcasted_iota(jnp.int32, (1, width), 1)
    return lax.rem(lane, 2 * spacing) == (spacing if parity else 0)


def own_lanes(width, level, high_only):
    spacing, shift = 1 << level, shift_of(level)
    lane = lax.broadcasted_iota(jnp.int32, (1, width), 1)
    if high_only:
        return lax.rem(lane, 2 * spacing) == spacing + shift
    return lax.rem(lane, spacing) == shift


def z_lift(value, spacing):
    width = value.shape[-1]
    axis = value.ndim - 1
    for step, weight in enumerate(STEPS):
        factor = jnp.where(lanes_of(width, spacing, step % 2 == 0), weight, 0.0)
        around = pltpu.roll(value, spacing, axis) + pltpu.roll(value, width - spacing, axis)
        value = value + factor * around
    return value


def x_lift(planes):
    def plus(one, other):
        return other if one is None else one if other is None else one + other

    planes = dict(planes)
    for step, weight in enumerate(STEPS):
        parity = 1 if step % 2 == 0 else 0
        for index in range(min(planes) - 1, max(planes) + 2):
            if index % 2 == parity:
                around = plus(planes.get(index - 1), planes.get(index + 1))
                if around is not None:
                    planes[index] = plus(planes.get(index), weight * around)
    return planes


def y_lift_split(even, odd):
    count = even.shape[0]
    a, b, c, d = STEPS
    odd = odd + a * (even + pltpu.roll(even, count - 1, 0))
    even = even + b * (pltpu.roll(odd, 1, 0) + odd)
    odd = odd + c * (even + pltpu.roll(even, count - 1, 0))
    even = even + d * (pltpu.roll(odd, 1, 0) + odd)
    return even, odd


def even_and_odd(parts, plane):
    return [
        jnp.concatenate([part[plane, pl.ds(start, part.shape[1] // 2, 2), :] for part in parts])
        for start in (0, 1)
    ]


def y_lift_whole(value):
    count = value.shape[0]
    row = lax.broadcasted_iota(jnp.int32, (count, 1), 0)
    for step, weight in enumerate(STEPS):
        factor = jnp.where(lax.rem(row, 2) == (1 if step % 2 == 0 else 0), weight, 0.0)
        value = value + factor * (pltpu.roll(value, 1, 0) + pltpu.roll(value, count - 1, 0))
    return value


def scaled_z(value, spacing):
    width = value.shape[-1]
    odd, even = lanes_of(width, spacing, True), lanes_of(width, spacing, False)
    return value * jnp.where(odd, SCALE, jnp.where(even, 1 / SCALE, 0.0))


def scaled(value, x_odd, y_odd):
    at = (SCALE if x_odd else 1 / SCALE) * (SCALE if y_odd else 1 / SCALE)
    return value if x_odd != y_odd else value * at


def spread_z(source, weights, spread, rows, start, size):
    width = source.shape[-1]
    value = source[start : start + size].reshape(size * rows, width)
    spread[start * rows : (start + size) * rows, :] = z_product(value, weights[...])


def spread_x(block, rows, spread, into, low, base):
    for at in range(0, rows, 8):
        planes = {x: spread[x * rows + at : x * rows + at + 8, :] for x in range(block)}
        for x, value in x_lift(planes).items():
            into[x - low, base + at : base + at + 8, :] = value


def matrix_kernel(*weights):
    width = weights[0].shape[0] // 2
    row = lax.broadcasted_iota(jnp.int32, (width, width), 0)
    lane = lax.broadcasted_iota(jnp.int32, (width, width), 1)
    value = jnp.where(row == lane, 1.0, 0.0)
    full = [scaled_z(z_lift(value, 1), 1), jnp.zeros((width, width), jnp.float32)]
    for level in range(1, LEVELS):
        spacing = 1 << level
        value = scaled_z(z_lift(value, spacing), spacing)
        full[1] += pltpu.roll(value, shift_of(level), 1) if shift_of(level) else value
        value = jnp.where(lanes_of(width, spacing, False), value, 0.0)
    for weight, matrix in zip(weights, full):
        high, middle, low = in_parts(matrix)
        for at, column in enumerate(((high, middle), (middle, high), (high, low))):
            for row, part in enumerate(column):
                weight[row * width : (row + 1) * width, at * width : (at + 1) * width] = part


def own_kernel(block, rows, velocity, weights, into, spread):
    step = max(1, min(block, PIECE // rows))
    for x in range(0, block, step):
        spread_z(velocity, weights, spread, rows, x, step)
    spread_x(block, rows, spread, into, windows(block)[0][0], 0)


def right_source(step, place, last):
    return place == last if step == 1 else (place == 0) | (place == last - 1)


def right_target(step, place):
    return (place == 0) & (step == 1)


def sends_right(step):
    core = lax.axis_index("gy") == 1
    return core == right_source(step, lax.axis_index("gx"), lax.axis_size("gx") - 1)


def takes_right(step):
    core = lax.axis_index("gy") == 1
    return core == right_target(step, lax.axis_index("gx"))


def shared_pairs(step, around):
    pairs = []
    for place in range(around):
        to, back = (place + step) % around, (place - step) % around
        source = int(right_source(step, place, around - 1))
        pairs.append((2 * place + source, 2 * to + int(right_target(step, to))))
        pairs.append((2 * place + 1 - source, 2 * back + 1 - int(right_target(step, back))))
    return pairs


def message_kernel(block, rows, width, count, places, *refs):
    refs = list(refs)

    def take(number):
        taken = refs[:number]
        del refs[:number]
        return taken

    shared = count == 2 and SHARED
    halves = 2 if shared else 1
    first = take(1)
    others = take(count - 1)
    weights = take(2)
    first += take(count - 1)
    lifted = [None] + take(LEVELS - 1)
    passed = take(2 if shared else len(places))
    (spread,) = take(1)
    coarse = take(LEVELS - 1)
    both = take(2) if shared else []
    messages = dict(zip(places, passed))
    spans = windows(block)
    total = count * rows
    tables = {to: message(block, rows, to) for to in places}
    lengths = {to: message(block, rows, to)[2] for to in places}
    if shared:
        for step, buffer in enumerate(both, 1):
            size = buffer.shape[0] // 4
            for side, to in enumerate((step, -step)):
                lengths[to] = size
                messages[to] = buffer.at[pl.ds(2 * side * size, 2 * size)]
    written = {to: set() for to in places}

    def post(to, at, number, value):
        here = range(at, at + 2 * number, 2)
        if written[to].isdisjoint(here):
            messages[to][pl.ds(at, number, 2), :] = value
        else:
            messages[to][pl.ds(at, number, 2), :] += value
        written[to].update(here)

    def put(level, plane, half, even, odd):
        number = (rows >> level) // 2
        low = level < LEVELS - 1 and plane % 2 == 0
        if level > 0 or low:
            even = jnp.where(own_lanes(width, level, low), even, 0.0)
        if level > 0:
            odd = jnp.where(own_lanes(width, level, False), odd, 0.0)
        to = plane // (block >> level)
        at, shift = tables[to][0][level, plane]
        at += half * lengths[to]
        if shift != shift_of(level):
            even, odd = (pltpu.roll(value, shift - shift_of(level), 1) for value in (even, odd))
        post(to, at, number, even)
        post(to, at + 1, number, odd)

    for level in range(LEVELS):
        low, high = spans[level]
        height = total >> level
        half, mine = height // 2, (rows >> level) // 2
        into = lifted[level]

        if level == 0:
            for part, source in enumerate(others):
                step = min(block, max(1, PIECE // rows))
                for x in range(0, block, step):
                    spread_z(source, weights[0], spread, rows, x, step)
                spread_x(block, rows, spread, first[part + 1], low, 0)
        else:
            start, stop = spans[level - 1][0] // 2, spans[level - 1][1] // 2 + 1
            source = coarse[level - 1]
            if level == 1:
                size = (stop - start) * height
                for at in range(0, size, PIECE):
                    end = min(size, at + PIECE)
                    source[at:end, :] = z_product(source[at:end, :], weights[level][...])
            for at in range(0, height, 8):
                planes = {}
                for x in range(start, stop):
                    row = (x - start) * height + at
                    planes[x] = source[row : row + 8, :]
                for x, value in x_lift(planes).items():
                    into[x - low, at : at + 8, :] = value

        for plane in range(low, high + 1):
            odd_plane = plane % 2 == 1
            to = plane // (block >> level)
            goes_on = level < LEVELS - 1 and not odd_plane
            sends = to != 0 and (level, plane) in tables[to][0]
            if not goes_on and not sends:
                continue
            at = plane - low
            split = half % 8 == 0
            if split:
                even, odd = y_lift_split(*even_and_odd([into] if level else first, at))
                even = scaled(even, odd_plane, False)
            else:
                into[at] = y_lift_whole(into[at])
                even = scaled(into[at, pl.ds(0, half, 2), :], odd_plane, False)
            if goes_on:
                row = ((plane - low) // 2) * half
                coarse[level][row : row + half, :] = even
            if not sends:
                continue
            for part in range(halves):
                if split:
                    here_even = even[part * mine : (part + 1) * mine]
                    here_odd = odd[part * mine : (part + 1) * mine]
                else:
                    here_even = into[at, pl.ds(2 * part * mine, mine, 2), :]
                    here_even = scaled(here_even, odd_plane, False)
                    here_odd = into[at, pl.ds(2 * part * mine + 1, mine, 2), :]
                put(level, plane, part, here_even, scaled(here_odd, odd_plane, True))

    for to in places:
        for row in range(halves * lengths[to]):
            if row not in written[to]:
                messages[to][row : row + 1, :] = jnp.zeros((1, width), jnp.float32)
    if shared:
        core = lax.axis_index("gy")
        for step, (target, buffer) in enumerate(zip(passed, both), 1):
            size = lengths[step]
            side = jnp.where(sends_right(step), 0, 2 * size)
            for half in range(2):
                here = side + (core if half == 0 else 1 - core) * size
                target[half * size : (half + 1) * size, :] = buffer[pl.ds(pl.multiple_of(here, 8), size), :]


def rest_kernel(block, rows, width, *refs):
    first, lifted, (out, spare) = refs[: 1 - LEVELS - 2], refs[1 - LEVELS - 2 : -2], refs[-2:]
    for level, (low, _) in enumerate(windows(block)):
        parts = [lifted[level - 1]] if level else first
        spacing, shift = 1 << level, shift_of(level)
        half, mine = sum(part.shape[1] for part in parts) // 2, (rows >> level) // 2
        for plane in range(block >> level):
            odd_plane = plane % 2 == 1
            at = plane - low
            if half % 8 == 0:
                even, odd = y_lift_split(*even_and_odd(parts, at))
                even, odd = even[:mine], odd[:mine]
            else:
                spare[plane] = y_lift_whole(parts[0][at])
                even, odd = spare[plane, pl.ds(0, mine, 2), :], spare[plane, pl.ds(1, mine, 2), :]
            even, odd = scaled(even, odd_plane, False), scaled(odd, odd_plane, True)
            further = level < LEVELS - 1 and not odd_plane
            if level > 0 or further:
                even = jnp.where(own_lanes(width, level, further), even, 0.0)
            x = plane * spacing
            if level == 0:
                out[x, pl.ds(0, mine, 2), :] = even
                out[x, pl.ds(1, mine, 2), :] = odd
                continue
            odd = jnp.where(own_lanes(width, level, False), odd, 0.0)
            if shift:
                even, odd = (pltpu.roll(value, width - shift, 1) for value in (even, odd))
            out[x, pl.ds(0, mine, 2 * spacing), :] += even
            out[x, pl.ds(spacing, mine, 2 * spacing), :] += odd


def additions(block, rows, to, arrived, base, out, clean):
    sent, derived, _ = message(block, rows, to)
    a, b, c, d = STEPS
    width = out.shape[-1]
    lane = lax.broadcasted_iota(jnp.int32, (1, width), 1)
    found_here = []
    for level in sorted({level for level, _ in sent}):
        spacing, height = 1 << level, rows >> level
        shape = (height, width)
        held = {}
        for shift in sorted({shift for (found, _), (_, shift) in sent.items() if found == level}):
            here = {
                plane: at for (found, plane), (at, by) in sent.items() if (found, by) == (level, shift)
            }
            start, stop = min(here.values()), -(-(max(here.values()) + height) // 8) * 8
            source, offset = arrived, base
            if level > 0:
                value = arrived[base + start : base + stop, :]
                if shift:
                    value = pltpu.roll(value, width - shift, 1)
                source, offset = clean[level if shift == shift_of(level) else 0], -start
                source[: stop - start, :] = jnp.where(lax.rem(lane, spacing) == 0, value, 0.0)
            held |= {plane: (source, at + offset) for plane, at in here.items()}

        def read(plane, held=held, height=height):
            source, at = held[plane]
            return source[at : at + height, :]

        def derive(far, near, read=read, shape=shape, spacing=spacing, last=level == LEVELS - 1):
            if near is None:
                value = (d / SCALE**2) * read(far)
            else:
                value = ((1 / c + d) / SCALE**2) * read(far) + (d / SCALE**2) * read(near)
            if last:
                return value
            row = lax.broadcasted_iota(jnp.int32, shape, 0)
            keep = (lax.rem(row, 2) == 1) | lanes_of(width, spacing, True)
            return jnp.where(keep, value, 0.0)

        values = {plane: functools.partial(read, plane) for plane in held}
        for (found, plane), (far, near) in derived.items():
            if found == level:
                values[plane] = functools.partial(derive, far, near)
        for plane, value in values.items():
            x = (plane - to * (block >> level)) * spacing

            def add(x=x, height=height, spacing=spacing, value=value):
                out[x, pl.ds(0, height, spacing), :] += value()

            found_here.append((x, add))
    return found_here


def add_message(*args):
    for _, add in additions(*args):
        add()


def copy_out(out, whole, done, part, parts):
    size = out.shape[0] // parts
    here = pl.ds(part * size, size)
    copy = pltpu.make_async_copy(out.at[here], whole.at[here], done.at[part])
    copy.start()
    return copy


def add_kernel(block, rows, places, last, own, *refs):
    received, refs = refs[: len(places)], refs[len(places) :]
    if last:
        whole, out, done, *clean = refs
    else:
        out, *clean = refs
    out[...] = own[...]
    for to, arrived in zip(places, received):
        add_message(block, rows, to, arrived, 0, out, clean)
    if last:
        for copy in [copy_out(out, whole, done, part, 2) for part in range(2)]:
            copy.wait()


def add_far(block, rows, right, arrived, base, out, clean):
    width, level = out.shape[-1], LEVELS - 1
    spacing, height, shift = 1 << level, rows >> level, shift_of(level)
    length = max(message(block, rows, to)[2] for to in (2, -2))
    lane = lax.broadcasted_iota(jnp.int32, (1, width), 1)
    value = pltpu.roll(arrived[base : base + length, :], width - shift, 1)
    value = jnp.where(lax.rem(lane, spacing) == 0, value, 0.0)
    for to, here in ((2, right), (-2, jnp.logical_not(right))):
        source = clean[0 if to > 0 else level]
        source[:length, :] = jnp.where(here, value, 0.0)
        sent, derived, _ = message(block, rows, to)
        parts = [(plane, at, 1.0) for (_, plane), (at, _) in sent.items()]
        parts += [
            (plane, sent[level, far][0], STEPS[3] / SCALE**2) for (_, plane), (far, _) in derived.items()
        ]
        for plane, at, factor in parts:
            x = (plane - to * (block >> level)) * spacing
            part = source[at : at + height, :]
            out[x, pl.ds(0, height, spacing), :] += part if factor == 1.0 else factor * part


def add_either(block, rows, right, step, arrived, base, out, clean):
    for side, here in ((step, right), (-step, jnp.logical_not(right))):

        @pl.when(here)
        def _():
            add_message(block, rows, side, arrived, base, out, clean)


def keep_kernel(block, rows, own, near, far, out, *clean):
    out[...] = own[...]
    core = lax.axis_index("gy")
    add_either(block, rows, takes_right(1), 1, half_of(near, core), 0, out, clean)
    add_far(block, rows, takes_right(2), half_of(far, core), 0, out, clean)


def half_of(arrived, core):
    size = arrived.shape[0] // 2
    return arrived.at[pl.ds(pl.multiple_of(core * size, 8), size)]


def pack_kernel(near, far, packed):
    one = near.shape[0] // 2
    other = 1 - lax.axis_index("gy")
    packed[:one, :] = half_of(near, other)[...]
    packed[one:, :] = half_of(far, other)[...]


def swap_kernel(block, rows, one, own, packed, whole, out, done, *clean):
    out[...] = own[...]
    add_far(block, rows, jnp.logical_not(takes_right(2)), packed, one, out, clean)
    right = jnp.logical_not(takes_right(1))
    for to, here in ((1, right), (-1, jnp.logical_not(right))):

        @pl.when(here)
        def _():
            tasks = additions(block, rows, to, packed, 0, out, clean)
            copies = []
            for part in ((1, 0) if to > 0 else (0, 1)):
                for x, add in tasks:
                    if 2 * x // block == part:
                        add()
                copies.append(copy_out(out, whole, done, part, 2))
            for copy in copies:
                copy.wait()


def call(body, name, outs, ins, scratch=(), flops=0, hbm_out=()):
    vmem, hbm = pl.BlockSpec(memory_space=pltpu.VMEM), pl.BlockSpec(memory_space=pltpu.HBM)
    f32 = jnp.float32
    shapes = [out if isinstance(out, jax.ShapeDtypeStruct) else jax.ShapeDtypeStruct(out, f32) for out in outs]
    moved = 4 * sum(int(np.prod(shape.shape)) for shape in shapes)
    return pl.pallas_call(
        body,
        out_shape=shapes,
        in_specs=[vmem] * len(ins),
        out_specs=[hbm if n in hbm_out else vmem for n in range(len(outs))],
        scratch_shapes=[pltpu.VMEM(shape, f32) if isinstance(shape, tuple) else shape for shape in scratch],
        compiler_params=pltpu.CompilerParams(vmem_limit_bytes=VMEM_BYTES),
        cost_estimate=pl.CostEstimate(flops=flops, bytes_accessed=2 * moved, transcendentals=0),
        name=name,
    )(*ins)


def local(velocity):
    block, rows, width = velocity.shape
    around, count = lax.axis_size("gx"), lax.axis_size("gy")
    shared = count == 2 and SHARED
    places = places_of(block)
    spans = windows(block)
    total = count * rows

    others = [
        lax.ppermute(velocity, "gy", [(i, (i - k) % count) for i in range(count)])
        for k in range(1, count)
    ]
    lifted = [
        (high - low + 1, total >> level, width) for level, (low, high) in enumerate(spans)
    ]
    coarse = [
        ((high // 2 - low // 2 + 1) * (total >> (level + 1)), width)
        for level, (low, high) in enumerate(spans[:-1])
    ]
    spread = (block * rows, width)
    part = (lifted[0][0], rows, width)
    owned = [(block >> level, rows >> level, width) for level in range(LEVELS)]
    lengths = {to: message(block, rows, to)[2] for to in places}
    one, two = max(lengths[1], lengths[-1]), max(lengths[2], lengths[-2])
    clean = [(one, width)] * LEVELS

    square = jax.ShapeDtypeStruct((2 * width, 3 * width), jnp.bfloat16)
    weights = call(matrix_kernel, "make_matrices", [square] * 2, [], flops=FIRST_FLOPS)
    (first,) = call(
        functools.partial(own_kernel, block, rows),
        "lift_own",
        [part],
        [velocity, weights[0]],
        [spread],
    )
    if shared:
        outs, scratch = ([(many * size, width) for size in (one, two)] for many in (2, 4))
    else:
        outs, scratch = [(lengths[to], width) for to in places], []
    values = call(
        functools.partial(message_kernel, block, rows, width, count, places),
        "make_messages",
        [part] * (count - 1) + lifted[1:] + outs,
        [first] + others + list(weights),
        [spread] + coarse + scratch,
    )
    before, messages = [first, *values[: count + LEVELS - 2]], values[count + LEVELS - 2 :]

    def rest():
        return call(
            functools.partial(rest_kernel, block, rows, width),
            "finish_own",
            [owned[0]],
            before,
            [(block >> LEVELS - 1, total >> LEVELS - 1, width)],
        )[0]

    written = [pltpu.SemaphoreType.DMA((2,))]
    if shared:
        near, far = (
            lax.ppermute(value, ("gx", "gy"), shared_pairs(step, around))
            for step, value in enumerate(messages, 1)
        )
        result = rest()
        (packed,) = call(pack_kernel, "pack_other", [(one + two, width)], [near, far])
        packed = lax.ppermute(packed, "gy", [(0, 1), (1, 0)])
        (result,) = call(
            functools.partial(keep_kernel, block, rows),
            "add_kept",
            [owned[0]],
            [result, near, far],
            clean,
        )
        (whole,) = call(
            functools.partial(swap_kernel, block, rows, one),
            "add_swapped",
            [owned[0]],
            [result, packed],
            [owned[0]] + written + clean,
            hbm_out=(0,),
        )
        return whole

    sent = dict(zip(places, messages))
    received = {
        to: lax.ppermute(sent[to], "gx", [(i, (i + to) % around) for i in range(around)])
        for to in sorted(places, key=lambda to: (to < 0, abs(to)))
    }
    right = [to for to in places if to > 0]
    left = [to for to in places if to < 0]
    (result,) = call(
        functools.partial(add_kernel, block, rows, right, False),
        "add_right",
        [owned[0]],
        [rest()] + [received[to] for to in right],
        clean,
        flops=FIRST_FLOPS,
    )
    (whole,) = call(
        functools.partial(add_kernel, block, rows, left, True),
        "add_left",
        [owned[0]],
        [result] + [received[to] for to in left],
        [owned[0]] + written + clean,
        hbm_out=(0,),
    )
    return whole


def solution(mesh):
    return jax.shard_map(
        local, mesh=mesh, in_specs=(P("gx", "gy", None),), out_specs=P("gx", "gy", None), check_vma=False
    )
```
